32 devices in a mesh: tiles: 2 (over x), rows: 16 (over z, y, core).
Axes of the slice: x: 2, y: 2, z: 4, core: 2. Of those that a mesh axis runs over, the one named last changes fastest.
Arguments:
- reflect: bfloat16 [128, 6, 32, 2048], P('rows', None, None, 'tiles'), parts along dimension 3, may hold values from 0 to 6.5
- clear_conf: int32 [128, 32, 2048], P('rows', None, 'tiles'), parts along dimension 2, may hold values from 0 to 100
- sun_view: int32 [128, 3, 32, 2048], P('rows', None, None, 'tiles'), parts along dimension 3, may hold values from 0 to 18000, as said below
- sensor_id: int32 [128], replicated, may hold values from 0 to 3
- band_gain: float32 [4, 6], replicated, may hold values from 0.5 to 1.5
- sensor_weight: float32 [4], replicated, may hold values from 0.5 to 2
- prior: float32 [32, 18, 2048], P('rows', None, 'tiles'), parts along dimension 2, may hold values from -1.75 to 1.75
Outputs:
- brdf_weights: float32 [32, 18, 2048], P('rows', None, 'tiles'), parts along dimension 2
The draws below stay inside these ranges and needn't reach their ends.
There are 2 independent parts, one for each index of `tiles`. The reference program is written for one: setup_inputs(seed, part) draws one part's arguments, and reference() takes and returns one part's arrays. A program takes and returns all parts, laid end to end along the dimension named above; an argument that names none is the same for every part. Nothing has to cross between parts.
Inputs may be any that keep to these rules, and one draw needn't show every extreme that they name: `sun_view`: component 0 is the solar zenith, 2000 to 7000; component 1 the view zenith, 0 to 1500; component 2 the relative azimuth, 0 to 18000.
All inputs are finite; a program needn't handle non-finite values.
Results may differ from the reference program's by a relative error of at most 0.0003.
Values may be sent and summed in bfloat16 or wider, within the bound.
No kernel may reach another device: no remote copies, remote signals or barrier semaphores. Data moves between devices by JAX's collectives and lax.ppermute only.
A program may use at most 128 MiB of HBM per device.

```python
import math
import jax
import jax.numpy as jnp
from jax import lax

DATES = 128
BANDS = 6
SENSORS = 4
COLS = 1024
ITERS = 3
COEFS = 18
ROWS_TOTAL = 32


def draw_reflect(key, part):
    key_albedo = jax.random.fold_in(key, 11)
    key_rough = jax.random.fold_in(key, 12)
    position = jnp.arange(ROWS_TOTAL, dtype=jnp.float32) / max(ROWS_TOTAL - 1, 1)
    rise = 3.0
    rough = jax.random.uniform(key_rough, (DATES, BANDS, ROWS_TOTAL, COLS), jnp.float32, 0.7, 1.3)
    gradient = jnp.exp(math.log(rise) * position)[None, None, :, None]
    albedo = jnp.exp(jax.random.uniform(key_albedo, (1, BANDS, ROWS_TOTAL, COLS), jnp.float32, math.log(0.05), math.log(0.5)))
    return (gradient * albedo * rough).astype(jnp.bfloat16)


def draw_sun_view(key, part):
    grid_shape = (DATES, 1, ROWS_TOTAL, COLS)
    sun_zen = jax.random.randint(jax.random.fold_in(key, 21), grid_shape, 2000, 7001, dtype=jnp.int32)
    view_zen = jax.random.randint(jax.random.fold_in(key, 22), grid_shape, 0, 1501, dtype=jnp.int32)
    azimuth = jax.random.randint(jax.random.fold_in(key, 23), grid_shape, 0, 18001, dtype=jnp.int32)
    return jnp.concatenate([sun_zen, view_zen, azimuth], axis=1)


def place_ends(values, rng, low, high):
    longest = values.shape.index(max(values.shape))
    spots = []
    for shift in (0, 1):
        where = [jax.random.randint(jax.random.fold_in(rng, axis), (), 0, length) for axis, length in enumerate(values.shape)]
        where[longest] = (where[longest] + shift) % values.shape[longest]
        spots.append(tuple(where))
    return values.at[spots[0]].set(low).at[spots[1]].set(high)


def shard_levels(stream_key, shape, shards, least, high):
    factor_of = 1.0
    for axis_at, blocks in shards:
        heights = jax.random.uniform(jax.random.fold_in(jax.random.fold_in(stream_key, 6), axis_at), (blocks,), jnp.float32, least / len(shards), high / len(shards))
        factor_of = factor_of * jnp.repeat(jnp.exp(heights), shape[axis_at] // blocks).reshape((-1,) + (1,) * (len(shape) - 1 - axis_at))
    return factor_of


def scatter_about(key, extent, scale, bound, pieces=(), kind=jnp.bfloat16):
    values = jax.random.normal(key, extent, jnp.float32) * scale
    if len(pieces) > 0:
        values = shard_levels(key, extent, pieces, -0.22, 0.18) * values
    return jnp.clip(values, min=-bound, max=bound).astype(kind)


def setup_inputs(seed: int = 0, part: int = 0) -> dict:
    seeds = jax.random.split(jax.random.key(seed), 8)
    part_keys = jax.random.split(jax.random.fold_in(seeds[7], part), 8)
    return {
        "reflect": draw_reflect(jax.random.fold_in(jax.random.fold_in(seeds[7], part), 71), part),
        "clear_conf": place_ends(jax.random.randint(part_keys[1], (DATES, ROWS_TOTAL, COLS), 0, 101), jax.random.fold_in(part_keys[1], 1), 0, 100).astype(jnp.int32),
        "sun_view": draw_sun_view(jax.random.fold_in(jax.random.fold_in(seeds[7], part), 71), part),
        "sensor_id": place_ends(jax.random.randint(seeds[3], (DATES,), 0, SENSORS), jax.random.fold_in(seeds[3], 1), 0, SENSORS - 1).astype(jnp.int32),
        "band_gain": jnp.clip(1.0 + 0.1 * jax.random.normal(seeds[4], (SENSORS, BANDS), jnp.float32), 0.5, 1.5),
        "sensor_weight": jnp.clip(jnp.exp(jax.random.uniform(seeds[5], (SENSORS,), jnp.float32, math.log(0.5), math.log(2.0))), 0.5, 2.0),
        "prior": scatter_about(part_keys[6], (ROWS_TOTAL, COEFS, COLS), 0.3, 1.75, ((0, 16),), jnp.float32),
    }


to_radian = math.pi / 18000.0
prior_pull = 0.1
smooth_pull = 0.5

def ross_li(sun_view):
    solar_zen = sun_view[:, 0].astype(jnp.float32) * to_radian
    view_zen = sun_view[:, 1].astype(jnp.float32) * to_radian
    azimuth = sun_view[:, 2].astype(jnp.float32) * to_radian
    cos_sun, sin_sun = (jnp.cos(solar_zen), jnp.sin(solar_zen))
    cos_view, sin_view = (jnp.cos(view_zen), jnp.sin(view_zen))
    cos_azim, sin_azim = (jnp.cos(azimuth), jnp.sin(azimuth))
    cos_phase = cos_sun * cos_view + sin_sun * sin_view * cos_azim
    phase_angle = jnp.arccos(cos_phase)
    volume = ((0.5 * math.pi - phase_angle) * cos_phase + jnp.sin(phase_angle)) / (cos_sun + cos_view) - 0.25 * math.pi
    tan_sun = sin_sun / cos_sun
    tan_view = sin_view / cos_view
    sec_sun = 1.0 / cos_sun
    sec_view = 1.0 / cos_view
    spread = tan_sun * tan_sun + tan_view * tan_view - 2.0 * tan_sun * tan_view * cos_azim
    cross_term = tan_sun * tan_view * sin_azim
    cos_correlation = jnp.minimum(2.0 * jnp.sqrt(spread + cross_term * cross_term) / (sec_sun + sec_view), 1.0)
    correlation_angle = jnp.arccos(cos_correlation)
    correlation = (correlation_angle - jnp.sin(correlation_angle) * cos_correlation) * (sec_sun + sec_view) / math.pi
    geometric = correlation - sec_sun - sec_view + 0.5 * (1.0 + cos_phase) * sec_sun * sec_view
    return (volume, geometric)

def normal_terms(reflect, clear_conf, sun_view, date_gain, date_weight):
    volume, geometric = ross_li(sun_view)
    weight = date_weight[:, None, None] * clear_conf.astype(jnp.float32) * 0.01
    weighted_vol = weight * volume
    weighted_geo = weight * geometric
    entries = [lax.optimization_barrier(jnp.sum(weight, 0)), lax.optimization_barrier(jnp.sum(weighted_vol, 0)), lax.optimization_barrier(jnp.sum(weighted_geo, 0)), lax.optimization_barrier(jnp.sum(weighted_vol * volume, 0)), lax.optimization_barrier(jnp.sum(weighted_vol * geometric, 0)), lax.optimization_barrier(jnp.sum(weighted_geo * geometric, 0))]
    signal = reflect.astype(jnp.float32) * date_gain[:, :, None, None]
    for band_index in range(signal.shape[1]):
        band_signal = signal[:, band_index]
        entries = entries + [lax.optimization_barrier(jnp.sum(weight * band_signal, 0)), lax.optimization_barrier(jnp.sum(weighted_vol * band_signal, 0)), lax.optimization_barrier(jnp.sum(weighted_geo * band_signal, 0))]
    return jnp.stack(entries, axis=1)

def couple(field, normal):
    row_count, coef_count, col_count = field.shape
    grouped = field.reshape(row_count, coef_count // 3, 3, col_count)
    iso_coef, vol_coef, geo_coef = (grouped[:, :, 0], grouped[:, :, 1], grouped[:, :, 2])
    entry = [normal[:, index_n:index_n + 1] for index_n in range(6)]
    result = jnp.stack([entry[0] * iso_coef + entry[1] * vol_coef + entry[2] * geo_coef, entry[1] * iso_coef + entry[3] * vol_coef + entry[4] * geo_coef, entry[2] * iso_coef + entry[4] * vol_coef + entry[5] * geo_coef], axis=2)
    return result.reshape(row_count, coef_count, col_count)

def apply_system(field, normal):
    row_count, coef_count, col_count = field.shape
    padded = jnp.pad(field, ((1, 1), (0, 0), (1, 1)))
    beside = padded[2:, :, 1:-1] + padded[:-2, :, 1:-1] + padded[1:-1, :, 2:] + padded[1:-1, :, :-2]
    row_pos = jnp.arange(row_count, dtype=jnp.int32)[:, None]
    col_pos = jnp.arange(col_count, dtype=jnp.int32)[None, :]
    degree = 4.0 - (row_pos == 0).astype(jnp.float32) - (row_pos == row_count - 1).astype(jnp.float32) - (col_pos == 0).astype(jnp.float32) - (col_pos == col_count - 1).astype(jnp.float32)
    return couple(field, normal) + prior_pull * field + smooth_pull * (degree[:, None, :] * field - beside)

def reference(reflect, clear_conf, sun_view, sensor_id, band_gain, sensor_weight, prior):
    date_gain = band_gain[sensor_id]
    date_weight = sensor_weight[sensor_id]
    block_count = DATES // 8

    def add_block(running, block_index):
        first_date = (block_index * 8).astype(jnp.int32)
        term = normal_terms(lax.dynamic_slice_in_dim(reflect, first_date, 8, 0), lax.dynamic_slice_in_dim(clear_conf, first_date, 8, 0), lax.dynamic_slice_in_dim(sun_view, first_date, 8, 0), lax.dynamic_slice_in_dim(date_gain, first_date, 8, 0), lax.dynamic_slice_in_dim(date_weight, first_date, 8, 0))
        return (running + term, None)
    start_sums = jnp.zeros((reflect.shape[2], 24, reflect.shape[3]), jnp.float32)
    sums, _ = lax.scan(add_block, start_sums, jnp.arange(block_count, dtype=jnp.int32))
    sums = sums * (1.0 / DATES)
    normal = sums[:, :6]
    target = sums[:, 6:] + prior_pull * prior
    solution = prior
    residual = target - apply_system(prior, normal)
    direction = residual
    rho_now = jnp.sum(residual * residual)
    for iteration in range(ITERS):
        image = apply_system(direction, normal)
        alpha = rho_now / jnp.sum(direction * image)
        solution = solution + alpha * direction
        residual = residual - alpha * image
        rho_next = jnp.sum(residual * residual)
        direction = residual + rho_next / rho_now * direction
        rho_now = rho_next
    return solution
```

```python
import functools
import math

import jax
import jax.numpy as jnp
from jax import lax
from jax.experimental import pallas as pl
from jax.experimental.pallas import tpu as pltpu
from jax.sharding import PartitionSpec as P

TO_RADIAN = math.pi / 18000.0
PRIOR_PULL = 0.1
SMOOTH_PULL = 0.5
SHIFT = 3.0
GAIN = 0.4
ENTRIES = 24
LANES = 128
QUANT = 32000.0
CHUNKS = 1

R_POLY = (0.9999997325, -0.07078975067, 0.01874461107, -0.007458902408, 0.003231534099, -0.001120316969, 0.0002021413586)
S_POLY = (0.5000000104, 0.1133791358, -0.01741075815, 0.006065742587, -0.002566941555, 0.0009184227696, -0.0001747441655)
SIN_25 = (0.9999999567, -0.1666626093, 0.008276695349)
COS_25 = (0.9999999997, -0.4999999562, 0.04166553086, -0.001379415437)
SIN_15 = (0.999999998, -0.1666661418, 0.008312938059)
COS_15 = (0.9999999858, -0.4999963087, 0.04152366947)
SIN_90 = (0.9999999947, -0.1666665666, 0.008333024663, -0.00019807389, 2.601844464e-06)


def horner(coefs, x):
    acc = coefs[-1] * x + coefs[-2]
    for coef in coefs[-3::-1]:
        acc = acc * x + coef
    return acc


def ross_li(sun, view, azim):
    x = (sun - 4500).astype(jnp.float32) * TO_RADIAN
    x2 = x * x
    half = math.sqrt(0.5)
    sin_x = horner([c * half for c in SIN_25], x2) * x
    cos_x = horner([c * half for c in COS_25], x2)
    cos_sun, sin_sun = cos_x - sin_x, cos_x + sin_x
    v = view.astype(jnp.float32) * TO_RADIAN
    v2 = v * v
    sin_view = horner(SIN_15, v2) * v
    cos_view = horner(COS_15, v2)
    a = (9000 - azim).astype(jnp.float32) * TO_RADIAN
    cos_azim = horner(SIN_90, a * a) * a
    prod = cos_sun * cos_view
    cos_phase = prod + sin_sun * sin_view * cos_azim
    total = cos_sun + cos_view
    recip = 1.0 / (total * prod)
    inv_total = recip * prod
    sec_prod = recip * total
    u = 1.0 - cos_phase
    u_up = 1.0 + cos_phase
    bent = u * (u * lax.rsqrt(u)) * horner(R_POLY, cos_phase)
    volume = (bent + (0.5 * math.pi) * cos_phase) * inv_total - 0.25 * math.pi
    sin2 = u * u_up
    sin_phase = sin2 * lax.rsqrt(sin2)
    cos_t = jnp.minimum((2.0 * inv_total) * sin_phase, 1.0)
    w = jnp.maximum(1.0 - cos_t, 1e-30)
    overlap = w * (w * lax.rsqrt(w)) * horner(S_POLY, cos_t)
    geometric = sec_prod * (total * (overlap - 1.0) + 0.5 * u_up)
    return volume, geometric


def encode(blocks, msg_ref):
    rows = blocks[0][0]().shape[0]
    top = None
    for block in blocks:
        for tile in block:
            size = jnp.abs(tile())
            top = size if top is None else jnp.maximum(top, size)
    level = jnp.ceil(8.0 * jnp.log2(jnp.maximum(top, 1e-30)))
    factor = QUANT * jnp.exp2(-0.125 * level)
    for j, block in enumerate(blocks):
        for c, tile in enumerate(block):
            msg_ref[j * rows : (j + 1) * rows, c * LANES : (c + 1) * LANES] = (
                jnp.round(tile() * factor).astype(jnp.int32).astype(jnp.int16)
            )
    base = len(blocks) * rows
    level = level.astype(jnp.int32).astype(jnp.int16)
    for c in range(len(blocks[0])):
        part = level[16 * c : 16 * c + 16] if 16 * c < rows else jnp.zeros((16, LANES), jnp.int16)
        msg_ref[base : base + 16, c * LANES : (c + 1) * LANES] = part


def decode_scale(msg_ref, rows):
    base = msg_ref.shape[0] - 16
    level = [msg_ref[base : base + 16, c * LANES : (c + 1) * LANES] for c in range(rows // 16)]
    level = jnp.concatenate(level, axis=0).astype(jnp.int32).astype(jnp.float32)
    return jnp.exp2(0.125 * level) * (1.0 / QUANT)


def decode(msg_ref, at, c, scale):
    return msg_ref[at, c * LANES : (c + 1) * LANES].astype(jnp.int32).astype(jnp.float32) * scale


def sums_kernel(
    me_ref, ids_ref, gain_ref, weight_ref, reflect_ref, conf_ref, sun_ref, prior_ref, keep_ref, msg_ref, sums_ref, *, scale, rows_here
):
    dates, bands, tile_rows, cols = reflect_ref.shape
    me = me_ref[0]
    block = rows_here * ENTRIES
    obs_count = 3 * bands
    tile_at = pl.program_id(0)
    base = pl.multiple_of(tile_at * (tile_rows * ENTRIES), 8)

    def lane_tile(index, carry):
        lanes = pl.ds(pl.multiple_of(index * LANES, LANES), LANES)
        for top in range(0, tile_rows, 8):
            acc = [None] * ENTRIES

            def add(entry, term):
                acc[entry] = term if acc[entry] is None else acc[entry] + term

            for d in range(dates):
                sensor = ids_ref[me * dates + d]
                volume, geometric = ross_li(
                    sun_ref[d, 0, top : top + 8, lanes], sun_ref[d, 1, top : top + 8, lanes], sun_ref[d, 2, top : top + 8, lanes]
                )
                weight = conf_ref[d, top : top + 8, lanes].astype(jnp.float32) * (weight_ref[sensor] * scale)
                weighted_vol = weight * volume
                weighted_geo = weight * geometric
                add(obs_count, weight)
                add(obs_count + 1, weighted_vol)
                add(obs_count + 2, weighted_geo)
                add(obs_count + 3, weighted_vol * volume)
                add(obs_count + 4, weighted_vol * geometric)
                add(obs_count + 5, weighted_geo * geometric)
                for b in range(bands):
                    tall = top // 16 * 16
                    signal = reflect_ref[d, b, tall : tall + 16, lanes].astype(jnp.float32)[top - tall : top - tall + 8]
                    signal = signal * gain_ref[sensor, b]
                    add(3 * b, weight * signal)
                    add(3 * b + 1, weighted_vol * signal)
                    add(3 * b + 2, weighted_geo * signal)
            for entry in range(ENTRIES):
                sums_ref[index, pl.ds(base + (top * ENTRIES + entry), 8, stride=ENTRIES), :] = acc[entry]
        return carry

    lax.fori_loop(0, cols // LANES, lane_tile, 0)

    @pl.when(tile_at == pl.num_programs(0) - 1)
    def _():
        rows = pl.num_programs(0) * tile_rows
        for row, source in ((me * rows_here - 1, 0), ((me + 1) * rows_here, rows_here - 1)):

            @pl.when((row >= 0) & (row < rows))
            def _():
                for c in range(cols // LANES):
                    lanes = slice(c * LANES, (c + 1) * LANES)
                    at = pl.ds(pl.multiple_of(row * ENTRIES, 8), obs_count)
                    part = jnp.concatenate([prior_ref[e, source : source + 1, lanes] for e in range(obs_count)], axis=0)
                    sums_ref[c, at, :] = sums_ref[c, at, :] + SMOOTH_PULL * part

        bit = me % 2
        tiles = range(cols // LANES)
        count = keep_ref.shape[0]
        for j in range(count):
            own = pl.ds(pl.multiple_of((2 * j + bit) * block, 8), block)
            for c in tiles:
                keep_ref[j, :, c * LANES : (c + 1) * LANES] = sums_ref[c, own, :]

        def tile(j, c):
            return lambda: sums_ref[c, pl.ds(pl.multiple_of((2 * j + 1 - bit) * block, 8), block), :]

        encode([[tile(j, c) for c in tiles] for j in range(count)], msg_ref)


def partial_sums(me, reflect, clear_conf, sun_view, sensor_id, band_gain, sensor_weight, prior, scale, chunk, width):
    dates, bands, rows, cols = reflect.shape
    rows_here = prior.shape[1]
    count = rows // rows_here
    tile_rows = 16
    block = rows_here * ENTRIES
    smem = pl.BlockSpec(memory_space=pltpu.SMEM)
    return pl.pallas_call(
        functools.partial(sums_kernel, scale=scale, rows_here=rows_here),
        grid=(rows // tile_rows,),
        in_specs=[
            smem,
            smem,
            smem,
            smem,
            pl.BlockSpec((dates, bands, tile_rows, width), lambda i: (0, 0, i, chunk)),
            pl.BlockSpec((dates, tile_rows, width), lambda i: (0, i, chunk)),
            pl.BlockSpec((dates, 3, tile_rows, width), lambda i: (0, 0, i, chunk)),
            pl.BlockSpec((3 * bands, rows_here, width), lambda i: (0, 0, chunk)),
        ],
        out_specs=[
            pl.BlockSpec((count // 2, block, width), lambda i: (0, 0, 0)),
            pl.BlockSpec((count // 2 * block + 16, width), lambda i: (0, 0)),
        ],
        out_shape=[
            jax.ShapeDtypeStruct((count // 2, block, width), jnp.float32),
            jax.ShapeDtypeStruct((count // 2 * block + 16, width), jnp.int16),
        ],
        scratch_shapes=[pltpu.VMEM((width // LANES, rows * ENTRIES, LANES), jnp.float32)],
        compiler_params=pltpu.CompilerParams(vmem_limit_bytes=60 * 2**20),
        name="partial_sums",
    )(me, sensor_id, band_gain, sensor_weight, reflect, clear_conf, sun_view, prior)


def add_split_kernel(bit_ref, kept_ref, got_ref, keep_ref, msg_ref):
    count, block, cols = keep_ref.shape
    bit = bit_ref[0]
    scale = decode_scale(got_ref, block)
    tiles = range(cols // LANES)

    def total(j, c):
        at = pl.ds(pl.multiple_of(j * block, 16), block)
        return kept_ref[j, :, c * LANES : (c + 1) * LANES] + decode(got_ref, at, c, scale)

    for j in range(count):
        for c in tiles:
            keep_ref[j, :, c * LANES : (c + 1) * LANES] = total(2 * j + bit, c)
    others = [[total(2 * j + 1 - bit, c) for c in tiles] for j in range(count)]
    encode([[functools.partial(lambda x: x, others[j][c]) for c in tiles] for j in range(count)], msg_ref)


def add_split(bit, kept, got):
    count, block, cols = kept.shape
    vmem = pl.BlockSpec(memory_space=pltpu.VMEM)
    return pl.pallas_call(
        add_split_kernel,
        in_specs=[pl.BlockSpec(memory_space=pltpu.SMEM), vmem, vmem],
        out_specs=[vmem, vmem],
        out_shape=[
            jax.ShapeDtypeStruct((count // 2, block, cols), jnp.float32),
            jax.ShapeDtypeStruct((count // 2 * block + 16, cols), jnp.int16),
        ],
        compiler_params=pltpu.CompilerParams(vmem_limit_bytes=24 * 2**20),
        name="add_split",
    )(bit, kept, got)


def take(ref, start, size, stride):
    at = pl.ds(start, size, stride=stride)
    return jnp.concatenate([ref[c, at, :] for c in range(ref.shape[0])], axis=1)


def put(ref, start, size, stride, value):
    at = pl.ds(start, size, stride=stride)
    for c in range(ref.shape[0]):
        ref[c, at, :] = value[:, c * LANES : (c + 1) * LANES]


def beside_columns(x):
    cols = x.shape[1]
    col = lax.broadcasted_iota(jnp.int32, x.shape, 1)
    left = jnp.where(col == 0, 0.0, pltpu.roll(x, 1, axis=1))
    right = jnp.where(col == cols - 1, 0.0, pltpu.roll(x, cols - 1, axis=1))
    return left + right


def degree_of(row, shape, total_rows):
    col = lax.broadcasted_iota(jnp.int32, shape, 1)
    edge = (
        (row == 0).astype(jnp.float32)
        + (row == total_rows - 1).astype(jnp.float32)
        + (col == 0).astype(jnp.float32)
        + (col == shape[1] - 1).astype(jnp.float32)
    )
    return 4.0 - edge


def couple(n, v):
    return (
        n[0] * v[0] + n[1] * v[1] + n[2] * v[2],
        n[1] * v[0] + n[3] * v[1] + n[4] * v[2],
        n[2] * v[0] + n[4] * v[1] + n[5] * v[2],
    )


def residual_kernel(me_ref, prior_ref, *refs, total_rows):
    obs_count, rows_here, cols = prior_ref.shape
    *parts, out_ref, sums_ref = refs
    block = rows_here * ENTRIES
    at = 0
    for kept_ref, got_ref in zip(parts[0::2], parts[1::2]):
        scale = decode_scale(got_ref, block)
        for c in range(kept_ref.shape[2] // LANES):
            sums_ref[at] = kept_ref[0, :, c * LANES : (c + 1) * LANES] + decode(got_ref, slice(0, block), c, scale)
            at += 1
    shape = (rows_here, cols)
    row = me_ref[0] * rows_here + lax.broadcasted_iota(jnp.int32, shape, 0)
    degree = degree_of(row, shape, total_rows)
    normal = [take(sums_ref, obs_count + k, rows_here, ENTRIES) for k in range(6)]
    for b in range(obs_count // 3):
        fields = [prior_ref[3 * b + i] for i in range(3)]
        coupled = couple(normal, fields)
        for i in range(3):
            field = fields[i]
            beside = beside_columns(field)
            if rows_here > 1:
                zero = jnp.zeros((1, cols), jnp.float32)
                beside = beside + jnp.concatenate([zero, field[:-1]], axis=0) + jnp.concatenate([field[1:], zero], axis=0)
            entry = 3 * b + i
            observed = take(sums_ref, entry, rows_here, ENTRIES)
            put(sums_ref, entry, rows_here, ENTRIES, observed - coupled[i] - SMOOTH_PULL * (degree * field - beside))
    for c in range(cols // LANES):
        out_ref[:, c * LANES : (c + 1) * LANES] = sums_ref[c]


def krylov_kernel(me_ref, own_ref, mate_ref, across_ref, far_ref, zero_ref, one_ref, two_ref, gram_ref, window_ref, *, total_rows, rows_here):
    cols = own_ref.shape[1]
    obs_count = ENTRIES - 6
    def lay(place, ref, r):
        put(window_ref, place, ENTRIES, 8, ref[r * ENTRIES : (r + 1) * ENTRIES, :])

    lay(2, own_ref, 0)
    lay(3, own_ref, 1)
    put(window_ref, 7, ENTRIES, 8, jnp.zeros((ENTRIES, cols), jnp.float32))

    @pl.when(me_ref[0] % 2 == 0)
    def _():
        lay(0, across_ref, 0)
        lay(1, across_ref, 1)
        lay(4, mate_ref, 0)
        lay(5, mate_ref, 1)
        lay(6, far_ref, 0)

    @pl.when(me_ref[0] % 2 == 1)
    def _():
        lay(0, mate_ref, 0)
        lay(1, mate_ref, 1)
        lay(4, across_ref, 0)
        lay(5, across_ref, 1)
        lay(6, across_ref, 2)

    window = lambda entry: jnp.concatenate([window_ref[c, entry * 8 : entry * 8 + 8, :] for c in range(cols // LANES)], axis=1)
    shape = (8, cols)
    place = lax.broadcasted_iota(jnp.int32, shape, 0)
    row = me_ref[0] * rows_here + place - 2
    inside = ((row >= 0) & (row < total_rows)).astype(jnp.float32) * GAIN
    own = (place == 2) | (place == 3)
    diag = inside * (PRIOR_PULL - SHIFT + SMOOTH_PULL * degree_of(row, shape, total_rows))
    pull = inside * SMOOTH_PULL
    normal = [window(obs_count + k) * inside for k in range(6)]
    acc = [jnp.zeros((8, LANES), jnp.float32) for _ in range(6)]

    def apply(v, last=False):
        coupled = couple(normal, v)
        out = []
        for i in range(3):
            x = v[i]
            above = pltpu.roll(x, 7, axis=0)
            beside = beside_columns(x) + (2.0 * above if last else above + pltpu.roll(x, 1, axis=0))
            out.append(coupled[i] + diag * x - pull * beside)
        return out

    def fold(x):
        total = x[:, 0:LANES]
        for c in range(LANES, cols, LANES):
            total = total + x[:, c : c + LANES]
        return total

    for b in range(obs_count // 3):
        zero = [window(3 * b + i) for i in range(3)]
        one = apply(zero)
        two = apply(one)
        three = apply(two, last=True)
        for i in range(3):
            zero_ref[3 * b + i] = zero[i][2:4]
            one_ref[3 * b + i] = one[i][2:4]
            two_ref[3 * b + i] = two[i][2:4]
            v = [zero[i], one[i], two[i], three[i]]
            for k in range(6):
                acc[k] = acc[k] + fold(v[k // 2] * v[(k + 1) // 2])
    own_tile = own[:, 0:LANES]
    tile_row = lax.broadcasted_iota(jnp.int32, (8, LANES), 0)
    gram = jnp.zeros((8, LANES), jnp.float32)
    for k in range(6):
        moment = jnp.sum(jnp.where(own_tile, acc[k], 0.0))
        gram = jnp.where(tile_row == k, moment, gram)
    gram_ref[...] = gram


def combine_kernel(gram_ref, last_ref, prior_ref, zero_ref, one_ref, two_ref, out_ref):
    gram = gram_ref[...] + last_ref[...]
    m = [gram[k : k + 1, :] for k in range(6)]
    h = {(i, j): m[i + j + 1] * (1.0 / GAIN) + SHIFT * m[i + j] for i in range(3) for j in range(i, 3)}
    l10 = h[0, 1] / h[0, 0]
    l20 = h[0, 2] / h[0, 0]
    d1 = h[1, 1] - l10 * h[0, 1]
    t = h[1, 2] - l20 * h[0, 1]
    ok1 = d1 > 1e-6 * h[1, 1]
    inv1 = jnp.where(ok1, 1.0 / jnp.where(ok1, d1, 1.0), 0.0)
    l21 = t * inv1
    d2 = h[2, 2] - l20 * h[0, 2] - l21 * t
    ok2 = ok1 & (d2 > 1e-6 * h[2, 2])
    inv2 = jnp.where(ok2, 1.0 / jnp.where(ok2, d2, 1.0), 0.0)
    z1 = m[1] - l10 * m[0]
    z2 = m[2] - l20 * m[0] - l21 * z1
    y2 = z2 * inv2
    y1 = z1 * inv1 - l21 * y2
    y0 = m[0] / h[0, 0] - l10 * y1 - l20 * y2
    cols = prior_ref.shape[2]
    for c in range(0, cols, LANES):
        lanes = slice(c, c + LANES)
        out_ref[:, :, lanes] = (
            prior_ref[:, :, lanes] + y0[None] * zero_ref[:, :, lanes] + y1[None] * one_ref[:, :, lanes] + y2[None] * two_ref[:, :, lanes]
        )


def swap(x, count, step):
    return lax.ppermute(x, "rows", [(i, i ^ step) for i in range(count)])


def on_device(reflect, clear_conf, sun_view, sensor_id, band_gain, sensor_weight, prior):
    rows_here, obs_count, cols = prior.shape
    prior = jnp.transpose(prior, (1, 0, 2))
    count = lax.axis_size("rows")
    total_rows = rows_here * count
    block = rows_here * ENTRIES
    index = lax.axis_index("rows").astype(jnp.int32)
    me = index.reshape(1)
    vmem = pl.BlockSpec(memory_space=pltpu.VMEM)
    smem = pl.BlockSpec(memory_space=pltpu.SMEM)
    params = pltpu.CompilerParams(vmem_limit_bytes=24 * 2**20)
    f32 = lambda *shape: jax.ShapeDtypeStruct(shape, jnp.float32)

    width = cols // CHUNKS
    scale = 0.01 / (reflect.shape[0] * count)
    parts = []
    for chunk in range(CHUNKS):
        kept, sent = partial_sums(
            me, reflect, clear_conf, sun_view, sensor_id, band_gain, sensor_weight, prior, scale, chunk, width
        )
        step = 1
        while True:
            got = swap(sent, count, step)
            step *= 2
            if step == count:
                break
            kept, sent = add_split((index // step % 2).reshape(1), kept, got)
        parts += [kept, got]

    own = pl.pallas_call(
        functools.partial(residual_kernel, total_rows=total_rows),
        in_specs=[smem] + [vmem] * (1 + len(parts)),
        out_specs=vmem,
        out_shape=f32(block, cols),
        scratch_shapes=[pltpu.VMEM((cols // LANES, block, LANES), jnp.float32)],
        compiler_params=params,
        name="residual",
    )(me, prior, *parts)

    mate = swap(own, count, 1)
    border = [(i, i + 1) for i in range(1, count - 1, 2)]
    across = lax.ppermute(
        jnp.concatenate([own, mate[:ENTRIES]], axis=0), "rows", border + [(target, source) for source, target in border]
    )
    far = swap(across[:ENTRIES], count, 1)
    zero, one, two, gram = pl.pallas_call(
        functools.partial(krylov_kernel, total_rows=total_rows, rows_here=rows_here),
        in_specs=[smem, vmem, vmem, vmem, vmem],
        out_specs=[vmem] * 4,
        out_shape=[f32(obs_count, rows_here, cols)] * 3 + [f32(8, LANES)],
        scratch_shapes=[pltpu.VMEM((cols // LANES, ENTRIES * 8, LANES), jnp.float32)],
        compiler_params=params,
        name="krylov",
    )(me, own, mate, across, far)

    step = 1
    while True:
        other = swap(gram, count, step)
        step *= 2
        if step == count:
            break
        gram = gram + other
    out = pl.pallas_call(
        combine_kernel,
        in_specs=[vmem] * 6,
        out_specs=vmem,
        out_shape=f32(obs_count, rows_here, cols),
        compiler_params=params,
        name="combine",
    )(gram, other, prior, zero, one, two)
    return jnp.transpose(out, (1, 0, 2))


def solution(mesh):
    return jax.shard_map(
        on_device,
        mesh=mesh,
        in_specs=(
            P("rows", None, None, "tiles"),
            P("rows", None, "tiles"),
            P("rows", None, None, "tiles"),
            P(),
            P(),
            P(),
            P("rows", None, "tiles"),
        ),
        out_specs=P("rows", None, "tiles"),
        check_vma=False,
    )
```

```python
import functools
import math

import jax
import jax.numpy as jnp
from jax import lax
from jax.experimental import pallas as pl
from jax.experimental.pallas import tpu as pltpu
from jax.sharding import PartitionSpec as P

TO_RADIAN = math.pi / 18000.0
PRIOR_PULL = 0.1
SMOOTH_PULL = 0.5
SHIFT = 3.0
GAIN = 0.4
ENTRIES = 24
LANES = 128
QUANT = 32000.0
GROUP = LANES // 4

R_POLY = (0.9999997325, -0.07078975067, 0.01874461107, -0.007458902408, 0.003231534099, -0.001120316969, 0.0002021413586)
S_POLY = (0.5000000104, 0.1133791358, -0.01741075815, 0.006065742587, -0.002566941555, 0.0009184227696, -0.0001747441655)
SIN_25 = (0.9999999567, -0.1666626093, 0.008276695349)
COS_25 = (0.9999999997, -0.4999999562, 0.04166553086, -0.001379415437)
SIN_15 = (0.999999998, -0.1666661418, 0.008312938059)
COS_15 = (0.9999999858, -0.4999963087, 0.04152366947)
SIN_90 = (0.9999999947, -0.1666665666, 0.008333024663, -0.00019807389, 2.601844464e-06)


def horner(coefs, x):
    acc = coefs[-1] * x + coefs[-2]
    for coef in coefs[-3::-1]:
        acc = acc * x + coef
    return acc


def ross_li(sun, view, azim):
    x = (sun - 4500).astype(jnp.float32) * TO_RADIAN
    x2 = x * x
    half = math.sqrt(0.5)
    sin_x = horner([c * half for c in SIN_25], x2) * x
    cos_x = horner([c * half for c in COS_25], x2)
    cos_sun, sin_sun = cos_x - sin_x, cos_x + sin_x
    v = view.astype(jnp.float32) * TO_RADIAN
    v2 = v * v
    sin_view = horner(SIN_15, v2) * v
    cos_view = horner(COS_15, v2)
    a = (9000 - azim).astype(jnp.float32) * TO_RADIAN
    cos_azim = horner(SIN_90, a * a) * a
    prod = cos_sun * cos_view
    cos_phase = prod + sin_sun * sin_view * cos_azim
    total = cos_sun + cos_view
    recip = 1.0 / (total * prod)
    inv_total = recip * prod
    sec_prod = recip * total
    u = 1.0 - cos_phase
    u_up = 1.0 + cos_phase
    bent = u * (u * lax.rsqrt(u)) * horner(R_POLY, cos_phase)
    volume = (bent + (0.5 * math.pi) * cos_phase) * inv_total - 0.25 * math.pi
    sin2 = u * u_up
    sin_phase = sin2 * lax.rsqrt(sin2)
    cos_t = jnp.minimum((2.0 * inv_total) * sin_phase, 1.0)
    w = jnp.maximum(1.0 - cos_t, 1e-30)
    overlap = w * (w * lax.rsqrt(w)) * horner(S_POLY, cos_t)
    geometric = sec_prod * (total * (overlap - 1.0) + 0.5 * u_up)
    return volume, geometric


def encode(blocks, msg_ref):
    rows = blocks[0][0]().shape[0]
    top = None
    for block in blocks:
        for tile in block:
            size = jnp.abs(tile())
            top = size if top is None else jnp.maximum(top, size)
    level = jnp.ceil(8.0 * jnp.log2(jnp.maximum(top, 1e-30)))
    factor = QUANT * jnp.exp2(-0.125 * level)
    for j, block in enumerate(blocks):
        for c, tile in enumerate(block):
            msg_ref[j * rows : (j + 1) * rows, c * LANES : (c + 1) * LANES] = (
                jnp.round(tile() * factor).astype(jnp.int32).astype(jnp.int16)
            )
    base = len(blocks) * rows
    level = level.astype(jnp.int32).astype(jnp.int16)
    for c in range(len(blocks[0])):
        part = level[16 * c : 16 * c + 16] if 16 * c < rows else jnp.zeros((16, LANES), jnp.int16)
        msg_ref[base : base + 16, c * LANES : (c + 1) * LANES] = part


def decode_scale(msg_ref, rows):
    base = msg_ref.shape[0] - 16
    level = [msg_ref[base : base + 16, c * LANES : (c + 1) * LANES] for c in range(rows // 16)]
    level = jnp.concatenate(level, axis=0).astype(jnp.int32).astype(jnp.float32)
    return jnp.exp2(0.125 * level) * (1.0 / QUANT)


def decode(msg_ref, at, c, scale):
    return msg_ref[at, c * LANES : (c + 1) * LANES].astype(jnp.int32).astype(jnp.float32) * scale


def lane_group(shape):
    return lax.broadcasted_iota(jnp.int32, shape, len(shape) - 1) // GROUP


def pack(tiles, write):
    rows = tiles[0].shape[0]
    top = jnp.abs(tiles[0])
    for tile in tiles[1:]:
        top = jnp.maximum(top, jnp.abs(tile))
    for shift in (LANES // 2, LANES // 4):
        top = jnp.maximum(top, pltpu.roll(top, shift, axis=1))
    level = jnp.ceil(8.0 * jnp.log2(jnp.maximum(top, 1e-30)))
    factor = QUANT * jnp.exp2(-0.125 * level)
    group = lane_group((16, LANES))
    scales = level[0:16]
    for t in range(1, rows // 16):
        scales = jnp.where(group == t, level[16 * t : 16 * t + 16], scales)
    write(0, scales.astype(jnp.int32).astype(jnp.int16))
    for c, tile in enumerate(tiles):
        coded = jnp.round(tile * factor).astype(jnp.int32).astype(jnp.int16)
        for t in range(rows // 16):
            write(1 + t * len(tiles) + c, coded[16 * t : 16 * t + 16])


def unpack(read, row_tiles, col_tiles):
    as_float = lambda x: x.astype(jnp.int32).astype(jnp.float32)
    scales = as_float(read(0))
    group = lane_group((16, LANES))
    factors = []
    for t in range(row_tiles):
        level = jnp.where(group == t, scales, 0.0)
        for shift in (LANES // 2, LANES // 4):
            level = level + pltpu.roll(level, shift, axis=1)
        factors.append(jnp.exp2(0.125 * level) * (1.0 / QUANT))
    return [
        jnp.concatenate([as_float(read(1 + t * col_tiles + c)) * factors[t] for t in range(row_tiles)], axis=0) for c in range(col_tiles)
    ]


def sums_kernel(
    me_ref, ids_ref, gain_ref, weight_ref, reflect_ref, conf_ref, sun_ref, prior_ref, keep_ref, msg_ref, sums_ref, *, scale, rows_here
):
    dates, bands, tile_rows, cols = reflect_ref.shape
    me = me_ref[0]
    block = rows_here * ENTRIES
    obs_count = 3 * bands
    base = pl.multiple_of(pl.program_id(0) * (tile_rows * ENTRIES), 8)
    first_tile = pl.program_id(1) * (cols // LANES)

    def lane_tile(index, carry):
        lanes = pl.ds(pl.multiple_of(index * LANES, LANES), LANES)
        for top in range(0, tile_rows, 8):
            acc = [None] * ENTRIES

            def add(entry, term):
                acc[entry] = term if acc[entry] is None else acc[entry] + term

            for d in range(dates):
                sensor = ids_ref[me * dates + d]
                volume, geometric = ross_li(
                    sun_ref[d, 0, top : top + 8, lanes], sun_ref[d, 1, top : top + 8, lanes], sun_ref[d, 2, top : top + 8, lanes]
                )
                weight = conf_ref[d, top : top + 8, lanes].astype(jnp.float32) * (weight_ref[sensor] * scale)
                weighted_vol = weight * volume
                weighted_geo = weight * geometric
                add(obs_count, weight)
                add(obs_count + 1, weighted_vol)
                add(obs_count + 2, weighted_geo)
                add(obs_count + 3, weighted_vol * volume)
                add(obs_count + 4, weighted_vol * geometric)
                add(obs_count + 5, weighted_geo * geometric)
                for b in range(bands):
                    tall = top // 16 * 16
                    signal = reflect_ref[d, b, tall : tall + 16, lanes].astype(jnp.float32)[top - tall : top - tall + 8]
                    signal = signal * gain_ref[sensor, b]
                    add(3 * b, weight * signal)
                    add(3 * b + 1, weighted_vol * signal)
                    add(3 * b + 2, weighted_geo * signal)
            for entry in range(ENTRIES):
                sums_ref[first_tile + index, pl.ds(base + (top * ENTRIES + entry), 8, stride=ENTRIES), :] = acc[entry]
        return carry

    lax.fori_loop(0, cols // LANES, lane_tile, 0)

    @pl.when((pl.program_id(0) == pl.num_programs(0) - 1) & (pl.program_id(1) == pl.num_programs(1) - 1))
    def _():
        rows = pl.num_programs(0) * tile_rows
        for row, source in ((me * rows_here - 1, 0), ((me + 1) * rows_here, rows_here - 1)):

            @pl.when((row >= 0) & (row < rows))
            def _():
                for c in range(sums_ref.shape[0]):
                    lanes = slice(c * LANES, (c + 1) * LANES)
                    at = pl.ds(pl.multiple_of(row * ENTRIES, 8), obs_count)
                    part = jnp.concatenate([prior_ref[e, source : source + 1, lanes] for e in range(obs_count)], axis=0)
                    sums_ref[c, at, :] = sums_ref[c, at, :] + SMOOTH_PULL * part

        bit = me % 2
        tiles = range(sums_ref.shape[0])
        count = keep_ref.shape[0]
        for j in range(count):
            own = pl.ds(pl.multiple_of((2 * j + bit) * block, 8), block)
            for c in tiles:
                keep_ref[j, :, c * LANES : (c + 1) * LANES] = sums_ref[c, own, :]

        def tile(j, c):
            return lambda: sums_ref[c, pl.ds(pl.multiple_of((2 * j + 1 - bit) * block, 8), block), :]

        encode([[tile(j, c) for c in tiles] for j in range(count)], msg_ref)


def partial_sums(me, reflect, clear_conf, sun_view, sensor_id, band_gain, sensor_weight, prior, scale):
    dates, bands, rows, cols = reflect.shape
    rows_here = prior.shape[1]
    count = rows // rows_here
    tile_rows = 16
    width = min(256, cols)
    block = rows_here * ENTRIES
    smem = pl.BlockSpec(memory_space=pltpu.SMEM)
    return pl.pallas_call(
        functools.partial(sums_kernel, scale=scale, rows_here=rows_here),
        grid=(rows // tile_rows, cols // width),
        in_specs=[
            smem,
            smem,
            smem,
            smem,
            pl.BlockSpec((dates, bands, tile_rows, width), lambda i, j: (0, 0, i, j)),
            pl.BlockSpec((dates, tile_rows, width), lambda i, j: (0, i, j)),
            pl.BlockSpec((dates, 3, tile_rows, width), lambda i, j: (0, 0, i, j)),
            pl.BlockSpec((3 * bands, rows_here, cols), lambda i, j: (0, 0, 0)),
        ],
        out_specs=[
            pl.BlockSpec((count // 2, block, cols), lambda i, j: (0, 0, 0)),
            pl.BlockSpec((count // 2 * block + 16, cols), lambda i, j: (0, 0)),
        ],
        out_shape=[
            jax.ShapeDtypeStruct((count // 2, block, cols), jnp.float32),
            jax.ShapeDtypeStruct((count // 2 * block + 16, cols), jnp.int16),
        ],
        scratch_shapes=[pltpu.VMEM((cols // LANES, rows * ENTRIES, LANES), jnp.float32)],
        compiler_params=pltpu.CompilerParams(vmem_limit_bytes=60 * 2**20),
        name="partial_sums",
    )(me, sensor_id, band_gain, sensor_weight, reflect, clear_conf, sun_view, prior)


def add_pack_kernel(kept_ref, got_ref, msg_ref):
    count, block, cols = kept_ref.shape
    scale = decode_scale(got_ref, block)

    def one(j, carry):
        at = pl.ds(pl.multiple_of(j * block, 16), block)
        tiles = [
            kept_ref[j, :, c * LANES : (c + 1) * LANES] + decode(got_ref, at, c, scale) for c in range(cols // LANES)
        ]

        def write(place, tile):
            msg_ref[j, place] = tile

        pack(tiles, write)
        return carry

    lax.fori_loop(0, count, one, 0)


def add_pack(kept, got):
    count, block, cols = kept.shape
    vmem = pl.BlockSpec(memory_space=pltpu.VMEM)
    return pl.pallas_call(
        add_pack_kernel,
        in_specs=[vmem, vmem],
        out_specs=vmem,
        out_shape=jax.ShapeDtypeStruct((count, 1 + block // 16 * (cols // LANES), 16, LANES), jnp.int16),
        compiler_params=pltpu.CompilerParams(vmem_limit_bytes=24 * 2**20),
        name="add_pack",
    )(kept, got)


def take(ref, start, size, stride):
    at = pl.ds(start, size, stride=stride)
    return jnp.concatenate([ref[c, at, :] for c in range(ref.shape[0])], axis=1)


def put(ref, start, size, stride, value):
    at = pl.ds(start, size, stride=stride)
    for c in range(ref.shape[0]):
        ref[c, at, :] = value[:, c * LANES : (c + 1) * LANES]


def beside_columns(x):
    cols = x.shape[1]
    col = lax.broadcasted_iota(jnp.int32, x.shape, 1)
    left = jnp.where(col == 0, 0.0, pltpu.roll(x, 1, axis=1))
    right = jnp.where(col == cols - 1, 0.0, pltpu.roll(x, cols - 1, axis=1))
    return left + right


def degree_of(row, shape, total_rows):
    col = lax.broadcasted_iota(jnp.int32, shape, 1)
    edge = (
        (row == 0).astype(jnp.float32)
        + (row == total_rows - 1).astype(jnp.float32)
        + (col == 0).astype(jnp.float32)
        + (col == shape[1] - 1).astype(jnp.float32)
    )
    return 4.0 - edge


def couple(n, v):
    return (
        n[0] * v[0] + n[1] * v[1] + n[2] * v[2],
        n[1] * v[0] + n[3] * v[1] + n[4] * v[2],
        n[2] * v[0] + n[4] * v[1] + n[5] * v[2],
    )


def residual_kernel(me_ref, prior_ref, got_ref, out_ref, msg_ref, sums_ref, *, total_rows):
    obs_count, rows_here, cols = prior_ref.shape
    block = rows_here * ENTRIES
    tiles = cols // LANES
    for j in range(got_ref.shape[0]):
        part = unpack(lambda place: got_ref[j, place], block // 16, tiles)
        for c in range(tiles):
            sums_ref[c] = part[c] if j == 0 else sums_ref[c] + part[c]
    shape = (rows_here, cols)
    row = me_ref[0] * rows_here + lax.broadcasted_iota(jnp.int32, shape, 0)
    degree = degree_of(row, shape, total_rows)
    normal = [take(sums_ref, obs_count + k, rows_here, ENTRIES) for k in range(6)]
    for b in range(obs_count // 3):
        fields = [prior_ref[3 * b + i] for i in range(3)]
        coupled = couple(normal, fields)
        for i in range(3):
            field = fields[i]
            beside = beside_columns(field)
            if rows_here > 1:
                zero = jnp.zeros((1, cols), jnp.float32)
                beside = beside + jnp.concatenate([zero, field[:-1]], axis=0) + jnp.concatenate([field[1:], zero], axis=0)
            entry = 3 * b + i
            observed = take(sums_ref, entry, rows_here, ENTRIES)
            put(sums_ref, entry, rows_here, ENTRIES, observed - coupled[i] - SMOOTH_PULL * (degree * field - beside))
    for c in range(tiles):
        out_ref[:, c * LANES : (c + 1) * LANES] = sums_ref[c]

    def write(place, tile):
        msg_ref[place] = tile

    pack([sums_ref[c] for c in range(tiles)], write)


def krylov_kernel(me_ref, own_ref, low_ref, high_ref, far_ref, zero_ref, one_ref, two_ref, gram_ref, window_ref, *, total_rows, rows_here):
    cols = own_ref.shape[1]
    obs_count = ENTRIES - 6
    tiles = cols // LANES
    row_tiles = own_ref.shape[0] // 16

    def lay(place, part, r):
        at = pl.ds(place, ENTRIES, stride=8)
        for c in range(tiles):
            window_ref[c, at, :] = part[c][r * ENTRIES : (r + 1) * ENTRIES]

    own = [own_ref[:, c * LANES : (c + 1) * LANES] for c in range(tiles)]
    low = unpack(lambda place: low_ref[place], row_tiles, tiles)
    high = unpack(lambda place: high_ref[place], row_tiles, tiles)
    far = unpack(lambda place: far_ref[place], 2, tiles)
    pieces = [(0, low, 0), (1, low, 1), (2, own, 0), (3, own, 1), (4, high, 0), (5, high, 1), (6, far, 0)]
    for piece in pieces:
        lay(*piece)
    put(window_ref, 7, ENTRIES, 8, jnp.zeros((ENTRIES, cols), jnp.float32))
    window = lambda entry: jnp.concatenate([window_ref[c, entry * 8 : entry * 8 + 8, :] for c in range(cols // LANES)], axis=1)
    shape = (8, cols)
    place = lax.broadcasted_iota(jnp.int32, shape, 0)
    row = me_ref[0] * rows_here + place - 2
    inside = ((row >= 0) & (row < total_rows)).astype(jnp.float32) * GAIN
    own_rows = (place == 2) | (place == 3)
    diag = inside * (PRIOR_PULL - SHIFT + SMOOTH_PULL * degree_of(row, shape, total_rows))
    pull = inside * SMOOTH_PULL
    normal = [window(obs_count + k) * inside for k in range(6)]
    acc = [jnp.zeros((8, LANES), jnp.float32) for _ in range(6)]

    def apply(v, last=False):
        coupled = couple(normal, v)
        out = []
        for i in range(3):
            x = v[i]
            above = pltpu.roll(x, 7, axis=0)
            beside = beside_columns(x) + (2.0 * above if last else above + pltpu.roll(x, 1, axis=0))
            out.append(coupled[i] + diag * x - pull * beside)
        return out

    def fold(x):
        total = x[:, 0:LANES]
        for c in range(LANES, cols, LANES):
            total = total + x[:, c : c + LANES]
        return total

    for b in range(obs_count // 3):
        zero = [window(3 * b + i) for i in range(3)]
        one = apply(zero)
        two = apply(one)
        three = apply(two, last=True)
        for i in range(3):
            zero_ref[3 * b + i] = zero[i][2:4]
            one_ref[3 * b + i] = one[i][2:4]
            two_ref[3 * b + i] = two[i][2:4]
            v = [zero[i], one[i], two[i], three[i]]
            for k in range(6):
                acc[k] = acc[k] + fold(v[k // 2] * v[(k + 1) // 2])
    own_tile = own_rows[:, 0:LANES]
    tile_row = lax.broadcasted_iota(jnp.int32, (8, LANES), 0)
    gram = jnp.zeros((8, LANES), jnp.float32)
    for k in range(6):
        moment = jnp.sum(jnp.where(own_tile, acc[k], 0.0))
        gram = jnp.where(tile_row == k, moment, gram)
    gram_ref[...] = gram


def combine_kernel(gram_ref, prior_ref, zero_ref, one_ref, two_ref, out_ref):
    gram = gram_ref[0]
    for k in range(1, gram_ref.shape[0]):
        gram = gram + gram_ref[k]
    m = [gram[k : k + 1, :] for k in range(6)]
    h = {(i, j): m[i + j + 1] * (1.0 / GAIN) + SHIFT * m[i + j] for i in range(3) for j in range(i, 3)}
    l10 = h[0, 1] / h[0, 0]
    l20 = h[0, 2] / h[0, 0]
    d1 = h[1, 1] - l10 * h[0, 1]
    t = h[1, 2] - l20 * h[0, 1]
    ok1 = d1 > 1e-6 * h[1, 1]
    inv1 = jnp.where(ok1, 1.0 / jnp.where(ok1, d1, 1.0), 0.0)
    l21 = t * inv1
    d2 = h[2, 2] - l20 * h[0, 2] - l21 * t
    ok2 = ok1 & (d2 > 1e-6 * h[2, 2])
    inv2 = jnp.where(ok2, 1.0 / jnp.where(ok2, d2, 1.0), 0.0)
    z1 = m[1] - l10 * m[0]
    z2 = m[2] - l20 * m[0] - l21 * z1
    y2 = z2 * inv2
    y1 = z1 * inv1 - l21 * y2
    y0 = m[0] / h[0, 0] - l10 * y1 - l20 * y2
    cols = prior_ref.shape[2]
    for c in range(0, cols, LANES):
        lanes = slice(c, c + LANES)
        out_ref[:, :, lanes] = (
            prior_ref[:, :, lanes] + y0[None] * zero_ref[:, :, lanes] + y1[None] * one_ref[:, :, lanes] + y2[None] * two_ref[:, :, lanes]
        )


def on_device(reflect, clear_conf, sun_view, sensor_id, band_gain, sensor_weight, prior):
    rows_here, obs_count, cols = prior.shape
    prior = jnp.transpose(prior, (1, 0, 2))
    count = lax.axis_size("rows")
    total_rows = rows_here * count
    block = rows_here * ENTRIES
    tiles = cols // LANES
    me = lax.axis_index("rows").astype(jnp.int32).reshape(1)
    vmem = pl.BlockSpec(memory_space=pltpu.VMEM)
    smem = pl.BlockSpec(memory_space=pltpu.SMEM)
    params = pltpu.CompilerParams(vmem_limit_bytes=24 * 2**20)
    f32 = lambda *shape: jax.ShapeDtypeStruct(shape, jnp.float32)

    scale = 0.01 / (reflect.shape[0] * count)
    kept, sent = partial_sums(me, reflect, clear_conf, sun_view, sensor_id, band_gain, sensor_weight, prior, scale)
    got = lax.ppermute(sent, "rows", [(i, i ^ 1) for i in range(count)])
    same_core = [list(range(core, count, 2)) for core in range(2)]
    got = lax.all_to_all(add_pack(kept, got), "rows", 0, 0, axis_index_groups=same_core)

    own, msg = pl.pallas_call(
        functools.partial(residual_kernel, total_rows=total_rows),
        in_specs=[smem, vmem, vmem],
        out_specs=[vmem, vmem],
        out_shape=[f32(block, cols), jax.ShapeDtypeStruct(got.shape[1:], jnp.int16)],
        scratch_shapes=[pltpu.VMEM((tiles, block, LANES), jnp.float32)],
        compiler_params=params,
        name="residual",
    )(me, prior, got)

    low = lax.ppermute(msg, "rows", [(i, i + 1) for i in range(count - 1)])
    high = lax.ppermute(msg, "rows", [(i + 1, i) for i in range(count - 1)])
    far = lax.ppermute(msg[: 1 + 2 * tiles], "rows", [(i + 2, i) for i in range(count - 2)])
    zero, one, two, gram = pl.pallas_call(
        functools.partial(krylov_kernel, total_rows=total_rows, rows_here=rows_here),
        in_specs=[smem, vmem, vmem, vmem, vmem],
        out_specs=[vmem] * 4,
        out_shape=[f32(obs_count, rows_here, cols)] * 3 + [f32(8, LANES)],
        scratch_shapes=[pltpu.VMEM((tiles, ENTRIES * 8, LANES), jnp.float32)],
        compiler_params=params,
        name="krylov",
    )(me, own, low, high, far)

    grams = lax.all_to_all(jnp.broadcast_to(gram[None], (count, 8, LANES)), "rows", 0, 0)
    out = pl.pallas_call(
        combine_kernel,
        in_specs=[vmem] * 5,
        out_specs=vmem,
        out_shape=f32(obs_count, rows_here, cols),
        compiler_params=params,
        name="combine",
    )(grams, prior, zero, one, two)
    return jnp.transpose(out, (1, 0, 2))


def solution(mesh):
    return jax.shard_map(
        on_device,
        mesh=mesh,
        in_specs=(
            P("rows", None, None, "tiles"),
            P("rows", None, "tiles"),
            P("rows", None, None, "tiles"),
            P(),
            P(),
            P(),
            P("rows", None, "tiles"),
        ),
        out_specs=P("rows", None, "tiles"),
        check_vma=False,
    )
```

```python
import functools
import math

import jax
import jax.numpy as jnp
from jax import lax
from jax.experimental import pallas as pl
from jax.experimental.pallas import tpu as pltpu
from jax.sharding import PartitionSpec as P

TO_RADIAN = math.pi / 18000.0
PRIOR_PULL = 0.1
SMOOTH_PULL = 0.5
SHIFT = 3.0
GAIN = 0.4
ENTRIES = 24
LANES = 128
QUANT = 32000.0
GROUP = LANES // 4
CHUNKS = 2

R_POLY = (0.9999997325, -0.07078975067, 0.01874461107, -0.007458902408, 0.003231534099, -0.001120316969, 0.0002021413586)
S_POLY = (0.5000000104, 0.1133791358, -0.01741075815, 0.006065742587, -0.002566941555, 0.0009184227696, -0.0001747441655)
SIN_25 = (0.9999999567, -0.1666626093, 0.008276695349)
COS_25 = (0.9999999997, -0.4999999562, 0.04166553086, -0.001379415437)
SIN_15 = (0.999999998, -0.1666661418, 0.008312938059)
COS_15 = (0.9999999858, -0.4999963087, 0.04152366947)
SIN_90 = (0.9999999947, -0.1666665666, 0.008333024663, -0.00019807389, 2.601844464e-06)


def horner(coefs, x):
    acc = coefs[-1] * x + coefs[-2]
    for coef in coefs[-3::-1]:
        acc = acc * x + coef
    return acc


def ross_li(sun, view, azim):
    x = (sun - 4500).astype(jnp.float32) * TO_RADIAN
    x2 = x * x
    half = math.sqrt(0.5)
    sin_x = horner([c * half for c in SIN_25], x2) * x
    cos_x = horner([c * half for c in COS_25], x2)
    cos_sun, sin_sun = cos_x - sin_x, cos_x + sin_x
    v = view.astype(jnp.float32) * TO_RADIAN
    v2 = v * v
    sin_view = horner(SIN_15, v2) * v
    cos_view = horner(COS_15, v2)
    a = (9000 - azim).astype(jnp.float32) * TO_RADIAN
    cos_azim = horner(SIN_90, a * a) * a
    prod = cos_sun * cos_view
    cos_phase = prod + sin_sun * sin_view * cos_azim
    total = cos_sun + cos_view
    recip = 1.0 / (total * prod)
    inv_total = recip * prod
    sec_prod = recip * total
    u = 1.0 - cos_phase
    u_up = 1.0 + cos_phase
    bent = u * (u * lax.rsqrt(u)) * horner(R_POLY, cos_phase)
    volume = (bent + (0.5 * math.pi) * cos_phase) * inv_total - 0.25 * math.pi
    sin2 = u * u_up
    sin_phase = sin2 * lax.rsqrt(sin2)
    cos_t = jnp.minimum((2.0 * inv_total) * sin_phase, 1.0)
    w = jnp.maximum(1.0 - cos_t, 1e-30)
    overlap = w * (w * lax.rsqrt(w)) * horner(S_POLY, cos_t)
    geometric = sec_prod * (total * (overlap - 1.0) + 0.5 * u_up)
    return volume, geometric


def encode(blocks, msg_ref):
    rows = blocks[0][0]().shape[0]
    top = None
    for block in blocks:
        for tile in block:
            size = jnp.abs(tile())
            top = size if top is None else jnp.maximum(top, size)
    level = jnp.ceil(8.0 * jnp.log2(jnp.maximum(top, 1e-30)))
    factor = QUANT * jnp.exp2(-0.125 * level)
    for j, block in enumerate(blocks):
        for c, tile in enumerate(block):
            msg_ref[j * rows : (j + 1) * rows, c * LANES : (c + 1) * LANES] = (
                jnp.round(tile() * factor).astype(jnp.int32).astype(jnp.int16)
            )
    base = len(blocks) * rows
    level = level.astype(jnp.int32).astype(jnp.int16)
    for c in range(len(blocks[0])):
        part = level[16 * c : 16 * c + 16] if 16 * c < rows else jnp.zeros((16, LANES), jnp.int16)
        msg_ref[base : base + 16, c * LANES : (c + 1) * LANES] = part


def decode_scale(msg_ref, rows):
    base = msg_ref.shape[0] - 16
    level = [msg_ref[base : base + 16, c * LANES : (c + 1) * LANES] for c in range(rows // 16)]
    level = jnp.concatenate(level, axis=0).astype(jnp.int32).astype(jnp.float32)
    return jnp.exp2(0.125 * level) * (1.0 / QUANT)


def decode(msg_ref, at, c, scale):
    return msg_ref[at, c * LANES : (c + 1) * LANES].astype(jnp.int32).astype(jnp.float32) * scale


def lane_group(shape):
    return lax.broadcasted_iota(jnp.int32, shape, len(shape) - 1) // GROUP


def pack(tiles, write):
    rows = tiles[0].shape[0]
    top = jnp.abs(tiles[0])
    for tile in tiles[1:]:
        top = jnp.maximum(top, jnp.abs(tile))
    for shift in (LANES // 2, LANES // 4):
        top = jnp.maximum(top, pltpu.roll(top, shift, axis=1))
    level = jnp.ceil(8.0 * jnp.log2(jnp.maximum(top, 1e-30)))
    factor = QUANT * jnp.exp2(-0.125 * level)
    group = lane_group((16, LANES))
    scales = level[0:16]
    for t in range(1, rows // 16):
        scales = jnp.where(group == t, level[16 * t : 16 * t + 16], scales)
    write(0, scales.astype(jnp.int32).astype(jnp.int16))
    for c, tile in enumerate(tiles):
        coded = jnp.round(tile * factor).astype(jnp.int32).astype(jnp.int16)
        for t in range(rows // 16):
            write(1 + t * len(tiles) + c, coded[16 * t : 16 * t + 16])


def unpack(read, row_tiles, col_tiles):
    as_float = lambda x: x.astype(jnp.int32).astype(jnp.float32)
    scales = as_float(read(0))
    group = lane_group((16, LANES))
    factors = []
    for t in range(row_tiles):
        level = jnp.where(group == t, scales, 0.0)
        for shift in (LANES // 2, LANES // 4):
            level = level + pltpu.roll(level, shift, axis=1)
        factors.append(jnp.exp2(0.125 * level) * (1.0 / QUANT))
    return [
        jnp.concatenate([as_float(read(1 + t * col_tiles + c)) * factors[t] for t in range(row_tiles)], axis=0) for c in range(col_tiles)
    ]


def sums_kernel(
    me_ref, ids_ref, gain_ref, weight_ref, reflect_ref, conf_ref, sun_ref, prior_ref, keep_ref, msg_ref, sums_ref, *, scale, rows_here
):
    dates, bands, tile_rows, cols = reflect_ref.shape
    me = me_ref[0]
    block = rows_here * ENTRIES
    obs_count = 3 * bands
    base = pl.multiple_of(pl.program_id(0) * (tile_rows * ENTRIES), 8)
    first_tile = pl.program_id(1) * (cols // LANES)

    def lane_tile(index, carry):
        lanes = pl.ds(pl.multiple_of(index * LANES, LANES), LANES)
        for top in range(0, tile_rows, 8):
            acc = [None] * ENTRIES

            def add(entry, term):
                acc[entry] = term if acc[entry] is None else acc[entry] + term

            for d in range(dates):
                sensor = ids_ref[me * dates + d]
                volume, geometric = ross_li(
                    sun_ref[d, 0, top : top + 8, lanes], sun_ref[d, 1, top : top + 8, lanes], sun_ref[d, 2, top : top + 8, lanes]
                )
                weight = conf_ref[d, top : top + 8, lanes].astype(jnp.float32) * (weight_ref[sensor] * scale)
                weighted_vol = weight * volume
                weighted_geo = weight * geometric
                add(obs_count, weight)
                add(obs_count + 1, weighted_vol)
                add(obs_count + 2, weighted_geo)
                add(obs_count + 3, weighted_vol * volume)
                add(obs_count + 4, weighted_vol * geometric)
                add(obs_count + 5, weighted_geo * geometric)
                for b in range(bands):
                    tall = top // 16 * 16
                    signal = reflect_ref[d, b, tall : tall + 16, lanes].astype(jnp.float32)[top - tall : top - tall + 8]
                    signal = signal * gain_ref[sensor, b]
                    add(3 * b, weight * signal)
                    add(3 * b + 1, weighted_vol * signal)
                    add(3 * b + 2, weighted_geo * signal)
            for entry in range(ENTRIES):
                sums_ref[first_tile + index, pl.ds(base + (top * ENTRIES + entry), 8, stride=ENTRIES), :] = acc[entry]
        return carry

    lax.fori_loop(0, cols // LANES, lane_tile, 0)

    @pl.when((pl.program_id(0) == pl.num_programs(0) - 1) & (pl.program_id(1) == pl.num_programs(1) - 1))
    def _():
        rows = pl.num_programs(0) * tile_rows
        for row, source in ((me * rows_here - 1, 0), ((me + 1) * rows_here, rows_here - 1)):

            @pl.when((row >= 0) & (row < rows))
            def _():
                for c in range(sums_ref.shape[0]):
                    lanes = slice(c * LANES, (c + 1) * LANES)
                    at = pl.ds(pl.multiple_of(row * ENTRIES, 8), obs_count)
                    part = jnp.concatenate([prior_ref[e, source : source + 1, lanes] for e in range(obs_count)], axis=0)
                    sums_ref[c, at, :] = sums_ref[c, at, :] + SMOOTH_PULL * part

        bit = me % 2
        tiles = range(sums_ref.shape[0])
        count = keep_ref.shape[0]
        for j in range(count):
            own = pl.ds(pl.multiple_of((2 * j + bit) * block, 8), block)
            for c in tiles:
                keep_ref[j, :, c * LANES : (c + 1) * LANES] = sums_ref[c, own, :]

        def tile(j, c):
            return lambda: sums_ref[c, pl.ds(pl.multiple_of((2 * j + 1 - bit) * block, 8), block), :]

        encode([[tile(j, c) for c in tiles] for j in range(count)], msg_ref)


def partial_sums(me, reflect, clear_conf, sun_view, sensor_id, band_gain, sensor_weight, prior, scale, chunk):
    dates, bands, rows, cols = reflect.shape
    cols = cols // CHUNKS
    rows_here = prior.shape[1]
    count = rows // rows_here
    tile_rows = 16
    width = min(256, cols)
    first = chunk * (cols // width)
    block = rows_here * ENTRIES
    smem = pl.BlockSpec(memory_space=pltpu.SMEM)
    return pl.pallas_call(
        functools.partial(sums_kernel, scale=scale, rows_here=rows_here),
        grid=(rows // tile_rows, cols // width),
        in_specs=[
            smem,
            smem,
            smem,
            smem,
            pl.BlockSpec((dates, bands, tile_rows, width), lambda i, j: (0, 0, i, first + j)),
            pl.BlockSpec((dates, tile_rows, width), lambda i, j: (0, i, first + j)),
            pl.BlockSpec((dates, 3, tile_rows, width), lambda i, j: (0, 0, i, first + j)),
            pl.BlockSpec((3 * bands, rows_here, cols), lambda i, j: (0, 0, chunk)),
        ],
        out_specs=[
            pl.BlockSpec((count // 2, block, cols), lambda i, j: (0, 0, 0)),
            pl.BlockSpec((count // 2 * block + 16, cols), lambda i, j: (0, 0)),
        ],
        out_shape=[
            jax.ShapeDtypeStruct((count // 2, block, cols), jnp.float32),
            jax.ShapeDtypeStruct((count // 2 * block + 16, cols), jnp.int16),
        ],
        scratch_shapes=[pltpu.VMEM((cols // LANES, rows * ENTRIES, LANES), jnp.float32)],
        compiler_params=pltpu.CompilerParams(vmem_limit_bytes=60 * 2**20),
        name="partial_sums",
    )(me, sensor_id, band_gain, sensor_weight, reflect, clear_conf, sun_view, prior)


def add_split_kernel(bit_ref, kept_ref, got_ref, keep_ref, msg_ref):
    count, block, cols = keep_ref.shape
    bit = bit_ref[0]
    scale = decode_scale(got_ref, block)
    tiles = range(cols // LANES)

    def total(j, c):
        at = pl.ds(pl.multiple_of(j * block, 16), block)
        return kept_ref[j, :, c * LANES : (c + 1) * LANES] + decode(got_ref, at, c, scale)

    for j in range(count):
        for c in tiles:
            keep_ref[j, :, c * LANES : (c + 1) * LANES] = total(2 * j + bit, c)
    others = [[total(2 * j + 1 - bit, c) for c in tiles] for j in range(count)]
    encode([[functools.partial(lambda x: x, others[j][c]) for c in tiles] for j in range(count)], msg_ref)


def add_split(bit, kept, got):
    count, block, cols = kept.shape
    vmem = pl.BlockSpec(memory_space=pltpu.VMEM)
    return pl.pallas_call(
        add_split_kernel,
        in_specs=[pl.BlockSpec(memory_space=pltpu.SMEM), vmem, vmem],
        out_specs=[vmem, vmem],
        out_shape=[
            jax.ShapeDtypeStruct((count // 2, block, cols), jnp.float32),
            jax.ShapeDtypeStruct((count // 2 * block + 16, cols), jnp.int16),
        ],
        compiler_params=pltpu.CompilerParams(vmem_limit_bytes=24 * 2**20),
        name="add_split",
    )(bit, kept, got)


def take(ref, start, size, stride):
    at = pl.ds(start, size, stride=stride)
    return jnp.concatenate([ref[c, at, :] for c in range(ref.shape[0])], axis=1)


def put(ref, start, size, stride, value):
    at = pl.ds(start, size, stride=stride)
    for c in range(ref.shape[0]):
        ref[c, at, :] = value[:, c * LANES : (c + 1) * LANES]


def beside_columns(x):
    cols = x.shape[1]
    col = lax.broadcasted_iota(jnp.int32, x.shape, 1)
    left = jnp.where(col == 0, 0.0, pltpu.roll(x, 1, axis=1))
    right = jnp.where(col == cols - 1, 0.0, pltpu.roll(x, cols - 1, axis=1))
    return left + right


def degree_of(row, shape, total_rows):
    col = lax.broadcasted_iota(jnp.int32, shape, 1)
    edge = (
        (row == 0).astype(jnp.float32)
        + (row == total_rows - 1).astype(jnp.float32)
        + (col == 0).astype(jnp.float32)
        + (col == shape[1] - 1).astype(jnp.float32)
    )
    return 4.0 - edge


def couple(n, v):
    return (
        n[0] * v[0] + n[1] * v[1] + n[2] * v[2],
        n[1] * v[0] + n[3] * v[1] + n[4] * v[2],
        n[2] * v[0] + n[4] * v[1] + n[5] * v[2],
    )


def residual_kernel(me_ref, prior_ref, *refs, total_rows):
    obs_count, rows_here, cols = prior_ref.shape
    *parts, out_ref, msg_ref, sums_ref = refs
    block = rows_here * ENTRIES
    tiles = cols // LANES
    at = 0
    for kept_ref, got_ref in zip(parts[0::2], parts[1::2]):
        scale = decode_scale(got_ref, block)
        for c in range(kept_ref.shape[2] // LANES):
            sums_ref[at] = kept_ref[0, :, c * LANES : (c + 1) * LANES] + decode(got_ref, slice(0, block), c, scale)
            at += 1
    shape = (rows_here, cols)
    row = me_ref[0] * rows_here + lax.broadcasted_iota(jnp.int32, shape, 0)
    degree = degree_of(row, shape, total_rows)
    normal = [take(sums_ref, obs_count + k, rows_here, ENTRIES) for k in range(6)]
    for b in range(obs_count // 3):
        fields = [prior_ref[3 * b + i] for i in range(3)]
        coupled = couple(normal, fields)
        for i in range(3):
            field = fields[i]
            beside = beside_columns(field)
            if rows_here > 1:
                zero = jnp.zeros((1, cols), jnp.float32)
                beside = beside + jnp.concatenate([zero, field[:-1]], axis=0) + jnp.concatenate([field[1:], zero], axis=0)
            entry = 3 * b + i
            observed = take(sums_ref, entry, rows_here, ENTRIES)
            put(sums_ref, entry, rows_here, ENTRIES, observed - coupled[i] - SMOOTH_PULL * (degree * field - beside))
    for c in range(tiles):
        out_ref[:, c * LANES : (c + 1) * LANES] = sums_ref[c]

    def write(place, tile):
        msg_ref[place] = tile

    pack([sums_ref[c] for c in range(tiles)], write)


def krylov_kernel(me_ref, own_ref, mate_ref, across_ref, far_ref, zero_ref, one_ref, two_ref, gram_ref, window_ref, *, total_rows, rows_here):
    cols = own_ref.shape[1]
    obs_count = ENTRIES - 6
    tiles = cols // LANES
    row_tiles = own_ref.shape[0] // 16

    def lay(place, part, r):
        at = pl.ds(place, ENTRIES, stride=8)
        for c in range(tiles):
            window_ref[c, at, :] = part[c][r * ENTRIES : (r + 1) * ENTRIES]

    own = [own_ref[:, c * LANES : (c + 1) * LANES] for c in range(tiles)]
    mate = unpack(lambda place: mate_ref[place], row_tiles, tiles)
    across = unpack(lambda place: across_ref[place], row_tiles, tiles)
    far = unpack(lambda place: far_ref[place], 2, tiles)
    odd = me_ref[0] % 2
    for r in range(2):
        lay(2 + r, own, r)
        lay(4 * (1 - odd) + r, mate, r)
        lay(4 * odd + r, across, r)
    lay(6, far, 0)
    put(window_ref, 7, ENTRIES, 8, jnp.zeros((ENTRIES, cols), jnp.float32))
    window = lambda entry: jnp.concatenate([window_ref[c, entry * 8 : entry * 8 + 8, :] for c in range(cols // LANES)], axis=1)
    shape = (8, cols)
    place = lax.broadcasted_iota(jnp.int32, shape, 0)
    row = me_ref[0] * rows_here + place - 2
    inside = ((row >= 0) & (row < total_rows)).astype(jnp.float32) * GAIN
    own_rows = (place == 2) | (place == 3)
    diag = inside * (PRIOR_PULL - SHIFT + SMOOTH_PULL * degree_of(row, shape, total_rows))
    pull = inside * SMOOTH_PULL
    normal = [window(obs_count + k) * inside for k in range(6)]
    acc = [jnp.zeros((8, LANES), jnp.float32) for _ in range(6)]

    def apply(v, last=False):
        coupled = couple(normal, v)
        out = []
        for i in range(3):
            x = v[i]
            above = pltpu.roll(x, 7, axis=0)
            beside = beside_columns(x) + (2.0 * above if last else above + pltpu.roll(x, 1, axis=0))
            out.append(coupled[i] + diag * x - pull * beside)
        return out

    def fold(x):
        total = x[:, 0:LANES]
        for c in range(LANES, cols, LANES):
            total = total + x[:, c : c + LANES]
        return total

    for b in range(obs_count // 3):
        zero = [window(3 * b + i) for i in range(3)]
        one = apply(zero)
        two = apply(one)
        three = apply(two, last=True)
        for i in range(3):
            zero_ref[3 * b + i] = zero[i][2:4]
            one_ref[3 * b + i] = one[i][2:4]
            two_ref[3 * b + i] = two[i][2:4]
            v = [zero[i], one[i], two[i], three[i]]
            for k in range(6):
                acc[k] = acc[k] + fold(v[k // 2] * v[(k + 1) // 2])
    own_tile = own_rows[:, 0:LANES]
    tile_row = lax.broadcasted_iota(jnp.int32, (8, LANES), 0)
    gram = jnp.zeros((8, LANES), jnp.float32)
    for k in range(6):
        moment = jnp.sum(jnp.where(own_tile, acc[k], 0.0))
        gram = jnp.where(tile_row == k, moment, gram)
    gram_ref[...] = gram


def combine_kernel(gram_ref, prior_ref, zero_ref, one_ref, two_ref, out_ref):
    gram = gram_ref[0]
    for k in range(1, gram_ref.shape[0]):
        gram = gram + gram_ref[k]
    m = [gram[k : k + 1, :] for k in range(6)]
    h = {(i, j): m[i + j + 1] * (1.0 / GAIN) + SHIFT * m[i + j] for i in range(3) for j in range(i, 3)}
    l10 = h[0, 1] / h[0, 0]
    l20 = h[0, 2] / h[0, 0]
    d1 = h[1, 1] - l10 * h[0, 1]
    t = h[1, 2] - l20 * h[0, 1]
    ok1 = d1 > 1e-6 * h[1, 1]
    inv1 = jnp.where(ok1, 1.0 / jnp.where(ok1, d1, 1.0), 0.0)
    l21 = t * inv1
    d2 = h[2, 2] - l20 * h[0, 2] - l21 * t
    ok2 = ok1 & (d2 > 1e-6 * h[2, 2])
    inv2 = jnp.where(ok2, 1.0 / jnp.where(ok2, d2, 1.0), 0.0)
    z1 = m[1] - l10 * m[0]
    z2 = m[2] - l20 * m[0] - l21 * z1
    y2 = z2 * inv2
    y1 = z1 * inv1 - l21 * y2
    y0 = m[0] / h[0, 0] - l10 * y1 - l20 * y2
    cols = prior_ref.shape[2]
    for c in range(0, cols, LANES):
        lanes = slice(c, c + LANES)
        out_ref[:, :, lanes] = (
            prior_ref[:, :, lanes] + y0[None] * zero_ref[:, :, lanes] + y1[None] * one_ref[:, :, lanes] + y2[None] * two_ref[:, :, lanes]
        )


def on_device(reflect, clear_conf, sun_view, sensor_id, band_gain, sensor_weight, prior):
    rows_here, obs_count, cols = prior.shape
    prior = jnp.transpose(prior, (1, 0, 2))
    count = lax.axis_size("rows")
    total_rows = rows_here * count
    block = rows_here * ENTRIES
    tiles = cols // LANES
    me = lax.axis_index("rows").astype(jnp.int32).reshape(1)
    vmem = pl.BlockSpec(memory_space=pltpu.VMEM)
    smem = pl.BlockSpec(memory_space=pltpu.SMEM)
    params = pltpu.CompilerParams(vmem_limit_bytes=24 * 2**20)
    f32 = lambda *shape: jax.ShapeDtypeStruct(shape, jnp.float32)

    scale = 0.01 / (reflect.shape[0] * count)
    index = me
    parts = []
    for chunk in range(CHUNKS):
        kept, sent = partial_sums(
            index, reflect, clear_conf, sun_view, sensor_id, band_gain, sensor_weight, prior, scale, chunk
        )
        index, _ = lax.optimization_barrier((me, sent))
        parts.append((kept, sent))
    step = 1
    while True:
        got = [lax.ppermute(sent, "rows", [(i, i ^ step) for i in range(count)]) for _, sent in parts]
        step *= 2
        if step == count:
            break
        parts = [add_split(me // step % 2, kept, new) for (kept, _), new in zip(parts, got)]
    parts = [x for (kept, _), new in zip(parts, got) for x in (kept, new)]

    own, msg = pl.pallas_call(
        functools.partial(residual_kernel, total_rows=total_rows),
        in_specs=[smem] + [vmem] * (1 + len(parts)),
        out_specs=[vmem, vmem],
        out_shape=[f32(block, cols), jax.ShapeDtypeStruct((1 + block // 16 * tiles, 16, LANES), jnp.int16)],
        scratch_shapes=[pltpu.VMEM((tiles, block, LANES), jnp.float32)],
        compiler_params=params,
        name="residual",
    )(me, prior, *parts)

    mate = lax.ppermute(msg, "rows", [(i, i ^ 1) for i in range(count)])
    border = [(i, i + 1) for i in range(1, count - 1, 2)]
    across = lax.ppermute(msg, "rows", border + [(target, source) for source, target in border])
    far = lax.ppermute(msg[: 1 + 2 * tiles], "rows", [(i + 2, i) for i in range(count - 2)])
    zero, one, two, gram = pl.pallas_call(
        functools.partial(krylov_kernel, total_rows=total_rows, rows_here=rows_here),
        in_specs=[smem, vmem, vmem, vmem, vmem],
        out_specs=[vmem] * 4,
        out_shape=[f32(obs_count, rows_here, cols)] * 3 + [f32(8, LANES)],
        scratch_shapes=[pltpu.VMEM((tiles, ENTRIES * 8, LANES), jnp.float32)],
        compiler_params=params,
        name="krylov",
    )(me, own, mate, across, far)

    grams = lax.all_to_all(jnp.broadcast_to(gram[None], (count, 8, LANES)), "rows", 0, 0)
    out = pl.pallas_call(
        combine_kernel,
        in_specs=[vmem] * 5,
        out_specs=vmem,
        out_shape=f32(obs_count, rows_here, cols),
        compiler_params=params,
        name="combine",
    )(grams, prior, zero, one, two)
    return jnp.transpose(out, (1, 0, 2))


def solution(mesh):
    return jax.shard_map(
        on_device,
        mesh=mesh,
        in_specs=(
            P("rows", None, None, "tiles"),
            P("rows", None, "tiles"),
            P("rows", None, None, "tiles"),
            P(),
            P(),
            P(),
            P("rows", None, "tiles"),
        ),
        out_specs=P("rows", None, "tiles"),
        check_vma=False,
    )
```

```python
import functools
import math

import jax
import jax.numpy as jnp
from jax import lax
from jax.experimental import pallas as pl
from jax.experimental.pallas import tpu as pltpu
from jax.sharding import PartitionSpec as P

TO_RADIAN = math.pi / 18000.0
PRIOR_PULL = 0.1
SMOOTH_PULL = 0.5
SHIFT = 3.0
GAIN = 0.4
ENTRIES = 24
LANES = 128
QUANT = 32000.0
GROUP = LANES // 4
CHUNKS = 2

R_POLY = (0.9999997325, -0.07078975067, 0.01874461107, -0.007458902408, 0.003231534099, -0.001120316969, 0.0002021413586)
S_POLY = (0.5000000104, 0.1133791358, -0.01741075815, 0.006065742587, -0.002566941555, 0.0009184227696, -0.0001747441655)
SIN_25 = (0.9999999567, -0.1666626093, 0.008276695349)
COS_25 = (0.9999999997, -0.4999999562, 0.04166553086, -0.001379415437)
SIN_15 = (0.999999998, -0.1666661418, 0.008312938059)
COS_15 = (0.9999999858, -0.4999963087, 0.04152366947)
SIN_90 = (0.9999999947, -0.1666665666, 0.008333024663, -0.00019807389, 2.601844464e-06)


def horner(coefs, x):
    acc = coefs[-1] * x + coefs[-2]
    for coef in coefs[-3::-1]:
        acc = acc * x + coef
    return acc


def ross_li(sun, view, azim):
    x = (sun - 4500).astype(jnp.float32) * TO_RADIAN
    x2 = x * x
    half = math.sqrt(0.5)
    sin_x = horner([c * half for c in SIN_25], x2) * x
    cos_x = horner([c * half for c in COS_25], x2)
    cos_sun, sin_sun = cos_x - sin_x, cos_x + sin_x
    v = view.astype(jnp.float32) * TO_RADIAN
    v2 = v * v
    sin_view = horner(SIN_15, v2) * v
    cos_view = horner(COS_15, v2)
    a = (9000 - azim).astype(jnp.float32) * TO_RADIAN
    cos_azim = horner(SIN_90, a * a) * a
    prod = cos_sun * cos_view
    cos_phase = prod + sin_sun * sin_view * cos_azim
    total = cos_sun + cos_view
    recip = 1.0 / (total * prod)
    inv_total = recip * prod
    sec_prod = recip * total
    u = 1.0 - cos_phase
    u_up = 1.0 + cos_phase
    bent = u * (u * lax.rsqrt(u)) * horner(R_POLY, cos_phase)
    volume = (bent + (0.5 * math.pi) * cos_phase) * inv_total - 0.25 * math.pi
    sin2 = u * u_up
    sin_phase = sin2 * lax.rsqrt(sin2)
    cos_t = jnp.minimum((2.0 * inv_total) * sin_phase, 1.0)
    w = jnp.maximum(1.0 - cos_t, 1e-30)
    overlap = w * (w * lax.rsqrt(w)) * horner(S_POLY, cos_t)
    geometric = sec_prod * (total * (overlap - 1.0) + 0.5 * u_up)
    return volume, geometric


def encode(blocks, msg_ref):
    rows = blocks[0][0]().shape[0]
    top = None
    for block in blocks:
        for tile in block:
            size = jnp.abs(tile())
            top = size if top is None else jnp.maximum(top, size)
    level = jnp.ceil(8.0 * jnp.log2(jnp.maximum(top, 1e-30)))
    factor = QUANT * jnp.exp2(-0.125 * level)
    for j, block in enumerate(blocks):
        for c, tile in enumerate(block):
            msg_ref[j * rows : (j + 1) * rows, c * LANES : (c + 1) * LANES] = (
                jnp.round(tile() * factor).astype(jnp.int32).astype(jnp.int16)
            )
    base = len(blocks) * rows
    level = level.astype(jnp.int32).astype(jnp.int16)
    for c in range(len(blocks[0])):
        part = level[16 * c : 16 * c + 16] if 16 * c < rows else jnp.zeros((16, LANES), jnp.int16)
        msg_ref[base : base + 16, c * LANES : (c + 1) * LANES] = part


def decode_scale(msg_ref, rows):
    base = msg_ref.shape[0] - 16
    level = [msg_ref[base : base + 16, c * LANES : (c + 1) * LANES] for c in range(rows // 16)]
    level = jnp.concatenate(level, axis=0).astype(jnp.int32).astype(jnp.float32)
    return jnp.exp2(0.125 * level) * (1.0 / QUANT)


def decode(msg_ref, at, c, scale):
    return msg_ref[at, c * LANES : (c + 1) * LANES].astype(jnp.int32).astype(jnp.float32) * scale


def lane_group(shape):
    return lax.broadcasted_iota(jnp.int32, shape, len(shape) - 1) // GROUP


def pack(tiles, write):
    rows = tiles[0].shape[0]
    top = jnp.abs(tiles[0])
    for tile in tiles[1:]:
        top = jnp.maximum(top, jnp.abs(tile))
    for shift in (LANES // 2, LANES // 4):
        top = jnp.maximum(top, pltpu.roll(top, shift, axis=1))
    level = jnp.ceil(8.0 * jnp.log2(jnp.maximum(top, 1e-30)))
    factor = QUANT * jnp.exp2(-0.125 * level)
    group = lane_group((16, LANES))
    scales = level[0:16]
    for t in range(1, rows // 16):
        scales = jnp.where(group == t, level[16 * t : 16 * t + 16], scales)
    write(0, scales.astype(jnp.int32).astype(jnp.int16))
    for c, tile in enumerate(tiles):
        coded = jnp.round(tile * factor).astype(jnp.int32).astype(jnp.int16)
        for t in range(rows // 16):
            write(1 + t * len(tiles) + c, coded[16 * t : 16 * t + 16])


def unpack(read, row_tiles, col_tiles):
    as_float = lambda x: x.astype(jnp.int32).astype(jnp.float32)
    scales = as_float(read(0))
    group = lane_group((16, LANES))
    factors = []
    for t in range(row_tiles):
        level = jnp.where(group == t, scales, 0.0)
        for shift in (LANES // 2, LANES // 4):
            level = level + pltpu.roll(level, shift, axis=1)
        factors.append(jnp.exp2(0.125 * level) * (1.0 / QUANT))
    return [
        jnp.concatenate([as_float(read(1 + t * col_tiles + c)) * factors[t] for t in range(row_tiles)], axis=0) for c in range(col_tiles)
    ]


def sums_kernel(
    me_ref, ids_ref, gain_ref, weight_ref, reflect_ref, conf_ref, sun_ref, prior_ref, keep_ref, msg_ref, sums_ref, *, scale, rows_here
):
    dates, bands, tile_rows, cols = reflect_ref.shape
    me = me_ref[0]
    block = rows_here * ENTRIES
    obs_count = 3 * bands
    base = pl.multiple_of(pl.program_id(0) * (tile_rows * ENTRIES), 8)
    first_tile = pl.program_id(1) * (cols // LANES)

    def lane_tile(index, carry):
        lanes = pl.ds(pl.multiple_of(index * LANES, LANES), LANES)
        for top in range(0, tile_rows, 8):
            acc = [None] * ENTRIES

            def add(entry, term):
                acc[entry] = term if acc[entry] is None else acc[entry] + term

            for d in range(dates):
                sensor = ids_ref[me * dates + d]
                volume, geometric = ross_li(
                    sun_ref[d, 0, top : top + 8, lanes], sun_ref[d, 1, top : top + 8, lanes], sun_ref[d, 2, top : top + 8, lanes]
                )
                weight = conf_ref[d, top : top + 8, lanes].astype(jnp.float32) * (weight_ref[sensor] * scale)
                weighted_vol = weight * volume
                weighted_geo = weight * geometric
                add(obs_count, weight)
                add(obs_count + 1, weighted_vol)
                add(obs_count + 2, weighted_geo)
                add(obs_count + 3, weighted_vol * volume)
                add(obs_count + 4, weighted_vol * geometric)
                add(obs_count + 5, weighted_geo * geometric)
                for b in range(bands):
                    tall = top // 16 * 16
                    signal = reflect_ref[d, b, tall : tall + 16, lanes].astype(jnp.float32)[top - tall : top - tall + 8]
                    signal = signal * gain_ref[sensor, b]
                    add(3 * b, weight * signal)
                    add(3 * b + 1, weighted_vol * signal)
                    add(3 * b + 2, weighted_geo * signal)
            for entry in range(ENTRIES):
                sums_ref[first_tile + index, pl.ds(base + (top * ENTRIES + entry), 8, stride=ENTRIES), :] = acc[entry]
        return carry

    lax.fori_loop(0, cols // LANES, lane_tile, 0)

    @pl.when((pl.program_id(0) == pl.num_programs(0) - 1) & (pl.program_id(1) == pl.num_programs(1) - 1))
    def _():
        rows = pl.num_programs(0) * tile_rows
        for row, source in ((me * rows_here - 1, 0), ((me + 1) * rows_here, rows_here - 1)):

            @pl.when((row >= 0) & (row < rows))
            def _():
                for c in range(sums_ref.shape[0]):
                    lanes = slice(c * LANES, (c + 1) * LANES)
                    at = pl.ds(pl.multiple_of(row * ENTRIES, 8), obs_count)
                    part = jnp.concatenate([prior_ref[e, source : source + 1, lanes] for e in range(obs_count)], axis=0)
                    sums_ref[c, at, :] = sums_ref[c, at, :] + SMOOTH_PULL * part

        bit = me % 2
        tiles = range(sums_ref.shape[0])
        count = keep_ref.shape[0]
        for j in range(count):
            own = pl.ds(pl.multiple_of((2 * j + bit) * block, 8), block)
            for c in tiles:
                keep_ref[j, :, c * LANES : (c + 1) * LANES] = sums_ref[c, own, :]

        def tile(j, c):
            return lambda: sums_ref[c, pl.ds(pl.multiple_of((2 * j + 1 - bit) * block, 8), block), :]

        encode([[tile(j, c) for c in tiles] for j in range(count)], msg_ref)


def partial_sums(me, reflect, clear_conf, sun_view, sensor_id, band_gain, sensor_weight, prior, scale, chunk):
    dates, bands, rows, cols = reflect.shape
    cols = cols // CHUNKS
    rows_here = prior.shape[1]
    count = rows // rows_here
    tile_rows = 16
    width = min(256, cols)
    first = chunk * (cols // width)
    block = rows_here * ENTRIES
    smem = pl.BlockSpec(memory_space=pltpu.SMEM)
    return pl.pallas_call(
        functools.partial(sums_kernel, scale=scale, rows_here=rows_here),
        grid=(rows // tile_rows, cols // width),
        in_specs=[
            smem,
            smem,
            smem,
            smem,
            pl.BlockSpec((dates, bands, tile_rows, width), lambda i, j: (0, 0, i, first + j)),
            pl.BlockSpec((dates, tile_rows, width), lambda i, j: (0, i, first + j)),
            pl.BlockSpec((dates, 3, tile_rows, width), lambda i, j: (0, 0, i, first + j)),
            pl.BlockSpec((3 * bands, rows_here, cols), lambda i, j: (0, 0, chunk)),
        ],
        out_specs=[
            pl.BlockSpec((count // 2, block, cols), lambda i, j: (0, 0, 0)),
            pl.BlockSpec((count // 2 * block + 16, cols), lambda i, j: (0, 0)),
        ],
        out_shape=[
            jax.ShapeDtypeStruct((count // 2, block, cols), jnp.float32),
            jax.ShapeDtypeStruct((count // 2 * block + 16, cols), jnp.int16),
        ],
        scratch_shapes=[pltpu.VMEM((cols // LANES, rows * ENTRIES, LANES), jnp.float32)],
        compiler_params=pltpu.CompilerParams(vmem_limit_bytes=60 * 2**20),
        name="partial_sums",
    )(me, sensor_id, band_gain, sensor_weight, reflect, clear_conf, sun_view, prior)


def add_split_kernel(bit_ref, *refs, place):
    *parts, keep_ref, msg_ref = refs
    count, block, _ = keep_ref.shape
    bit = bit_ref[0]
    own, other = [[] for _ in range(count)], [[] for _ in range(count)]
    at = 0
    for kept_ref, got_ref in zip(parts[0::2], parts[1::2]):
        scale = decode_scale(got_ref, block)
        for c in range(kept_ref.shape[2] // LANES):

            def total(j):
                rows = pl.ds(pl.multiple_of(j * block, 16), block)
                return kept_ref[j, :, c * LANES : (c + 1) * LANES] + decode(got_ref, rows, c, scale)

            for q in range(count):
                low = q % 2**place
                first = (q - low) * 2 + low
                keep_ref[q, :, at * LANES : (at + 1) * LANES] = total(first + bit * 2**place)
                other[q].append(total(first + (1 - bit) * 2**place))
            at += 1
    encode([[functools.partial(lambda x: x, tile) for tile in tiles] for tiles in other], msg_ref)


def add_split(bit, place, *parts):
    count, block, _ = parts[0].shape
    cols = sum(kept.shape[2] for kept in parts[0::2])
    vmem = pl.BlockSpec(memory_space=pltpu.VMEM)
    return pl.pallas_call(
        functools.partial(add_split_kernel, place=place),
        in_specs=[pl.BlockSpec(memory_space=pltpu.SMEM)] + [vmem] * len(parts),
        out_specs=[vmem, vmem],
        out_shape=[
            jax.ShapeDtypeStruct((count // 2, block, cols), jnp.float32),
            jax.ShapeDtypeStruct((count // 2 * block + 16, cols), jnp.int16),
        ],
        compiler_params=pltpu.CompilerParams(vmem_limit_bytes=24 * 2**20),
        name="add_split",
    )(bit, *parts)


def take(ref, start, size, stride):
    at = pl.ds(start, size, stride=stride)
    return jnp.concatenate([ref[c, at, :] for c in range(ref.shape[0])], axis=1)


def put(ref, start, size, stride, value):
    at = pl.ds(start, size, stride=stride)
    for c in range(ref.shape[0]):
        ref[c, at, :] = value[:, c * LANES : (c + 1) * LANES]


def beside_columns(x):
    cols = x.shape[1]
    col = lax.broadcasted_iota(jnp.int32, x.shape, 1)
    left = jnp.where(col == 0, 0.0, pltpu.roll(x, 1, axis=1))
    right = jnp.where(col == cols - 1, 0.0, pltpu.roll(x, cols - 1, axis=1))
    return left + right


def degree_of(row, shape, total_rows):
    col = lax.broadcasted_iota(jnp.int32, shape, 1)
    edge = (
        (row == 0).astype(jnp.float32)
        + (row == total_rows - 1).astype(jnp.float32)
        + (col == 0).astype(jnp.float32)
        + (col == shape[1] - 1).astype(jnp.float32)
    )
    return 4.0 - edge


def couple(n, v):
    return (
        n[0] * v[0] + n[1] * v[1] + n[2] * v[2],
        n[1] * v[0] + n[3] * v[1] + n[4] * v[2],
        n[2] * v[0] + n[4] * v[1] + n[5] * v[2],
    )


def residual_kernel(me_ref, prior_ref, *refs, total_rows):
    obs_count, rows_here, cols = prior_ref.shape
    *parts, out_ref, msg_ref, sums_ref = refs
    block = rows_here * ENTRIES
    tiles = cols // LANES
    at = 0
    for kept_ref, got_ref in zip(parts[0::2], parts[1::2]):
        scale = decode_scale(got_ref, block)
        for c in range(kept_ref.shape[2] // LANES):
            sums_ref[at] = kept_ref[0, :, c * LANES : (c + 1) * LANES] + decode(got_ref, slice(0, block), c, scale)
            at += 1
    shape = (rows_here, cols)
    row = me_ref[0] * rows_here + lax.broadcasted_iota(jnp.int32, shape, 0)
    degree = degree_of(row, shape, total_rows)
    normal = [take(sums_ref, obs_count + k, rows_here, ENTRIES) for k in range(6)]
    for b in range(obs_count // 3):
        fields = [prior_ref[3 * b + i] for i in range(3)]
        coupled = couple(normal, fields)
        for i in range(3):
            field = fields[i]
            beside = beside_columns(field)
            if rows_here > 1:
                zero = jnp.zeros((1, cols), jnp.float32)
                beside = beside + jnp.concatenate([zero, field[:-1]], axis=0) + jnp.concatenate([field[1:], zero], axis=0)
            entry = 3 * b + i
            observed = take(sums_ref, entry, rows_here, ENTRIES)
            put(sums_ref, entry, rows_here, ENTRIES, observed - coupled[i] - SMOOTH_PULL * (degree * field - beside))
    for c in range(tiles):
        out_ref[:, c * LANES : (c + 1) * LANES] = sums_ref[c]

    def write(place, tile):
        msg_ref[place] = tile

    pack([sums_ref[c] for c in range(tiles)], write)


def krylov_kernel(me_ref, own_ref, mate_ref, near0_ref, near1_ref, zero_ref, one_ref, two_ref, gram_ref, window_ref, *, total_rows, rows_here):
    cols = own_ref.shape[1]
    obs_count = ENTRIES - 6
    tiles = cols // LANES
    row_tiles = own_ref.shape[0] // 16

    def lay(place, part, r):
        at = pl.ds(place, ENTRIES, stride=8)
        for c in range(tiles):
            window_ref[c, at, :] = part[c][r * ENTRIES : (r + 1) * ENTRIES]

    own = [own_ref[:, c * LANES : (c + 1) * LANES] for c in range(tiles)]
    mate = unpack(lambda place: mate_ref[place], row_tiles, tiles)
    core, chip = me_ref[0] % 2, me_ref[0] // 2 % 2

    def pick(first, from_first):
        tile = lambda ref, place: ref[first + place].astype(jnp.int32)
        return lambda place: jnp.where(from_first, tile(near0_ref, place), tile(near1_ref, place))

    beyond = unpack(pick(0, core != chip), row_tiles, tiles)
    far = unpack(pick(1 + row_tiles * tiles, chip == 0), 2, tiles)
    for r in range(2):
        lay(2 + r, own, r)
        lay(4 * (1 - core) + r, mate, r)
        lay(4 * core + r, beyond, r)
    lay(6, far, 0)
    put(window_ref, 7, ENTRIES, 8, jnp.zeros((ENTRIES, cols), jnp.float32))
    window = lambda entry: jnp.concatenate([window_ref[c, entry * 8 : entry * 8 + 8, :] for c in range(cols // LANES)], axis=1)
    shape = (8, cols)
    place = lax.broadcasted_iota(jnp.int32, shape, 0)
    row = me_ref[0] * rows_here + place - 2
    inside = ((row >= 0) & (row < total_rows)).astype(jnp.float32) * GAIN
    own_rows = (place == 2) | (place == 3)
    diag = inside * (PRIOR_PULL - SHIFT + SMOOTH_PULL * degree_of(row, shape, total_rows))
    pull = inside * SMOOTH_PULL
    normal = [window(obs_count + k) * inside for k in range(6)]
    acc = [jnp.zeros((8, LANES), jnp.float32) for _ in range(6)]

    def apply(v, last=False):
        coupled = couple(normal, v)
        out = []
        for i in range(3):
            x = v[i]
            above = pltpu.roll(x, 7, axis=0)
            beside = beside_columns(x) + (2.0 * above if last else above + pltpu.roll(x, 1, axis=0))
            out.append(coupled[i] + diag * x - pull * beside)
        return out

    def fold(x):
        total = x[:, 0:LANES]
        for c in range(LANES, cols, LANES):
            total = total + x[:, c : c + LANES]
        return total

    for b in range(obs_count // 3):
        zero = [window(3 * b + i) for i in range(3)]
        one = apply(zero)
        two = apply(one)
        three = apply(two, last=True)
        for i in range(3):
            zero_ref[3 * b + i] = zero[i][2:4]
            one_ref[3 * b + i] = one[i][2:4]
            two_ref[3 * b + i] = two[i][2:4]
            v = [zero[i], one[i], two[i], three[i]]
            for k in range(6):
                acc[k] = acc[k] + fold(v[k // 2] * v[(k + 1) // 2])
    own_tile = own_rows[:, 0:LANES]
    tile_row = lax.broadcasted_iota(jnp.int32, (8, LANES), 0)
    gram = jnp.zeros((8, LANES), jnp.float32)
    for k in range(6):
        moment = jnp.sum(jnp.where(own_tile, acc[k], 0.0))
        gram = jnp.where(tile_row == k, moment, gram)
    gram_ref[...] = gram


def combine_kernel(gram_ref, prior_ref, zero_ref, one_ref, two_ref, out_ref):
    gram = gram_ref[0]
    for k in range(1, gram_ref.shape[0]):
        gram = gram + gram_ref[k]
    m = [gram[k : k + 1, :] for k in range(6)]
    h = {(i, j): m[i + j + 1] * (1.0 / GAIN) + SHIFT * m[i + j] for i in range(3) for j in range(i, 3)}
    l10 = h[0, 1] / h[0, 0]
    l20 = h[0, 2] / h[0, 0]
    d1 = h[1, 1] - l10 * h[0, 1]
    t = h[1, 2] - l20 * h[0, 1]
    ok1 = d1 > 1e-6 * h[1, 1]
    inv1 = jnp.where(ok1, 1.0 / jnp.where(ok1, d1, 1.0), 0.0)
    l21 = t * inv1
    d2 = h[2, 2] - l20 * h[0, 2] - l21 * t
    ok2 = ok1 & (d2 > 1e-6 * h[2, 2])
    inv2 = jnp.where(ok2, 1.0 / jnp.where(ok2, d2, 1.0), 0.0)
    z1 = m[1] - l10 * m[0]
    z2 = m[2] - l20 * m[0] - l21 * z1
    y2 = z2 * inv2
    y1 = z1 * inv1 - l21 * y2
    y0 = m[0] / h[0, 0] - l10 * y1 - l20 * y2
    cols = prior_ref.shape[2]
    for c in range(0, cols, LANES):
        lanes = slice(c, c + LANES)
        out_ref[:, :, lanes] = (
            prior_ref[:, :, lanes] + y0[None] * zero_ref[:, :, lanes] + y1[None] * one_ref[:, :, lanes] + y2[None] * two_ref[:, :, lanes]
        )


def on_device(reflect, clear_conf, sun_view, sensor_id, band_gain, sensor_weight, prior):
    rows_here, obs_count, cols = prior.shape
    prior = jnp.transpose(prior, (1, 0, 2))
    count = lax.axis_size("rows")
    total_rows = rows_here * count
    block = rows_here * ENTRIES
    tiles = cols // LANES
    me = lax.axis_index("rows").astype(jnp.int32).reshape(1)
    vmem = pl.BlockSpec(memory_space=pltpu.VMEM)
    smem = pl.BlockSpec(memory_space=pltpu.SMEM)
    params = pltpu.CompilerParams(vmem_limit_bytes=24 * 2**20)
    f32 = lambda *shape: jax.ShapeDtypeStruct(shape, jnp.float32)

    scale = 0.01 / (reflect.shape[0] * count)
    index = me
    parts = []
    for chunk in range(CHUNKS):
        kept, sent = partial_sums(
            index, reflect, clear_conf, sun_view, sensor_id, band_gain, sensor_weight, prior, scale, chunk
        )
        index, _ = lax.optimization_barrier((me, sent))
        parts.append((kept, sent))
    swap = lambda x, bit: lax.ppermute(x, "rows", [(i, i ^ 1 << bit) for i in range(count)])
    bits = list(range(1, count.bit_length() - 1))
    parts = [(kept, swap(sent, 0)) for kept, sent in parts]
    if len(bits) >= 2:
        orders = [((bits[0], 0), (bits[1], 0)), ((bits[1], 1), (bits[0], 0))]
        for step in range(2):
            for chunk in range(CHUNKS):
                bit, place = orders[chunk % 2][step]
                kept, sent = add_split(me // 2**bit % 2, place, *parts[chunk])
                parts[chunk] = (kept, swap(sent, bit))
        bits = bits[2:]
    parts = [x for part in parts for x in part]
    for bit in bits:
        kept, sent = add_split(me // 2**bit % 2, 0, *parts)
        parts = [kept, swap(sent, bit)]

    own, msg = pl.pallas_call(
        functools.partial(residual_kernel, total_rows=total_rows),
        in_specs=[smem] + [vmem] * (1 + len(parts)),
        out_specs=[vmem, vmem],
        out_shape=[f32(block, cols), jax.ShapeDtypeStruct((1 + block // 16 * tiles, 16, LANES), jnp.int16)],
        scratch_shapes=[pltpu.VMEM((tiles, block, LANES), jnp.float32)],
        compiler_params=params,
        name="residual",
    )(me, prior, *parts)

    mate = swap(msg, 0)
    both = jnp.concatenate([mate, msg[: 1 + 2 * tiles]], axis=0)
    near = []
    for first in range(2):
        down = [(i + 2, i) for chip in range(first, count // 2 - 1, 2) for i in (2 * chip, 2 * chip + 1)]
        up = [(i, i + 2) for chip in range(first, count // 2 - 1, 2) for i in (2 * chip,)]
        near.append(lax.ppermute(both, "rows", down + up))
    zero, one, two, gram = pl.pallas_call(
        functools.partial(krylov_kernel, total_rows=total_rows, rows_here=rows_here),
        in_specs=[smem, vmem, vmem, vmem, vmem],
        out_specs=[vmem] * 4,
        out_shape=[f32(obs_count, rows_here, cols)] * 3 + [f32(8, LANES)],
        scratch_shapes=[pltpu.VMEM((tiles, ENTRIES * 8, LANES), jnp.float32)],
        compiler_params=params,
        name="krylov",
    )(me, own, mate, *near)

    grams = lax.all_to_all(jnp.broadcast_to(gram[None], (count, 8, LANES)), "rows", 0, 0)
    out = pl.pallas_call(
        combine_kernel,
        in_specs=[vmem] * 5,
        out_specs=vmem,
        out_shape=f32(obs_count, rows_here, cols),
        compiler_params=params,
        name="combine",
    )(grams, prior, zero, one, two)
    return jnp.transpose(out, (1, 0, 2))


def solution(mesh):
    return jax.shard_map(
        on_device,
        mesh=mesh,
        in_specs=(
            P("rows", None, None, "tiles"),
            P("rows", None, "tiles"),
            P("rows", None, None, "tiles"),
            P(),
            P(),
            P(),
            P("rows", None, "tiles"),
        ),
        out_specs=P("rows", None, "tiles"),
        check_vma=False,
    )
```

```python
import functools
import math

import jax
import jax.numpy as jnp
from jax import lax
from jax.experimental import pallas as pl
from jax.experimental.pallas import tpu as pltpu
from jax.sharding import PartitionSpec as P

TO_RADIAN = math.pi / 18000.0
PRIOR_PULL = 0.1
SMOOTH_PULL = 0.5
SHIFT = 3.0
GAIN = 0.4
ENTRIES = 24
LANES = 128
QUANT = 32000.0
GROUP = LANES // 4
CHUNKS = 2


R_POLY = (0.9428089773, 0.04714460664, 0.007527079489, 0.001965302741, 9.052799897e-05, 0.0004621408027)
S_POLY = (0.6002109608, -0.09003726006, -0.007977343822, -0.001801806492, 3.702625389e-06, -0.0003981650976)
SIN_25 = (0.9999999567, -0.1666626093, 0.008276695349)
COS_25 = (0.9999999997, -0.4999999562, 0.04166553086, -0.001379415437)
SIN_15 = (0.999999998, -0.1666661418, 0.008312938059)
COS_15 = (0.9999999858, -0.4999963087, 0.04152366947)
SIN_90 = (0.9999999947, -0.1666665666, 0.008333024663, -0.00019807389, 2.601844464e-06)


def horner(coefs, x):
    acc = coefs[-1] * x + coefs[-2]
    for coef in coefs[-3::-1]:
        acc = acc * x + coef
    return acc


def of_degrees(coefs, x, x2, factor, odd):
    scaled = [factor * coef * TO_RADIAN ** (2 * k + odd) for k, coef in enumerate(coefs)]
    value = horner(scaled, x2)
    return value * x if odd else value


def ross_li(sun, view, azim):
    x = (sun - 4500).astype(jnp.float32)
    x2 = x * x
    half = math.sqrt(0.5)
    sin_x, cos_x = of_degrees(SIN_25, x, x2, half, 1), of_degrees(COS_25, x, x2, half, 0)
    cos_sun, sin_sun = cos_x - sin_x, cos_x + sin_x
    v = view.astype(jnp.float32)
    v2 = v * v
    sin_view, cos_view = of_degrees(SIN_15, v, v2, 1.0, 1), of_degrees(COS_15, v, v2, 1.0, 0)
    a = (9000 - azim).astype(jnp.float32)
    cos_azim = of_degrees(SIN_90, a, a * a, 1.0, 1)
    prod = cos_sun * cos_view
    cos_phase = prod + sin_sun * sin_view * cos_azim
    total = cos_sun + cos_view
    recip = pl.reciprocal(total * prod, approx=False)
    inv_total = recip * prod
    sec_prod = recip * total
    u = 1.0 - cos_phase
    u_up = 1.0 + cos_phase
    bent = u * (u * lax.rsqrt(u)) * horner(R_POLY, u)
    volume = (bent + (0.5 * math.pi) * cos_phase) * inv_total - 0.25 * math.pi
    sin2 = u * u_up
    sin_phase = sin2 * lax.rsqrt(sin2)
    w = jnp.maximum(1.0 - (2.0 * inv_total) * sin_phase, 1e-30)
    overlap = w * (w * lax.rsqrt(w)) * horner(S_POLY, w)
    geometric = sec_prod * (total * (overlap - 1.0) + 0.5 * u_up)
    return volume, geometric


def lane_group(shape):
    return lax.broadcasted_iota(jnp.int32, shape, len(shape) - 1) // GROUP


def pack(tiles, msg_ref, block):
    rows = tiles[0].shape[0]
    top = jnp.abs(tiles[0])
    for tile in tiles[1:]:
        top = jnp.maximum(top, jnp.abs(tile))
    for shift in (LANES // 2, LANES // 4):
        top = jnp.maximum(top, pltpu.roll(top, shift, axis=1))
    level = jnp.ceil(8.0 * jnp.log2(jnp.maximum(top, 1e-30)))
    factor = QUANT * jnp.exp2(-0.125 * level)
    group = lane_group((16, LANES))
    scales = level[0:16]
    for t in range(1, rows // 16):
        scales = jnp.where(group == t, level[16 * t : 16 * t + 16], scales)
    msg_ref[block, 0] = (scales.astype(jnp.int32).astype(jnp.int16))
    for c, tile in enumerate(tiles):
        coded = jnp.round(tile * factor).astype(jnp.int32).astype(jnp.int16)
        for t in range(rows // 16):
            msg_ref[block, 1 + t * len(tiles) + c] = coded[16 * t : 16 * t + 16]


def unpack(read, row_tiles, col_tiles):
    as_float = lambda x: x.astype(jnp.int32).astype(jnp.float32)
    scales = as_float(read(0))
    group = lane_group((16, LANES))
    factors = []
    for t in range(row_tiles):
        level = jnp.where(group == t, scales, 0.0)
        for shift in (LANES // 2, LANES // 4):
            level = level + pltpu.roll(level, shift, axis=1)
        factors.append(jnp.exp2(0.125 * level) * (1.0 / QUANT))
    return [
        jnp.concatenate([as_float(read(1 + t * col_tiles + c)) * factors[t] for t in range(row_tiles)], axis=0) for c in range(col_tiles)
    ]


def sums_kernel(
    me_ref, ids_ref, gain_ref, weight_ref, reflect_ref, conf_ref, sun_ref, prior_ref, keep_ref, msg_ref, sums_ref, *, scale, rows_here
):
    dates, bands, tile_rows, cols = reflect_ref.shape
    me = me_ref[0]
    block = rows_here * ENTRIES
    obs_count = 3 * bands
    first_tile = pl.program_id(1) * (cols // LANES)

    def lane_tile(index, carry):
        lanes = pl.ds(pl.multiple_of(index * LANES, LANES), LANES)
        for top in range(0, tile_rows, 8):
            acc = [None] * ENTRIES

            def add(entry, term):
                acc[entry] = term if acc[entry] is None else acc[entry] + term

            for d in range(dates):
                sensor = ids_ref[me * dates + d]
                volume, geometric = ross_li(
                    sun_ref[d, 0, top : top + 8, lanes], sun_ref[d, 1, top : top + 8, lanes], sun_ref[d, 2, top : top + 8, lanes]
                )
                weight = conf_ref[d, top : top + 8, lanes].astype(jnp.float32) * (weight_ref[sensor] * scale)
                weighted_vol = weight * volume
                weighted_geo = weight * geometric
                add(obs_count, weight)
                add(obs_count + 1, weighted_vol)
                add(obs_count + 2, weighted_geo)
                add(obs_count + 3, weighted_vol * volume)
                add(obs_count + 4, weighted_vol * geometric)
                add(obs_count + 5, weighted_geo * geometric)
                for b in range(bands):
                    tall = top // 16 * 16
                    signal = reflect_ref[d, b, tall : tall + 16, lanes].astype(jnp.float32)[top - tall : top - tall + 8]
                    signal = signal * gain_ref[sensor, b]
                    add(3 * b, weight * signal)
                    add(3 * b + 1, weighted_vol * signal)
                    add(3 * b + 2, weighted_geo * signal)
            for entry in range(ENTRIES):
                sums_ref[first_tile + index, pl.ds(top * ENTRIES + entry, 8, stride=ENTRIES), :] = acc[entry]
        return carry

    lax.fori_loop(0, cols // LANES, lane_tile, 0)

    @pl.when(pl.program_id(1) == pl.num_programs(1) - 1)
    def _():
        tiles = range(sums_ref.shape[0])
        first_row = pl.program_id(0) * tile_rows
        for row, source in ((me * rows_here - 1 - first_row, 0), ((me + 1) * rows_here - first_row, rows_here - 1)):

            @pl.when((row >= 0) & (row < tile_rows))
            def _():
                for c in tiles:
                    lanes = slice(c * LANES, (c + 1) * LANES)
                    at = pl.ds(pl.multiple_of(row * ENTRIES, 8), obs_count)
                    part = jnp.concatenate([prior_ref[e, source : source + 1, lanes] for e in range(obs_count)], axis=0)
                    sums_ref[c, at, :] = sums_ref[c, at, :] + SMOOTH_PULL * part

        bit = me % 2
        for j in range(keep_ref.shape[0]):
            own = pl.ds(pl.multiple_of((2 * j + bit) * block, 8), block)
            other = pl.ds(pl.multiple_of((2 * j + 1 - bit) * block, 8), block)
            for c in tiles:
                keep_ref[j, :, c * LANES : (c + 1) * LANES] = sums_ref[c, own, :]
            pack([sums_ref[c, other, :] for c in tiles], msg_ref, j)


def partial_sums(me, reflect, clear_conf, sun_view, sensor_id, band_gain, sensor_weight, prior, scale, chunk):
    dates, bands, rows, cols = reflect.shape
    cols = cols // CHUNKS
    rows_here = prior.shape[1]
    count = rows // rows_here
    tile_rows = 16
    width = min(256, cols)
    first = chunk * (cols // width)
    block = rows_here * ENTRIES
    per_tile = tile_rows // rows_here // 2
    places = 1 + block // 16 * (cols // LANES)
    smem = pl.BlockSpec(memory_space=pltpu.SMEM)
    return pl.pallas_call(
        functools.partial(sums_kernel, scale=scale, rows_here=rows_here),
        grid=(rows // tile_rows, cols // width),
        in_specs=[
            smem,
            smem,
            smem,
            smem,
            pl.BlockSpec((dates, bands, tile_rows, width), lambda i, j: (0, 0, i, first + j)),
            pl.BlockSpec((dates, tile_rows, width), lambda i, j: (0, i, first + j)),
            pl.BlockSpec((dates, 3, tile_rows, width), lambda i, j: (0, 0, i, first + j)),
            pl.BlockSpec((3 * bands, rows_here, cols), lambda i, j: (0, 0, chunk)),
        ],
        out_specs=[
            pl.BlockSpec((per_tile, block, cols), lambda i, j: (i, 0, 0)),
            pl.BlockSpec((per_tile, places, 16, LANES), lambda i, j: (i, 0, 0, 0)),
        ],
        out_shape=[
            jax.ShapeDtypeStruct((count // 2, block, cols), jnp.float32),
            jax.ShapeDtypeStruct((count // 2, places, 16, LANES), jnp.int16),
        ],
        scratch_shapes=[pltpu.VMEM((cols // LANES, tile_rows * ENTRIES, LANES), jnp.float32)],
        compiler_params=pltpu.CompilerParams(vmem_limit_bytes=(62 if chunk == 0 else 52) * 2**20),
        name="partial_sums",
    )(me, sensor_id, band_gain, sensor_weight, reflect, clear_conf, sun_view, prior)


def add_split_kernel(bit_ref, *refs, place):
    *parts, keep_ref, msg_ref = refs
    count, block, _ = keep_ref.shape
    bit = bit_ref[0]

    def total(j):
        tiles = []
        for kept_ref, got_ref in zip(parts[0::2], parts[1::2]):
            here = kept_ref.shape[2] // LANES
            came = unpack(lambda at: got_ref[j, at], block // 16, here)
            tiles += [kept_ref[j, :, c * LANES : (c + 1) * LANES] + came[c] for c in range(here)]
        return tiles

    for q in range(count):
        low = q % 2**place
        first = (q - low) * 2 + low
        pack(total(first + (1 - bit) * 2**place), msg_ref, q)
        for c, tile in enumerate(total(first + bit * 2**place)):
            keep_ref[q, :, c * LANES : (c + 1) * LANES] = tile


def add_split(bit, place, *parts):
    count, block, _ = parts[0].shape
    cols = sum(kept.shape[2] for kept in parts[0::2])
    vmem = pl.BlockSpec(memory_space=pltpu.VMEM)
    return pl.pallas_call(
        functools.partial(add_split_kernel, place=place),
        in_specs=[pl.BlockSpec(memory_space=pltpu.SMEM)] + [vmem] * len(parts),
        out_specs=[vmem, vmem],
        out_shape=[
            jax.ShapeDtypeStruct((count // 2, block, cols), jnp.float32),
            jax.ShapeDtypeStruct((count // 2, 1 + block // 16 * (cols // LANES), 16, LANES), jnp.int16),
        ],
        compiler_params=pltpu.CompilerParams(vmem_limit_bytes=24 * 2**20),
        name="add_split",
    )(bit, *parts)


def take(ref, start, size, stride):
    at = pl.ds(start, size, stride=stride)
    return jnp.concatenate([ref[c, at, :] for c in range(ref.shape[0])], axis=1)


def put(ref, start, size, stride, value):
    at = pl.ds(start, size, stride=stride)
    for c in range(ref.shape[0]):
        ref[c, at, :] = value[:, c * LANES : (c + 1) * LANES]


def beside_columns(x):
    cols = x.shape[1]
    col = lax.broadcasted_iota(jnp.int32, x.shape, 1)
    left = jnp.where(col == 0, 0.0, pltpu.roll(x, 1, axis=1))
    right = jnp.where(col == cols - 1, 0.0, pltpu.roll(x, cols - 1, axis=1))
    return left + right


def degree_of(row, shape, total_rows):
    col = lax.broadcasted_iota(jnp.int32, shape, 1)
    edge = (
        (row == 0).astype(jnp.float32)
        + (row == total_rows - 1).astype(jnp.float32)
        + (col == 0).astype(jnp.float32)
        + (col == shape[1] - 1).astype(jnp.float32)
    )
    return 4.0 - edge


def couple(n, v):
    return (
        n[0] * v[0] + n[1] * v[1] + n[2] * v[2],
        n[1] * v[0] + n[3] * v[1] + n[4] * v[2],
        n[2] * v[0] + n[4] * v[1] + n[5] * v[2],
    )


def residual_kernel(me_ref, prior_ref, *refs, total_rows):
    obs_count, rows_here, cols = prior_ref.shape
    *parts, out_ref, msg_ref, sums_ref = refs
    block = rows_here * ENTRIES
    tiles = cols // LANES
    at = 0
    for kept_ref, got_ref in zip(parts[0::2], parts[1::2]):
        here = kept_ref.shape[2] // LANES
        came = unpack(lambda place: got_ref[0, place], block // 16, here)
        for c in range(here):
            sums_ref[at] = kept_ref[0, :, c * LANES : (c + 1) * LANES] + came[c]
            at += 1
    shape = (rows_here, cols)
    row = me_ref[0] * rows_here + lax.broadcasted_iota(jnp.int32, shape, 0)
    degree = degree_of(row, shape, total_rows)
    normal = [take(sums_ref, obs_count + k, rows_here, ENTRIES) for k in range(6)]
    for b in range(obs_count // 3):
        fields = [prior_ref[3 * b + i] for i in range(3)]
        coupled = couple(normal, fields)
        for i in range(3):
            field = fields[i]
            beside = beside_columns(field)
            if rows_here > 1:
                zero = jnp.zeros((1, cols), jnp.float32)
                beside = beside + jnp.concatenate([zero, field[:-1]], axis=0) + jnp.concatenate([field[1:], zero], axis=0)
            entry = 3 * b + i
            observed = take(sums_ref, entry, rows_here, ENTRIES)
            put(sums_ref, entry, rows_here, ENTRIES, observed - coupled[i] - SMOOTH_PULL * (degree * field - beside))
    for c in range(tiles):
        out_ref[:, c * LANES : (c + 1) * LANES] = sums_ref[c]
    pack([sums_ref[c] for c in range(tiles)], msg_ref, 0)


def krylov_kernel(me_ref, own_ref, mate_ref, across_ref, far_ref, zero_ref, one_ref, two_ref, gram_ref, window_ref, *, total_rows, rows_here):
    cols = own_ref.shape[1]
    obs_count = ENTRIES - 6
    tiles = cols // LANES
    row_tiles = own_ref.shape[0] // 16

    def lay(place, part, r):
        at = pl.ds(place, ENTRIES, stride=8)
        for c in range(tiles):
            window_ref[c, at, :] = part[c][r * ENTRIES : (r + 1) * ENTRIES]

    own = [own_ref[:, c * LANES : (c + 1) * LANES] for c in range(tiles)]
    mate = unpack(lambda place: mate_ref[place], row_tiles, tiles)
    across = unpack(lambda place: across_ref[place], row_tiles, tiles)
    far = unpack(lambda place: far_ref[place], 2, tiles)
    odd = me_ref[0] % 2
    for r in range(2):
        lay(2 + r, own, r)
        lay(4 * (1 - odd) + r, mate, r)
        lay(4 * odd + r, across, r)
    lay(6, far, 0)
    put(window_ref, 7, ENTRIES, 8, jnp.zeros((ENTRIES, cols), jnp.float32))
    window = lambda entry: jnp.concatenate([window_ref[c, entry * 8 : entry * 8 + 8, :] for c in range(cols // LANES)], axis=1)
    shape = (8, cols)
    place = lax.broadcasted_iota(jnp.int32, shape, 0)
    row = me_ref[0] * rows_here + place - 2
    inside = ((row >= 0) & (row < total_rows)).astype(jnp.float32) * GAIN
    own_rows = (place == 2) | (place == 3)
    diag = inside * (PRIOR_PULL - SHIFT + SMOOTH_PULL * degree_of(row, shape, total_rows))
    pull = inside * SMOOTH_PULL
    normal = [window(obs_count + k) * inside for k in range(6)]
    acc = [jnp.zeros((8, LANES), jnp.float32) for _ in range(6)]

    def apply(v, last=False):
        coupled = couple(normal, v)
        out = []
        for i in range(3):
            x = v[i]
            above = pltpu.roll(x, 7, axis=0)
            beside = beside_columns(x) + (2.0 * above if last else above + pltpu.roll(x, 1, axis=0))
            out.append(coupled[i] + diag * x - pull * beside)
        return out

    def fold(x):
        total = x[:, 0:LANES]
        for c in range(LANES, cols, LANES):
            total = total + x[:, c : c + LANES]
        return total

    for b in range(obs_count // 3):
        zero = [window(3 * b + i) for i in range(3)]
        one = apply(zero)
        two = apply(one)
        three = apply(two, last=True)
        for i in range(3):
            zero_ref[3 * b + i] = zero[i][2:4]
            one_ref[3 * b + i] = one[i][2:4]
            two_ref[3 * b + i] = two[i][2:4]
            v = [zero[i], one[i], two[i], three[i]]
            for k in range(6):
                acc[k] = acc[k] + fold(v[k // 2] * v[(k + 1) // 2])
    own_tile = own_rows[:, 0:LANES]
    tile_row = lax.broadcasted_iota(jnp.int32, (8, LANES), 0)
    gram = jnp.zeros((8, LANES), jnp.float32)
    for k in range(6):
        moment = jnp.sum(jnp.where(own_tile, acc[k], 0.0))
        gram = jnp.where(tile_row == k, moment, gram)
    gram_ref[...] = gram


def combine_kernel(gram_ref, prior_ref, zero_ref, one_ref, two_ref, out_ref):
    gram = gram_ref[0]
    for k in range(1, gram_ref.shape[0]):
        gram = gram + gram_ref[k]
    m = [gram[k : k + 1, :] for k in range(6)]
    h = {(i, j): m[i + j + 1] * (1.0 / GAIN) + SHIFT * m[i + j] for i in range(3) for j in range(i, 3)}
    l10 = h[0, 1] / h[0, 0]
    l20 = h[0, 2] / h[0, 0]
    d1 = h[1, 1] - l10 * h[0, 1]
    t = h[1, 2] - l20 * h[0, 1]
    ok1 = d1 > 1e-6 * h[1, 1]
    inv1 = jnp.where(ok1, 1.0 / jnp.where(ok1, d1, 1.0), 0.0)
    l21 = t * inv1
    d2 = h[2, 2] - l20 * h[0, 2] - l21 * t
    ok2 = ok1 & (d2 > 1e-6 * h[2, 2])
    inv2 = jnp.where(ok2, 1.0 / jnp.where(ok2, d2, 1.0), 0.0)
    z1 = m[1] - l10 * m[0]
    z2 = m[2] - l20 * m[0] - l21 * z1
    y2 = z2 * inv2
    y1 = z1 * inv1 - l21 * y2
    y0 = m[0] / h[0, 0] - l10 * y1 - l20 * y2
    cols = prior_ref.shape[2]
    for c in range(0, cols, LANES):
        lanes = slice(c, c + LANES)
        out_ref[:, :, lanes] = (
            prior_ref[:, :, lanes] + y0[None] * zero_ref[:, :, lanes] + y1[None] * one_ref[:, :, lanes] + y2[None] * two_ref[:, :, lanes]
        )


def on_device(reflect, clear_conf, sun_view, sensor_id, band_gain, sensor_weight, prior):
    rows_here, obs_count, cols = prior.shape
    prior = jnp.transpose(prior, (1, 0, 2))
    count = lax.axis_size("rows")
    total_rows = rows_here * count
    block = rows_here * ENTRIES
    tiles = cols // LANES
    me = lax.axis_index("rows").astype(jnp.int32).reshape(1)
    vmem = pl.BlockSpec(memory_space=pltpu.VMEM)
    smem = pl.BlockSpec(memory_space=pltpu.SMEM)
    params = pltpu.CompilerParams(vmem_limit_bytes=24 * 2**20)
    f32 = lambda *shape: jax.ShapeDtypeStruct(shape, jnp.float32)

    scale = 0.01 / (reflect.shape[0] * count)
    index = me
    parts = []
    for chunk in range(CHUNKS):
        kept, sent = partial_sums(
            index, reflect, clear_conf, sun_view, sensor_id, band_gain, sensor_weight, prior, scale, chunk
        )
        index, _ = lax.optimization_barrier((me, sent))
        parts.append((kept, sent))
    swap = lambda x, bit: lax.ppermute(x, "rows", [(i, i ^ 1 << bit) for i in range(count)])
    bits = list(range(1, count.bit_length() - 1))
    parts = [(kept, swap(sent, 0)) for kept, sent in parts]
    if len(bits) >= 2:
        orders = [((bits[0], 0), (bits[1], 0)), ((bits[1], 1), (bits[0], 0))]
        for step in range(2):
            for chunk in range(CHUNKS):
                bit, place = orders[chunk % 2][step]
                kept, sent = add_split(me // 2**bit % 2, place, *parts[chunk])
                parts[chunk] = (kept, swap(sent, bit))
        bits = bits[2:]
    parts = [x for part in parts for x in part]
    for bit in bits:
        kept, sent = add_split(me // 2**bit % 2, 0, *parts)
        parts = [kept, swap(sent, bit)]

    own, msg = pl.pallas_call(
        functools.partial(residual_kernel, total_rows=total_rows),
        in_specs=[smem] + [vmem] * (1 + len(parts)),
        out_specs=[vmem, vmem],
        out_shape=[f32(block, cols), jax.ShapeDtypeStruct((1, 1 + block // 16 * tiles, 16, LANES), jnp.int16)],
        scratch_shapes=[pltpu.VMEM((tiles, block, LANES), jnp.float32)],
        compiler_params=params,
        name="residual",
    )(me, prior, *parts)

    msg = msg[0]
    mate = swap(msg, 0)
    border = [(i, i + 1) for i in range(1, count - 1, 2)]
    across = lax.ppermute(msg, "rows", border + [(target, source) for source, target in border])
    far = lax.ppermute(msg[: 1 + 2 * tiles], "rows", [(i + 2, i) for i in range(count - 2)])
    zero, one, two, gram = pl.pallas_call(
        functools.partial(krylov_kernel, total_rows=total_rows, rows_here=rows_here),
        in_specs=[smem, vmem, vmem, vmem, vmem],
        out_specs=[vmem] * 4,
        out_shape=[f32(obs_count, rows_here, cols)] * 3 + [f32(8, LANES)],
        scratch_shapes=[pltpu.VMEM((tiles, ENTRIES * 8, LANES), jnp.float32)],
        compiler_params=params,
        name="krylov",
    )(me, own, mate, across, far)

    grams = lax.all_to_all(jnp.broadcast_to(gram[None], (count, 8, LANES)), "rows", 0, 0)
    out = pl.pallas_call(
        combine_kernel,
        in_specs=[vmem] * 5,
        out_specs=vmem,
        out_shape=f32(obs_count, rows_here, cols),
        compiler_params=params,
        name="combine",
    )(grams, prior, zero, one, two)
    return jnp.transpose(out, (1, 0, 2))


def solution(mesh):
    return jax.shard_map(
        on_device,
        mesh=mesh,
        in_specs=(
            P("rows", None, None, "tiles"),
            P("rows", None, "tiles"),
            P("rows", None, None, "tiles"),
            P(),
            P(),
            P(),
            P("rows", None, "tiles"),
        ),
        out_specs=P("rows", None, "tiles"),
        check_vma=False,
    )
```

```python
import functools
import math

import jax
import jax.numpy as jnp
from jax import lax
from jax.experimental import pallas as pl
from jax.experimental.pallas import tpu as pltpu
from jax.sharding import PartitionSpec as P

TO_RADIAN = math.pi / 18000.0
PRIOR_PULL = 0.1
SMOOTH_PULL = 0.5
SHIFT = 3.0
GAIN = 0.4
ENTRIES = 24
LANES = 128
QUANT = 32000.0
GROUP = LANES // 4
CHUNKS = 2


R_POLY = (0.9428089773, 0.04714460664, 0.007527079489, 0.001965302741, 9.052799897e-05, 0.0004621408027)
S_POLY = (0.6002109608, -0.09003726006, -0.007977343822, -0.001801806492, 3.702625389e-06, -0.0003981650976)
SIN_25 = (0.9999999567, -0.1666626093, 0.008276695349)
COS_25 = (0.9999999997, -0.4999999562, 0.04166553086, -0.001379415437)
SIN_15 = (0.999999998, -0.1666661418, 0.008312938059)
COS_15 = (0.9999999858, -0.4999963087, 0.04152366947)
SIN_90 = (0.9999999947, -0.1666665666, 0.008333024663, -0.00019807389, 2.601844464e-06)


def horner(coefs, x):
    acc = coefs[-1] * x + coefs[-2]
    for coef in coefs[-3::-1]:
        acc = acc * x + coef
    return acc


def of_degrees(coefs, x, x2, factor, odd):
    scaled = [factor * coef * TO_RADIAN ** (2 * k + odd) for k, coef in enumerate(coefs)]
    value = horner(scaled, x2)
    return value * x if odd else value


def ross_li(sun, view, azim):
    x = (sun - 4500).astype(jnp.float32)
    x2 = x * x
    half = math.sqrt(0.5)
    sin_x, cos_x = of_degrees(SIN_25, x, x2, half, 1), of_degrees(COS_25, x, x2, half, 0)
    cos_sun, sin_sun = cos_x - sin_x, cos_x + sin_x
    v = view.astype(jnp.float32)
    v2 = v * v
    sin_view, cos_view = of_degrees(SIN_15, v, v2, 1.0, 1), of_degrees(COS_15, v, v2, 1.0, 0)
    a = (9000 - azim).astype(jnp.float32)
    cos_azim = of_degrees(SIN_90, a, a * a, 1.0, 1)
    prod = cos_sun * cos_view
    cos_phase = prod + sin_sun * sin_view * cos_azim
    total = cos_sun + cos_view
    recip = pl.reciprocal(total * prod, approx=False)
    inv_total = recip * prod
    sec_prod = recip * total
    u = 1.0 - cos_phase
    u_up = 1.0 + cos_phase
    bent = u * (u * lax.rsqrt(u)) * horner(R_POLY, u)
    volume = (bent + (0.5 * math.pi) * cos_phase) * inv_total - 0.25 * math.pi
    sin2 = u * u_up
    sin_phase = sin2 * lax.rsqrt(sin2)
    w = jnp.maximum(1.0 - (2.0 * inv_total) * sin_phase, 1e-30)
    overlap = w * (w * lax.rsqrt(w)) * horner(S_POLY, w)
    geometric = sec_prod * (total * (overlap - 1.0) + 0.5 * u_up)
    return volume, geometric


def lane_group(shape):
    return lax.broadcasted_iota(jnp.int32, shape, len(shape) - 1) // GROUP


def pack(tiles, msg_ref, block):
    rows = tiles[0].shape[0]
    top = jnp.abs(tiles[0])
    for tile in tiles[1:]:
        top = jnp.maximum(top, jnp.abs(tile))
    for shift in (LANES // 2, LANES // 4):
        top = jnp.maximum(top, pltpu.roll(top, shift, axis=1))
    level = jnp.ceil(8.0 * jnp.log2(jnp.maximum(top, 1e-30)))
    factor = QUANT * jnp.exp2(-0.125 * level)
    group = lane_group((16, LANES))
    scales = level[0:16]
    for t in range(1, rows // 16):
        scales = jnp.where(group == t, level[16 * t : 16 * t + 16], scales)
    scales = scales.astype(jnp.int32).astype(jnp.int16)
    msg_ref[block, 0] = scales
    numbers = [jnp.round(tile * factor).astype(jnp.int32) for tile in tiles]
    for c, number in enumerate(numbers):
        coded = number.astype(jnp.int16)
        for t in range(rows // 16):
            msg_ref[block, 1 + t * len(tiles) + c] = coded[16 * t : 16 * t + 16]
    return scales, numbers


def as_float(x):
    return x.astype(jnp.int32).astype(jnp.float32)


def factors_of(scales, row_tiles):
    scales = as_float(scales)
    group = lane_group((16, LANES))
    factors = []
    for t in range(row_tiles):
        level = jnp.where(group == t, scales, 0.0)
        for shift in (LANES // 2, LANES // 4):
            level = level + pltpu.roll(level, shift, axis=1)
        factors.append(jnp.exp2(0.125 * level) * (1.0 / QUANT))
    return factors


def unpack(read, row_tiles, col_tiles):
    factors = factors_of(read(0), row_tiles)
    return [
        jnp.concatenate([as_float(read(1 + t * col_tiles + c)) * factors[t] for t in range(row_tiles)], axis=0) for c in range(col_tiles)
    ]


def sums_kernel(
    me_ref, ids_ref, gain_ref, weight_ref, reflect_ref, conf_ref, sun_ref, prior_ref, keep_ref, msg_ref, sums_ref, *, scale, rows_here
):
    dates, bands, tile_rows, cols = reflect_ref.shape
    me = me_ref[0]
    block = rows_here * ENTRIES
    obs_count = 3 * bands
    first_tile = pl.program_id(1) * (cols // LANES)

    def lane_tile(index, carry):
        lanes = pl.ds(pl.multiple_of(index * LANES, LANES), LANES)
        for top in range(0, tile_rows, 8):
            acc = [None] * ENTRIES

            def add(entry, term):
                acc[entry] = term if acc[entry] is None else acc[entry] + term

            for d in range(dates):
                sensor = ids_ref[me * dates + d]
                volume, geometric = ross_li(
                    sun_ref[d, 0, top : top + 8, lanes], sun_ref[d, 1, top : top + 8, lanes], sun_ref[d, 2, top : top + 8, lanes]
                )
                weight = conf_ref[d, top : top + 8, lanes].astype(jnp.float32) * (weight_ref[sensor] * scale)
                weighted_vol = weight * volume
                weighted_geo = weight * geometric
                add(obs_count, weight)
                add(obs_count + 1, weighted_vol)
                add(obs_count + 2, weighted_geo)
                add(obs_count + 3, weighted_vol * volume)
                add(obs_count + 4, weighted_vol * geometric)
                add(obs_count + 5, weighted_geo * geometric)
                for b in range(bands):
                    tall = top // 16 * 16
                    signal = reflect_ref[d, b, tall : tall + 16, lanes].astype(jnp.float32)[top - tall : top - tall + 8]
                    signal = signal * gain_ref[sensor, b]
                    add(3 * b, weight * signal)
                    add(3 * b + 1, weighted_vol * signal)
                    add(3 * b + 2, weighted_geo * signal)
            for entry in range(ENTRIES):
                sums_ref[first_tile + index, pl.ds(top * ENTRIES + entry, 8, stride=ENTRIES), :] = acc[entry]
        return carry

    lax.fori_loop(0, cols // LANES, lane_tile, 0)

    @pl.when(pl.program_id(1) == pl.num_programs(1) - 1)
    def _():
        tiles = range(sums_ref.shape[0])
        first_row = pl.program_id(0) * tile_rows
        for row, source in ((me * rows_here - 1 - first_row, 0), ((me + 1) * rows_here - first_row, rows_here - 1)):

            @pl.when((row >= 0) & (row < tile_rows))
            def _():
                for c in tiles:
                    lanes = slice(c * LANES, (c + 1) * LANES)
                    at = pl.ds(pl.multiple_of(row * ENTRIES, 8), obs_count)
                    part = jnp.concatenate([prior_ref[e, source : source + 1, lanes] for e in range(obs_count)], axis=0)
                    sums_ref[c, at, :] = sums_ref[c, at, :] + SMOOTH_PULL * part

        bit = me % 2
        for j in range(keep_ref.shape[0]):
            own = pl.ds(pl.multiple_of((2 * j + bit) * block, 8), block)
            other = pl.ds(pl.multiple_of((2 * j + 1 - bit) * block, 8), block)
            for c in tiles:
                keep_ref[j, :, c * LANES : (c + 1) * LANES] = sums_ref[c, own, :]
            pack([sums_ref[c, other, :] for c in tiles], msg_ref, j)


def partial_sums(me, reflect, clear_conf, sun_view, sensor_id, band_gain, sensor_weight, prior, scale, chunk):
    dates, bands, rows, cols = reflect.shape
    cols = cols // CHUNKS
    rows_here = prior.shape[1]
    count = rows // rows_here
    tile_rows = 16
    width = min(256, cols)
    first = chunk * (cols // width)
    block = rows_here * ENTRIES
    per_tile = tile_rows // rows_here // 2
    places = 1 + block // 16 * (cols // LANES)
    smem = pl.BlockSpec(memory_space=pltpu.SMEM)
    return pl.pallas_call(
        functools.partial(sums_kernel, scale=scale, rows_here=rows_here),
        grid=(rows // tile_rows, cols // width),
        in_specs=[
            smem,
            smem,
            smem,
            smem,
            pl.BlockSpec((dates, bands, tile_rows, width), lambda i, j: (0, 0, i, first + j)),
            pl.BlockSpec((dates, tile_rows, width), lambda i, j: (0, i, first + j)),
            pl.BlockSpec((dates, 3, tile_rows, width), lambda i, j: (0, 0, i, first + j)),
            pl.BlockSpec((3 * bands, rows_here, cols), lambda i, j: (0, 0, chunk)),
        ],
        out_specs=[
            pl.BlockSpec((per_tile, block, cols), lambda i, j: (i, 0, 0)),
            pl.BlockSpec((per_tile, places, 16, LANES), lambda i, j: (i, 0, 0, 0)),
        ],
        out_shape=[
            jax.ShapeDtypeStruct((count // 2, block, cols), jnp.float32),
            jax.ShapeDtypeStruct((count // 2, places, 16, LANES), jnp.int16),
        ],
        scratch_shapes=[pltpu.VMEM((cols // LANES, tile_rows * ENTRIES, LANES), jnp.float32)],
        compiler_params=pltpu.CompilerParams(vmem_limit_bytes=(62 if chunk == 0 else 52) * 2**20),
        name="partial_sums",
    )(me, sensor_id, band_gain, sensor_weight, reflect, clear_conf, sun_view, prior)


def add_split_kernel(bit_ref, *refs, place):
    *parts, keep_ref, msg_ref = refs
    count, block, _ = keep_ref.shape
    bit = bit_ref[0]

    def total(j):
        tiles = []
        for kept_ref, got_ref in zip(parts[0::2], parts[1::2]):
            here = kept_ref.shape[2] // LANES
            came = unpack(lambda at: got_ref[j, at], block // 16, here)
            tiles += [kept_ref[j, :, c * LANES : (c + 1) * LANES] + came[c] for c in range(here)]
        return tiles

    for q in range(count):
        low = q % 2**place
        first = (q - low) * 2 + low
        pack(total(first + (1 - bit) * 2**place), msg_ref, q)
        for c, tile in enumerate(total(first + bit * 2**place)):
            keep_ref[q, :, c * LANES : (c + 1) * LANES] = tile


def add_split(bit, place, *parts):
    count, block, _ = parts[0].shape
    cols = sum(kept.shape[2] for kept in parts[0::2])
    vmem = pl.BlockSpec(memory_space=pltpu.VMEM)
    return pl.pallas_call(
        functools.partial(add_split_kernel, place=place),
        in_specs=[pl.BlockSpec(memory_space=pltpu.SMEM)] + [vmem] * len(parts),
        out_specs=[vmem, vmem],
        out_shape=[
            jax.ShapeDtypeStruct((count // 2, block, cols), jnp.float32),
            jax.ShapeDtypeStruct((count // 2, 1 + block // 16 * (cols // LANES), 16, LANES), jnp.int16),
        ],
        compiler_params=pltpu.CompilerParams(vmem_limit_bytes=24 * 2**20),
        name="add_split",
    )(bit, *parts)


def take(ref, start, size, stride):
    at = pl.ds(start, size, stride=stride)
    return jnp.concatenate([ref[c, at, :] for c in range(ref.shape[0])], axis=1)


def put(ref, start, size, stride, value):
    at = pl.ds(start, size, stride=stride)
    for c in range(ref.shape[0]):
        ref[c, at, :] = value[:, c * LANES : (c + 1) * LANES]


def beside_columns(x):
    cols = x.shape[1]
    col = lax.broadcasted_iota(jnp.int32, x.shape, 1)
    left = jnp.where(col == 0, 0.0, pltpu.roll(x, 1, axis=1))
    right = jnp.where(col == cols - 1, 0.0, pltpu.roll(x, cols - 1, axis=1))
    return left + right


def degree_of(row, shape, total_rows):
    col = lax.broadcasted_iota(jnp.int32, shape, 1)
    edge = (
        (row == 0).astype(jnp.float32)
        + (row == total_rows - 1).astype(jnp.float32)
        + (col == 0).astype(jnp.float32)
        + (col == shape[1] - 1).astype(jnp.float32)
    )
    return 4.0 - edge


def couple(n, v):
    return (
        n[0] * v[0] + n[1] * v[1] + n[2] * v[2],
        n[1] * v[0] + n[3] * v[1] + n[4] * v[2],
        n[2] * v[0] + n[4] * v[1] + n[5] * v[2],
    )


def residual_kernel(me_ref, prior_ref, *refs, total_rows):
    obs_count, rows_here, cols = prior_ref.shape
    *parts, out_ref, msg_ref, first_ref, sums_ref = refs
    block = rows_here * ENTRIES
    tiles = cols // LANES
    at = 0
    for kept_ref, got_ref in zip(parts[0::2], parts[1::2]):
        here = kept_ref.shape[2] // LANES
        came = unpack(lambda place: got_ref[0, place], block // 16, here)
        for c in range(here):
            sums_ref[at] = kept_ref[0, :, c * LANES : (c + 1) * LANES] + came[c]
            at += 1
    shape = (rows_here, cols)
    row = me_ref[0] * rows_here + lax.broadcasted_iota(jnp.int32, shape, 0)
    degree = degree_of(row, shape, total_rows)
    normal = [take(sums_ref, obs_count + k, rows_here, ENTRIES) for k in range(6)]
    for b in range(obs_count // 3):
        fields = [prior_ref[3 * b + i] for i in range(3)]
        coupled = couple(normal, fields)
        for i in range(3):
            field = fields[i]
            beside = beside_columns(field)
            if rows_here > 1:
                zero = jnp.zeros((1, cols), jnp.float32)
                beside = beside + jnp.concatenate([zero, field[:-1]], axis=0) + jnp.concatenate([field[1:], zero], axis=0)
            entry = 3 * b + i
            observed = take(sums_ref, entry, rows_here, ENTRIES)
            put(sums_ref, entry, rows_here, ENTRIES, observed - coupled[i] - SMOOTH_PULL * (degree * field - beside))
    for c in range(tiles):
        out_ref[:, c * LANES : (c + 1) * LANES] = sums_ref[c]
    scales, numbers = pack([sums_ref[c] for c in range(tiles)], msg_ref, 0)
    first_ref[0] = scales
    for c in range(tiles):
        first_ref[1 + c] = numbers[c][0:16].astype(jnp.int16)
    left = jnp.concatenate([number[16:obs_count] for number in numbers], axis=0)
    spare = (first_ref.shape[0] - 1 - tiles) * 16 - left.shape[0]
    if spare:
        left = jnp.concatenate([left, jnp.zeros((spare, LANES), jnp.int32)], axis=0)
    for t in range(left.shape[0] // 16):
        first_ref[1 + tiles + t] = left[16 * t : 16 * t + 16].astype(jnp.int16)


def krylov_kernel(me_ref, own_ref, mate_ref, across_ref, zero_ref, one_ref, two_ref, gram_ref, window_ref, *, total_rows, rows_here):
    cols = own_ref.shape[1]
    obs_count = ENTRIES - 6
    tiles = cols // LANES
    row_tiles = own_ref.shape[0] // 16

    def lay(place, part, r):
        at = pl.ds(place, ENTRIES, stride=8)
        for c in range(tiles):
            window_ref[c, at, :] = part[c][r * ENTRIES : (r + 1) * ENTRIES]

    own = [own_ref[:, c * LANES : (c + 1) * LANES] for c in range(tiles)]
    mate = unpack(lambda place: mate_ref[place], row_tiles, tiles)
    across = unpack(lambda place: across_ref[place], row_tiles, tiles)
    odd = me_ref[0] % 2
    for r in range(2):
        lay(2 + r, own, r)
        lay(4 * (1 - odd) + r, mate, r)
        lay(4 * odd + r, across, r)
    for empty in (6, 7):
        put(window_ref, empty, ENTRIES, 8, jnp.zeros((ENTRIES, cols), jnp.float32))
    window = lambda entry: jnp.concatenate([window_ref[c, entry * 8 : entry * 8 + 8, :] for c in range(cols // LANES)], axis=1)
    shape = (8, cols)
    place = lax.broadcasted_iota(jnp.int32, shape, 0)
    row = me_ref[0] * rows_here + place - 2
    inside = ((row >= 0) & (row < total_rows)).astype(jnp.float32) * GAIN
    own_rows = (place == 2) | (place == 3)
    diag = inside * (PRIOR_PULL - SHIFT + SMOOTH_PULL * degree_of(row, shape, total_rows))
    pull = inside * SMOOTH_PULL
    normal = [window(obs_count + k) * inside for k in range(6)]
    acc = [jnp.zeros((8, LANES), jnp.float32) for _ in range(6)]

    def apply(v, last=False):
        coupled = couple(normal, v)
        out = []
        for i in range(3):
            x = v[i]
            above = pltpu.roll(x, 7, axis=0)
            beside = beside_columns(x) + (2.0 * above if last else above + pltpu.roll(x, 1, axis=0))
            out.append(coupled[i] + diag * x - pull * beside)
        return out

    def fold(x):
        total = x[:, 0:LANES]
        for c in range(LANES, cols, LANES):
            total = total + x[:, c : c + LANES]
        return total

    for b in range(obs_count // 3):
        zero = [window(3 * b + i) for i in range(3)]
        one = apply(zero)
        two = apply(one)
        three = apply(two, last=True)
        for i in range(3):
            zero_ref[3 * b + i] = zero[i][2:4]
            one_ref[3 * b + i] = one[i][2:4]
            two_ref[3 * b + i] = two[i][2:4]
            v = [zero[i], one[i], two[i], three[i]]
            for k in range(6):
                acc[k] = acc[k] + fold(v[k // 2] * v[(k + 1) // 2])
    own_tile = own_rows[:, 0:LANES]
    tile_row = lax.broadcasted_iota(jnp.int32, (8, LANES), 0)
    gram = jnp.zeros((8, LANES), jnp.float32)
    for k in range(6):
        moment = jnp.sum(jnp.where(own_tile, acc[k], 0.0))
        gram = jnp.where(tile_row == k, moment, gram)
    gram_ref[...] = gram


def far_kernel(gram_ref, two_ref, far_ref, out_ref):
    obs_count, _, cols = two_ref.shape
    tiles = cols // LANES
    rest = obs_count - 16
    factors = factors_of(far_ref[0], 2)
    left = jnp.concatenate([as_float(far_ref[t]) for t in range(1 + tiles, far_ref.shape[0])], axis=0)
    total = jnp.zeros((obs_count, LANES), jnp.float32)
    for c in range(tiles):
        far = jnp.concatenate([as_float(far_ref[1 + c]) * factors[0], left[rest * c : rest * (c + 1)] * factors[1][0:rest]], axis=0)
        mine = jnp.concatenate([two_ref[e, 1:2, c * LANES : (c + 1) * LANES] for e in range(obs_count)], axis=0)
        total = total + far * mine
    part = (-2.0 * (GAIN * SMOOTH_PULL) ** 3) * jnp.sum(total)
    row = lax.broadcasted_iota(jnp.int32, (8, LANES), 0)
    out_ref[...] = gram_ref[...] + jnp.where(row == 5, part, 0.0)


def combine_kernel(*refs):
    *gram_refs, prior_ref, zero_ref, one_ref, two_ref, out_ref = refs
    gram = gram_refs[0][...]
    for ref in gram_refs[1:]:
        gram = gram + ref[...]
    m = [gram[k : k + 1, :] for k in range(6)]
    h = {(i, j): m[i + j + 1] * (1.0 / GAIN) + SHIFT * m[i + j] for i in range(3) for j in range(i, 3)}
    l10 = h[0, 1] / h[0, 0]
    l20 = h[0, 2] / h[0, 0]
    d1 = h[1, 1] - l10 * h[0, 1]
    t = h[1, 2] - l20 * h[0, 1]
    ok1 = d1 > 1e-6 * h[1, 1]
    inv1 = jnp.where(ok1, 1.0 / jnp.where(ok1, d1, 1.0), 0.0)
    l21 = t * inv1
    d2 = h[2, 2] - l20 * h[0, 2] - l21 * t
    ok2 = ok1 & (d2 > 1e-6 * h[2, 2])
    inv2 = jnp.where(ok2, 1.0 / jnp.where(ok2, d2, 1.0), 0.0)
    z1 = m[1] - l10 * m[0]
    z2 = m[2] - l20 * m[0] - l21 * z1
    y2 = z2 * inv2
    y1 = z1 * inv1 - l21 * y2
    y0 = m[0] / h[0, 0] - l10 * y1 - l20 * y2
    cols = prior_ref.shape[2]
    for c in range(0, cols, LANES):
        lanes = slice(c, c + LANES)
        out_ref[:, :, lanes] = (
            prior_ref[:, :, lanes] + y0[None] * zero_ref[:, :, lanes] + y1[None] * one_ref[:, :, lanes] + y2[None] * two_ref[:, :, lanes]
        )


def on_device(reflect, clear_conf, sun_view, sensor_id, band_gain, sensor_weight, prior):
    rows_here, obs_count, cols = prior.shape
    prior = jnp.transpose(prior, (1, 0, 2))
    count = lax.axis_size("rows")
    total_rows = rows_here * count
    block = rows_here * ENTRIES
    tiles = cols // LANES
    me = lax.axis_index("rows").astype(jnp.int32).reshape(1)
    vmem = pl.BlockSpec(memory_space=pltpu.VMEM)
    smem = pl.BlockSpec(memory_space=pltpu.SMEM)
    params = pltpu.CompilerParams(vmem_limit_bytes=24 * 2**20)
    f32 = lambda *shape: jax.ShapeDtypeStruct(shape, jnp.float32)
    packed = lambda *shape: jax.ShapeDtypeStruct(shape + (16, LANES), jnp.int16)

    scale = 0.01 / (reflect.shape[0] * count)
    index = me
    parts = []
    for chunk in range(CHUNKS):
        kept, sent = partial_sums(
            index, reflect, clear_conf, sun_view, sensor_id, band_gain, sensor_weight, prior, scale, chunk
        )
        index, _ = lax.optimization_barrier((me, sent))
        parts.append((kept, sent))
    flip = lambda x, mask: lax.ppermute(x, "rows", [(i, i ^ mask) for i in range(count)])
    swap = lambda x, bit: flip(x, 1 << bit)
    bits = list(range(1, count.bit_length() - 1))
    parts = [(kept, swap(sent, 0)) for kept, sent in parts]
    if len(bits) >= 2:
        orders = [((bits[0], 0), (bits[1], 0)), ((bits[1], 1), (bits[0], 0))]
        for step in range(2):
            for chunk in range(CHUNKS):
                bit, place = orders[chunk % 2][step]
                kept, sent = add_split(me // 2**bit % 2, place, *parts[chunk])
                parts[chunk] = (kept, swap(sent, bit))
        bits = bits[2:]
    parts = [x for part in parts for x in part]
    for bit in bits:
        kept, sent = add_split(me // 2**bit % 2, 0, *parts)
        parts = [kept, swap(sent, bit)]

    own, msg, first = pl.pallas_call(
        functools.partial(residual_kernel, total_rows=total_rows),
        in_specs=[smem] + [vmem] * (1 + len(parts)),
        out_specs=[vmem, vmem, vmem],
        out_shape=[f32(block, cols), packed(1, 1 + block // 16 * tiles), packed(1 + tiles + -(-(obs_count - 16) * tiles // 16))],
        scratch_shapes=[pltpu.VMEM((tiles, block, LANES), jnp.float32)],
        compiler_params=params,
        name="residual",
    )(me, prior, *parts)

    msg = msg[0]
    mate = swap(msg, 0)
    border = [(i, i + 1) for i in range(1, count - 1, 2)]
    across = lax.ppermute(msg, "rows", border + [(target, source) for source, target in border])
    far = lax.ppermute(first, "rows", [(i + 2, i) for i in range(count - 2)])
    zero, one, two, gram = pl.pallas_call(
        functools.partial(krylov_kernel, total_rows=total_rows, rows_here=rows_here),
        in_specs=[smem, vmem, vmem, vmem],
        out_specs=[vmem] * 4,
        out_shape=[f32(obs_count, rows_here, cols)] * 3 + [f32(8, LANES)],
        scratch_shapes=[pltpu.VMEM((tiles, ENTRIES * 8, LANES), jnp.float32)],
        compiler_params=params,
        name="krylov",
    )(me, own, mate, across)

    grams = [
        pl.pallas_call(
            far_kernel, in_specs=[vmem] * 3, out_specs=vmem, out_shape=f32(8, LANES), compiler_params=params, name="far"
        )(gram, two, far)
    ]
    for bit in range(0, count.bit_length() - 1, 2):
        masks = [mask << bit for mask in (1, 2, 3) if mask << bit < count]
        gram = sum(grams[1:], grams[0])
        grams = [gram] + [flip(gram, mask) for mask in masks]
    out = pl.pallas_call(
        combine_kernel,
        in_specs=[vmem] * (len(grams) + 4),
        out_specs=vmem,
        out_shape=f32(obs_count, rows_here, cols),
        compiler_params=params,
        name="combine",
    )(*grams, prior, zero, one, two)
    return jnp.transpose(out, (1, 0, 2))


def solution(mesh):
    return jax.shard_map(
        on_device,
        mesh=mesh,
        in_specs=(
            P("rows", None, None, "tiles"),
            P("rows", None, "tiles"),
            P("rows", None, None, "tiles"),
            P(),
            P(),
            P(),
            P("rows", None, "tiles"),
        ),
        out_specs=P("rows", None, "tiles"),
        check_vma=False,
    )
```

```python
import functools
import math

import jax
import jax.numpy as jnp
from jax import lax
from jax.experimental import pallas as pl
from jax.experimental.pallas import tpu as pltpu
from jax.sharding import PartitionSpec as P

TO_RADIAN = math.pi / 18000.0
PRIOR_PULL = 0.1
SMOOTH_PULL = 0.5
SHIFT = 3.0
GAIN = 0.4
ENTRIES = 24
LANES = 128
QUANT = 32000.0
GROUP = LANES // 4
CHUNKS = 2


R_POLY = (0.9428089773, 0.04714460664, 0.007527079489, 0.001965302741, 9.052799897e-05, 0.0004621408027)
S_POLY = (0.6002109608, -0.09003726006, -0.007977343822, -0.001801806492, 3.702625389e-06, -0.0003981650976)
SIN_25 = (0.9999999567, -0.1666626093, 0.008276695349)
COS_25 = (0.9999999997, -0.4999999562, 0.04166553086, -0.001379415437)
SIN_15 = (0.999999998, -0.1666661418, 0.008312938059)
COS_15 = (0.9999999858, -0.4999963087, 0.04152366947)
SIN_90 = (0.9999999947, -0.1666665666, 0.008333024663, -0.00019807389, 2.601844464e-06)


def horner(coefs, x):
    acc = coefs[-1] * x + coefs[-2]
    for coef in coefs[-3::-1]:
        acc = acc * x + coef
    return acc


def of_degrees(coefs, x, x2, factor, odd):
    scaled = [factor * coef * TO_RADIAN ** (2 * k + odd) for k, coef in enumerate(coefs)]
    value = horner(scaled, x2)
    return value * x if odd else value


def ross_li(sun, view, azim):
    x = (sun - 4500).astype(jnp.float32)
    x2 = x * x
    half = math.sqrt(0.5)
    sin_x, cos_x = of_degrees(SIN_25, x, x2, half, 1), of_degrees(COS_25, x, x2, half, 0)
    cos_sun, sin_sun = cos_x - sin_x, cos_x + sin_x
    v = view.astype(jnp.float32)
    v2 = v * v
    sin_view, cos_view = of_degrees(SIN_15, v, v2, 1.0, 1), of_degrees(COS_15, v, v2, 1.0, 0)
    a = (9000 - azim).astype(jnp.float32)
    cos_azim = of_degrees(SIN_90, a, a * a, 1.0, 1)
    prod = cos_sun * cos_view
    cos_phase = prod + sin_sun * sin_view * cos_azim
    total = cos_sun + cos_view
    recip = pl.reciprocal(total * prod, approx=False)
    inv_total = recip * prod
    sec_prod = recip * total
    u = 1.0 - cos_phase
    u_up = 1.0 + cos_phase
    bent = u * (u * lax.rsqrt(u)) * horner(R_POLY, u)
    volume = (bent + (0.5 * math.pi) * cos_phase) * inv_total - 0.25 * math.pi
    sin2 = u * u_up
    sin_phase = sin2 * lax.rsqrt(sin2)
    w = jnp.maximum(1.0 - (2.0 * inv_total) * sin_phase, 1e-30)
    overlap = w * (w * lax.rsqrt(w)) * horner(S_POLY, w)
    geometric = sec_prod * (total * (overlap - 1.0) + 0.5 * u_up)
    return volume, geometric


def lane_group(shape):
    return lax.broadcasted_iota(jnp.int32, shape, len(shape) - 1) // GROUP


def pack(tiles, msg_ref, block):
    rows = tiles[0].shape[0]
    top = jnp.abs(tiles[0])
    for tile in tiles[1:]:
        top = jnp.maximum(top, jnp.abs(tile))
    for shift in (LANES // 2, LANES // 4):
        top = jnp.maximum(top, pltpu.roll(top, shift, axis=1))
    level = jnp.ceil(8.0 * jnp.log2(jnp.maximum(top, 1e-30)))
    factor = QUANT * jnp.exp2(-0.125 * level)
    group = lane_group((16, LANES))
    scales = level[0:16]
    for t in range(1, rows // 16):
        scales = jnp.where(group == t, level[16 * t : 16 * t + 16], scales)
    scales = scales.astype(jnp.int32).astype(jnp.int16)
    msg_ref[block, 0] = scales
    numbers = [jnp.round(tile * factor).astype(jnp.int32) for tile in tiles]
    for c, number in enumerate(numbers):
        coded = number.astype(jnp.int16)
        for t in range(rows // 16):
            msg_ref[block, 1 + t * len(tiles) + c] = coded[16 * t : 16 * t + 16]
    return scales, numbers


def as_float(x):
    return x.astype(jnp.int32).astype(jnp.float32)


def factors_of(scales, row_tiles):
    scales = as_float(scales)
    group = lane_group((16, LANES))
    factors = []
    for t in range(row_tiles):
        level = jnp.where(group == t, scales, 0.0)
        for shift in (LANES // 2, LANES // 4):
            level = level + pltpu.roll(level, shift, axis=1)
        factors.append(jnp.exp2(0.125 * level) * (1.0 / QUANT))
    return factors


def unpack(read, row_tiles, col_tiles):
    factors = factors_of(read(0), row_tiles)
    return [
        jnp.concatenate([as_float(read(1 + t * col_tiles + c)) * factors[t] for t in range(row_tiles)], axis=0) for c in range(col_tiles)
    ]


def sums_kernel(
    me_ref, ids_ref, gain_ref, weight_ref, reflect_ref, conf_ref, sun_ref, prior_ref, keep_ref, msg_ref, sums_ref, kernels_ref, *, scale, rows_here
):
    dates, bands, tile_rows, cols = reflect_ref.shape
    me = me_ref[0]
    block = rows_here * ENTRIES
    obs_count = 3 * bands
    first_tile = pl.program_id(1) * (cols // LANES)

    def lane_tile(index, carry):
        lanes = pl.ds(pl.multiple_of(index * LANES, LANES), LANES)
        sensors = [ids_ref[me * dates + d] for d in range(dates)]

        def store(top, entry, total):
            sums_ref[first_tile + index, pl.ds(top * ENTRIES + entry, 8, stride=ENTRIES), :] = total

        def plus(total, term):
            return term if total is None else total + term

        for top in range(0, tile_rows, 8):
            normal = [None] * 6
            for d in range(dates):
                volume, geometric = ross_li(
                    sun_ref[d, 0, top : top + 8, lanes], sun_ref[d, 1, top : top + 8, lanes], sun_ref[d, 2, top : top + 8, lanes]
                )
                weight = conf_ref[d, top : top + 8, lanes].astype(jnp.float32) * (weight_ref[sensors[d]] * scale)
                weighted_vol = weight * volume
                weighted_geo = weight * geometric
                for i, value in enumerate((weight, weighted_vol, weighted_geo)):
                    kernels_ref[d, i, top : top + 8, :] = value
                terms = (weight, weighted_vol, weighted_geo, weighted_vol * volume, weighted_vol * geometric, weighted_geo * geometric)
                normal = [plus(total, term) for total, term in zip(normal, terms)]
            for k in range(6):
                store(top, obs_count + k, normal[k])
        for b in range(bands):
            observed = [None] * 3
            for d in range(dates):
                signal = reflect_ref[d, b, :, lanes].astype(jnp.float32) * gain_ref[sensors[d], b]
                observed = [plus(total, kernels_ref[d, i] * signal) for i, total in enumerate(observed)]
            for i in range(3):
                for top in range(0, tile_rows, 8):
                    store(top, 3 * b + i, observed[i][top : top + 8])
        return carry

    lax.fori_loop(0, cols // LANES, lane_tile, 0)

    @pl.when(pl.program_id(1) == pl.num_programs(1) - 1)
    def _():
        tiles = range(sums_ref.shape[0])
        first_row = pl.program_id(0) * tile_rows
        for row, source in ((me * rows_here - 1 - first_row, 0), ((me + 1) * rows_here - first_row, rows_here - 1)):

            @pl.when((row >= 0) & (row < tile_rows))
            def _():
                for c in tiles:
                    lanes = slice(c * LANES, (c + 1) * LANES)
                    at = pl.ds(pl.multiple_of(row * ENTRIES, 8), obs_count)
                    part = jnp.concatenate([prior_ref[e, source : source + 1, lanes] for e in range(obs_count)], axis=0)
                    sums_ref[c, at, :] = sums_ref[c, at, :] + SMOOTH_PULL * part

        bit = me % 2
        for j in range(keep_ref.shape[0]):
            own = pl.ds(pl.multiple_of((2 * j + bit) * block, 8), block)
            other = pl.ds(pl.multiple_of((2 * j + 1 - bit) * block, 8), block)
            for c in tiles:
                keep_ref[j, :, c * LANES : (c + 1) * LANES] = sums_ref[c, own, :]
            pack([sums_ref[c, other, :] for c in tiles], msg_ref, j)


def partial_sums(me, reflect, clear_conf, sun_view, sensor_id, band_gain, sensor_weight, prior, scale, chunk):
    dates, bands, rows, cols = reflect.shape
    cols = cols // CHUNKS
    rows_here = prior.shape[1]
    count = rows // rows_here
    tile_rows = 16
    width = min(256, cols)
    first = chunk * (cols // width)
    block = rows_here * ENTRIES
    per_tile = tile_rows // rows_here // 2
    places = 1 + block // 16 * (cols // LANES)
    smem = pl.BlockSpec(memory_space=pltpu.SMEM)
    return pl.pallas_call(
        functools.partial(sums_kernel, scale=scale, rows_here=rows_here),
        grid=(rows // tile_rows, cols // width),
        in_specs=[
            smem,
            smem,
            smem,
            smem,
            pl.BlockSpec((dates, bands, tile_rows, width), lambda i, j: (0, 0, i, first + j)),
            pl.BlockSpec((dates, tile_rows, width), lambda i, j: (0, i, first + j)),
            pl.BlockSpec((dates, 3, tile_rows, width), lambda i, j: (0, 0, i, first + j)),
            pl.BlockSpec((3 * bands, rows_here, cols), lambda i, j: (0, 0, chunk)),
        ],
        out_specs=[
            pl.BlockSpec((per_tile, block, cols), lambda i, j: (i, 0, 0)),
            pl.BlockSpec((per_tile, places, 16, LANES), lambda i, j: (i, 0, 0, 0)),
        ],
        out_shape=[
            jax.ShapeDtypeStruct((count // 2, block, cols), jnp.float32),
            jax.ShapeDtypeStruct((count // 2, places, 16, LANES), jnp.int16),
        ],
        scratch_shapes=[
            pltpu.VMEM((cols // LANES, tile_rows * ENTRIES, LANES), jnp.float32),
            pltpu.VMEM((dates, 3, tile_rows, LANES), jnp.float32),
        ],
        compiler_params=pltpu.CompilerParams(vmem_limit_bytes=(62 if chunk == 0 else 52) * 2**20),
        name="partial_sums",
    )(me, sensor_id, band_gain, sensor_weight, reflect, clear_conf, sun_view, prior)


def add_split_kernel(bit_ref, *refs, place):
    *parts, keep_ref, msg_ref = refs
    count, block, _ = keep_ref.shape
    bit = bit_ref[0]

    def total(j):
        tiles = []
        for kept_ref, got_ref in zip(parts[0::2], parts[1::2]):
            here = kept_ref.shape[2] // LANES
            came = unpack(lambda at: got_ref[j, at], block // 16, here)
            tiles += [kept_ref[j, :, c * LANES : (c + 1) * LANES] + came[c] for c in range(here)]
        return tiles

    for q in range(count):
        low = q % 2**place
        first = (q - low) * 2 + low
        pack(total(first + (1 - bit) * 2**place), msg_ref, q)
        for c, tile in enumerate(total(first + bit * 2**place)):
            keep_ref[q, :, c * LANES : (c + 1) * LANES] = tile


def add_split(bit, place, *parts):
    count, block, _ = parts[0].shape
    cols = sum(kept.shape[2] for kept in parts[0::2])
    vmem = pl.BlockSpec(memory_space=pltpu.VMEM)
    return pl.pallas_call(
        functools.partial(add_split_kernel, place=place),
        in_specs=[pl.BlockSpec(memory_space=pltpu.SMEM)] + [vmem] * len(parts),
        out_specs=[vmem, vmem],
        out_shape=[
            jax.ShapeDtypeStruct((count // 2, block, cols), jnp.float32),
            jax.ShapeDtypeStruct((count // 2, 1 + block // 16 * (cols // LANES), 16, LANES), jnp.int16),
        ],
        compiler_params=pltpu.CompilerParams(vmem_limit_bytes=24 * 2**20),
        name="add_split",
    )(bit, *parts)


def take(ref, start, size, stride):
    at = pl.ds(start, size, stride=stride)
    return jnp.concatenate([ref[c, at, :] for c in range(ref.shape[0])], axis=1)


def put(ref, start, size, stride, value):
    at = pl.ds(start, size, stride=stride)
    for c in range(ref.shape[0]):
        ref[c, at, :] = value[:, c * LANES : (c + 1) * LANES]


def beside_columns(x):
    cols = x.shape[1]
    col = lax.broadcasted_iota(jnp.int32, x.shape, 1)
    left = jnp.where(col == 0, 0.0, pltpu.roll(x, 1, axis=1))
    right = jnp.where(col == cols - 1, 0.0, pltpu.roll(x, cols - 1, axis=1))
    return left + right


def degree_of(row, shape, total_rows):
    col = lax.broadcasted_iota(jnp.int32, shape, 1)
    edge = (
        (row == 0).astype(jnp.float32)
        + (row == total_rows - 1).astype(jnp.float32)
        + (col == 0).astype(jnp.float32)
        + (col == shape[1] - 1).astype(jnp.float32)
    )
    return 4.0 - edge


def couple(n, v):
    return (
        n[0] * v[0] + n[1] * v[1] + n[2] * v[2],
        n[1] * v[0] + n[3] * v[1] + n[4] * v[2],
        n[2] * v[0] + n[4] * v[1] + n[5] * v[2],
    )


def residual_kernel(me_ref, prior_ref, *refs, total_rows):
    obs_count, rows_here, cols = prior_ref.shape
    *parts, out_ref, msg_ref, first_ref, sums_ref = refs
    block = rows_here * ENTRIES
    tiles = cols // LANES
    at = 0
    for kept_ref, got_ref in zip(parts[0::2], parts[1::2]):
        here = kept_ref.shape[2] // LANES
        came = unpack(lambda place: got_ref[0, place], block // 16, here)
        for c in range(here):
            sums_ref[at] = kept_ref[0, :, c * LANES : (c + 1) * LANES] + came[c]
            at += 1
    shape = (rows_here, cols)
    row = me_ref[0] * rows_here + lax.broadcasted_iota(jnp.int32, shape, 0)
    degree = degree_of(row, shape, total_rows)
    normal = [take(sums_ref, obs_count + k, rows_here, ENTRIES) for k in range(6)]
    for b in range(obs_count // 3):
        fields = [prior_ref[3 * b + i] for i in range(3)]
        coupled = couple(normal, fields)
        for i in range(3):
            field = fields[i]
            beside = beside_columns(field)
            if rows_here > 1:
                zero = jnp.zeros((1, cols), jnp.float32)
                beside = beside + jnp.concatenate([zero, field[:-1]], axis=0) + jnp.concatenate([field[1:], zero], axis=0)
            entry = 3 * b + i
            observed = take(sums_ref, entry, rows_here, ENTRIES)
            put(sums_ref, entry, rows_here, ENTRIES, observed - coupled[i] - SMOOTH_PULL * (degree * field - beside))
    for c in range(tiles):
        out_ref[:, c * LANES : (c + 1) * LANES] = sums_ref[c]
    scales, numbers = pack([sums_ref[c] for c in range(tiles)], msg_ref, 0)
    first_ref[0] = scales
    for c in range(tiles):
        first_ref[1 + c] = numbers[c][0:16].astype(jnp.int16)
    left = jnp.concatenate([number[16:obs_count] for number in numbers], axis=0)
    spare = (first_ref.shape[0] - 1 - tiles) * 16 - left.shape[0]
    if spare:
        left = jnp.concatenate([left, jnp.zeros((spare, LANES), jnp.int32)], axis=0)
    for t in range(left.shape[0] // 16):
        first_ref[1 + tiles + t] = left[16 * t : 16 * t + 16].astype(jnp.int16)


def krylov_kernel(me_ref, own_ref, mate_ref, across_ref, zero_ref, one_ref, two_ref, gram_ref, window_ref, *, total_rows, rows_here):
    cols = own_ref.shape[1]
    obs_count = ENTRIES - 6
    tiles = cols // LANES
    row_tiles = own_ref.shape[0] // 16

    def lay(place, part, r):
        at = pl.ds(place, ENTRIES, stride=8)
        for c in range(tiles):
            window_ref[c, at, :] = part[c][r * ENTRIES : (r + 1) * ENTRIES]

    own = [own_ref[:, c * LANES : (c + 1) * LANES] for c in range(tiles)]
    mate = unpack(lambda place: mate_ref[place], row_tiles, tiles)
    across = unpack(lambda place: across_ref[place], row_tiles, tiles)
    odd = me_ref[0] % 2
    for r in range(2):
        lay(2 + r, own, r)
        lay(4 * (1 - odd) + r, mate, r)
        lay(4 * odd + r, across, r)
    for empty in (6, 7):
        put(window_ref, empty, ENTRIES, 8, jnp.zeros((ENTRIES, cols), jnp.float32))
    window = lambda entry: jnp.concatenate([window_ref[c, entry * 8 : entry * 8 + 8, :] for c in range(cols // LANES)], axis=1)
    shape = (8, cols)
    place = lax.broadcasted_iota(jnp.int32, shape, 0)
    row = me_ref[0] * rows_here + place - 2
    inside = ((row >= 0) & (row < total_rows)).astype(jnp.float32) * GAIN
    own_rows = (place == 2) | (place == 3)
    diag = inside * (PRIOR_PULL - SHIFT + SMOOTH_PULL * degree_of(row, shape, total_rows))
    pull = inside * SMOOTH_PULL
    normal = [window(obs_count + k) * inside for k in range(6)]
    acc = [jnp.zeros((8, LANES), jnp.float32) for _ in range(6)]

    def apply(v, last=False):
        coupled = couple(normal, v)
        out = []
        for i in range(3):
            x = v[i]
            above = pltpu.roll(x, 7, axis=0)
            beside = beside_columns(x) + (2.0 * above if last else above + pltpu.roll(x, 1, axis=0))
            out.append(coupled[i] + diag * x - pull * beside)
        return out

    def fold(x):
        total = x[:, 0:LANES]
        for c in range(LANES, cols, LANES):
            total = total + x[:, c : c + LANES]
        return total

    for b in range(obs_count // 3):
        zero = [window(3 * b + i) for i in range(3)]
        one = apply(zero)
        two = apply(one)
        three = apply(two, last=True)
        for i in range(3):
            zero_ref[3 * b + i] = zero[i][2:4]
            one_ref[3 * b + i] = one[i][2:4]
            two_ref[3 * b + i] = two[i][2:4]
            v = [zero[i], one[i], two[i], three[i]]
            for k in range(6):
                acc[k] = acc[k] + fold(v[k // 2] * v[(k + 1) // 2])
    own_tile = own_rows[:, 0:LANES]
    tile_row = lax.broadcasted_iota(jnp.int32, (8, LANES), 0)
    gram = jnp.zeros((8, LANES), jnp.float32)
    for k in range(6):
        moment = jnp.sum(jnp.where(own_tile, acc[k], 0.0))
        gram = jnp.where(tile_row == k, moment, gram)
    gram_ref[...] = gram


def far_kernel(gram_ref, two_ref, far_ref, out_ref):
    obs_count, _, cols = two_ref.shape
    tiles = cols // LANES
    rest = obs_count - 16
    factors = factors_of(far_ref[0], 2)
    left = jnp.concatenate([as_float(far_ref[t]) for t in range(1 + tiles, far_ref.shape[0])], axis=0)
    total = jnp.zeros((obs_count, LANES), jnp.float32)
    for c in range(tiles):
        far = jnp.concatenate([as_float(far_ref[1 + c]) * factors[0], left[rest * c : rest * (c + 1)] * factors[1][0:rest]], axis=0)
        mine = jnp.concatenate([two_ref[e, 1:2, c * LANES : (c + 1) * LANES] for e in range(obs_count)], axis=0)
        total = total + far * mine
    part = (-2.0 * (GAIN * SMOOTH_PULL) ** 3) * jnp.sum(total)
    row = lax.broadcasted_iota(jnp.int32, (8, LANES), 0)
    out_ref[...] = gram_ref[...] + jnp.where(row == 5, part, 0.0)


def combine_kernel(*refs):
    *gram_refs, prior_ref, zero_ref, one_ref, two_ref, out_ref = refs
    gram = gram_refs[0][...]
    for ref in gram_refs[1:]:
        gram = gram + ref[...]
    m = [gram[k : k + 1, :] for k in range(6)]
    h = {(i, j): m[i + j + 1] * (1.0 / GAIN) + SHIFT * m[i + j] for i in range(3) for j in range(i, 3)}
    l10 = h[0, 1] / h[0, 0]
    l20 = h[0, 2] / h[0, 0]
    d1 = h[1, 1] - l10 * h[0, 1]
    t = h[1, 2] - l20 * h[0, 1]
    ok1 = d1 > 1e-6 * h[1, 1]
    inv1 = jnp.where(ok1, 1.0 / jnp.where(ok1, d1, 1.0), 0.0)
    l21 = t * inv1
    d2 = h[2, 2] - l20 * h[0, 2] - l21 * t
    ok2 = ok1 & (d2 > 1e-6 * h[2, 2])
    inv2 = jnp.where(ok2, 1.0 / jnp.where(ok2, d2, 1.0), 0.0)
    z1 = m[1] - l10 * m[0]
    z2 = m[2] - l20 * m[0] - l21 * z1
    y2 = z2 * inv2
    y1 = z1 * inv1 - l21 * y2
    y0 = m[0] / h[0, 0] - l10 * y1 - l20 * y2
    cols = prior_ref.shape[2]
    for c in range(0, cols, LANES):
        lanes = slice(c, c + LANES)
        out_ref[:, :, lanes] = (
            prior_ref[:, :, lanes] + y0[None] * zero_ref[:, :, lanes] + y1[None] * one_ref[:, :, lanes] + y2[None] * two_ref[:, :, lanes]
        )


def on_device(reflect, clear_conf, sun_view, sensor_id, band_gain, sensor_weight, prior):
    rows_here, obs_count, cols = prior.shape
    prior = jnp.transpose(prior, (1, 0, 2))
    count = lax.axis_size("rows")
    total_rows = rows_here * count
    block = rows_here * ENTRIES
    tiles = cols // LANES
    me = lax.axis_index("rows").astype(jnp.int32).reshape(1)
    vmem = pl.BlockSpec(memory_space=pltpu.VMEM)
    smem = pl.BlockSpec(memory_space=pltpu.SMEM)
    params = pltpu.CompilerParams(vmem_limit_bytes=24 * 2**20)
    f32 = lambda *shape: jax.ShapeDtypeStruct(shape, jnp.float32)
    packed = lambda *shape: jax.ShapeDtypeStruct(shape + (16, LANES), jnp.int16)

    scale = 0.01 / (reflect.shape[0] * count)
    index = me
    parts = []
    for chunk in range(CHUNKS):
        kept, sent = partial_sums(
            index, reflect, clear_conf, sun_view, sensor_id, band_gain, sensor_weight, prior, scale, chunk
        )
        index, _ = lax.optimization_barrier((me, sent))
        parts.append((kept, sent))
    flip = lambda x, mask: lax.ppermute(x, "rows", [(i, i ^ mask) for i in range(count)])
    swap = lambda x, bit: flip(x, 1 << bit)
    bits = list(range(1, count.bit_length() - 1))
    parts = [(kept, swap(sent, 0)) for kept, sent in parts]
    if len(bits) >= 2:
        orders = [((bits[0], 0), (bits[1], 0)), ((bits[1], 1), (bits[0], 0))]
        for step in range(2):
            for chunk in range(CHUNKS):
                bit, place = orders[chunk % 2][step]
                kept, sent = add_split(me // 2**bit % 2, place, *parts[chunk])
                parts[chunk] = (kept, swap(sent, bit))
        bits = bits[2:]
    parts = [x for part in parts for x in part]
    for bit in bits:
        kept, sent = add_split(me // 2**bit % 2, 0, *parts)
        parts = [kept, swap(sent, bit)]

    own, msg, first = pl.pallas_call(
        functools.partial(residual_kernel, total_rows=total_rows),
        in_specs=[smem] + [vmem] * (1 + len(parts)),
        out_specs=[vmem, vmem, vmem],
        out_shape=[f32(block, cols), packed(1, 1 + block // 16 * tiles), packed(1 + tiles + -(-(obs_count - 16) * tiles // 16))],
        scratch_shapes=[pltpu.VMEM((tiles, block, LANES), jnp.float32)],
        compiler_params=params,
        name="residual",
    )(me, prior, *parts)

    msg = msg[0]
    mate = swap(msg, 0)
    border = [(i, i + 1) for i in range(1, count - 1, 2)]
    across = lax.ppermute(msg, "rows", border + [(target, source) for source, target in border])
    far = lax.ppermute(first, "rows", [(i + 2, i) for i in range(count - 2)])
    zero, one, two, gram = pl.pallas_call(
        functools.partial(krylov_kernel, total_rows=total_rows, rows_here=rows_here),
        in_specs=[smem, vmem, vmem, vmem],
        out_specs=[vmem] * 4,
        out_shape=[f32(obs_count, rows_here, cols)] * 3 + [f32(8, LANES)],
        scratch_shapes=[pltpu.VMEM((tiles, ENTRIES * 8, LANES), jnp.float32)],
        compiler_params=params,
        name="krylov",
    )(me, own, mate, across)

    grams = [
        pl.pallas_call(
            far_kernel, in_specs=[vmem] * 3, out_specs=vmem, out_shape=f32(8, LANES), compiler_params=params, name="far"
        )(gram, two, far)
    ]
    for bit in range(0, count.bit_length() - 1, 2):
        masks = [mask << bit for mask in (1, 2, 3) if mask << bit < count]
        gram = sum(grams[1:], grams[0])
        grams = [gram] + [flip(gram, mask) for mask in masks]
    out = pl.pallas_call(
        combine_kernel,
        in_specs=[vmem] * (len(grams) + 4),
        out_specs=vmem,
        out_shape=f32(obs_count, rows_here, cols),
        compiler_params=params,
        name="combine",
    )(*grams, prior, zero, one, two)
    return jnp.transpose(out, (1, 0, 2))


def solution(mesh):
    return jax.shard_map(
        on_device,
        mesh=mesh,
        in_specs=(
            P("rows", None, None, "tiles"),
            P("rows", None, "tiles"),
            P("rows", None, None, "tiles"),
            P(),
            P(),
            P(),
            P("rows", None, "tiles"),
        ),
        out_specs=P("rows", None, "tiles"),
        check_vma=False,
    )
```

```python
import functools
import math

import jax
import jax.numpy as jnp
from jax import lax
from jax.experimental import pallas as pl
from jax.experimental.pallas import tpu as pltpu
from jax.sharding import PartitionSpec as P

TO_RADIAN = math.pi / 18000.0
PRIOR_PULL = 0.1
SMOOTH_PULL = 0.5
SHIFT = 3.0
GAIN = 0.4
ENTRIES = 24
LANES = 128
QUANT = 32000.0
GROUP = LANES // 4
CHUNKS = 2


R_POLY = (0.9428089773, 0.04714460664, 0.007527079489, 0.001965302741, 9.052799897e-05, 0.0004621408027)
S_POLY = (0.6002109608, -0.09003726006, -0.007977343822, -0.001801806492, 3.702625389e-06, -0.0003981650976)
SIN_25 = (0.9999999567, -0.1666626093, 0.008276695349)
COS_25 = (0.9999999997, -0.4999999562, 0.04166553086, -0.001379415437)
SIN_15 = (0.999999998, -0.1666661418, 0.008312938059)
COS_15 = (0.9999999858, -0.4999963087, 0.04152366947)
SIN_90 = (0.9999999947, -0.1666665666, 0.008333024663, -0.00019807389, 2.601844464e-06)


def horner(coefs, x):
    acc = coefs[-1] * x + coefs[-2]
    for coef in coefs[-3::-1]:
        acc = acc * x + coef
    return acc


def of_degrees(coefs, x, x2, factor, odd):
    scaled = [factor * coef * TO_RADIAN ** (2 * k + odd) for k, coef in enumerate(coefs)]
    value = horner(scaled, x2)
    return value * x if odd else value


def ross_li(sun, view, azim):
    x = (sun - 4500).astype(jnp.float32)
    x2 = x * x
    half = math.sqrt(0.5)
    sin_x, cos_x = of_degrees(SIN_25, x, x2, half, 1), of_degrees(COS_25, x, x2, half, 0)
    cos_sun, sin_sun = cos_x - sin_x, cos_x + sin_x
    v = view.astype(jnp.float32)
    v2 = v * v
    sin_view, cos_view = of_degrees(SIN_15, v, v2, 1.0, 1), of_degrees(COS_15, v, v2, 1.0, 0)
    a = (9000 - azim).astype(jnp.float32)
    cos_azim = of_degrees(SIN_90, a, a * a, 1.0, 1)
    prod = cos_sun * cos_view
    cos_phase = prod + sin_sun * sin_view * cos_azim
    total = cos_sun + cos_view
    recip = pl.reciprocal(total * prod, approx=False)
    inv_total = recip * prod
    sec_prod = recip * total
    u = 1.0 - cos_phase
    u_up = 1.0 + cos_phase
    bent = u * (u * lax.rsqrt(u)) * horner(R_POLY, u)
    volume = (bent + (0.5 * math.pi) * cos_phase) * inv_total - 0.25 * math.pi
    sin2 = u * u_up
    sin_phase = sin2 * lax.rsqrt(sin2)
    w = jnp.maximum(1.0 - (2.0 * inv_total) * sin_phase, 1e-30)
    overlap = w * (w * lax.rsqrt(w)) * horner(S_POLY, w)
    geometric = sec_prod * (total * (overlap - 1.0) + 0.5 * u_up)
    return volume, geometric


def lane_group(shape):
    return lax.broadcasted_iota(jnp.int32, shape, len(shape) - 1) // GROUP


def pack(tiles, msg_ref, block):
    rows = tiles[0].shape[0]
    top = jnp.abs(tiles[0])
    for tile in tiles[1:]:
        top = jnp.maximum(top, jnp.abs(tile))
    for shift in (LANES // 2, LANES // 4):
        top = jnp.maximum(top, pltpu.roll(top, shift, axis=1))
    level = jnp.ceil(8.0 * jnp.log2(jnp.maximum(top, 1e-30)))
    factor = QUANT * jnp.exp2(-0.125 * level)
    group = lane_group((16, LANES))
    scales = level[0:16]
    for t in range(1, rows // 16):
        scales = jnp.where(group == t, level[16 * t : 16 * t + 16], scales)
    scales = scales.astype(jnp.int32).astype(jnp.int16)
    msg_ref[block, 0] = scales
    numbers = [jnp.round(tile * factor).astype(jnp.int32) for tile in tiles]
    for c, number in enumerate(numbers):
        coded = number.astype(jnp.int16)
        for t in range(rows // 16):
            msg_ref[block, 1 + t * len(tiles) + c] = coded[16 * t : 16 * t + 16]
    return scales, numbers


def as_float(x):
    return x.astype(jnp.int32).astype(jnp.float32)


def factors_of(scales, row_tiles):
    scales = as_float(scales)
    group = lane_group((16, LANES))
    factors = []
    for t in range(row_tiles):
        level = jnp.where(group == t, scales, 0.0)
        for shift in (LANES // 2, LANES // 4):
            level = level + pltpu.roll(level, shift, axis=1)
        factors.append(jnp.exp2(0.125 * level) * (1.0 / QUANT))
    return factors


def unpack(read, row_tiles, col_tiles):
    factors = factors_of(read(0), row_tiles)
    return [
        jnp.concatenate([as_float(read(1 + t * col_tiles + c)) * factors[t] for t in range(row_tiles)], axis=0) for c in range(col_tiles)
    ]


def sums_kernel(
    me_ref,
    ids_ref,
    gain_ref,
    weight_ref,
    reflect_hbm,
    conf_hbm,
    sun_hbm,
    prior_ref,
    keep_ref,
    msg_ref,
    sums_ref,
    kernels_ref,
    reflect_ref,
    conf_ref,
    sun_ref,
    sems,
    *,
    scale,
    rows_here,
    first_col,
):
    steps, dates, bands, tile_rows, _ = reflect_ref.shape
    lane_tiles = sums_ref.shape[0]
    me = me_ref[0]
    block = rows_here * ENTRIES
    obs_count = 3 * bands

    def copies(step):
        rows = pl.ds(pl.multiple_of(step // lane_tiles * tile_rows, tile_rows), tile_rows)
        cols = pl.ds(pl.multiple_of(first_col + step % lane_tiles * LANES, LANES), LANES)
        return (
            pltpu.make_async_copy(sun_hbm.at[:, :, rows, cols], sun_ref.at[step], sems.at[step, 0]),
            pltpu.make_async_copy(conf_hbm.at[:, rows, cols], conf_ref.at[step], sems.at[step, 1]),
            pltpu.make_async_copy(reflect_hbm.at[:, :, rows, cols], reflect_ref.at[step], sems.at[step, 2]),
        )

    def start(step, carry):
        for copy in copies(step):
            copy.start()
        return carry

    lax.fori_loop(0, steps, start, 0)

    def lane_tile(index, row_tile):
        step = row_tile * lane_tiles + index
        for copy in copies(step):
            copy.wait()
        sensors = [ids_ref[me * dates + d] for d in range(dates)]

        def store(top, entry, total):
            sums_ref[index, pl.ds(top * ENTRIES + entry, 8, stride=ENTRIES), :] = total

        def plus(total, term):
            return term if total is None else total + term

        for top in range(0, tile_rows, 8):
            here = slice(top, top + 8)
            normal = [None] * 6
            for d in range(dates):
                volume, geometric = ross_li(*[sun_ref[step, d, angle, here, :] for angle in range(3)])
                weight = conf_ref[step, d, here, :].astype(jnp.float32) * (weight_ref[sensors[d]] * scale)
                weighted_vol = weight * volume
                weighted_geo = weight * geometric
                for i, value in enumerate((weight, weighted_vol, weighted_geo)):
                    kernels_ref[d, i, here, :] = value
                terms = (weight, weighted_vol, weighted_geo, weighted_vol * volume, weighted_vol * geometric, weighted_geo * geometric)
                normal = [plus(total, term) for total, term in zip(normal, terms)]
            for k in range(6):
                store(top, obs_count + k, normal[k])
        for b in range(bands):
            observed = [None] * 3
            for d in range(dates):
                signal = reflect_ref[step, d, b].astype(jnp.float32) * gain_ref[sensors[d], b]
                observed = [plus(total, kernels_ref[d, i] * signal) for i, total in enumerate(observed)]
            for i in range(3):
                for top in range(0, tile_rows, 8):
                    store(top, 3 * b + i, observed[i][top : top + 8])
        return row_tile

    def row_tile_sums(row_tile, carry):
        lax.fori_loop(0, lane_tiles, lane_tile, row_tile)
        tiles = range(lane_tiles)
        first_row = row_tile * tile_rows
        for row, source in ((me * rows_here - 1 - first_row, 0), ((me + 1) * rows_here - first_row, rows_here - 1)):

            @pl.when((row >= 0) & (row < tile_rows))
            def _():
                for c in tiles:
                    lanes = slice(c * LANES, (c + 1) * LANES)
                    at = pl.ds(pl.multiple_of(row * ENTRIES, 8), obs_count)
                    part = jnp.concatenate([prior_ref[e, source : source + 1, lanes] for e in range(obs_count)], axis=0)
                    sums_ref[c, at, :] = sums_ref[c, at, :] + SMOOTH_PULL * part

        bit = me % 2
        per_tile = tile_rows // rows_here // 2
        for j in range(per_tile):
            own = pl.ds(pl.multiple_of((2 * j + bit) * block, 8), block)
            other = pl.ds(pl.multiple_of((2 * j + 1 - bit) * block, 8), block)
            for c in tiles:
                keep_ref[row_tile * per_tile + j, :, c * LANES : (c + 1) * LANES] = sums_ref[c, own, :]
            pack([sums_ref[c, other, :] for c in tiles], msg_ref, row_tile * per_tile + j)
        return carry

    lax.fori_loop(0, steps // lane_tiles, row_tile_sums, 0)


def partial_sums(me, reflect, clear_conf, sun_view, sensor_id, band_gain, sensor_weight, prior, scale, chunk):
    dates, bands, rows, cols = reflect.shape
    cols = cols // CHUNKS
    rows_here = prior.shape[1]
    count = rows // rows_here
    tile_rows = 16
    block = rows_here * ENTRIES
    lane_tiles = cols // LANES
    steps = rows // tile_rows * lane_tiles
    smem = pl.BlockSpec(memory_space=pltpu.SMEM)
    vmem = pl.BlockSpec(memory_space=pltpu.VMEM)
    hbm = pl.BlockSpec(memory_space=pl.ANY)
    return pl.pallas_call(
        functools.partial(sums_kernel, scale=scale, rows_here=rows_here, first_col=chunk * cols),
        grid=(1,),
        in_specs=[smem] * 4 + [hbm] * 3 + [pl.BlockSpec((3 * bands, rows_here, cols), lambda i: (0, 0, chunk))],
        out_specs=[vmem, vmem],
        out_shape=[
            jax.ShapeDtypeStruct((count // 2, block, cols), jnp.float32),
            jax.ShapeDtypeStruct((count // 2, 1 + block // 16 * lane_tiles, 16, LANES), jnp.int16),
        ],
        scratch_shapes=[
            pltpu.VMEM((lane_tiles, tile_rows * ENTRIES, LANES), jnp.float32),
            pltpu.VMEM((dates, 3, tile_rows, LANES), jnp.float32),
            pltpu.VMEM((steps, dates, bands, tile_rows, LANES), reflect.dtype),
            pltpu.VMEM((steps, dates, tile_rows, LANES), jnp.int32),
            pltpu.VMEM((steps, dates, 3, tile_rows, LANES), jnp.int32),
            pltpu.SemaphoreType.DMA((steps, 3)),
        ],
        compiler_params=pltpu.CompilerParams(vmem_limit_bytes=(62 if chunk == 0 else 52) * 2**20),
        name="partial_sums",
    )(me, sensor_id, band_gain, sensor_weight, reflect, clear_conf, sun_view, prior)


def add_split_kernel(bit_ref, *refs, place):
    *parts, keep_ref, msg_ref = refs
    count, block, _ = keep_ref.shape
    bit = bit_ref[0]

    def total(j):
        tiles = []
        for kept_ref, got_ref in zip(parts[0::2], parts[1::2]):
            here = kept_ref.shape[2] // LANES
            came = unpack(lambda at: got_ref[j, at], block // 16, here)
            tiles += [kept_ref[j, :, c * LANES : (c + 1) * LANES] + came[c] for c in range(here)]
        return tiles

    for q in range(count):
        low = q % 2**place
        first = (q - low) * 2 + low
        pack(total(first + (1 - bit) * 2**place), msg_ref, q)
        for c, tile in enumerate(total(first + bit * 2**place)):
            keep_ref[q, :, c * LANES : (c + 1) * LANES] = tile


def add_split(bit, place, *parts):
    count, block, _ = parts[0].shape
    cols = sum(kept.shape[2] for kept in parts[0::2])
    vmem = pl.BlockSpec(memory_space=pltpu.VMEM)
    return pl.pallas_call(
        functools.partial(add_split_kernel, place=place),
        in_specs=[pl.BlockSpec(memory_space=pltpu.SMEM)] + [vmem] * len(parts),
        out_specs=[vmem, vmem],
        out_shape=[
            jax.ShapeDtypeStruct((count // 2, block, cols), jnp.float32),
            jax.ShapeDtypeStruct((count // 2, 1 + block // 16 * (cols // LANES), 16, LANES), jnp.int16),
        ],
        compiler_params=pltpu.CompilerParams(vmem_limit_bytes=24 * 2**20),
        name="add_split",
    )(bit, *parts)


def take(ref, start, size, stride):
    at = pl.ds(start, size, stride=stride)
    return jnp.concatenate([ref[c, at, :] for c in range(ref.shape[0])], axis=1)


def put(ref, start, size, stride, value):
    at = pl.ds(start, size, stride=stride)
    for c in range(ref.shape[0]):
        ref[c, at, :] = value[:, c * LANES : (c + 1) * LANES]


def beside_columns(x):
    cols = x.shape[1]
    col = lax.broadcasted_iota(jnp.int32, x.shape, 1)
    left = jnp.where(col == 0, 0.0, pltpu.roll(x, 1, axis=1))
    right = jnp.where(col == cols - 1, 0.0, pltpu.roll(x, cols - 1, axis=1))
    return left + right


def degree_of(row, shape, total_rows):
    col = lax.broadcasted_iota(jnp.int32, shape, 1)
    edge = (
        (row == 0).astype(jnp.float32)
        + (row == total_rows - 1).astype(jnp.float32)
        + (col == 0).astype(jnp.float32)
        + (col == shape[1] - 1).astype(jnp.float32)
    )
    return 4.0 - edge


def couple(n, v):
    return (
        n[0] * v[0] + n[1] * v[1] + n[2] * v[2],
        n[1] * v[0] + n[3] * v[1] + n[4] * v[2],
        n[2] * v[0] + n[4] * v[1] + n[5] * v[2],
    )


def residual_kernel(me_ref, prior_ref, *refs, total_rows):
    obs_count, rows_here, cols = prior_ref.shape
    *parts, out_ref, msg_ref, first_ref, sums_ref = refs
    block = rows_here * ENTRIES
    tiles = cols // LANES
    at = 0
    for kept_ref, got_ref in zip(parts[0::2], parts[1::2]):
        here = kept_ref.shape[2] // LANES
        came = unpack(lambda place: got_ref[0, place], block // 16, here)
        for c in range(here):
            sums_ref[at] = kept_ref[0, :, c * LANES : (c + 1) * LANES] + came[c]
            at += 1
    shape = (rows_here, cols)
    row = me_ref[0] * rows_here + lax.broadcasted_iota(jnp.int32, shape, 0)
    degree = degree_of(row, shape, total_rows)
    normal = [take(sums_ref, obs_count + k, rows_here, ENTRIES) for k in range(6)]
    for b in range(obs_count // 3):
        fields = [prior_ref[3 * b + i] for i in range(3)]
        coupled = couple(normal, fields)
        for i in range(3):
            field = fields[i]
            beside = beside_columns(field)
            if rows_here > 1:
                zero = jnp.zeros((1, cols), jnp.float32)
                beside = beside + jnp.concatenate([zero, field[:-1]], axis=0) + jnp.concatenate([field[1:], zero], axis=0)
            entry = 3 * b + i
            observed = take(sums_ref, entry, rows_here, ENTRIES)
            put(sums_ref, entry, rows_here, ENTRIES, observed - coupled[i] - SMOOTH_PULL * (degree * field - beside))
    for c in range(tiles):
        out_ref[:, c * LANES : (c + 1) * LANES] = sums_ref[c]
    scales, numbers = pack([sums_ref[c] for c in range(tiles)], msg_ref, 0)
    first_ref[0] = scales
    for c in range(tiles):
        first_ref[1 + c] = numbers[c][0:16].astype(jnp.int16)
    left = jnp.concatenate([number[16:obs_count] for number in numbers], axis=0)
    spare = (first_ref.shape[0] - 1 - tiles) * 16 - left.shape[0]
    if spare:
        left = jnp.concatenate([left, jnp.zeros((spare, LANES), jnp.int32)], axis=0)
    for t in range(left.shape[0] // 16):
        first_ref[1 + tiles + t] = left[16 * t : 16 * t + 16].astype(jnp.int16)


def krylov_kernel(me_ref, own_ref, mate_ref, across_ref, zero_ref, one_ref, two_ref, gram_ref, window_ref, *, total_rows, rows_here):
    cols = own_ref.shape[1]
    obs_count = ENTRIES - 6
    tiles = cols // LANES
    row_tiles = own_ref.shape[0] // 16

    def lay(place, part, r):
        at = pl.ds(place, ENTRIES, stride=8)
        for c in range(tiles):
            window_ref[c, at, :] = part[c][r * ENTRIES : (r + 1) * ENTRIES]

    own = [own_ref[:, c * LANES : (c + 1) * LANES] for c in range(tiles)]
    mate = unpack(lambda place: mate_ref[place], row_tiles, tiles)
    across = unpack(lambda place: across_ref[place], row_tiles, tiles)
    odd = me_ref[0] % 2
    for r in range(2):
        lay(2 + r, own, r)
        lay(4 * (1 - odd) + r, mate, r)
        lay(4 * odd + r, across, r)
    for empty in (6, 7):
        put(window_ref, empty, ENTRIES, 8, jnp.zeros((ENTRIES, cols), jnp.float32))
    window = lambda entry: jnp.concatenate([window_ref[c, entry * 8 : entry * 8 + 8, :] for c in range(cols // LANES)], axis=1)
    shape = (8, cols)
    place = lax.broadcasted_iota(jnp.int32, shape, 0)
    row = me_ref[0] * rows_here + place - 2
    inside = ((row >= 0) & (row < total_rows)).astype(jnp.float32) * GAIN
    own_rows = (place == 2) | (place == 3)
    diag = inside * (PRIOR_PULL - SHIFT + SMOOTH_PULL * degree_of(row, shape, total_rows))
    pull = inside * SMOOTH_PULL
    normal = [window(obs_count + k) * inside for k in range(6)]
    acc = [jnp.zeros((8, LANES), jnp.float32) for _ in range(6)]

    def apply(v, last=False):
        coupled = couple(normal, v)
        out = []
        for i in range(3):
            x = v[i]
            above = pltpu.roll(x, 7, axis=0)
            beside = beside_columns(x) + (2.0 * above if last else above + pltpu.roll(x, 1, axis=0))
            out.append(coupled[i] + diag * x - pull * beside)
        return out

    def fold(x):
        total = x[:, 0:LANES]
        for c in range(LANES, cols, LANES):
            total = total + x[:, c : c + LANES]
        return total

    for b in range(obs_count // 3):
        zero = [window(3 * b + i) for i in range(3)]
        one = apply(zero)
        two = apply(one)
        three = apply(two, last=True)
        for i in range(3):
            zero_ref[3 * b + i] = zero[i][2:4]
            one_ref[3 * b + i] = one[i][2:4]
            two_ref[3 * b + i] = two[i][2:4]
            v = [zero[i], one[i], two[i], three[i]]
            for k in range(6):
                acc[k] = acc[k] + fold(v[k // 2] * v[(k + 1) // 2])
    own_tile = own_rows[:, 0:LANES]
    tile_row = lax.broadcasted_iota(jnp.int32, (8, LANES), 0)
    gram = jnp.zeros((8, LANES), jnp.float32)
    for k in range(6):
        moment = jnp.sum(jnp.where(own_tile, acc[k], 0.0))
        gram = jnp.where(tile_row == k, moment, gram)
    gram_ref[...] = gram


def far_kernel(gram_ref, two_ref, far_ref, out_ref):
    obs_count, _, cols = two_ref.shape
    tiles = cols // LANES
    rest = obs_count - 16
    factors = factors_of(far_ref[0], 2)
    left = jnp.concatenate([as_float(far_ref[t]) for t in range(1 + tiles, far_ref.shape[0])], axis=0)
    total = jnp.zeros((obs_count, LANES), jnp.float32)
    for c in range(tiles):
        far = jnp.concatenate([as_float(far_ref[1 + c]) * factors[0], left[rest * c : rest * (c + 1)] * factors[1][0:rest]], axis=0)
        mine = jnp.concatenate([two_ref[e, 1:2, c * LANES : (c + 1) * LANES] for e in range(obs_count)], axis=0)
        total = total + far * mine
    part = (-2.0 * (GAIN * SMOOTH_PULL) ** 3) * jnp.sum(total)
    row = lax.broadcasted_iota(jnp.int32, (8, LANES), 0)
    out_ref[...] = gram_ref[...] + jnp.where(row == 5, part, 0.0)


def combine_kernel(*refs):
    *gram_refs, prior_ref, zero_ref, one_ref, two_ref, out_ref = refs
    gram = gram_refs[0][...]
    for ref in gram_refs[1:]:
        gram = gram + ref[...]
    m = [gram[k : k + 1, :] for k in range(6)]
    h = {(i, j): m[i + j + 1] * (1.0 / GAIN) + SHIFT * m[i + j] for i in range(3) for j in range(i, 3)}
    l10 = h[0, 1] / h[0, 0]
    l20 = h[0, 2] / h[0, 0]
    d1 = h[1, 1] - l10 * h[0, 1]
    t = h[1, 2] - l20 * h[0, 1]
    ok1 = d1 > 1e-6 * h[1, 1]
    inv1 = jnp.where(ok1, 1.0 / jnp.where(ok1, d1, 1.0), 0.0)
    l21 = t * inv1
    d2 = h[2, 2] - l20 * h[0, 2] - l21 * t
    ok2 = ok1 & (d2 > 1e-6 * h[2, 2])
    inv2 = jnp.where(ok2, 1.0 / jnp.where(ok2, d2, 1.0), 0.0)
    z1 = m[1] - l10 * m[0]
    z2 = m[2] - l20 * m[0] - l21 * z1
    y2 = z2 * inv2
    y1 = z1 * inv1 - l21 * y2
    y0 = m[0] / h[0, 0] - l10 * y1 - l20 * y2
    cols = prior_ref.shape[2]
    for c in range(0, cols, LANES):
        lanes = slice(c, c + LANES)
        out_ref[:, :, lanes] = (
            prior_ref[:, :, lanes] + y0[None] * zero_ref[:, :, lanes] + y1[None] * one_ref[:, :, lanes] + y2[None] * two_ref[:, :, lanes]
        )


def on_device(reflect, clear_conf, sun_view, sensor_id, band_gain, sensor_weight, prior):
    rows_here, obs_count, cols = prior.shape
    prior = jnp.transpose(prior, (1, 0, 2))
    count = lax.axis_size("rows")
    total_rows = rows_here * count
    block = rows_here * ENTRIES
    tiles = cols // LANES
    me = lax.axis_index("rows").astype(jnp.int32).reshape(1)
    vmem = pl.BlockSpec(memory_space=pltpu.VMEM)
    smem = pl.BlockSpec(memory_space=pltpu.SMEM)
    params = pltpu.CompilerParams(vmem_limit_bytes=24 * 2**20)
    f32 = lambda *shape: jax.ShapeDtypeStruct(shape, jnp.float32)
    packed = lambda *shape: jax.ShapeDtypeStruct(shape + (16, LANES), jnp.int16)

    scale = 0.01 / (reflect.shape[0] * count)
    index = me
    parts = []
    for chunk in range(CHUNKS):
        kept, sent = partial_sums(
            index, reflect, clear_conf, sun_view, sensor_id, band_gain, sensor_weight, prior, scale, chunk
        )
        index, _ = lax.optimization_barrier((me, sent))
        parts.append((kept, sent))
    flip = lambda x, mask: lax.ppermute(x, "rows", [(i, i ^ mask) for i in range(count)])
    swap = lambda x, bit: flip(x, 1 << bit)
    bits = list(range(1, count.bit_length() - 1))
    parts = [(kept, swap(sent, 0)) for kept, sent in parts]
    if len(bits) >= 2:
        orders = [((bits[0], 0), (bits[1], 0)), ((bits[1], 1), (bits[0], 0))]
        for step in range(2):
            for chunk in range(CHUNKS):
                bit, place = orders[chunk % 2][step]
                kept, sent = add_split(me // 2**bit % 2, place, *parts[chunk])
                parts[chunk] = (kept, swap(sent, bit))
        bits = bits[2:]
    parts = [x for part in parts for x in part]
    for bit in bits:
        kept, sent = add_split(me // 2**bit % 2, 0, *parts)
        parts = [kept, swap(sent, bit)]

    own, msg, first = pl.pallas_call(
        functools.partial(residual_kernel, total_rows=total_rows),
        in_specs=[smem] + [vmem] * (1 + len(parts)),
        out_specs=[vmem, vmem, vmem],
        out_shape=[f32(block, cols), packed(1, 1 + block // 16 * tiles), packed(1 + tiles + -(-(obs_count - 16) * tiles // 16))],
        scratch_shapes=[pltpu.VMEM((tiles, block, LANES), jnp.float32)],
        compiler_params=params,
        name="residual",
    )(me, prior, *parts)

    msg = msg[0]
    mate = swap(msg, 0)
    border = [(i, i + 1) for i in range(1, count - 1, 2)]
    across = lax.ppermute(msg, "rows", border + [(target, source) for source, target in border])
    far = lax.ppermute(first, "rows", [(i + 2, i) for i in range(count - 2)])
    zero, one, two, gram = pl.pallas_call(
        functools.partial(krylov_kernel, total_rows=total_rows, rows_here=rows_here),
        in_specs=[smem, vmem, vmem, vmem],
        out_specs=[vmem] * 4,
        out_shape=[f32(obs_count, rows_here, cols)] * 3 + [f32(8, LANES)],
        scratch_shapes=[pltpu.VMEM((tiles, ENTRIES * 8, LANES), jnp.float32)],
        compiler_params=params,
        name="krylov",
    )(me, own, mate, across)

    grams = [
        pl.pallas_call(
            far_kernel, in_specs=[vmem] * 3, out_specs=vmem, out_shape=f32(8, LANES), compiler_params=params, name="far"
        )(gram, two, far)
    ]
    for bit in range(0, count.bit_length() - 1, 2):
        masks = [mask << bit for mask in (1, 2, 3) if mask << bit < count]
        gram = sum(grams[1:], grams[0])
        grams = [gram] + [flip(gram, mask) for mask in masks]
    out = pl.pallas_call(
        combine_kernel,
        in_specs=[vmem] * (len(grams) + 4),
        out_specs=vmem,
        out_shape=f32(obs_count, rows_here, cols),
        compiler_params=params,
        name="combine",
    )(*grams, prior, zero, one, two)
    return jnp.transpose(out, (1, 0, 2))


def solution(mesh):
    return jax.shard_map(
        on_device,
        mesh=mesh,
        in_specs=(
            P("rows", None, None, "tiles"),
            P("rows", None, "tiles"),
            P("rows", None, None, "tiles"),
            P(),
            P(),
            P(),
            P("rows", None, "tiles"),
        ),
        out_specs=P("rows", None, "tiles"),
        check_vma=False,
    )
```

```python
import functools
import math

import jax
import jax.numpy as jnp
from jax import lax
from jax.experimental import pallas as pl
from jax.experimental.pallas import tpu as pltpu
from jax.sharding import PartitionSpec as P

TO_RADIAN = math.pi / 18000.0
PRIOR_PULL = 0.1
SMOOTH_PULL = 0.5
SHIFT = 3.0
GAIN = 0.4
ENTRIES = 24
LANES = 128
QUANT = 32000.0
GROUP = LANES // 4
FIRST_ORDER = [4 * (2 * m + h) + j for m in range(3) for j in range(4) for h in range(2)]
CHUNKS = 2


R_POLY = (0.9428089773, 0.04714460664, 0.007527079489, 0.001965302741, 9.052799897e-05, 0.0004621408027)
S_POLY = (0.6002109608, -0.09003726006, -0.007977343822, -0.001801806492, 3.702625389e-06, -0.0003981650976)
SIN_25 = (0.9999999567, -0.1666626093, 0.008276695349)
COS_25 = (0.9999999997, -0.4999999562, 0.04166553086, -0.001379415437)
SIN_15 = (0.999999998, -0.1666661418, 0.008312938059)
COS_15 = (0.9999999858, -0.4999963087, 0.04152366947)
SIN_90 = (0.9999999947, -0.1666665666, 0.008333024663, -0.00019807389, 2.601844464e-06)


def horner(coefs, x):
    acc = coefs[-1] * x + coefs[-2]
    for coef in coefs[-3::-1]:
        acc = acc * x + coef
    return acc


def of_degrees(coefs, x, x2, factor, odd):
    scaled = [factor * coef * TO_RADIAN ** (2 * k + odd) for k, coef in enumerate(coefs)]
    value = horner(scaled, x2)
    return value * x if odd else value


def ross_li(sun, view, azim):
    x = (sun - 4500).astype(jnp.float32)
    x2 = x * x
    half = math.sqrt(0.5)
    sin_x, cos_x = of_degrees(SIN_25, x, x2, half, 1), of_degrees(COS_25, x, x2, half, 0)
    cos_sun, sin_sun = cos_x - sin_x, cos_x + sin_x
    v = view.astype(jnp.float32)
    v2 = v * v
    sin_view, cos_view = of_degrees(SIN_15, v, v2, 1.0, 1), of_degrees(COS_15, v, v2, 1.0, 0)
    a = (9000 - azim).astype(jnp.float32)
    cos_azim = of_degrees(SIN_90, a, a * a, 1.0, 1)
    prod = cos_sun * cos_view
    cos_phase = prod + sin_sun * sin_view * cos_azim
    total = cos_sun + cos_view
    recip = pl.reciprocal(total * prod, approx=False)
    inv_total = recip * prod
    sec_prod = recip * total
    u = 1.0 - cos_phase
    u_up = 1.0 + cos_phase
    bent = u * (u * lax.rsqrt(u)) * horner(R_POLY, u)
    volume = (bent + (0.5 * math.pi) * cos_phase) * inv_total - 0.25 * math.pi
    sin2 = u * u_up
    sin_phase = sin2 * lax.rsqrt(sin2)
    w = jnp.maximum(1.0 - (2.0 * inv_total) * sin_phase, 1e-30)
    overlap = w * (w * lax.rsqrt(w)) * horner(S_POLY, w)
    geometric = sec_prod * (total * (overlap - 1.0) + 0.5 * u_up)
    return volume, geometric


def lane_group(shape):
    return lax.broadcasted_iota(jnp.int32, shape, len(shape) - 1) // GROUP


def pack(tiles, msg_ref, block):
    rows = tiles[0].shape[0]
    top = jnp.abs(tiles[0])
    for tile in tiles[1:]:
        top = jnp.maximum(top, jnp.abs(tile))
    for shift in (LANES // 2, LANES // 4):
        top = jnp.maximum(top, pltpu.roll(top, shift, axis=1))
    level = jnp.ceil(8.0 * jnp.log2(jnp.maximum(top, 1e-30)))
    factor = QUANT * jnp.exp2(-0.125 * level)
    group = lane_group((16, LANES))
    scales = level[0:16]
    for t in range(1, rows // 16):
        scales = jnp.where(group == t, level[16 * t : 16 * t + 16], scales)
    scales = scales.astype(jnp.int32).astype(jnp.int16)
    msg_ref[block, 0] = scales
    numbers = [jnp.round(tile * factor).astype(jnp.int32) for tile in tiles]
    for c, number in enumerate(numbers):
        coded = number.astype(jnp.int16)
        for t in range(rows // 16):
            msg_ref[block, 1 + t * len(tiles) + c] = coded[16 * t : 16 * t + 16]
    return scales, numbers


def as_float(x):
    return x.astype(jnp.int32).astype(jnp.float32)


def factors_of(scales, row_tiles):
    scales = as_float(scales)
    group = lane_group((16, LANES))
    factors = []
    for t in range(row_tiles):
        level = jnp.where(group == t, scales, 0.0)
        for shift in (LANES // 2, LANES // 4):
            level = level + pltpu.roll(level, shift, axis=1)
        factors.append(jnp.exp2(0.125 * level) * (1.0 / QUANT))
    return factors


def unpack(read, row_tiles, col_tiles):
    factors = factors_of(read(0), row_tiles)
    return [
        jnp.concatenate([as_float(read(1 + t * col_tiles + c)) * factors[t] for t in range(row_tiles)], axis=0) for c in range(col_tiles)
    ]


def part_rows(tiles):
    sublane = lax.broadcasted_iota(jnp.int32, (8, LANES), 0)
    odd, upper = sublane // 2 % 2 == 1, sublane >= 4
    pairs = []
    for first, second in (tiles[0:2], tiles[2:4]):
        pairs.append((jnp.where(odd, pltpu.roll(second, 2, axis=0), first), jnp.where(odd, second, pltpu.roll(first, 6, axis=0))))
    low = [jnp.where(upper, pltpu.roll(pairs[1][core], 4, axis=0), pairs[0][core]) for core in range(2)]
    high = [jnp.where(upper, pairs[1][core], pltpu.roll(pairs[0][core], 4, axis=0)) for core in range(2)]
    return low + high


def sums_kernel(
    me_ref,
    ids_ref,
    gain_ref,
    weight_ref,
    reflect_hbm,
    conf_hbm,
    sun_hbm,
    prior_ref,
    keep_ref,
    msg_ref,
    sums_ref,
    kernels_ref,
    reflect_ref,
    conf_ref,
    sun_ref,
    sems,
    *,
    scale,
    rows_here,
    first_col,
):
    steps, dates, bands, tile_rows, _ = reflect_ref.shape
    lane_tiles = sums_ref.shape[0]
    me = me_ref[0]
    block = rows_here * ENTRIES
    obs_count = 3 * bands

    def copies(step):
        rows = pl.ds(pl.multiple_of(step // lane_tiles * tile_rows, tile_rows), tile_rows)
        cols = pl.ds(pl.multiple_of(first_col + step % lane_tiles * LANES, LANES), LANES)
        return (
            pltpu.make_async_copy(sun_hbm.at[:, :, rows, cols], sun_ref.at[step], sems.at[step, 0]),
            pltpu.make_async_copy(conf_hbm.at[:, rows, cols], conf_ref.at[step], sems.at[step, 1]),
            pltpu.make_async_copy(reflect_hbm.at[:, :, rows, cols], reflect_ref.at[step], sems.at[step, 2]),
        )

    def start(step, carry):
        for copy in copies(step):
            copy.start()
        return carry

    lax.fori_loop(0, steps, start, 0)

    def lane_tile(index, row_tile):
        step = row_tile * lane_tiles + index
        for copy in copies(step):
            copy.wait()
        sensors = [ids_ref[me * dates + d] for d in range(dates)]

        def plus(total, term):
            return term if total is None else total + term

        tops = range(0, tile_rows, 8)
        normals = []
        for top in tops:
            here = slice(top, top + 8)
            normal = [None] * 6
            for d in range(dates):
                volume, geometric = ross_li(*[sun_ref[step, d, angle, here, :] for angle in range(3)])
                weight = conf_ref[step, d, here, :].astype(jnp.float32) * (weight_ref[sensors[d]] * scale)
                weighted_vol = weight * volume
                weighted_geo = weight * geometric
                for i, value in enumerate((weight, weighted_vol, weighted_geo)):
                    kernels_ref[d, i, here, :] = value
                terms = (weight, weighted_vol, weighted_geo, weighted_vol * volume, weighted_vol * geometric, weighted_geo * geometric)
                normal = [plus(total, term) for total, term in zip(normal, terms)]
            normals.append(normal)
        waiting = [[] for _ in tops]
        done = 0
        for b in range(bands + 1):
            if b < bands:
                observed = [None] * 3
                for d in range(dates):
                    signal = reflect_ref[step, d, b].astype(jnp.float32) * gain_ref[sensors[d], b]
                    observed = [plus(total, kernels_ref[d, i] * signal) for i, total in enumerate(observed)]
            for at, top in enumerate(tops):
                waiting[at] += [total[top : top + 8] for total in observed] if b < bands else normals[at]
            while len(waiting[0]) >= 4:
                for at, top in enumerate(tops):
                    for unit, rows in enumerate(part_rows(waiting[at][:4])):
                        sums_ref[index, pl.ds((top // 2 + unit) * block + done * 2, 8), :] = rows
                    waiting[at] = waiting[at][4:]
                done += 4
        return row_tile

    def row_tile_sums(row_tile, carry):
        lax.fori_loop(0, lane_tiles, lane_tile, row_tile)
        tiles = range(lane_tiles)
        first_row = row_tile * tile_rows
        for row, source in ((me * rows_here - 1 - first_row, 0), ((me + 1) * rows_here - first_row, rows_here - 1)):

            @pl.when((row >= 0) & (row < tile_rows))
            def _():
                at = pl.ds(pl.multiple_of(row // rows_here * block, 8), obs_count * rows_here)
                target = rows_here - 1 - source
                zero = jnp.zeros((1, LANES), jnp.float32)
                for c in tiles:
                    lanes = slice(c * LANES, (c + 1) * LANES)
                    part = []
                    for e in range(obs_count):
                        part += [prior_ref[e, source : source + 1, lanes] if r == target else zero for r in range(rows_here)]
                    sums_ref[c, at, :] = sums_ref[c, at, :] + SMOOTH_PULL * jnp.concatenate(part, axis=0)

        bit = me % 2
        per_tile = tile_rows // rows_here // 2
        for j in range(per_tile):
            own = pl.ds(pl.multiple_of((2 * j + bit) * block, 8), block)
            other = pl.ds(pl.multiple_of((2 * j + 1 - bit) * block, 8), block)
            for c in tiles:
                keep_ref[row_tile * per_tile + j, :, c * LANES : (c + 1) * LANES] = sums_ref[c, own, :]
            pack([sums_ref[c, other, :] for c in tiles], msg_ref, row_tile * per_tile + j)
        return carry

    lax.fori_loop(0, steps // lane_tiles, row_tile_sums, 0)


def partial_sums(me, reflect, clear_conf, sun_view, sensor_id, band_gain, sensor_weight, prior, scale, chunk):
    dates, bands, rows, cols = reflect.shape
    cols = cols // CHUNKS
    rows_here = prior.shape[1]
    count = rows // rows_here
    tile_rows = 16
    block = rows_here * ENTRIES
    lane_tiles = cols // LANES
    steps = rows // tile_rows * lane_tiles
    smem = pl.BlockSpec(memory_space=pltpu.SMEM)
    vmem = pl.BlockSpec(memory_space=pltpu.VMEM)
    hbm = pl.BlockSpec(memory_space=pl.ANY)
    return pl.pallas_call(
        functools.partial(sums_kernel, scale=scale, rows_here=rows_here, first_col=chunk * cols),
        grid=(1,),
        in_specs=[smem] * 4 + [hbm] * 3 + [pl.BlockSpec((3 * bands, rows_here, cols), lambda i: (0, 0, chunk))],
        out_specs=[vmem, vmem],
        out_shape=[
            jax.ShapeDtypeStruct((count // 2, block, cols), jnp.float32),
            jax.ShapeDtypeStruct((count // 2, 1 + block // 16 * lane_tiles, 16, LANES), jnp.int16),
        ],
        scratch_shapes=[
            pltpu.VMEM((lane_tiles, tile_rows * ENTRIES, LANES), jnp.float32),
            pltpu.VMEM((dates, 3, tile_rows, LANES), jnp.float32),
            pltpu.VMEM((steps, dates, bands, tile_rows, LANES), reflect.dtype),
            pltpu.VMEM((steps, dates, tile_rows, LANES), jnp.int32),
            pltpu.VMEM((steps, dates, 3, tile_rows, LANES), jnp.int32),
            pltpu.SemaphoreType.DMA((steps, 3)),
        ],
        compiler_params=pltpu.CompilerParams(vmem_limit_bytes=(62 if chunk == 0 else 52) * 2**20),
        name="partial_sums",
    )(me, sensor_id, band_gain, sensor_weight, reflect, clear_conf, sun_view, prior)


def add_split_kernel(bit_ref, *refs, place):
    *parts, keep_ref, msg_ref = refs
    count, block, _ = keep_ref.shape
    bit = bit_ref[0]

    def total(j):
        tiles = []
        for kept_ref, got_ref in zip(parts[0::2], parts[1::2]):
            here = kept_ref.shape[2] // LANES
            came = unpack(lambda at: got_ref[j, at], block // 16, here)
            tiles += [kept_ref[j, :, c * LANES : (c + 1) * LANES] + came[c] for c in range(here)]
        return tiles

    for q in range(count):
        low = q % 2**place
        first = (q - low) * 2 + low
        pack(total(first + (1 - bit) * 2**place), msg_ref, q)
        for c, tile in enumerate(total(first + bit * 2**place)):
            keep_ref[q, :, c * LANES : (c + 1) * LANES] = tile


def add_split(bit, place, *parts):
    count, block, _ = parts[0].shape
    cols = sum(kept.shape[2] for kept in parts[0::2])
    vmem = pl.BlockSpec(memory_space=pltpu.VMEM)
    return pl.pallas_call(
        functools.partial(add_split_kernel, place=place),
        in_specs=[pl.BlockSpec(memory_space=pltpu.SMEM)] + [vmem] * len(parts),
        out_specs=[vmem, vmem],
        out_shape=[
            jax.ShapeDtypeStruct((count // 2, block, cols), jnp.float32),
            jax.ShapeDtypeStruct((count // 2, 1 + block // 16 * (cols // LANES), 16, LANES), jnp.int16),
        ],
        compiler_params=pltpu.CompilerParams(vmem_limit_bytes=24 * 2**20),
        name="add_split",
    )(bit, *parts)


def take(ref, entry, rows):
    return jnp.concatenate([ref[c, entry * rows : (entry + 1) * rows, :] for c in range(ref.shape[0])], axis=1)


def put(ref, entry, rows, value):
    for c in range(ref.shape[0]):
        ref[c, entry * rows : (entry + 1) * rows, :] = value[:, c * LANES : (c + 1) * LANES]


def beside_columns(x):
    cols = x.shape[1]
    col = lax.broadcasted_iota(jnp.int32, x.shape, 1)
    left = jnp.where(col == 0, 0.0, pltpu.roll(x, 1, axis=1))
    right = jnp.where(col == cols - 1, 0.0, pltpu.roll(x, cols - 1, axis=1))
    return left + right


def degree_of(row, shape, total_rows):
    col = lax.broadcasted_iota(jnp.int32, shape, 1)
    edge = (
        (row == 0).astype(jnp.float32)
        + (row == total_rows - 1).astype(jnp.float32)
        + (col == 0).astype(jnp.float32)
        + (col == shape[1] - 1).astype(jnp.float32)
    )
    return 4.0 - edge


def couple(n, v):
    return (
        n[0] * v[0] + n[1] * v[1] + n[2] * v[2],
        n[1] * v[0] + n[3] * v[1] + n[4] * v[2],
        n[2] * v[0] + n[4] * v[1] + n[5] * v[2],
    )


def residual_kernel(me_ref, prior_ref, *refs, total_rows):
    obs_count, rows_here, cols = prior_ref.shape
    *parts, out_ref, msg_ref, first_ref, sums_ref = refs
    block = rows_here * ENTRIES
    tiles = cols // LANES
    at = 0
    for kept_ref, got_ref in zip(parts[0::2], parts[1::2]):
        here = kept_ref.shape[2] // LANES
        came = unpack(lambda place: got_ref[0, place], block // 16, here)
        for c in range(here):
            sums_ref[at] = kept_ref[0, :, c * LANES : (c + 1) * LANES] + came[c]
            at += 1
    shape = (rows_here, cols)
    row = me_ref[0] * rows_here + lax.broadcasted_iota(jnp.int32, shape, 0)
    degree = degree_of(row, shape, total_rows)
    normal = [take(sums_ref, obs_count + k, rows_here) for k in range(6)]
    for b in range(obs_count // 3):
        fields = [prior_ref[3 * b + i] for i in range(3)]
        coupled = couple(normal, fields)
        for i in range(3):
            field = fields[i]
            beside = beside_columns(field)
            if rows_here > 1:
                zero = jnp.zeros((1, cols), jnp.float32)
                beside = beside + jnp.concatenate([zero, field[:-1]], axis=0) + jnp.concatenate([field[1:], zero], axis=0)
            entry = 3 * b + i
            observed = take(sums_ref, entry, rows_here)
            put(sums_ref, entry, rows_here, observed - coupled[i] - SMOOTH_PULL * (degree * field - beside))
    for c in range(tiles):
        out_ref[:, c * LANES : (c + 1) * LANES] = sums_ref[c]
    scales, numbers = pack([sums_ref[c] for c in range(tiles)], msg_ref, 0)
    first_ref[0] = scales
    lefts = []
    for c in range(tiles):
        rows = first_rows(numbers[c])
        first_ref[1 + c] = rows[0:16].astype(jnp.int16)
        lefts.append(rows[16:24])
    for t in range(tiles // 2):
        first_ref[1 + tiles + t] = jnp.concatenate(lefts[2 * t : 2 * t + 2], axis=0).astype(jnp.int16)


def first_rows(block):
    odd = lax.broadcasted_iota(jnp.int32, (8, LANES), 0) % 2 == 1
    rows = [block[8 * k : 8 * k + 8] for k in range(6)]
    return jnp.concatenate([jnp.where(odd, pltpu.roll(rows[k + 1], 1, axis=0), rows[k]) for k in (0, 2, 4)], axis=0)


def krylov_kernel(me_ref, own_ref, mate_ref, across_ref, zero_ref, one_ref, two_ref, gram_ref, window_ref, *, total_rows, rows_here):
    cols = own_ref.shape[1]
    obs_count = ENTRIES - 6
    tiles = cols // LANES
    row_tiles = own_ref.shape[0] // 16

    own = [own_ref[:, c * LANES : (c + 1) * LANES] for c in range(tiles)]
    mate = unpack(lambda place: mate_ref[place], row_tiles, tiles)
    across = unpack(lambda place: across_ref[place], row_tiles, tiles)
    odd = me_ref[0] % 2 == 1
    sublane = lax.broadcasted_iota(jnp.int32, (8, LANES), 0)
    for c in range(tiles):
        low = jnp.where(odd, mate[c], across[c])
        high = jnp.where(odd, across[c], mate[c])
        for entry in range(ENTRIES):
            here, at = slice(entry // 4 * 8, entry // 4 * 8 + 8), entry % 4 * 2
            rows = [pltpu.roll(part[here], (2 * k - at) % 8, axis=0) for k, part in enumerate((low, own[c], high))]
            tile = jnp.where(sublane < 2, rows[0], jnp.where(sublane < 4, rows[1], jnp.where(sublane < 6, rows[2], 0.0)))
            window_ref[c, entry * 8 : entry * 8 + 8, :] = tile
    window = lambda entry: jnp.concatenate([window_ref[c, entry * 8 : entry * 8 + 8, :] for c in range(cols // LANES)], axis=1)
    shape = (8, cols)
    place = lax.broadcasted_iota(jnp.int32, shape, 0)
    row = me_ref[0] * rows_here + place - 2
    inside = ((row >= 0) & (row < total_rows)).astype(jnp.float32) * GAIN
    own_rows = (place == 2) | (place == 3)
    diag = inside * (PRIOR_PULL - SHIFT + SMOOTH_PULL * degree_of(row, shape, total_rows))
    pull = inside * SMOOTH_PULL
    normal = [window(obs_count + k) * inside for k in range(6)]
    acc = [jnp.zeros((8, LANES), jnp.float32) for _ in range(6)]

    def apply(v, last=False):
        coupled = couple(normal, v)
        out = []
        for i in range(3):
            x = v[i]
            above = pltpu.roll(x, 7, axis=0)
            beside = beside_columns(x) + (2.0 * above if last else above + pltpu.roll(x, 1, axis=0))
            out.append(coupled[i] + diag * x - pull * beside)
        return out

    def fold(x):
        total = x[:, 0:LANES]
        for c in range(LANES, cols, LANES):
            total = total + x[:, c : c + LANES]
        return total

    for b in range(obs_count // 3):
        zero = [window(3 * b + i) for i in range(3)]
        one = apply(zero)
        two = apply(one)
        three = apply(two, last=True)
        for i in range(3):
            zero_ref[3 * b + i] = zero[i][2:4]
            one_ref[3 * b + i] = one[i][2:4]
            two_ref[3 * b + i] = two[i][2:4]
            v = [zero[i], one[i], two[i], three[i]]
            for k in range(6):
                acc[k] = acc[k] + fold(v[k // 2] * v[(k + 1) // 2])
    own_tile = own_rows[:, 0:LANES]
    tile_row = lax.broadcasted_iota(jnp.int32, (8, LANES), 0)
    gram = jnp.zeros((8, LANES), jnp.float32)
    for k in range(6):
        moment = jnp.sum(jnp.where(own_tile, acc[k], 0.0))
        gram = jnp.where(tile_row == k, moment, gram)
    gram_ref[...] = gram


def far_kernel(gram_ref, two_ref, far_ref, out_ref):
    obs_count, _, cols = two_ref.shape
    tiles = cols // LANES
    factors = first_rows(jnp.concatenate(factors_of(far_ref[0], 3), axis=0))
    total = jnp.zeros((ENTRIES, LANES), jnp.float32)
    zero = jnp.zeros((1, LANES), jnp.float32)
    for c in range(tiles):
        left = as_float(far_ref[1 + tiles + c // 2])[c % 2 * 8 : c % 2 * 8 + 8]
        far = jnp.concatenate([as_float(far_ref[1 + c]), left], axis=0) * factors
        lanes = slice(c * LANES, (c + 1) * LANES)
        mine = [two_ref[e, 1:2, lanes] if e < obs_count else zero for e in FIRST_ORDER]
        total = total + far * jnp.concatenate(mine, axis=0)
    part = (-2.0 * (GAIN * SMOOTH_PULL) ** 3) * jnp.sum(total)
    row = lax.broadcasted_iota(jnp.int32, (8, LANES), 0)
    out_ref[...] = gram_ref[...] + jnp.where(row == 5, part, 0.0)


def combine_kernel(*refs):
    *gram_refs, prior_ref, zero_ref, one_ref, two_ref, out_ref = refs
    gram = gram_refs[0][...]
    for ref in gram_refs[1:]:
        gram = gram + ref[...]
    m = [gram[k : k + 1, :] for k in range(6)]
    h = {(i, j): m[i + j + 1] * (1.0 / GAIN) + SHIFT * m[i + j] for i in range(3) for j in range(i, 3)}
    l10 = h[0, 1] / h[0, 0]
    l20 = h[0, 2] / h[0, 0]
    d1 = h[1, 1] - l10 * h[0, 1]
    t = h[1, 2] - l20 * h[0, 1]
    ok1 = d1 > 1e-6 * h[1, 1]
    inv1 = jnp.where(ok1, 1.0 / jnp.where(ok1, d1, 1.0), 0.0)
    l21 = t * inv1
    d2 = h[2, 2] - l20 * h[0, 2] - l21 * t
    ok2 = ok1 & (d2 > 1e-6 * h[2, 2])
    inv2 = jnp.where(ok2, 1.0 / jnp.where(ok2, d2, 1.0), 0.0)
    z1 = m[1] - l10 * m[0]
    z2 = m[2] - l20 * m[0] - l21 * z1
    y2 = z2 * inv2
    y1 = z1 * inv1 - l21 * y2
    y0 = m[0] / h[0, 0] - l10 * y1 - l20 * y2
    cols = prior_ref.shape[2]
    for c in range(0, cols, LANES):
        lanes = slice(c, c + LANES)
        out_ref[:, :, lanes] = (
            prior_ref[:, :, lanes] + y0[None] * zero_ref[:, :, lanes] + y1[None] * one_ref[:, :, lanes] + y2[None] * two_ref[:, :, lanes]
        )


def on_device(reflect, clear_conf, sun_view, sensor_id, band_gain, sensor_weight, prior):
    rows_here, obs_count, cols = prior.shape
    prior = jnp.transpose(prior, (1, 0, 2))
    count = lax.axis_size("rows")
    total_rows = rows_here * count
    block = rows_here * ENTRIES
    tiles = cols // LANES
    me = lax.axis_index("rows").astype(jnp.int32).reshape(1)
    vmem = pl.BlockSpec(memory_space=pltpu.VMEM)
    smem = pl.BlockSpec(memory_space=pltpu.SMEM)
    params = pltpu.CompilerParams(vmem_limit_bytes=24 * 2**20)
    f32 = lambda *shape: jax.ShapeDtypeStruct(shape, jnp.float32)
    packed = lambda *shape: jax.ShapeDtypeStruct(shape + (16, LANES), jnp.int16)

    scale = 0.01 / (reflect.shape[0] * count)
    index = me
    parts = []
    for chunk in range(CHUNKS):
        kept, sent = partial_sums(
            index, reflect, clear_conf, sun_view, sensor_id, band_gain, sensor_weight, prior, scale, chunk
        )
        index, _ = lax.optimization_barrier((me, sent))
        parts.append((kept, sent))
    flip = lambda x, mask: lax.ppermute(x, "rows", [(i, i ^ mask) for i in range(count)])
    swap = lambda x, bit: flip(x, 1 << bit)
    bits = list(range(1, count.bit_length() - 1))
    parts = [(kept, swap(sent, 0)) for kept, sent in parts]
    if len(bits) >= 2:
        orders = [((bits[0], 0), (bits[1], 0)), ((bits[1], 1), (bits[0], 0))]
        for step in range(2):
            for chunk in range(CHUNKS):
                bit, place = orders[chunk % 2][step]
                kept, sent = add_split(me // 2**bit % 2, place, *parts[chunk])
                parts[chunk] = (kept, swap(sent, bit))
        bits = bits[2:]
    parts = [x for part in parts for x in part]
    for bit in bits:
        kept, sent = add_split(me // 2**bit % 2, 0, *parts)
        parts = [kept, swap(sent, bit)]

    own, msg, first = pl.pallas_call(
        functools.partial(residual_kernel, total_rows=total_rows),
        in_specs=[smem] + [vmem] * (1 + len(parts)),
        out_specs=[vmem, vmem, vmem],
        out_shape=[f32(block, cols), packed(1, 1 + block // 16 * tiles), packed(1 + tiles + tiles // 2)],
        scratch_shapes=[pltpu.VMEM((tiles, block, LANES), jnp.float32)],
        compiler_params=params,
        name="residual",
    )(me, prior, *parts)

    msg = msg[0]
    mate = swap(msg, 0)
    border = [(i, i + 1) for i in range(1, count - 1, 2)]
    across = lax.ppermute(msg, "rows", border + [(target, source) for source, target in border])
    far = lax.ppermute(first, "rows", [(i + 2, i) for i in range(count - 2)])
    zero, one, two, gram = pl.pallas_call(
        functools.partial(krylov_kernel, total_rows=total_rows, rows_here=rows_here),
        in_specs=[smem, vmem, vmem, vmem],
        out_specs=[vmem] * 4,
        out_shape=[f32(obs_count, rows_here, cols)] * 3 + [f32(8, LANES)],
        scratch_shapes=[pltpu.VMEM((tiles, ENTRIES * 8, LANES), jnp.float32)],
        compiler_params=params,
        name="krylov",
    )(me, own, mate, across)

    grams = [
        pl.pallas_call(
            far_kernel, in_specs=[vmem] * 3, out_specs=vmem, out_shape=f32(8, LANES), compiler_params=params, name="far"
        )(gram, two, far)
    ]
    for bit in range(0, count.bit_length() - 1, 2):
        masks = [mask << bit for mask in (1, 2, 3) if mask << bit < count]
        gram = sum(grams[1:], grams[0])
        grams = [gram] + [flip(gram, mask) for mask in masks]
    out = pl.pallas_call(
        combine_kernel,
        in_specs=[vmem] * (len(grams) + 4),
        out_specs=vmem,
        out_shape=f32(obs_count, rows_here, cols),
        compiler_params=params,
        name="combine",
    )(*grams, prior, zero, one, two)
    return jnp.transpose(out, (1, 0, 2))


def solution(mesh):
    return jax.shard_map(
        on_device,
        mesh=mesh,
        in_specs=(
            P("rows", None, None, "tiles"),
            P("rows", None, "tiles"),
            P("rows", None, None, "tiles"),
            P(),
            P(),
            P(),
            P("rows", None, "tiles"),
        ),
        out_specs=P("rows", None, "tiles"),
        check_vma=False,
    )
```

```python
import functools
import math

import jax
import jax.numpy as jnp
from jax import lax
from jax.experimental import pallas as pl
from jax.experimental.pallas import tpu as pltpu
from jax.sharding import PartitionSpec as P

TO_RADIAN = math.pi / 18000.0
PRIOR_PULL = 0.1
SMOOTH_PULL = 0.5
SHIFT = 3.0
GAIN = 0.4
ENTRIES = 24
LANES = 128
QUANT = 32000.0
GROUP = LANES // 4
SHARES = (1, 1)


R_POLY = (0.9428089773, 0.04714460664, 0.007527079489, 0.001965302741, 9.052799897e-05, 0.0004621408027)
S_POLY = (0.6002109608, -0.09003726006, -0.007977343822, -0.001801806492, 3.702625389e-06, -0.0003981650976)
COS_42 = (0.9999999797, -0.4999988914, 0.04165696265, -0.001361318541)
SIN_90 = (0.9999999947, -0.1666665666, 0.008333024663, -0.00019807389, 2.601844464e-06)


def horner(coefs, x):
    acc = coefs[-1] * x + coefs[-2]
    for coef in coefs[-3::-1]:
        acc = acc * x + coef
    return acc


def ross_li(sun, view, azim):
    less, more = (sun - view).astype(jnp.float32), (sun + view).astype(jnp.float32)
    half = lambda x: horner([c * (0.5 * TO_RADIAN) ** (2 * k) for k, c in enumerate(COS_42)], x * x)
    cos_less, cos_more = half(less), half(more)
    a = (9000 - azim).astype(jnp.float32)
    cos_azim = horner([c * TO_RADIAN ** (2 * k + 1) for k, c in enumerate(SIN_90)], a * a) * a
    square_less, square_more = cos_less * cos_less, cos_more * cos_more
    prod = square_less + square_more - 1.0
    cos_phase = prod + (square_less - square_more) * cos_azim
    total = cos_less * cos_more
    recip = pl.reciprocal(total * prod, approx=False)
    inv_total = recip * prod
    sec_prod = recip * total
    u = 1.0 - cos_phase
    u_up = 1.0 + cos_phase
    bent = u * (u * lax.rsqrt(u)) * horner([0.5 * c for c in R_POLY], u)
    volume = (bent + (0.25 * math.pi) * cos_phase) * inv_total - 0.25 * math.pi
    sin2 = u * u_up
    sin_phase = sin2 * lax.rsqrt(sin2)
    w = jnp.maximum(1.0 - inv_total * sin_phase, 1e-30)
    overlap = w * (w * lax.rsqrt(w)) * horner([2.0 * c for c in S_POLY], w)
    geometric = sec_prod * (total * (overlap - 2.0) + 0.5 * u_up)
    return volume, geometric


def lane_group(shape):
    return lax.broadcasted_iota(jnp.int32, shape, len(shape) - 1) // GROUP


def pack(tiles, msg_ref, block):
    rows = tiles[0].shape[0]
    top = jnp.abs(tiles[0])
    for tile in tiles[1:]:
        top = jnp.maximum(top, jnp.abs(tile))
    for shift in (LANES // 2, LANES // 4):
        top = jnp.maximum(top, pltpu.roll(top, shift, axis=1))
    level = jnp.ceil(8.0 * jnp.log2(jnp.maximum(top, 1e-30)))
    factor = QUANT * jnp.exp2(-0.125 * level)
    group = lane_group((16, LANES))
    scales = level[0:16]
    for t in range(1, rows // 16):
        scales = jnp.where(group == t, level[16 * t : 16 * t + 16], scales)
    scales = scales.astype(jnp.int32).astype(jnp.int16)
    msg_ref[block, 0] = scales
    numbers = [jnp.round(tile * factor).astype(jnp.int32) for tile in tiles]
    for c, number in enumerate(numbers):
        coded = number.astype(jnp.int16)
        for t in range(rows // 16):
            msg_ref[block, 1 + t * len(tiles) + c] = coded[16 * t : 16 * t + 16]
    return scales, numbers


def as_float(x):
    return x.astype(jnp.int32).astype(jnp.float32)


def factors_of(scales, row_tiles):
    scales = as_float(scales)
    group = lane_group((16, LANES))
    factors = []
    for t in range(row_tiles):
        level = jnp.where(group == t, scales, 0.0)
        for shift in (LANES // 2, LANES // 4):
            level = level + pltpu.roll(level, shift, axis=1)
        factors.append(jnp.exp2(0.125 * level) * (1.0 / QUANT))
    return factors


def unpack(read, row_tiles, col_tiles):
    factors = factors_of(read(0), row_tiles)
    return [
        jnp.concatenate([as_float(read(1 + t * col_tiles + c)) * factors[t] for t in range(row_tiles)], axis=0) for c in range(col_tiles)
    ]


def sums_kernel(
    me_ref,
    ids_ref,
    gain_ref,
    weight_ref,
    reflect_hbm,
    conf_hbm,
    sun_hbm,
    prior_ref,
    keep_ref,
    msg_ref,
    sums_ref,
    kernels_ref,
    reflect_ref,
    conf_ref,
    sun_ref,
    sems,
    *,
    scale,
    rows_here,
    first_col,
):
    steps, dates, bands, tile_rows, _ = reflect_ref.shape
    lane_tiles = sums_ref.shape[0]
    me = me_ref[0]
    block = rows_here * ENTRIES
    obs_count = 3 * bands

    def copies(step):
        rows = pl.ds(pl.multiple_of(step // lane_tiles * tile_rows, tile_rows), tile_rows)
        cols = pl.ds(pl.multiple_of(first_col + step % lane_tiles * LANES, LANES), LANES)
        return (
            pltpu.make_async_copy(sun_hbm.at[:, :, rows, cols], sun_ref.at[step], sems.at[step, 0]),
            pltpu.make_async_copy(conf_hbm.at[:, rows, cols], conf_ref.at[step], sems.at[step, 1]),
            pltpu.make_async_copy(reflect_hbm.at[:, :, rows, cols], reflect_ref.at[step], sems.at[step, 2]),
        )

    def start(step, carry):
        for copy in copies(step):
            copy.start()
        return carry

    lax.fori_loop(0, steps, start, 0)

    def lane_tile(index, row_tile):
        step = row_tile * lane_tiles + index
        for copy in copies(step):
            copy.wait()
        sensors = [ids_ref[me * dates + d] for d in range(dates)]

        def store(top, entry, total):
            sums_ref[index, pl.ds(top * ENTRIES + entry, 8, stride=ENTRIES), :] = total

        def plus(total, term):
            return term if total is None else total + term

        for top in range(0, tile_rows, 8):
            here = slice(top, top + 8)
            normal = [None] * 6
            for d in range(dates):
                volume, geometric = ross_li(*[sun_ref[step, d, angle, here, :] for angle in range(3)])
                weight = conf_ref[step, d, here, :].astype(jnp.float32) * (weight_ref[sensors[d]] * scale)
                weighted_vol = weight * volume
                weighted_geo = weight * geometric
                for i, value in enumerate((weight, weighted_vol, weighted_geo)):
                    kernels_ref[d, i, here, :] = value
                terms = (weight, weighted_vol, weighted_geo, weighted_vol * volume, weighted_vol * geometric, weighted_geo * geometric)
                normal = [plus(total, term) for total, term in zip(normal, terms)]
            for k in range(6):
                store(top, obs_count + k, normal[k])
        for b in range(bands):
            observed = [None] * 3
            for d in range(dates):
                signal = reflect_ref[step, d, b].astype(jnp.float32) * gain_ref[sensors[d], b]
                observed = [plus(total, kernels_ref[d, i] * signal) for i, total in enumerate(observed)]
            for i in range(3):
                for top in range(0, tile_rows, 8):
                    store(top, 3 * b + i, observed[i][top : top + 8])
        return row_tile

    def row_tile_sums(row_tile, carry):
        lax.fori_loop(0, lane_tiles, lane_tile, row_tile)
        tiles = range(lane_tiles)
        first_row = row_tile * tile_rows
        for row, source in ((me * rows_here - 1 - first_row, 0), ((me + 1) * rows_here - first_row, rows_here - 1)):

            @pl.when((row >= 0) & (row < tile_rows))
            def _():
                for c in tiles:
                    lanes = slice(c * LANES, (c + 1) * LANES)
                    at = pl.ds(pl.multiple_of(row * ENTRIES, 8), obs_count)
                    part = jnp.concatenate([prior_ref[e, source : source + 1, lanes] for e in range(obs_count)], axis=0)
                    sums_ref[c, at, :] = sums_ref[c, at, :] + SMOOTH_PULL * part

        bit = me % 2
        per_tile = tile_rows // rows_here // 2
        for j in range(per_tile):
            own = pl.ds(pl.multiple_of((2 * j + bit) * block, 8), block)
            other = pl.ds(pl.multiple_of((2 * j + 1 - bit) * block, 8), block)
            for c in tiles:
                keep_ref[row_tile * per_tile + j, :, c * LANES : (c + 1) * LANES] = sums_ref[c, own, :]
            pack([sums_ref[c, other, :] for c in tiles], msg_ref, row_tile * per_tile + j)
        return carry

    lax.fori_loop(0, steps // lane_tiles, row_tile_sums, 0)


def partial_sums(me, reflect, clear_conf, sun_view, sensor_id, band_gain, sensor_weight, prior, scale, first_col, cols):
    dates, bands, rows, _ = reflect.shape
    rows_here = prior.shape[1]
    count = rows // rows_here
    tile_rows = 16
    block = rows_here * ENTRIES
    lane_tiles = cols // LANES
    steps = rows // tile_rows * lane_tiles
    smem = pl.BlockSpec(memory_space=pltpu.SMEM)
    vmem = pl.BlockSpec(memory_space=pltpu.VMEM)
    hbm = pl.BlockSpec(memory_space=pl.ANY)
    return pl.pallas_call(
        functools.partial(sums_kernel, scale=scale, rows_here=rows_here, first_col=first_col),
        grid=(1,),
        in_specs=[smem] * 4 + [hbm] * 3 + [pl.BlockSpec((3 * bands, rows_here, cols), lambda i: (0, 0, first_col // cols))],
        out_specs=[vmem, vmem],
        out_shape=[
            jax.ShapeDtypeStruct((count // 2, block, cols), jnp.float32),
            jax.ShapeDtypeStruct((count // 2, 1 + block // 16 * lane_tiles, 16, LANES), jnp.int16),
        ],
        scratch_shapes=[
            pltpu.VMEM((lane_tiles, tile_rows * ENTRIES, LANES), jnp.float32),
            pltpu.VMEM((dates, 3, tile_rows, LANES), jnp.float32),
            pltpu.VMEM((steps, dates, bands, tile_rows, LANES), reflect.dtype),
            pltpu.VMEM((steps, dates, tile_rows, LANES), jnp.int32),
            pltpu.VMEM((steps, dates, 3, tile_rows, LANES), jnp.int32),
            pltpu.SemaphoreType.DMA((steps, 3)),
        ],
        compiler_params=pltpu.CompilerParams(vmem_limit_bytes=(62 if first_col == 0 else 52) * 2**20),
        name="partial_sums",
    )(me, sensor_id, band_gain, sensor_weight, reflect, clear_conf, sun_view, prior)


def add_split_kernel(bit_ref, *refs, place):
    *parts, keep_ref, msg_ref = refs
    count, block, _ = keep_ref.shape
    bit = bit_ref[0]

    def total(j):
        tiles = []
        for kept_ref, got_ref in zip(parts[0::2], parts[1::2]):
            here = kept_ref.shape[2] // LANES
            came = unpack(lambda at: got_ref[j, at], block // 16, here)
            tiles += [kept_ref[j, :, c * LANES : (c + 1) * LANES] + came[c] for c in range(here)]
        return tiles

    for q in range(count):
        low = q % 2**place
        first = (q - low) * 2 + low
        pack(total(first + (1 - bit) * 2**place), msg_ref, q)
        for c, tile in enumerate(total(first + bit * 2**place)):
            keep_ref[q, :, c * LANES : (c + 1) * LANES] = tile


def add_split(bit, place, *parts):
    count, block, _ = parts[0].shape
    cols = sum(kept.shape[2] for kept in parts[0::2])
    vmem = pl.BlockSpec(memory_space=pltpu.VMEM)
    return pl.pallas_call(
        functools.partial(add_split_kernel, place=place),
        in_specs=[pl.BlockSpec(memory_space=pltpu.SMEM)] + [vmem] * len(parts),
        out_specs=[vmem, vmem],
        out_shape=[
            jax.ShapeDtypeStruct((count // 2, block, cols), jnp.float32),
            jax.ShapeDtypeStruct((count // 2, 1 + block // 16 * (cols // LANES), 16, LANES), jnp.int16),
        ],
        compiler_params=pltpu.CompilerParams(vmem_limit_bytes=24 * 2**20),
        name="add_split",
    )(bit, *parts)


def take(ref, start, size, stride):
    at = pl.ds(start, size, stride=stride)
    return jnp.concatenate([ref[c, at, :] for c in range(ref.shape[0])], axis=1)


def put(ref, start, size, stride, value):
    at = pl.ds(start, size, stride=stride)
    for c in range(ref.shape[0]):
        ref[c, at, :] = value[:, c * LANES : (c + 1) * LANES]


def beside_columns(x):
    cols = x.shape[1]
    col = lax.broadcasted_iota(jnp.int32, x.shape, 1)
    left = jnp.where(col == 0, 0.0, pltpu.roll(x, 1, axis=1))
    right = jnp.where(col == cols - 1, 0.0, pltpu.roll(x, cols - 1, axis=1))
    return left + right


def degree_of(row, shape, total_rows):
    col = lax.broadcasted_iota(jnp.int32, shape, 1)
    edge = (
        (row == 0).astype(jnp.float32)
        + (row == total_rows - 1).astype(jnp.float32)
        + (col == 0).astype(jnp.float32)
        + (col == shape[1] - 1).astype(jnp.float32)
    )
    return 4.0 - edge


def couple(n, v):
    return (
        n[0] * v[0] + n[1] * v[1] + n[2] * v[2],
        n[1] * v[0] + n[3] * v[1] + n[4] * v[2],
        n[2] * v[0] + n[4] * v[1] + n[5] * v[2],
    )


def residual_kernel(me_ref, prior_ref, *refs, total_rows):
    obs_count, rows_here, cols = prior_ref.shape
    *parts, out_ref, msg_ref, first_ref, sums_ref = refs
    block = rows_here * ENTRIES
    tiles = cols // LANES
    at = 0
    for kept_ref, got_ref in zip(parts[0::2], parts[1::2]):
        here = kept_ref.shape[2] // LANES
        came = unpack(lambda place: got_ref[0, place], block // 16, here)
        for c in range(here):
            sums_ref[at] = kept_ref[0, :, c * LANES : (c + 1) * LANES] + came[c]
            at += 1
    shape = (rows_here, cols)
    row = me_ref[0] * rows_here + lax.broadcasted_iota(jnp.int32, shape, 0)
    degree = degree_of(row, shape, total_rows)
    normal = [take(sums_ref, obs_count + k, rows_here, ENTRIES) for k in range(6)]
    for b in range(obs_count // 3):
        fields = [prior_ref[3 * b + i] for i in range(3)]
        coupled = couple(normal, fields)
        for i in range(3):
            field = fields[i]
            beside = beside_columns(field)
            if rows_here > 1:
                zero = jnp.zeros((1, cols), jnp.float32)
                beside = beside + jnp.concatenate([zero, field[:-1]], axis=0) + jnp.concatenate([field[1:], zero], axis=0)
            entry = 3 * b + i
            observed = take(sums_ref, entry, rows_here, ENTRIES)
            put(sums_ref, entry, rows_here, ENTRIES, observed - coupled[i] - SMOOTH_PULL * (degree * field - beside))
    for c in range(tiles):
        out_ref[:, c * LANES : (c + 1) * LANES] = sums_ref[c]
    scales, numbers = pack([sums_ref[c] for c in range(tiles)], msg_ref, 0)
    first_ref[0] = scales
    for c in range(tiles):
        first_ref[1 + c] = numbers[c][0:16].astype(jnp.int16)
    left = jnp.concatenate([number[16:obs_count] for number in numbers], axis=0)
    spare = (first_ref.shape[0] - 1 - tiles) * 16 - left.shape[0]
    if spare:
        left = jnp.concatenate([left, jnp.zeros((spare, LANES), jnp.int32)], axis=0)
    for t in range(left.shape[0] // 16):
        first_ref[1 + tiles + t] = left[16 * t : 16 * t + 16].astype(jnp.int16)


def krylov_kernel(me_ref, own_ref, mate_ref, across_ref, zero_ref, one_ref, two_ref, gram_ref, window_ref, *, total_rows, rows_here):
    cols = own_ref.shape[1]
    obs_count = ENTRIES - 6
    tiles = cols // LANES
    row_tiles = own_ref.shape[0] // 16

    def lay(place, part, r):
        at = pl.ds(place, ENTRIES, stride=8)
        for c in range(tiles):
            window_ref[c, at, :] = part[c][r * ENTRIES : (r + 1) * ENTRIES]

    own = [own_ref[:, c * LANES : (c + 1) * LANES] for c in range(tiles)]
    mate = unpack(lambda place: mate_ref[place], row_tiles, tiles)
    across = unpack(lambda place: across_ref[place], row_tiles, tiles)
    odd = me_ref[0] % 2
    for r in range(2):
        lay(2 + r, own, r)
        lay(4 * (1 - odd) + r, mate, r)
        lay(4 * odd + r, across, r)
    for empty in (6, 7):
        put(window_ref, empty, ENTRIES, 8, jnp.zeros((ENTRIES, cols), jnp.float32))
    window = lambda entry: jnp.concatenate([window_ref[c, entry * 8 : entry * 8 + 8, :] for c in range(cols // LANES)], axis=1)
    shape = (8, cols)
    place = lax.broadcasted_iota(jnp.int32, shape, 0)
    row = me_ref[0] * rows_here + place - 2
    inside = ((row >= 0) & (row < total_rows)).astype(jnp.float32) * GAIN
    own_rows = (place == 2) | (place == 3)
    diag = inside * (PRIOR_PULL - SHIFT + SMOOTH_PULL * degree_of(row, shape, total_rows))
    pull = inside * SMOOTH_PULL
    normal = [window(obs_count + k) * inside for k in range(6)]
    acc = [jnp.zeros((8, LANES), jnp.float32) for _ in range(6)]

    def apply(v, last=False):
        coupled = couple(normal, v)
        out = []
        for i in range(3):
            x = v[i]
            above = pltpu.roll(x, 7, axis=0)
            beside = beside_columns(x) + (2.0 * above if last else above + pltpu.roll(x, 1, axis=0))
            out.append(coupled[i] + diag * x - pull * beside)
        return out

    def fold(x):
        total = x[:, 0:LANES]
        for c in range(LANES, cols, LANES):
            total = total + x[:, c : c + LANES]
        return total

    for b in range(obs_count // 3):
        zero = [window(3 * b + i) for i in range(3)]
        one = apply(zero)
        two = apply(one)
        three = apply(two, last=True)
        for i in range(3):
            zero_ref[3 * b + i] = zero[i][2:4]
            one_ref[3 * b + i] = one[i][2:4]
            two_ref[3 * b + i] = two[i][2:4]
            v = [zero[i], one[i], two[i], three[i]]
            for k in range(6):
                acc[k] = acc[k] + fold(v[k // 2] * v[(k + 1) // 2])
    own_tile = own_rows[:, 0:LANES]
    tile_row = lax.broadcasted_iota(jnp.int32, (8, LANES), 0)
    gram = jnp.zeros((8, LANES), jnp.float32)
    for k in range(6):
        moment = jnp.sum(jnp.where(own_tile, acc[k], 0.0))
        gram = jnp.where(tile_row == k, moment, gram)
    gram_ref[...] = gram


def far_kernel(gram_ref, two_ref, far_ref, out_ref):
    obs_count, _, cols = two_ref.shape
    tiles = cols // LANES
    rest = obs_count - 16
    factors = factors_of(far_ref[0], 2)
    left = jnp.concatenate([as_float(far_ref[t]) for t in range(1 + tiles, far_ref.shape[0])], axis=0)
    total = jnp.zeros((obs_count, LANES), jnp.float32)
    for c in range(tiles):
        far = jnp.concatenate([as_float(far_ref[1 + c]) * factors[0], left[rest * c : rest * (c + 1)] * factors[1][0:rest]], axis=0)
        mine = jnp.concatenate([two_ref[e, 1:2, c * LANES : (c + 1) * LANES] for e in range(obs_count)], axis=0)
        total = total + far * mine
    part = (-2.0 * (GAIN * SMOOTH_PULL) ** 3) * jnp.sum(total)
    row = lax.broadcasted_iota(jnp.int32, (8, LANES), 0)
    out_ref[...] = gram_ref[...] + jnp.where(row == 5, part, 0.0)


def combine_kernel(gram_ref, prior_ref, zero_ref, one_ref, two_ref, out_ref):
    gram = gram_ref[0]
    for k in range(1, gram_ref.shape[0]):
        gram = gram + gram_ref[k]
    m = [gram[k : k + 1, :] for k in range(6)]
    h = {(i, j): m[i + j + 1] * (1.0 / GAIN) + SHIFT * m[i + j] for i in range(3) for j in range(i, 3)}
    l10 = h[0, 1] / h[0, 0]
    l20 = h[0, 2] / h[0, 0]
    d1 = h[1, 1] - l10 * h[0, 1]
    t = h[1, 2] - l20 * h[0, 1]
    ok1 = d1 > 1e-6 * h[1, 1]
    inv1 = jnp.where(ok1, 1.0 / jnp.where(ok1, d1, 1.0), 0.0)
    l21 = t * inv1
    d2 = h[2, 2] - l20 * h[0, 2] - l21 * t
    ok2 = ok1 & (d2 > 1e-6 * h[2, 2])
    inv2 = jnp.where(ok2, 1.0 / jnp.where(ok2, d2, 1.0), 0.0)
    z1 = m[1] - l10 * m[0]
    z2 = m[2] - l20 * m[0] - l21 * z1
    y2 = z2 * inv2
    y1 = z1 * inv1 - l21 * y2
    y0 = m[0] / h[0, 0] - l10 * y1 - l20 * y2
    cols = prior_ref.shape[2]
    for c in range(0, cols, LANES):
        lanes = slice(c, c + LANES)
        out_ref[:, :, lanes] = (
            prior_ref[:, :, lanes] + y0[None] * zero_ref[:, :, lanes] + y1[None] * one_ref[:, :, lanes] + y2[None] * two_ref[:, :, lanes]
        )


def on_device(reflect, clear_conf, sun_view, sensor_id, band_gain, sensor_weight, prior):
    rows_here, obs_count, cols = prior.shape
    prior = jnp.transpose(prior, (1, 0, 2))
    count = lax.axis_size("rows")
    total_rows = rows_here * count
    block = rows_here * ENTRIES
    tiles = cols // LANES
    me = lax.axis_index("rows").astype(jnp.int32).reshape(1)
    vmem = pl.BlockSpec(memory_space=pltpu.VMEM)
    smem = pl.BlockSpec(memory_space=pltpu.SMEM)
    params = pltpu.CompilerParams(vmem_limit_bytes=24 * 2**20)
    f32 = lambda *shape: jax.ShapeDtypeStruct(shape, jnp.float32)
    packed = lambda *shape: jax.ShapeDtypeStruct(shape + (16, LANES), jnp.int16)

    scale = 0.01 / (reflect.shape[0] * count)
    flip = lambda x, mask: lax.ppermute(x, "rows", [(i, i ^ mask) for i in range(count)])
    swap = lambda x, bit: flip(x, 1 << bit)
    bits = list(range(1, count.bit_length() - 1))
    orders = [((bits[0], 0), (bits[1], 0)), ((bits[1], 1), (bits[0], 0))] if len(bits) >= 2 else [(), ()]

    parts = []
    after = me
    for chunk, share in enumerate(SHARES):
        width = cols // sum(SHARES) * share
        first_col = cols // sum(SHARES) * sum(SHARES[:chunk])
        kept, sent = partial_sums(
            after, reflect, clear_conf, sun_view, sensor_id, band_gain, sensor_weight, prior, scale, first_col, width
        )
        after, _ = lax.optimization_barrier((me, sent))
        parts.append((kept, swap(sent, 0)))
    for step, _ in enumerate(orders[0]):
        for chunk in range(len(parts)):
            bit, place = orders[min(chunk, 1)][step]
            kept, sent = add_split(me // 2**bit % 2, place, *parts[chunk])
            parts[chunk] = (kept, swap(sent, bit))
    bits = bits[len(orders[0]) :]
    parts = [x for part in parts for x in part]
    for bit in bits:
        kept, sent = add_split(me // 2**bit % 2, 0, *parts)
        parts = [kept, swap(sent, bit)]

    own, msg, first = pl.pallas_call(
        functools.partial(residual_kernel, total_rows=total_rows),
        in_specs=[smem] + [vmem] * (1 + len(parts)),
        out_specs=[vmem, vmem, vmem],
        out_shape=[f32(block, cols), packed(1, 1 + block // 16 * tiles), packed(1 + tiles + -(-(obs_count - 16) * tiles // 16))],
        scratch_shapes=[pltpu.VMEM((tiles, block, LANES), jnp.float32)],
        compiler_params=params,
        name="residual",
    )(me, prior, *parts)

    msg = msg[0]
    mate = swap(msg, 0)
    border = [(i, i + 1) for i in range(1, count - 1, 2)]
    across = lax.ppermute(msg, "rows", border + [(target, source) for source, target in border])
    zero, one, two, gram = pl.pallas_call(
        functools.partial(krylov_kernel, total_rows=total_rows, rows_here=rows_here),
        in_specs=[smem, vmem, vmem, vmem],
        out_specs=[vmem] * 4,
        out_shape=[f32(obs_count, rows_here, cols)] * 3 + [f32(8, LANES)],
        scratch_shapes=[pltpu.VMEM((tiles, ENTRIES * 8, LANES), jnp.float32)],
        compiler_params=params,
        name="krylov",
    )(me, own, mate, across)

    first, gram = lax.optimization_barrier((first, gram))
    far = lax.ppermute(first, "rows", [(i + 2, i) for i in range(count - 2)])
    grams = [
        pl.pallas_call(
            far_kernel, in_specs=[vmem] * 3, out_specs=vmem, out_shape=f32(8, LANES), compiler_params=params, name="far"
        )(gram, two, far)
    ]
    near = min(4, count)
    grams += [flip(grams[0], mask) for mask in range(1, near)]
    gram = sum(grams[1:], grams[0])
    groups = [list(range(first, count, near)) for first in range(near)]
    grams = lax.all_to_all(jnp.broadcast_to(gram[None], (count // near, 8, LANES)), "rows", 0, 0, axis_index_groups=groups)
    out = pl.pallas_call(
        combine_kernel,
        in_specs=[vmem] * 5,
        out_specs=vmem,
        out_shape=f32(obs_count, rows_here, cols),
        compiler_params=params,
        name="combine",
    )(grams, prior, zero, one, two)
    return jnp.transpose(out, (1, 0, 2))


def solution(mesh):
    return jax.shard_map(
        on_device,
        mesh=mesh,
        in_specs=(
            P("rows", None, None, "tiles"),
            P("rows", None, "tiles"),
            P("rows", None, None, "tiles"),
            P(),
            P(),
            P(),
            P("rows", None, "tiles"),
        ),
        out_specs=P("rows", None, "tiles"),
        check_vma=False,
    )
```

```python
import functools
import math

import jax
import jax.numpy as jnp
from jax import lax
from jax.experimental import pallas as pl
from jax.experimental.pallas import tpu as pltpu
from jax.sharding import PartitionSpec as P

TO_RADIAN = math.pi / 18000.0
PRIOR_PULL = 0.1
SMOOTH_PULL = 0.5
SHIFT = 3.0
GAIN = 0.4
ENTRIES = 24
LANES = 128
QUANT = 32000.0
GROUP = LANES // 4
CHUNKS = 2


R_POLY = (0.9428089773, 0.04714460664, 0.007527079489, 0.001965302741, 9.052799897e-05, 0.0004621408027)
S_POLY = (0.6002109608, -0.09003726006, -0.007977343822, -0.001801806492, 3.702625389e-06, -0.0003981650976)
SIN_25 = (0.9999999567, -0.1666626093, 0.008276695349)
COS_25 = (0.9999999997, -0.4999999562, 0.04166553086, -0.001379415437)
SIN_15 = (0.999999998, -0.1666661418, 0.008312938059)
COS_15 = (0.9999999858, -0.4999963087, 0.04152366947)
SIN_90 = (0.9999999947, -0.1666665666, 0.008333024663, -0.00019807389, 2.601844464e-06)


def horner(coefs, x):
    acc = coefs[-1] * x + coefs[-2]
    for coef in coefs[-3::-1]:
        acc = acc * x + coef
    return acc


def of_degrees(coefs, x, x2, factor, odd):
    scaled = [factor * coef * TO_RADIAN ** (2 * k + odd) for k, coef in enumerate(coefs)]
    value = horner(scaled, x2)
    return value * x if odd else value


def ross_li(sun, view, azim):
    x = (sun - 4500).astype(jnp.float32)
    x2 = x * x
    half = math.sqrt(0.5)
    sin_x, cos_x = of_degrees(SIN_25, x, x2, half, 1), of_degrees(COS_25, x, x2, half, 0)
    cos_sun, sin_sun = cos_x - sin_x, cos_x + sin_x
    v = view.astype(jnp.float32)
    v2 = v * v
    sin_view, cos_view = of_degrees(SIN_15, v, v2, 1.0, 1), of_degrees(COS_15, v, v2, 1.0, 0)
    a = (9000 - azim).astype(jnp.float32)
    cos_azim = of_degrees(SIN_90, a, a * a, 1.0, 1)
    prod = cos_sun * cos_view
    cos_phase = prod + sin_sun * sin_view * cos_azim
    total = cos_sun + cos_view
    recip = pl.reciprocal(total * prod, approx=False)
    inv_total = recip * prod
    sec_prod = recip * total
    u = 1.0 - cos_phase
    u_up = 1.0 + cos_phase
    bent = u * (u * lax.rsqrt(u)) * horner(R_POLY, u)
    volume = (bent + (0.5 * math.pi) * cos_phase) * inv_total - 0.25 * math.pi
    sin2 = u * u_up
    sin_phase = sin2 * lax.rsqrt(sin2)
    w = jnp.maximum(1.0 - (2.0 * inv_total) * sin_phase, 1e-30)
    overlap = w * (w * lax.rsqrt(w)) * horner(S_POLY, w)
    geometric = sec_prod * (total * (overlap - 1.0) + 0.5 * u_up)
    return volume, geometric


def lane_group(shape):
    return lax.broadcasted_iota(jnp.int32, shape, len(shape) - 1) // GROUP


def pack(tiles, msg_ref, block):
    rows = tiles[0].shape[0]
    top = jnp.abs(tiles[0])
    for tile in tiles[1:]:
        top = jnp.maximum(top, jnp.abs(tile))
    for shift in (LANES // 2, LANES // 4):
        top = jnp.maximum(top, pltpu.roll(top, shift, axis=1))
    level = jnp.ceil(8.0 * jnp.log2(jnp.maximum(top, 1e-30)))
    factor = QUANT * jnp.exp2(-0.125 * level)
    group = lane_group((16, LANES))
    scales = level[0:16]
    for t in range(1, rows // 16):
        scales = jnp.where(group == t, level[16 * t : 16 * t + 16], scales)
    scales = scales.astype(jnp.int32).astype(jnp.int16)
    msg_ref[block, 0] = scales
    numbers = [jnp.round(tile * factor).astype(jnp.int32) for tile in tiles]
    for c, number in enumerate(numbers):
        coded = number.astype(jnp.int16)
        for t in range(rows // 16):
            msg_ref[block, 1 + t * len(tiles) + c] = coded[16 * t : 16 * t + 16]
    return scales, numbers


def as_float(x):
    return x.astype(jnp.int32).astype(jnp.float32)


def factors_of(scales, row_tiles):
    scales = as_float(scales)
    group = lane_group((16, LANES))
    factors = []
    for t in range(row_tiles):
        level = jnp.where(group == t, scales, 0.0)
        for shift in (LANES // 2, LANES // 4):
            level = level + pltpu.roll(level, shift, axis=1)
        factors.append(jnp.exp2(0.125 * level) * (1.0 / QUANT))
    return factors


def unpack(read, row_tiles, col_tiles):
    factors = factors_of(read(0), row_tiles)
    return [
        jnp.concatenate([as_float(read(1 + t * col_tiles + c)) * factors[t] for t in range(row_tiles)], axis=0) for c in range(col_tiles)
    ]


def sums_kernel(
    me_ref,
    ids_ref,
    gain_ref,
    weight_ref,
    reflect_hbm,
    conf_hbm,
    sun_hbm,
    prior_ref,
    keep_ref,
    msg_ref,
    sums_ref,
    kernels_ref,
    reflect_ref,
    conf_ref,
    sun_ref,
    sems,
    *,
    scale,
    rows_here,
    first_col,
):
    steps, dates, bands, tile_rows, _ = reflect_ref.shape
    lane_tiles = sums_ref.shape[0]
    me = me_ref[0]
    block = rows_here * ENTRIES
    obs_count = 3 * bands

    def copies(step):
        rows = pl.ds(pl.multiple_of(step // lane_tiles * tile_rows, tile_rows), tile_rows)
        cols = pl.ds(pl.multiple_of(first_col + step % lane_tiles * LANES, LANES), LANES)
        return (
            pltpu.make_async_copy(sun_hbm.at[:, :, rows, cols], sun_ref.at[step], sems.at[step, 0]),
            pltpu.make_async_copy(conf_hbm.at[:, rows, cols], conf_ref.at[step], sems.at[step, 1]),
            pltpu.make_async_copy(reflect_hbm.at[:, :, rows, cols], reflect_ref.at[step], sems.at[step, 2]),
        )

    def start(step, carry):
        for copy in copies(step):
            copy.start()
        return carry

    lax.fori_loop(0, steps, start, 0)

    def lane_tile(index, row_tile):
        step = row_tile * lane_tiles + index
        for copy in copies(step):
            copy.wait()
        sensors = [ids_ref[me * dates + d] for d in range(dates)]

        def store(top, entry, total):
            sums_ref[index, pl.ds(top * ENTRIES + entry, 8, stride=ENTRIES), :] = total

        def plus(total, term):
            return term if total is None else total + term

        for top in range(0, tile_rows, 8):
            here = slice(top, top + 8)
            normal = [None] * 6
            for d in range(dates):
                volume, geometric = ross_li(*[sun_ref[step, d, angle, here, :] for angle in range(3)])
                weight = conf_ref[step, d, here, :].astype(jnp.float32) * (weight_ref[sensors[d]] * scale)
                weighted_vol = weight * volume
                weighted_geo = weight * geometric
                for i, value in enumerate((weight, weighted_vol, weighted_geo)):
                    kernels_ref[d, i, here, :] = value
                terms = (weight, weighted_vol, weighted_geo, weighted_vol * volume, weighted_vol * geometric, weighted_geo * geometric)
                normal = [plus(total, term) for total, term in zip(normal, terms)]
            for k in range(6):
                store(top, obs_count + k, normal[k])
        for b in range(bands):
            observed = [None] * 3
            for d in range(dates):
                signal = reflect_ref[step, d, b].astype(jnp.float32) * gain_ref[sensors[d], b]
                observed = [plus(total, kernels_ref[d, i] * signal) for i, total in enumerate(observed)]
            for i in range(3):
                for top in range(0, tile_rows, 8):
                    store(top, 3 * b + i, observed[i][top : top + 8])
        return row_tile

    def row_tile_sums(row_tile, carry):
        lax.fori_loop(0, lane_tiles, lane_tile, row_tile)
        tiles = range(lane_tiles)
        first_row = row_tile * tile_rows
        for row, source in ((me * rows_here - 1 - first_row, 0), ((me + 1) * rows_here - first_row, rows_here - 1)):

            @pl.when((row >= 0) & (row < tile_rows))
            def _():
                for c in tiles:
                    lanes = slice(c * LANES, (c + 1) * LANES)
                    at = pl.ds(pl.multiple_of(row * ENTRIES, 8), obs_count)
                    part = jnp.concatenate([prior_ref[e, source : source + 1, lanes] for e in range(obs_count)], axis=0)
                    sums_ref[c, at, :] = sums_ref[c, at, :] + SMOOTH_PULL * part

        bit = me % 2
        per_tile = tile_rows // rows_here // 2
        for j in range(per_tile):
            own = pl.ds(pl.multiple_of((2 * j + bit) * block, 8), block)
            other = pl.ds(pl.multiple_of((2 * j + 1 - bit) * block, 8), block)
            for c in tiles:
                keep_ref[row_tile * per_tile + j, :, c * LANES : (c + 1) * LANES] = sums_ref[c, own, :]
            pack([sums_ref[c, other, :] for c in tiles], msg_ref, row_tile * per_tile + j)
        return carry

    lax.fori_loop(0, steps // lane_tiles, row_tile_sums, 0)


def partial_sums(me, reflect, clear_conf, sun_view, sensor_id, band_gain, sensor_weight, prior, scale, chunk):
    dates, bands, rows, cols = reflect.shape
    cols = cols // CHUNKS
    rows_here = prior.shape[1]
    count = rows // rows_here
    tile_rows = 16
    block = rows_here * ENTRIES
    lane_tiles = cols // LANES
    steps = rows // tile_rows * lane_tiles
    smem = pl.BlockSpec(memory_space=pltpu.SMEM)
    vmem = pl.BlockSpec(memory_space=pltpu.VMEM)
    hbm = pl.BlockSpec(memory_space=pl.ANY)
    return pl.pallas_call(
        functools.partial(sums_kernel, scale=scale, rows_here=rows_here, first_col=chunk * cols),
        grid=(1,),
        in_specs=[smem] * 4 + [hbm] * 3 + [pl.BlockSpec((3 * bands, rows_here, cols), lambda i: (0, 0, chunk))],
        out_specs=[vmem, vmem],
        out_shape=[
            jax.ShapeDtypeStruct((count // 2, block, cols), jnp.float32),
            jax.ShapeDtypeStruct((count // 2, 1 + block // 16 * lane_tiles, 16, LANES), jnp.int16),
        ],
        scratch_shapes=[
            pltpu.VMEM((lane_tiles, tile_rows * ENTRIES, LANES), jnp.float32),
            pltpu.VMEM((dates, 3, tile_rows, LANES), jnp.float32),
            pltpu.VMEM((steps, dates, bands, tile_rows, LANES), reflect.dtype),
            pltpu.VMEM((steps, dates, tile_rows, LANES), jnp.int32),
            pltpu.VMEM((steps, dates, 3, tile_rows, LANES), jnp.int32),
            pltpu.SemaphoreType.DMA((steps, 3)),
        ],
        compiler_params=pltpu.CompilerParams(vmem_limit_bytes=(62 if chunk == 0 else 52) * 2**20),
        name="partial_sums",
    )(me, sensor_id, band_gain, sensor_weight, reflect, clear_conf, sun_view, prior)


def add_split_kernel(bit_ref, *refs, place):
    *parts, keep_ref, msg_ref = refs
    count, block, _ = keep_ref.shape
    bit = bit_ref[0]

    def total(j):
        tiles = []
        for kept_ref, got_ref in zip(parts[0::2], parts[1::2]):
            here = kept_ref.shape[2] // LANES
            came = unpack(lambda at: got_ref[j, at], block // 16, here)
            tiles += [kept_ref[j, :, c * LANES : (c + 1) * LANES] + came[c] for c in range(here)]
        return tiles

    for q in range(count):
        low = q % 2**place
        first = (q - low) * 2 + low
        pack(total(first + (1 - bit) * 2**place), msg_ref, q)
        for c, tile in enumerate(total(first + bit * 2**place)):
            keep_ref[q, :, c * LANES : (c + 1) * LANES] = tile


def add_split(bit, place, *parts):
    count, block, _ = parts[0].shape
    cols = sum(kept.shape[2] for kept in parts[0::2])
    vmem = pl.BlockSpec(memory_space=pltpu.VMEM)
    return pl.pallas_call(
        functools.partial(add_split_kernel, place=place),
        in_specs=[pl.BlockSpec(memory_space=pltpu.SMEM)] + [vmem] * len(parts),
        out_specs=[vmem, vmem],
        out_shape=[
            jax.ShapeDtypeStruct((count // 2, block, cols), jnp.float32),
            jax.ShapeDtypeStruct((count // 2, 1 + block // 16 * (cols // LANES), 16, LANES), jnp.int16),
        ],
        compiler_params=pltpu.CompilerParams(vmem_limit_bytes=24 * 2**20),
        name="add_split",
    )(bit, *parts)


def take(ref, start, size, stride):
    at = pl.ds(start, size, stride=stride)
    return jnp.concatenate([ref[c, at, :] for c in range(ref.shape[0])], axis=1)


def put(ref, start, size, stride, value):
    at = pl.ds(start, size, stride=stride)
    for c in range(ref.shape[0]):
        ref[c, at, :] = value[:, c * LANES : (c + 1) * LANES]


def beside_columns(x):
    cols = x.shape[1]
    col = lax.broadcasted_iota(jnp.int32, x.shape, 1)
    left = jnp.where(col == 0, 0.0, pltpu.roll(x, 1, axis=1))
    right = jnp.where(col == cols - 1, 0.0, pltpu.roll(x, cols - 1, axis=1))
    return left + right


def degree_of(row, shape, total_rows):
    col = lax.broadcasted_iota(jnp.int32, shape, 1)
    edge = (
        (row == 0).astype(jnp.float32)
        + (row == total_rows - 1).astype(jnp.float32)
        + (col == 0).astype(jnp.float32)
        + (col == shape[1] - 1).astype(jnp.float32)
    )
    return 4.0 - edge


def couple(n, v):
    return (
        n[0] * v[0] + n[1] * v[1] + n[2] * v[2],
        n[1] * v[0] + n[3] * v[1] + n[4] * v[2],
        n[2] * v[0] + n[4] * v[1] + n[5] * v[2],
    )


def residual_kernel(me_ref, prior_ref, *refs, total_rows):
    obs_count, rows_here, cols = prior_ref.shape
    *parts, out_ref, msg_ref, first_ref, sums_ref = refs
    block = rows_here * ENTRIES
    tiles = cols // LANES
    at = 0
    for kept_ref, got_ref in zip(parts[0::2], parts[1::2]):
        here = kept_ref.shape[2] // LANES
        came = unpack(lambda place: got_ref[0, place], block // 16, here)
        for c in range(here):
            sums_ref[at] = kept_ref[0, :, c * LANES : (c + 1) * LANES] + came[c]
            at += 1
    shape = (rows_here, cols)
    row = me_ref[0] * rows_here + lax.broadcasted_iota(jnp.int32, shape, 0)
    degree = degree_of(row, shape, total_rows)
    normal = [take(sums_ref, obs_count + k, rows_here, ENTRIES) for k in range(6)]
    for b in range(obs_count // 3):
        fields = [prior_ref[3 * b + i] for i in range(3)]
        coupled = couple(normal, fields)
        for i in range(3):
            field = fields[i]
            beside = beside_columns(field)
            if rows_here > 1:
                zero = jnp.zeros((1, cols), jnp.float32)
                beside = beside + jnp.concatenate([zero, field[:-1]], axis=0) + jnp.concatenate([field[1:], zero], axis=0)
            entry = 3 * b + i
            observed = take(sums_ref, entry, rows_here, ENTRIES)
            put(sums_ref, entry, rows_here, ENTRIES, observed - coupled[i] - SMOOTH_PULL * (degree * field - beside))
    for c in range(tiles):
        out_ref[:, c * LANES : (c + 1) * LANES] = sums_ref[c]
    scales, numbers = pack([sums_ref[c] for c in range(tiles)], msg_ref, 0)
    first_ref[0] = scales
    for c in range(tiles):
        first_ref[1 + c] = numbers[c][0:16].astype(jnp.int16)
    left = jnp.concatenate([number[16:obs_count] for number in numbers], axis=0)
    spare = (first_ref.shape[0] - 1 - tiles) * 16 - left.shape[0]
    if spare:
        left = jnp.concatenate([left, jnp.zeros((spare, LANES), jnp.int32)], axis=0)
    for t in range(left.shape[0] // 16):
        first_ref[1 + tiles + t] = left[16 * t : 16 * t + 16].astype(jnp.int16)


def krylov_kernel(me_ref, own_ref, mate_ref, across_ref, zero_ref, one_ref, two_ref, gram_ref, window_ref, *, total_rows, rows_here):
    cols = own_ref.shape[1]
    obs_count = ENTRIES - 6
    tiles = cols // LANES
    row_tiles = own_ref.shape[0] // 16

    def lay(place, part, r):
        at = pl.ds(place, ENTRIES, stride=8)
        for c in range(tiles):
            window_ref[c, at, :] = part[c][r * ENTRIES : (r + 1) * ENTRIES]

    own = [own_ref[:, c * LANES : (c + 1) * LANES] for c in range(tiles)]
    mate = unpack(lambda place: mate_ref[place], row_tiles, tiles)
    across = unpack(lambda place: across_ref[place], row_tiles, tiles)
    odd = me_ref[0] % 2
    for r in range(2):
        lay(2 + r, own, r)
        lay(4 * (1 - odd) + r, mate, r)
        lay(4 * odd + r, across, r)
    for empty in (6, 7):
        put(window_ref, empty, ENTRIES, 8, jnp.zeros((ENTRIES, cols), jnp.float32))
    window = lambda entry: jnp.concatenate([window_ref[c, entry * 8 : entry * 8 + 8, :] for c in range(cols // LANES)], axis=1)
    shape = (8, cols)
    place = lax.broadcasted_iota(jnp.int32, shape, 0)
    row = me_ref[0] * rows_here + place - 2
    inside = ((row >= 0) & (row < total_rows)).astype(jnp.float32) * GAIN
    own_rows = (place == 2) | (place == 3)
    diag = inside * (PRIOR_PULL - SHIFT + SMOOTH_PULL * degree_of(row, shape, total_rows))
    pull = inside * SMOOTH_PULL
    normal = [window(obs_count + k) * inside for k in range(6)]
    acc = [jnp.zeros((8, LANES), jnp.float32) for _ in range(6)]

    def apply(v, last=False):
        coupled = couple(normal, v)
        out = []
        for i in range(3):
            x = v[i]
            above = pltpu.roll(x, 7, axis=0)
            beside = beside_columns(x) + (2.0 * above if last else above + pltpu.roll(x, 1, axis=0))
            out.append(coupled[i] + diag * x - pull * beside)
        return out

    def fold(x):
        total = x[:, 0:LANES]
        for c in range(LANES, cols, LANES):
            total = total + x[:, c : c + LANES]
        return total

    for b in range(obs_count // 3):
        zero = [window(3 * b + i) for i in range(3)]
        one = apply(zero)
        two = apply(one)
        three = apply(two, last=True)
        for i in range(3):
            zero_ref[3 * b + i] = zero[i][2:4]
            one_ref[3 * b + i] = one[i][2:4]
            two_ref[3 * b + i] = two[i][2:4]
            v = [zero[i], one[i], two[i], three[i]]
            for k in range(6):
                acc[k] = acc[k] + fold(v[k // 2] * v[(k + 1) // 2])
    own_tile = own_rows[:, 0:LANES]
    tile_row = lax.broadcasted_iota(jnp.int32, (8, LANES), 0)
    gram = jnp.zeros((8, LANES), jnp.float32)
    for k in range(6):
        moment = jnp.sum(jnp.where(own_tile, acc[k], 0.0))
        gram = jnp.where(tile_row == k, moment, gram)
    gram_ref[...] = gram


def far_kernel(me_ref, gram_ref, two_ref, mate_ref, beyond_ref, out_ref):
    obs_count, _, cols = two_ref.shape
    tiles = cols // LANES
    rest = obs_count - 16
    core0 = me_ref[0] % 2 == 0
    from_mate = unpack(lambda place: mate_ref[place], 2, tiles)
    short = beyond_ref.shape[0] - (1 + tiles + -(-rest * tiles // 16))
    factors = factors_of(beyond_ref[short], 2)
    left = jnp.concatenate([as_float(beyond_ref[t]) for t in range(short + 1 + tiles, beyond_ref.shape[0])], axis=0)
    total = jnp.zeros((obs_count, LANES), jnp.float32)
    for c in range(tiles):
        rows = as_float(beyond_ref[short + 1 + c]) * factors[0], left[rest * c : rest * (c + 1)] * factors[1][0:rest]
        far = jnp.where(core0, from_mate[c][0:obs_count], jnp.concatenate(rows, axis=0))
        mine = jnp.concatenate([two_ref[e, 1:2, c * LANES : (c + 1) * LANES] for e in range(obs_count)], axis=0)
        total = total + far * mine
    part = (-2.0 * (GAIN * SMOOTH_PULL) ** 3) * jnp.sum(total)
    row = lax.broadcasted_iota(jnp.int32, (8, LANES), 0)
    out_ref[...] = gram_ref[...] + jnp.where(row == 5, part, 0.0)


def combine_kernel(*refs):
    *gram_refs, prior_ref, zero_ref, one_ref, two_ref, out_ref = refs
    gram = gram_refs[0][...]
    for ref in gram_refs[1:]:
        gram = gram + ref[...]
    m = [gram[k : k + 1, :] for k in range(6)]
    h = {(i, j): m[i + j + 1] * (1.0 / GAIN) + SHIFT * m[i + j] for i in range(3) for j in range(i, 3)}
    l10 = h[0, 1] / h[0, 0]
    l20 = h[0, 2] / h[0, 0]
    d1 = h[1, 1] - l10 * h[0, 1]
    t = h[1, 2] - l20 * h[0, 1]
    ok1 = d1 > 1e-6 * h[1, 1]
    inv1 = jnp.where(ok1, 1.0 / jnp.where(ok1, d1, 1.0), 0.0)
    l21 = t * inv1
    d2 = h[2, 2] - l20 * h[0, 2] - l21 * t
    ok2 = ok1 & (d2 > 1e-6 * h[2, 2])
    inv2 = jnp.where(ok2, 1.0 / jnp.where(ok2, d2, 1.0), 0.0)
    z1 = m[1] - l10 * m[0]
    z2 = m[2] - l20 * m[0] - l21 * z1
    y2 = z2 * inv2
    y1 = z1 * inv1 - l21 * y2
    y0 = m[0] / h[0, 0] - l10 * y1 - l20 * y2
    cols = prior_ref.shape[2]
    for c in range(0, cols, LANES):
        lanes = slice(c, c + LANES)
        out_ref[:, :, lanes] = (
            prior_ref[:, :, lanes] + y0[None] * zero_ref[:, :, lanes] + y1[None] * one_ref[:, :, lanes] + y2[None] * two_ref[:, :, lanes]
        )


def on_device(reflect, clear_conf, sun_view, sensor_id, band_gain, sensor_weight, prior):
    rows_here, obs_count, cols = prior.shape
    prior = jnp.transpose(prior, (1, 0, 2))
    count = lax.axis_size("rows")
    total_rows = rows_here * count
    block = rows_here * ENTRIES
    tiles = cols // LANES
    me = lax.axis_index("rows").astype(jnp.int32).reshape(1)
    vmem = pl.BlockSpec(memory_space=pltpu.VMEM)
    smem = pl.BlockSpec(memory_space=pltpu.SMEM)
    params = pltpu.CompilerParams(vmem_limit_bytes=24 * 2**20)
    f32 = lambda *shape: jax.ShapeDtypeStruct(shape, jnp.float32)
    packed = lambda *shape: jax.ShapeDtypeStruct(shape + (16, LANES), jnp.int16)

    scale = 0.01 / (reflect.shape[0] * count)
    index = me
    parts = []
    for chunk in range(CHUNKS):
        kept, sent = partial_sums(
            index, reflect, clear_conf, sun_view, sensor_id, band_gain, sensor_weight, prior, scale, chunk
        )
        index, _ = lax.optimization_barrier((me, sent))
        parts.append((kept, sent))
    flip = lambda x, mask: lax.ppermute(x, "rows", [(i, i ^ mask) for i in range(count)])
    swap = lambda x, bit: flip(x, 1 << bit)
    bits = list(range(1, count.bit_length() - 1))
    parts = [(kept, swap(sent, 0)) for kept, sent in parts]
    if len(bits) >= 2:
        orders = [((bits[0], 0), (bits[1], 0)), ((bits[1], 1), (bits[0], 0))]
        for step in range(2):
            for chunk in range(CHUNKS):
                bit, place = orders[chunk % 2][step]
                kept, sent = add_split(me // 2**bit % 2, place, *parts[chunk])
                parts[chunk] = (kept, swap(sent, bit))
        bits = bits[2:]
    parts = [x for part in parts for x in part]
    for bit in bits:
        kept, sent = add_split(me // 2**bit % 2, 0, *parts)
        parts = [kept, swap(sent, bit)]

    own, msg, first = pl.pallas_call(
        functools.partial(residual_kernel, total_rows=total_rows),
        in_specs=[smem] + [vmem] * (1 + len(parts)),
        out_specs=[vmem, vmem, vmem],
        out_shape=[f32(block, cols), packed(1, 1 + block // 16 * tiles), packed(1 + tiles + -(-(obs_count - 16) * tiles // 16))],
        scratch_shapes=[pltpu.VMEM((tiles, block, LANES), jnp.float32)],
        compiler_params=params,
        name="residual",
    )(me, prior, *parts)

    msg = msg[0]
    mate = swap(msg, 0)
    payload = jnp.concatenate([mate, first], axis=0)
    near = []
    for parity in range(2):
        chips = range(parity, count // 2 - 1, 2)
        pairs = [(2 * chip, 2 * chip + 2) for chip in chips] + [(2 * chip + 3, 2 * chip + 1) for chip in chips]
        near.append(lax.ppermute(payload, "rows", pairs))
    beyond = jnp.where(((me[0] ^ (me[0] >> 1)) & 1) == 1, near[0], near[1])
    far = swap(beyond[: 1 + 2 * tiles], 0)
    zero, one, two, gram = pl.pallas_call(
        functools.partial(krylov_kernel, total_rows=total_rows, rows_here=rows_here),
        in_specs=[smem, vmem, vmem, vmem],
        out_specs=[vmem] * 4,
        out_shape=[f32(obs_count, rows_here, cols)] * 3 + [f32(8, LANES)],
        scratch_shapes=[pltpu.VMEM((tiles, ENTRIES * 8, LANES), jnp.float32)],
        compiler_params=params,
        name="krylov",
    )(me, own, mate, beyond)

    grams = [
        pl.pallas_call(
            far_kernel, in_specs=[smem] + [vmem] * 4, out_specs=vmem, out_shape=f32(8, LANES), compiler_params=params, name="far"
        )(me, gram, two, far, beyond)
    ]
    for bit in range(0, count.bit_length() - 1, 2):
        masks = [mask << bit for mask in (1, 2, 3) if mask << bit < count]
        gram = sum(grams[1:], grams[0])
        grams = [gram] + [flip(gram, mask) for mask in masks]
    out = pl.pallas_call(
        combine_kernel,
        in_specs=[vmem] * (len(grams) + 4),
        out_specs=vmem,
        out_shape=f32(obs_count, rows_here, cols),
        compiler_params=params,
        name="combine",
    )(*grams, prior, zero, one, two)
    return jnp.transpose(out, (1, 0, 2))


def solution(mesh):
    return jax.shard_map(
        on_device,
        mesh=mesh,
        in_specs=(
            P("rows", None, None, "tiles"),
            P("rows", None, "tiles"),
            P("rows", None, None, "tiles"),
            P(),
            P(),
            P(),
            P("rows", None, "tiles"),
        ),
        out_specs=P("rows", None, "tiles"),
        check_vma=False,
    )
```

```python
import functools
import math

import jax
import jax.numpy as jnp
from jax import lax
from jax.experimental import pallas as pl
from jax.experimental.pallas import tpu as pltpu
from jax.sharding import PartitionSpec as P

TO_RADIAN = math.pi / 18000.0
PRIOR_PULL = 0.1
SMOOTH_PULL = 0.5
SHIFT = 3.0
GAIN = 0.4
ENTRIES = 24
LANES = 128
QUANT = 32000.0
GROUP = LANES // 4
CHUNKS = 2


R_POLY = (0.9428089773, 0.04714460664, 0.007527079489, 0.001965302741, 9.052799897e-05, 0.0004621408027)
S_POLY = (0.6002109608, -0.09003726006, -0.007977343822, -0.001801806492, 3.702625389e-06, -0.0003981650976)
SIN_25 = (0.9999999567, -0.1666626093, 0.008276695349)
COS_25 = (0.9999999997, -0.4999999562, 0.04166553086, -0.001379415437)
SIN_15 = (0.999999998, -0.1666661418, 0.008312938059)
COS_15 = (0.9999999858, -0.4999963087, 0.04152366947)
SIN_90 = (0.9999999947, -0.1666665666, 0.008333024663, -0.00019807389, 2.601844464e-06)


def horner(coefs, x):
    acc = coefs[-1] * x + coefs[-2]
    for coef in coefs[-3::-1]:
        acc = acc * x + coef
    return acc


def of_degrees(coefs, x, x2, factor, odd):
    scaled = [factor * coef * TO_RADIAN ** (2 * k + odd) for k, coef in enumerate(coefs)]
    value = horner(scaled, x2)
    return value * x if odd else value


def ross_li(sun, view, azim):
    x = (sun - 4500).astype(jnp.float32)
    x2 = x * x
    half = math.sqrt(0.5)
    sin_x, cos_x = of_degrees(SIN_25, x, x2, half, 1), of_degrees(COS_25, x, x2, half, 0)
    cos_sun, sin_sun = cos_x - sin_x, cos_x + sin_x
    v = view.astype(jnp.float32)
    v2 = v * v
    sin_view, cos_view = of_degrees(SIN_15, v, v2, 1.0, 1), of_degrees(COS_15, v, v2, 1.0, 0)
    a = (9000 - azim).astype(jnp.float32)
    cos_azim = of_degrees(SIN_90, a, a * a, 1.0, 1)
    prod = cos_sun * cos_view
    cos_phase = prod + sin_sun * sin_view * cos_azim
    total = cos_sun + cos_view
    recip = pl.reciprocal(total * prod, approx=False)
    inv_total = recip * prod
    sec_prod = recip * total
    u = 1.0 - cos_phase
    u_up = 1.0 + cos_phase
    bent = u * (u * lax.rsqrt(u)) * horner(R_POLY, u)
    volume = (bent + (0.5 * math.pi) * cos_phase) * inv_total - 0.25 * math.pi
    sin2 = u * u_up
    sin_phase = sin2 * lax.rsqrt(sin2)
    w = jnp.maximum(1.0 - (2.0 * inv_total) * sin_phase, 1e-30)
    overlap = w * (w * lax.rsqrt(w)) * horner(S_POLY, w)
    geometric = sec_prod * (total * (overlap - 1.0) + 0.5 * u_up)
    return volume, geometric


def lane_group(shape):
    return lax.broadcasted_iota(jnp.int32, shape, len(shape) - 1) // GROUP


def pack(tiles, msg_ref, block):
    rows = tiles[0].shape[0]
    top = jnp.abs(tiles[0])
    for tile in tiles[1:]:
        top = jnp.maximum(top, jnp.abs(tile))
    for shift in (LANES // 2, LANES // 4):
        top = jnp.maximum(top, pltpu.roll(top, shift, axis=1))
    level = jnp.ceil(8.0 * jnp.log2(jnp.maximum(top, 1e-30)))
    factor = QUANT * jnp.exp2(-0.125 * level)
    group = lane_group((16, LANES))
    scales = level[0:16]
    for t in range(1, rows // 16):
        scales = jnp.where(group == t, level[16 * t : 16 * t + 16], scales)
    scales = scales.astype(jnp.int32).astype(jnp.int16)
    msg_ref[block, 0] = scales
    numbers = [jnp.round(tile * factor).astype(jnp.int32) for tile in tiles]
    for c, number in enumerate(numbers):
        coded = number.astype(jnp.int16)
        for t in range(rows // 16):
            msg_ref[block, 1 + t * len(tiles) + c] = coded[16 * t : 16 * t + 16]
    return scales, numbers


def as_float(x):
    return x.astype(jnp.int32).astype(jnp.float32)


def factors_of(scales, row_tiles):
    scales = as_float(scales)
    group = lane_group((16, LANES))
    factors = []
    for t in range(row_tiles):
        level = jnp.where(group == t, scales, 0.0)
        for shift in (LANES // 2, LANES // 4):
            level = level + pltpu.roll(level, shift, axis=1)
        factors.append(jnp.exp2(0.125 * level) * (1.0 / QUANT))
    return factors


def unpack(read, row_tiles, col_tiles):
    factors = factors_of(read(0), row_tiles)
    return [
        jnp.concatenate([as_float(read(1 + t * col_tiles + c)) * factors[t] for t in range(row_tiles)], axis=0) for c in range(col_tiles)
    ]


def sums_kernel(
    me_ref,
    ids_ref,
    gain_ref,
    weight_ref,
    reflect_hbm,
    conf_hbm,
    sun_hbm,
    prior_ref,
    keep_ref,
    msg_ref,
    sums_ref,
    kernels_ref,
    reflect_ref,
    conf_ref,
    sun_ref,
    sems,
    *,
    scale,
    rows_here,
    first_col,
):
    steps, dates, bands, tile_rows, _ = reflect_ref.shape
    lane_tiles = sums_ref.shape[0]
    me = me_ref[0]
    block = rows_here * ENTRIES
    obs_count = 3 * bands

    def copies(step):
        rows = pl.ds(pl.multiple_of(step // lane_tiles * tile_rows, tile_rows), tile_rows)
        cols = pl.ds(pl.multiple_of(first_col + step % lane_tiles * LANES, LANES), LANES)
        return (
            pltpu.make_async_copy(sun_hbm.at[:, :, rows, cols], sun_ref.at[step], sems.at[step, 0]),
            pltpu.make_async_copy(conf_hbm.at[:, rows, cols], conf_ref.at[step], sems.at[step, 1]),
            pltpu.make_async_copy(reflect_hbm.at[:, :, rows, cols], reflect_ref.at[step], sems.at[step, 2]),
        )

    def start(step, carry):
        for copy in copies(step):
            copy.start()
        return carry

    lax.fori_loop(0, steps, start, 0)

    def lane_tile(index, row_tile):
        step = row_tile * lane_tiles + index
        for copy in copies(step):
            copy.wait()
        sensors = [ids_ref[me * dates + d] for d in range(dates)]

        def store(top, entry, total):
            sums_ref[index, pl.ds(top * ENTRIES + entry, 8, stride=ENTRIES), :] = total

        def plus(total, term):
            return term if total is None else total + term

        for top in range(0, tile_rows, 8):
            here = slice(top, top + 8)
            normal = [None] * 6
            for d in range(dates):
                volume, geometric = ross_li(*[sun_ref[step, d, angle, here, :] for angle in range(3)])
                weight = conf_ref[step, d, here, :].astype(jnp.float32) * (weight_ref[sensors[d]] * scale)
                weighted_vol = weight * volume
                weighted_geo = weight * geometric
                for i, value in enumerate((weight, weighted_vol, weighted_geo)):
                    kernels_ref[d, i, here, :] = value
                terms = (weight, weighted_vol, weighted_geo, weighted_vol * volume, weighted_vol * geometric, weighted_geo * geometric)
                normal = [plus(total, term) for total, term in zip(normal, terms)]
            for k in range(6):
                store(top, obs_count + k, normal[k])
        for b in range(bands):
            observed = [None] * 3
            for d in range(dates):
                signal = reflect_ref[step, d, b].astype(jnp.float32) * gain_ref[sensors[d], b]
                observed = [plus(total, kernels_ref[d, i] * signal) for i, total in enumerate(observed)]
            for i in range(3):
                for top in range(0, tile_rows, 8):
                    store(top, 3 * b + i, observed[i][top : top + 8])
        return row_tile

    def row_tile_sums(row_tile, carry):
        lax.fori_loop(0, lane_tiles, lane_tile, row_tile)
        tiles = range(lane_tiles)
        first_row = row_tile * tile_rows
        for row, source in ((me * rows_here - 1 - first_row, 0), ((me + 1) * rows_here - first_row, rows_here - 1)):

            @pl.when((row >= 0) & (row < tile_rows))
            def _():
                for c in tiles:
                    lanes = slice(c * LANES, (c + 1) * LANES)
                    at = pl.ds(pl.multiple_of(row * ENTRIES, 8), obs_count)
                    part = jnp.concatenate([prior_ref[e, source : source + 1, lanes] for e in range(obs_count)], axis=0)
                    sums_ref[c, at, :] = sums_ref[c, at, :] + SMOOTH_PULL * part

        bit = me % 2
        per_tile = tile_rows // rows_here // 2
        for j in range(per_tile):
            own = pl.ds(pl.multiple_of((2 * j + bit) * block, 8), block)
            other = pl.ds(pl.multiple_of((2 * j + 1 - bit) * block, 8), block)
            for c in tiles:
                keep_ref[row_tile * per_tile + j, :, c * LANES : (c + 1) * LANES] = sums_ref[c, own, :]
            pack([sums_ref[c, other, :] for c in tiles], msg_ref, row_tile * per_tile + j)
        return carry

    lax.fori_loop(0, steps // lane_tiles, row_tile_sums, 0)


def partial_sums(me, reflect, clear_conf, sun_view, sensor_id, band_gain, sensor_weight, prior, scale, chunk):
    dates, bands, rows, cols = reflect.shape
    cols = cols // CHUNKS
    rows_here = prior.shape[1]
    count = rows // rows_here
    tile_rows = 16
    block = rows_here * ENTRIES
    lane_tiles = cols // LANES
    steps = rows // tile_rows * lane_tiles
    smem = pl.BlockSpec(memory_space=pltpu.SMEM)
    vmem = pl.BlockSpec(memory_space=pltpu.VMEM)
    hbm = pl.BlockSpec(memory_space=pl.ANY)
    return pl.pallas_call(
        functools.partial(sums_kernel, scale=scale, rows_here=rows_here, first_col=chunk * cols),
        grid=(1,),
        in_specs=[smem] * 4 + [hbm] * 3 + [pl.BlockSpec((3 * bands, rows_here, cols), lambda i: (0, 0, chunk))],
        out_specs=[vmem, vmem],
        out_shape=[
            jax.ShapeDtypeStruct((count // 2, block, cols), jnp.float32),
            jax.ShapeDtypeStruct((count // 2, 1 + block // 16 * lane_tiles, 16, LANES), jnp.int16),
        ],
        scratch_shapes=[
            pltpu.VMEM((lane_tiles, tile_rows * ENTRIES, LANES), jnp.float32),
            pltpu.VMEM((dates, 3, tile_rows, LANES), jnp.float32),
            pltpu.VMEM((steps, dates, bands, tile_rows, LANES), reflect.dtype),
            pltpu.VMEM((steps, dates, tile_rows, LANES), jnp.int32),
            pltpu.VMEM((steps, dates, 3, tile_rows, LANES), jnp.int32),
            pltpu.SemaphoreType.DMA((steps, 3)),
        ],
        compiler_params=pltpu.CompilerParams(vmem_limit_bytes=(62 if chunk == 0 else 52) * 2**20),
        name="partial_sums",
    )(me, sensor_id, band_gain, sensor_weight, reflect, clear_conf, sun_view, prior)


def add_split_kernel(bit_ref, *refs, place):
    *parts, keep_ref, msg_ref = refs
    count, block, _ = keep_ref.shape
    bit = bit_ref[0]

    def total(j):
        tiles = []
        for kept_ref, got_ref in zip(parts[0::2], parts[1::2]):
            here = kept_ref.shape[2] // LANES
            came = unpack(lambda at: got_ref[j, at], block // 16, here)
            tiles += [kept_ref[j, :, c * LANES : (c + 1) * LANES] + came[c] for c in range(here)]
        return tiles

    for q in range(count):
        low = q % 2**place
        first = (q - low) * 2 + low
        pack(total(first + (1 - bit) * 2**place), msg_ref, q)
        for c, tile in enumerate(total(first + bit * 2**place)):
            keep_ref[q, :, c * LANES : (c + 1) * LANES] = tile


def add_split(bit, place, *parts):
    count, block, _ = parts[0].shape
    cols = sum(kept.shape[2] for kept in parts[0::2])
    vmem = pl.BlockSpec(memory_space=pltpu.VMEM)
    return pl.pallas_call(
        functools.partial(add_split_kernel, place=place),
        in_specs=[pl.BlockSpec(memory_space=pltpu.SMEM)] + [vmem] * len(parts),
        out_specs=[vmem, vmem],
        out_shape=[
            jax.ShapeDtypeStruct((count // 2, block, cols), jnp.float32),
            jax.ShapeDtypeStruct((count // 2, 1 + block // 16 * (cols // LANES), 16, LANES), jnp.int16),
        ],
        compiler_params=pltpu.CompilerParams(vmem_limit_bytes=24 * 2**20),
        name="add_split",
    )(bit, *parts)


def take(ref, start, size, stride):
    at = pl.ds(start, size, stride=stride)
    return jnp.concatenate([ref[c, at, :] for c in range(ref.shape[0])], axis=1)


def put(ref, start, size, stride, value):
    at = pl.ds(start, size, stride=stride)
    for c in range(ref.shape[0]):
        ref[c, at, :] = value[:, c * LANES : (c + 1) * LANES]


def beside_columns(x):
    cols = x.shape[1]
    col = lax.broadcasted_iota(jnp.int32, x.shape, 1)
    left = jnp.where(col == 0, 0.0, pltpu.roll(x, 1, axis=1))
    right = jnp.where(col == cols - 1, 0.0, pltpu.roll(x, cols - 1, axis=1))
    return left + right


def degree_of(row, shape, total_rows):
    col = lax.broadcasted_iota(jnp.int32, shape, 1)
    edge = (
        (row == 0).astype(jnp.float32)
        + (row == total_rows - 1).astype(jnp.float32)
        + (col == 0).astype(jnp.float32)
        + (col == shape[1] - 1).astype(jnp.float32)
    )
    return 4.0 - edge


def couple(n, v):
    return (
        n[0] * v[0] + n[1] * v[1] + n[2] * v[2],
        n[1] * v[0] + n[3] * v[1] + n[4] * v[2],
        n[2] * v[0] + n[4] * v[1] + n[5] * v[2],
    )


def residual_kernel(me_ref, prior_ref, *refs, total_rows):
    obs_count, rows_here, cols = prior_ref.shape
    *parts, out_ref, msg_ref, first_ref, sums_ref = refs
    block = rows_here * ENTRIES
    tiles = cols // LANES
    at = 0
    for kept_ref, got_ref in zip(parts[0::2], parts[1::2]):
        here = kept_ref.shape[2] // LANES
        came = unpack(lambda place: got_ref[0, place], block // 16, here)
        for c in range(here):
            sums_ref[at] = kept_ref[0, :, c * LANES : (c + 1) * LANES] + came[c]
            at += 1
    shape = (rows_here, cols)
    row = me_ref[0] * rows_here + lax.broadcasted_iota(jnp.int32, shape, 0)
    degree = degree_of(row, shape, total_rows)
    normal = [take(sums_ref, obs_count + k, rows_here, ENTRIES) for k in range(6)]
    for b in range(obs_count // 3):
        fields = [prior_ref[3 * b + i] for i in range(3)]
        coupled = couple(normal, fields)
        for i in range(3):
            field = fields[i]
            beside = beside_columns(field)
            if rows_here > 1:
                zero = jnp.zeros((1, cols), jnp.float32)
                beside = beside + jnp.concatenate([zero, field[:-1]], axis=0) + jnp.concatenate([field[1:], zero], axis=0)
            entry = 3 * b + i
            observed = take(sums_ref, entry, rows_here, ENTRIES)
            put(sums_ref, entry, rows_here, ENTRIES, observed - coupled[i] - SMOOTH_PULL * (degree * field - beside))
    for c in range(tiles):
        out_ref[:, c * LANES : (c + 1) * LANES] = sums_ref[c]
    scales, numbers = pack([sums_ref[c] for c in range(tiles)], msg_ref, 0)
    first_ref[0] = scales
    for c in range(tiles):
        first_ref[1 + c] = numbers[c][0:16].astype(jnp.int16)
    left = jnp.concatenate([number[16:obs_count] for number in numbers], axis=0)
    spare = (first_ref.shape[0] - 1 - tiles) * 16 - left.shape[0]
    if spare:
        left = jnp.concatenate([left, jnp.zeros((spare, LANES), jnp.int32)], axis=0)
    for t in range(left.shape[0] // 16):
        first_ref[1 + tiles + t] = left[16 * t : 16 * t + 16].astype(jnp.int16)


def krylov_kernel(me_ref, own_ref, mate_ref, across_ref, zero_ref, one_ref, two_ref, gram_ref, window_ref, *, total_rows, rows_here):
    cols = own_ref.shape[1]
    obs_count = ENTRIES - 6
    tiles = cols // LANES
    row_tiles = own_ref.shape[0] // 16

    def lay(place, part, r):
        at = pl.ds(place, ENTRIES, stride=8)
        for c in range(tiles):
            window_ref[c, at, :] = part[c][r * ENTRIES : (r + 1) * ENTRIES]

    own = [own_ref[:, c * LANES : (c + 1) * LANES] for c in range(tiles)]
    mate = unpack(lambda place: mate_ref[place], row_tiles, tiles)
    across = unpack(lambda place: across_ref[place], row_tiles, tiles)
    odd = me_ref[0] % 2
    for r in range(2):
        lay(2 + r, own, r)
        lay(4 * (1 - odd) + r, mate, r)
        lay(4 * odd + r, across, r)
    for empty in (6, 7):
        put(window_ref, empty, ENTRIES, 8, jnp.zeros((ENTRIES, cols), jnp.float32))
    window = lambda entry: jnp.concatenate([window_ref[c, entry * 8 : entry * 8 + 8, :] for c in range(cols // LANES)], axis=1)
    shape = (8, cols)
    place = lax.broadcasted_iota(jnp.int32, shape, 0)
    row = me_ref[0] * rows_here + place - 2
    inside = ((row >= 0) & (row < total_rows)).astype(jnp.float32) * GAIN
    own_rows = (place == 2) | (place == 3)
    diag = inside * (PRIOR_PULL - SHIFT + SMOOTH_PULL * degree_of(row, shape, total_rows))
    pull = inside * SMOOTH_PULL
    normal = [window(obs_count + k) * inside for k in range(6)]
    acc = [jnp.zeros((8, LANES), jnp.float32) for _ in range(6)]

    def apply(v, last=False):
        coupled = couple(normal, v)
        out = []
        for i in range(3):
            x = v[i]
            above = pltpu.roll(x, 7, axis=0)
            beside = beside_columns(x) + (2.0 * above if last else above + pltpu.roll(x, 1, axis=0))
            out.append(coupled[i] + diag * x - pull * beside)
        return out

    def fold(x):
        total = x[:, 0:LANES]
        for c in range(LANES, cols, LANES):
            total = total + x[:, c : c + LANES]
        return total

    for b in range(obs_count // 3):
        zero = [window(3 * b + i) for i in range(3)]
        one = apply(zero)
        two = apply(one)
        three = apply(two, last=True)
        for i in range(3):
            zero_ref[3 * b + i] = zero[i][2:4]
            one_ref[3 * b + i] = one[i][2:4]
            two_ref[3 * b + i] = two[i][2:4]
            v = [zero[i], one[i], two[i], three[i]]
            for k in range(6):
                acc[k] = acc[k] + fold(v[k // 2] * v[(k + 1) // 2])
    own_tile = own_rows[:, 0:LANES]
    tile_row = lax.broadcasted_iota(jnp.int32, (8, LANES), 0)
    gram = jnp.zeros((8, LANES), jnp.float32)
    for k in range(6):
        moment = jnp.sum(jnp.where(own_tile, acc[k], 0.0))
        gram = jnp.where(tile_row == k, moment, gram)
    gram_ref[...] = gram


def far_kernel(gram_ref, two_ref, far_ref, out_ref):
    obs_count, _, cols = two_ref.shape
    tiles = cols // LANES
    rest = obs_count - 16
    factors = factors_of(far_ref[0], 2)
    left = jnp.concatenate([as_float(far_ref[t]) for t in range(1 + tiles, far_ref.shape[0])], axis=0)
    total = jnp.zeros((obs_count, LANES), jnp.float32)
    for c in range(tiles):
        far = jnp.concatenate([as_float(far_ref[1 + c]) * factors[0], left[rest * c : rest * (c + 1)] * factors[1][0:rest]], axis=0)
        mine = jnp.concatenate([two_ref[e, 1:2, c * LANES : (c + 1) * LANES] for e in range(obs_count)], axis=0)
        total = total + far * mine
    part = (-2.0 * (GAIN * SMOOTH_PULL) ** 3) * jnp.sum(total)
    row = lax.broadcasted_iota(jnp.int32, (8, LANES), 0)
    out_ref[...] = gram_ref[...] + jnp.where(row == 5, part, 0.0)


def combine_kernel(*refs):
    *gram_refs, prior_ref, zero_ref, one_ref, two_ref, out_ref = refs
    gram = gram_refs[0][...]
    for ref in gram_refs[1:]:
        gram = gram + ref[...]
    m = [gram[k : k + 1, :] for k in range(6)]
    h = {(i, j): m[i + j + 1] * (1.0 / GAIN) + SHIFT * m[i + j] for i in range(3) for j in range(i, 3)}
    l10 = h[0, 1] / h[0, 0]
    l20 = h[0, 2] / h[0, 0]
    d1 = h[1, 1] - l10 * h[0, 1]
    t = h[1, 2] - l20 * h[0, 1]
    ok1 = d1 > 1e-6 * h[1, 1]
    inv1 = jnp.where(ok1, 1.0 / jnp.where(ok1, d1, 1.0), 0.0)
    l21 = t * inv1
    d2 = h[2, 2] - l20 * h[0, 2] - l21 * t
    ok2 = ok1 & (d2 > 1e-6 * h[2, 2])
    inv2 = jnp.where(ok2, 1.0 / jnp.where(ok2, d2, 1.0), 0.0)
    z1 = m[1] - l10 * m[0]
    z2 = m[2] - l20 * m[0] - l21 * z1
    y2 = z2 * inv2
    y1 = z1 * inv1 - l21 * y2
    y0 = m[0] / h[0, 0] - l10 * y1 - l20 * y2
    cols = prior_ref.shape[2]
    for c in range(0, cols, LANES):
        lanes = slice(c, c + LANES)
        out_ref[:, :, lanes] = (
            prior_ref[:, :, lanes] + y0[None] * zero_ref[:, :, lanes] + y1[None] * one_ref[:, :, lanes] + y2[None] * two_ref[:, :, lanes]
        )


def on_device(reflect, clear_conf, sun_view, sensor_id, band_gain, sensor_weight, prior):
    rows_here, obs_count, cols = prior.shape
    prior = jnp.transpose(prior, (1, 0, 2))
    count = lax.axis_size("rows")
    total_rows = rows_here * count
    block = rows_here * ENTRIES
    tiles = cols // LANES
    me = lax.axis_index("rows").astype(jnp.int32).reshape(1)
    vmem = pl.BlockSpec(memory_space=pltpu.VMEM)
    smem = pl.BlockSpec(memory_space=pltpu.SMEM)
    params = pltpu.CompilerParams(vmem_limit_bytes=24 * 2**20)
    f32 = lambda *shape: jax.ShapeDtypeStruct(shape, jnp.float32)
    packed = lambda *shape: jax.ShapeDtypeStruct(shape + (16, LANES), jnp.int16)

    scale = 0.01 / (reflect.shape[0] * count)
    index = me
    parts = []
    for chunk in range(CHUNKS):
        kept, sent = partial_sums(
            index, reflect, clear_conf, sun_view, sensor_id, band_gain, sensor_weight, prior, scale, chunk
        )
        index, _ = lax.optimization_barrier((me, sent))
        parts.append((kept, sent))
    flip = lambda x, mask: lax.ppermute(x, "rows", [(i, i ^ mask) for i in range(count)])
    swap = lambda x, bit: flip(x, 1 << bit)
    parts = [(kept, swap(sent, 0)) for kept, sent in parts]
    bits = list(range(1, count.bit_length() - 1))
    for step in range(len(bits)):
        for chunk in range(CHUNKS):
            turned = chunk % 2 == 1 and len(bits) >= 2 and step < 2
            bit, place = (bits[1 - step], 1 - step) if turned else (bits[step], 0)
            kept, sent = add_split(me // 2**bit % 2, place, *parts[chunk])
            parts[chunk] = (kept, swap(sent, bit))
    parts = [x for part in parts for x in part]

    own, msg, first = pl.pallas_call(
        functools.partial(residual_kernel, total_rows=total_rows),
        in_specs=[smem] + [vmem] * (1 + len(parts)),
        out_specs=[vmem, vmem, vmem],
        out_shape=[f32(block, cols), packed(1, 1 + block // 16 * tiles), packed(1 + tiles + -(-(obs_count - 16) * tiles // 16))],
        scratch_shapes=[pltpu.VMEM((tiles, block, LANES), jnp.float32)],
        compiler_params=params,
        name="residual",
    )(me, prior, *parts)

    msg = msg[0]
    mate = swap(msg, 0)
    border = [(i, i + 1) for i in range(1, count - 1, 2)]
    across = lax.ppermute(msg, "rows", border + [(target, source) for source, target in border])
    far = lax.ppermute(first, "rows", [(i + 2, i) for i in range(count - 2)])
    zero, one, two, gram = pl.pallas_call(
        functools.partial(krylov_kernel, total_rows=total_rows, rows_here=rows_here),
        in_specs=[smem, vmem, vmem, vmem],
        out_specs=[vmem] * 4,
        out_shape=[f32(obs_count, rows_here, cols)] * 3 + [f32(8, LANES)],
        scratch_shapes=[pltpu.VMEM((tiles, ENTRIES * 8, LANES), jnp.float32)],
        compiler_params=params,
        name="krylov",
    )(me, own, mate, across)

    grams = [
        pl.pallas_call(
            far_kernel, in_specs=[vmem] * 3, out_specs=vmem, out_shape=f32(8, LANES), compiler_params=params, name="far"
        )(gram, two, far)
    ]
    for bit in range(0, count.bit_length() - 1, 2):
        masks = [mask << bit for mask in (1, 2, 3) if mask << bit < count]
        gram = sum(grams[1:], grams[0])
        grams = [gram] + [flip(gram, mask) for mask in masks]
    out = pl.pallas_call(
        combine_kernel,
        in_specs=[vmem] * (len(grams) + 4),
        out_specs=vmem,
        out_shape=f32(obs_count, rows_here, cols),
        compiler_params=params,
        name="combine",
    )(*grams, prior, zero, one, two)
    return jnp.transpose(out, (1, 0, 2))


def solution(mesh):
    return jax.shard_map(
        on_device,
        mesh=mesh,
        in_specs=(
            P("rows", None, None, "tiles"),
            P("rows", None, "tiles"),
            P("rows", None, None, "tiles"),
            P(),
            P(),
            P(),
            P("rows", None, "tiles"),
        ),
        out_specs=P("rows", None, "tiles"),
        check_vma=False,
    )
```

```python
import functools
import math

import jax
import jax.numpy as jnp
from jax import lax
from jax.experimental import pallas as pl
from jax.experimental.pallas import tpu as pltpu
from jax.sharding import PartitionSpec as P

TO_RADIAN = math.pi / 18000.0
PRIOR_PULL = 0.1
SMOOTH_PULL = 0.5
SHIFT = 3.0
GAIN = 0.4
ENTRIES = 24
LANES = 128
QUANT = 32000.0
GROUP = LANES // 4
SHARES = (3, 2, 3)


R_POLY = (0.9428089773, 0.04714460664, 0.007527079489, 0.001965302741, 9.052799897e-05, 0.0004621408027)
S_POLY = (0.6002109608, -0.09003726006, -0.007977343822, -0.001801806492, 3.702625389e-06, -0.0003981650976)
SIN_25 = (0.9999999567, -0.1666626093, 0.008276695349)
COS_25 = (0.9999999997, -0.4999999562, 0.04166553086, -0.001379415437)
SIN_15 = (0.999999998, -0.1666661418, 0.008312938059)
COS_15 = (0.9999999858, -0.4999963087, 0.04152366947)
SIN_90 = (0.9999999947, -0.1666665666, 0.008333024663, -0.00019807389, 2.601844464e-06)


def horner(coefs, x):
    acc = coefs[-1] * x + coefs[-2]
    for coef in coefs[-3::-1]:
        acc = acc * x + coef
    return acc


def of_degrees(coefs, x, x2, factor, odd):
    scaled = [factor * coef * TO_RADIAN ** (2 * k + odd) for k, coef in enumerate(coefs)]
    value = horner(scaled, x2)
    return value * x if odd else value


def ross_li(sun, view, azim):
    x = (sun - 4500).astype(jnp.float32)
    x2 = x * x
    half = math.sqrt(0.5)
    sin_x, cos_x = of_degrees(SIN_25, x, x2, half, 1), of_degrees(COS_25, x, x2, half, 0)
    cos_sun, sin_sun = cos_x - sin_x, cos_x + sin_x
    v = view.astype(jnp.float32)
    v2 = v * v
    sin_view, cos_view = of_degrees(SIN_15, v, v2, 1.0, 1), of_degrees(COS_15, v, v2, 1.0, 0)
    a = (9000 - azim).astype(jnp.float32)
    cos_azim = of_degrees(SIN_90, a, a * a, 1.0, 1)
    prod = cos_sun * cos_view
    cos_phase = prod + sin_sun * sin_view * cos_azim
    total = cos_sun + cos_view
    recip = pl.reciprocal(total * prod, approx=False)
    inv_total = recip * prod
    sec_prod = recip * total
    u = 1.0 - cos_phase
    u_up = 1.0 + cos_phase
    bent = u * (u * lax.rsqrt(u)) * horner(R_POLY, u)
    volume = (bent + (0.5 * math.pi) * cos_phase) * inv_total - 0.25 * math.pi
    sin2 = u * u_up
    sin_phase = sin2 * lax.rsqrt(sin2)
    w = jnp.maximum(1.0 - (2.0 * inv_total) * sin_phase, 1e-30)
    overlap = w * (w * lax.rsqrt(w)) * horner(S_POLY, w)
    geometric = sec_prod * (total * (overlap - 1.0) + 0.5 * u_up)
    return volume, geometric


def lane_group(shape):
    return lax.broadcasted_iota(jnp.int32, shape, len(shape) - 1) // GROUP


def pack(tiles, msg_ref, block):
    rows = tiles[0].shape[0]
    top = jnp.abs(tiles[0])
    for tile in tiles[1:]:
        top = jnp.maximum(top, jnp.abs(tile))
    for shift in (LANES // 2, LANES // 4):
        top = jnp.maximum(top, pltpu.roll(top, shift, axis=1))
    level = jnp.ceil(8.0 * jnp.log2(jnp.maximum(top, 1e-30)))
    factor = QUANT * jnp.exp2(-0.125 * level)
    group = lane_group((16, LANES))
    scales = level[0:16]
    for t in range(1, rows // 16):
        scales = jnp.where(group == t, level[16 * t : 16 * t + 16], scales)
    scales = scales.astype(jnp.int32).astype(jnp.int16)
    msg_ref[block, 0] = scales
    numbers = [jnp.round(tile * factor).astype(jnp.int32) for tile in tiles]
    for c, number in enumerate(numbers):
        coded = number.astype(jnp.int16)
        for t in range(rows // 16):
            msg_ref[block, 1 + t * len(tiles) + c] = coded[16 * t : 16 * t + 16]
    return scales, numbers


def as_float(x):
    return x.astype(jnp.int32).astype(jnp.float32)


def factors_of(scales, row_tiles):
    scales = as_float(scales)
    group = lane_group((16, LANES))
    factors = []
    for t in range(row_tiles):
        level = jnp.where(group == t, scales, 0.0)
        for shift in (LANES // 2, LANES // 4):
            level = level + pltpu.roll(level, shift, axis=1)
        factors.append(jnp.exp2(0.125 * level) * (1.0 / QUANT))
    return factors


def unpack(read, row_tiles, col_tiles):
    factors = factors_of(read(0), row_tiles)
    return [
        jnp.concatenate([as_float(read(1 + t * col_tiles + c)) * factors[t] for t in range(row_tiles)], axis=0) for c in range(col_tiles)
    ]


def sums_kernel(
    me_ref,
    ids_ref,
    gain_ref,
    weight_ref,
    reflect_hbm,
    conf_hbm,
    sun_hbm,
    prior_ref,
    keep_ref,
    msg_ref,
    sums_ref,
    kernels_ref,
    reflect_ref,
    conf_ref,
    sun_ref,
    sems,
    *,
    scale,
    rows_here,
    first_col,
):
    steps, dates, bands, tile_rows, _ = reflect_ref.shape
    lane_tiles = sums_ref.shape[0]
    me = me_ref[0]
    block = rows_here * ENTRIES
    obs_count = 3 * bands

    def copies(step):
        rows = pl.ds(pl.multiple_of(step // lane_tiles * tile_rows, tile_rows), tile_rows)
        cols = pl.ds(pl.multiple_of(first_col + step % lane_tiles * LANES, LANES), LANES)
        return (
            pltpu.make_async_copy(sun_hbm.at[:, :, rows, cols], sun_ref.at[step], sems.at[step, 0]),
            pltpu.make_async_copy(conf_hbm.at[:, rows, cols], conf_ref.at[step], sems.at[step, 1]),
            pltpu.make_async_copy(reflect_hbm.at[:, :, rows, cols], reflect_ref.at[step], sems.at[step, 2]),
        )

    def start(step, carry):
        for copy in copies(step):
            copy.start()
        return carry

    lax.fori_loop(0, steps, start, 0)

    def lane_tile(index, row_tile):
        step = row_tile * lane_tiles + index
        for copy in copies(step):
            copy.wait()
        sensors = [ids_ref[me * dates + d] for d in range(dates)]

        def store(top, entry, total):
            sums_ref[index, pl.ds(top * ENTRIES + entry, 8, stride=ENTRIES), :] = total

        def plus(total, term):
            return term if total is None else total + term

        for top in range(0, tile_rows, 8):
            here = slice(top, top + 8)
            normal = [None] * 6
            for d in range(dates):
                volume, geometric = ross_li(*[sun_ref[step, d, angle, here, :] for angle in range(3)])
                weight = conf_ref[step, d, here, :].astype(jnp.float32) * (weight_ref[sensors[d]] * scale)
                weighted_vol = weight * volume
                weighted_geo = weight * geometric
                for i, value in enumerate((weight, weighted_vol, weighted_geo)):
                    kernels_ref[d, i, here, :] = value
                terms = (weight, weighted_vol, weighted_geo, weighted_vol * volume, weighted_vol * geometric, weighted_geo * geometric)
                normal = [plus(total, term) for total, term in zip(normal, terms)]
            for k in range(6):
                store(top, obs_count + k, normal[k])
        for b in range(bands):
            observed = [None] * 3
            for d in range(dates):
                signal = reflect_ref[step, d, b].astype(jnp.float32) * gain_ref[sensors[d], b]
                observed = [plus(total, kernels_ref[d, i] * signal) for i, total in enumerate(observed)]
            for i in range(3):
                for top in range(0, tile_rows, 8):
                    store(top, 3 * b + i, observed[i][top : top + 8])
        return row_tile

    def row_tile_sums(row_tile, carry):
        lax.fori_loop(0, lane_tiles, lane_tile, row_tile)
        tiles = range(lane_tiles)
        first_row = row_tile * tile_rows
        for row, source in ((me * rows_here - 1 - first_row, 0), ((me + 1) * rows_here - first_row, rows_here - 1)):

            @pl.when((row >= 0) & (row < tile_rows))
            def _():
                for c in tiles:
                    lanes = slice(first_col + c * LANES, first_col + (c + 1) * LANES)
                    at = pl.ds(pl.multiple_of(row * ENTRIES, 8), obs_count)
                    part = jnp.concatenate([prior_ref[e, source : source + 1, lanes] for e in range(obs_count)], axis=0)
                    sums_ref[c, at, :] = sums_ref[c, at, :] + SMOOTH_PULL * part

        bit = me % 2
        per_tile = tile_rows // rows_here // 2
        for j in range(per_tile):
            own = pl.ds(pl.multiple_of((2 * j + bit) * block, 8), block)
            other = pl.ds(pl.multiple_of((2 * j + 1 - bit) * block, 8), block)
            for c in tiles:
                keep_ref[row_tile * per_tile + j, :, c * LANES : (c + 1) * LANES] = sums_ref[c, own, :]
            pack([sums_ref[c, other, :] for c in tiles], msg_ref, row_tile * per_tile + j)
        return carry

    lax.fori_loop(0, steps // lane_tiles, row_tile_sums, 0)


def partial_sums(me, reflect, clear_conf, sun_view, sensor_id, band_gain, sensor_weight, prior, scale, first_col, cols):
    dates, bands, rows, _ = reflect.shape
    rows_here = prior.shape[1]
    count = rows // rows_here
    tile_rows = 16
    block = rows_here * ENTRIES
    lane_tiles = cols // LANES
    steps = rows // tile_rows * lane_tiles
    smem = pl.BlockSpec(memory_space=pltpu.SMEM)
    vmem = pl.BlockSpec(memory_space=pltpu.VMEM)
    hbm = pl.BlockSpec(memory_space=pl.ANY)
    return pl.pallas_call(
        functools.partial(sums_kernel, scale=scale, rows_here=rows_here, first_col=first_col),
        in_specs=[smem] * 4 + [hbm] * 3 + [vmem],
        out_specs=[vmem, vmem],
        out_shape=[
            jax.ShapeDtypeStruct((count // 2, block, cols), jnp.float32),
            jax.ShapeDtypeStruct((count // 2, 1 + block // 16 * lane_tiles, 16, LANES), jnp.int16),
        ],
        scratch_shapes=[
            pltpu.VMEM((lane_tiles, tile_rows * ENTRIES, LANES), jnp.float32),
            pltpu.VMEM((dates, 3, tile_rows, LANES), jnp.float32),
            pltpu.VMEM((steps, dates, bands, tile_rows, LANES), reflect.dtype),
            pltpu.VMEM((steps, dates, tile_rows, LANES), jnp.int32),
            pltpu.VMEM((steps, dates, 3, tile_rows, LANES), jnp.int32),
            pltpu.SemaphoreType.DMA((steps, 3)),
        ],
        compiler_params=pltpu.CompilerParams(vmem_limit_bytes=(62 if first_col == 0 else 52) * 2**20),
        name="partial_sums",
    )(me, sensor_id, band_gain, sensor_weight, reflect, clear_conf, sun_view, prior)


def add_split_kernel(bit_ref, *refs, place):
    *parts, keep_ref, msg_ref = refs
    count, block, _ = keep_ref.shape
    bit = bit_ref[0]

    def total(j):
        tiles = []
        for kept_ref, got_ref in zip(parts[0::2], parts[1::2]):
            here = kept_ref.shape[2] // LANES
            came = unpack(lambda at: got_ref[j, at], block // 16, here)
            tiles += [kept_ref[j, :, c * LANES : (c + 1) * LANES] + came[c] for c in range(here)]
        return tiles

    for q in range(count):
        low = q % 2**place
        first = (q - low) * 2 + low
        pack(total(first + (1 - bit) * 2**place), msg_ref, q)
        for c, tile in enumerate(total(first + bit * 2**place)):
            keep_ref[q, :, c * LANES : (c + 1) * LANES] = tile


def add_split(bit, place, *parts):
    count, block, _ = parts[0].shape
    cols = sum(kept.shape[2] for kept in parts[0::2])
    vmem = pl.BlockSpec(memory_space=pltpu.VMEM)
    return pl.pallas_call(
        functools.partial(add_split_kernel, place=place),
        in_specs=[pl.BlockSpec(memory_space=pltpu.SMEM)] + [vmem] * len(parts),
        out_specs=[vmem, vmem],
        out_shape=[
            jax.ShapeDtypeStruct((count // 2, block, cols), jnp.float32),
            jax.ShapeDtypeStruct((count // 2, 1 + block // 16 * (cols // LANES), 16, LANES), jnp.int16),
        ],
        compiler_params=pltpu.CompilerParams(vmem_limit_bytes=24 * 2**20),
        name="add_split",
    )(bit, *parts)


def take(ref, start, size, stride):
    at = pl.ds(start, size, stride=stride)
    return jnp.concatenate([ref[c, at, :] for c in range(ref.shape[0])], axis=1)


def put(ref, start, size, stride, value):
    at = pl.ds(start, size, stride=stride)
    for c in range(ref.shape[0]):
        ref[c, at, :] = value[:, c * LANES : (c + 1) * LANES]


def beside_columns(x):
    cols = x.shape[1]
    col = lax.broadcasted_iota(jnp.int32, x.shape, 1)
    left = jnp.where(col == 0, 0.0, pltpu.roll(x, 1, axis=1))
    right = jnp.where(col == cols - 1, 0.0, pltpu.roll(x, cols - 1, axis=1))
    return left + right


def degree_of(row, shape, total_rows):
    col = lax.broadcasted_iota(jnp.int32, shape, 1)
    edge = (
        (row == 0).astype(jnp.float32)
        + (row == total_rows - 1).astype(jnp.float32)
        + (col == 0).astype(jnp.float32)
        + (col == shape[1] - 1).astype(jnp.float32)
    )
    return 4.0 - edge


def couple(n, v):
    return (
        n[0] * v[0] + n[1] * v[1] + n[2] * v[2],
        n[1] * v[0] + n[3] * v[1] + n[4] * v[2],
        n[2] * v[0] + n[4] * v[1] + n[5] * v[2],
    )


def residual_kernel(me_ref, prior_ref, *refs, total_rows):
    obs_count, rows_here, cols = prior_ref.shape
    *parts, out_ref, msg_ref, first_ref, sums_ref = refs
    block = rows_here * ENTRIES
    tiles = cols // LANES
    at = 0
    for kept_ref, got_ref in zip(parts[0::2], parts[1::2]):
        here = kept_ref.shape[2] // LANES
        came = unpack(lambda place: got_ref[0, place], block // 16, here)
        for c in range(here):
            sums_ref[at] = kept_ref[0, :, c * LANES : (c + 1) * LANES] + came[c]
            at += 1
    shape = (rows_here, cols)
    row = me_ref[0] * rows_here + lax.broadcasted_iota(jnp.int32, shape, 0)
    degree = degree_of(row, shape, total_rows)
    normal = [take(sums_ref, obs_count + k, rows_here, ENTRIES) for k in range(6)]
    for b in range(obs_count // 3):
        fields = [prior_ref[3 * b + i] for i in range(3)]
        coupled = couple(normal, fields)
        for i in range(3):
            field = fields[i]
            beside = beside_columns(field)
            if rows_here > 1:
                zero = jnp.zeros((1, cols), jnp.float32)
                beside = beside + jnp.concatenate([zero, field[:-1]], axis=0) + jnp.concatenate([field[1:], zero], axis=0)
            entry = 3 * b + i
            observed = take(sums_ref, entry, rows_here, ENTRIES)
            put(sums_ref, entry, rows_here, ENTRIES, observed - coupled[i] - SMOOTH_PULL * (degree * field - beside))
    for c in range(tiles):
        out_ref[:, c * LANES : (c + 1) * LANES] = sums_ref[c]
    scales, numbers = pack([sums_ref[c] for c in range(tiles)], msg_ref, 0)
    first_ref[0] = scales
    for c in range(tiles):
        first_ref[1 + c] = numbers[c][0:16].astype(jnp.int16)
    left = jnp.concatenate([number[16:obs_count] for number in numbers], axis=0)
    spare = (first_ref.shape[0] - 1 - tiles) * 16 - left.shape[0]
    if spare:
        left = jnp.concatenate([left, jnp.zeros((spare, LANES), jnp.int32)], axis=0)
    for t in range(left.shape[0] // 16):
        first_ref[1 + tiles + t] = left[16 * t : 16 * t + 16].astype(jnp.int16)


def krylov_kernel(me_ref, own_ref, mate_ref, across_ref, zero_ref, one_ref, two_ref, gram_ref, window_ref, *, total_rows, rows_here):
    cols = own_ref.shape[1]
    obs_count = ENTRIES - 6
    tiles = cols // LANES
    row_tiles = own_ref.shape[0] // 16

    def lay(place, part, r):
        at = pl.ds(place, ENTRIES, stride=8)
        for c in range(tiles):
            window_ref[c, at, :] = part[c][r * ENTRIES : (r + 1) * ENTRIES]

    own = [own_ref[:, c * LANES : (c + 1) * LANES] for c in range(tiles)]
    mate = unpack(lambda place: mate_ref[place], row_tiles, tiles)
    across = unpack(lambda place: across_ref[place], row_tiles, tiles)
    odd = me_ref[0] % 2
    for r in range(2):
        lay(2 + r, own, r)
        lay(4 * (1 - odd) + r, mate, r)
        lay(4 * odd + r, across, r)
    for empty in (6, 7):
        put(window_ref, empty, ENTRIES, 8, jnp.zeros((ENTRIES, cols), jnp.float32))
    window = lambda entry: jnp.concatenate([window_ref[c, entry * 8 : entry * 8 + 8, :] for c in range(cols // LANES)], axis=1)
    shape = (8, cols)
    place = lax.broadcasted_iota(jnp.int32, shape, 0)
    row = me_ref[0] * rows_here + place - 2
    inside = ((row >= 0) & (row < total_rows)).astype(jnp.float32) * GAIN
    own_rows = (place == 2) | (place == 3)
    diag = inside * (PRIOR_PULL - SHIFT + SMOOTH_PULL * degree_of(row, shape, total_rows))
    pull = inside * SMOOTH_PULL
    normal = [window(obs_count + k) * inside for k in range(6)]
    acc = [jnp.zeros((8, LANES), jnp.float32) for _ in range(6)]

    def apply(v, last=False):
        coupled = couple(normal, v)
        out = []
        for i in range(3):
            x = v[i]
            above = pltpu.roll(x, 7, axis=0)
            beside = beside_columns(x) + (2.0 * above if last else above + pltpu.roll(x, 1, axis=0))
            out.append(coupled[i] + diag * x - pull * beside)
        return out

    def fold(x):
        total = x[:, 0:LANES]
        for c in range(LANES, cols, LANES):
            total = total + x[:, c : c + LANES]
        return total

    for b in range(obs_count // 3):
        zero = [window(3 * b + i) for i in range(3)]
        one = apply(zero)
        two = apply(one)
        three = apply(two, last=True)
        for i in range(3):
            zero_ref[3 * b + i] = zero[i][2:4]
            one_ref[3 * b + i] = one[i][2:4]
            two_ref[3 * b + i] = two[i][2:4]
            v = [zero[i], one[i], two[i], three[i]]
            for k in range(6):
                acc[k] = acc[k] + fold(v[k // 2] * v[(k + 1) // 2])
    own_tile = own_rows[:, 0:LANES]
    tile_row = lax.broadcasted_iota(jnp.int32, (8, LANES), 0)
    gram = jnp.zeros((8, LANES), jnp.float32)
    for k in range(6):
        moment = jnp.sum(jnp.where(own_tile, acc[k], 0.0))
        gram = jnp.where(tile_row == k, moment, gram)
    gram_ref[...] = gram


def far_kernel(gram_ref, two_ref, far_ref, out_ref):
    obs_count, _, cols = two_ref.shape
    tiles = cols // LANES
    rest = obs_count - 16
    factors = factors_of(far_ref[0], 2)
    left = jnp.concatenate([as_float(far_ref[t]) for t in range(1 + tiles, far_ref.shape[0])], axis=0)
    total = jnp.zeros((obs_count, LANES), jnp.float32)
    for c in range(tiles):
        far = jnp.concatenate([as_float(far_ref[1 + c]) * factors[0], left[rest * c : rest * (c + 1)] * factors[1][0:rest]], axis=0)
        mine = jnp.concatenate([two_ref[e, 1:2, c * LANES : (c + 1) * LANES] for e in range(obs_count)], axis=0)
        total = total + far * mine
    part = (-2.0 * (GAIN * SMOOTH_PULL) ** 3) * jnp.sum(total)
    row = lax.broadcasted_iota(jnp.int32, (8, LANES), 0)
    out_ref[...] = gram_ref[...] + jnp.where(row == 5, part, 0.0)


def combine_kernel(*refs):
    *gram_refs, prior_ref, zero_ref, one_ref, two_ref, out_ref = refs
    gram = gram_refs[0][...]
    for ref in gram_refs[1:]:
        gram = gram + ref[...]
    m = [gram[k : k + 1, :] for k in range(6)]
    h = {(i, j): m[i + j + 1] * (1.0 / GAIN) + SHIFT * m[i + j] for i in range(3) for j in range(i, 3)}
    l10 = h[0, 1] / h[0, 0]
    l20 = h[0, 2] / h[0, 0]
    d1 = h[1, 1] - l10 * h[0, 1]
    t = h[1, 2] - l20 * h[0, 1]
    ok1 = d1 > 1e-6 * h[1, 1]
    inv1 = jnp.where(ok1, 1.0 / jnp.where(ok1, d1, 1.0), 0.0)
    l21 = t * inv1
    d2 = h[2, 2] - l20 * h[0, 2] - l21 * t
    ok2 = ok1 & (d2 > 1e-6 * h[2, 2])
    inv2 = jnp.where(ok2, 1.0 / jnp.where(ok2, d2, 1.0), 0.0)
    z1 = m[1] - l10 * m[0]
    z2 = m[2] - l20 * m[0] - l21 * z1
    y2 = z2 * inv2
    y1 = z1 * inv1 - l21 * y2
    y0 = m[0] / h[0, 0] - l10 * y1 - l20 * y2
    cols = prior_ref.shape[2]
    for c in range(0, cols, LANES):
        lanes = slice(c, c + LANES)
        out_ref[:, :, lanes] = (
            prior_ref[:, :, lanes] + y0[None] * zero_ref[:, :, lanes] + y1[None] * one_ref[:, :, lanes] + y2[None] * two_ref[:, :, lanes]
        )


def on_device(reflect, clear_conf, sun_view, sensor_id, band_gain, sensor_weight, prior):
    rows_here, obs_count, cols = prior.shape
    prior = jnp.transpose(prior, (1, 0, 2))
    count = lax.axis_size("rows")
    total_rows = rows_here * count
    block = rows_here * ENTRIES
    tiles = cols // LANES
    me = lax.axis_index("rows").astype(jnp.int32).reshape(1)
    vmem = pl.BlockSpec(memory_space=pltpu.VMEM)
    smem = pl.BlockSpec(memory_space=pltpu.SMEM)
    params = pltpu.CompilerParams(vmem_limit_bytes=24 * 2**20)
    f32 = lambda *shape: jax.ShapeDtypeStruct(shape, jnp.float32)
    packed = lambda *shape: jax.ShapeDtypeStruct(shape + (16, LANES), jnp.int16)

    scale = 0.01 / (reflect.shape[0] * count)
    flip = lambda x, mask: lax.ppermute(x, "rows", [(i, i ^ mask) for i in range(count)])
    swap = lambda x, bit: flip(x, 1 << bit)
    bits = list(range(1, count.bit_length() - 1))

    def halve(part, chunk, step):
        turned = chunk >= 1 and len(bits) >= 2 and step < 2
        bit, place = (bits[1 - step], 1 - step) if turned else (bits[step], 0)
        kept, sent = add_split(me // 2**bit % 2, place, *part)
        return kept, sent, bit

    parts = []
    after = me
    for chunk, share in enumerate(SHARES):
        width = cols // sum(SHARES) * share
        first_col = cols // sum(SHARES) * sum(SHARES[:chunk])
        kept, sent = partial_sums(
            after, reflect, clear_conf, sun_view, sensor_id, band_gain, sensor_weight, prior, scale, first_col, width
        )
        if chunk == 2:
            sent, parts[0], parts[1] = lax.optimization_barrier((sent, parts[0], parts[1]))
        parts.append((kept, swap(sent, 0)))
        if chunk == 1:
            parts[0], _ = lax.optimization_barrier((parts[0], sent))
            kept, sent, bit = halve(parts[0], 0, 0)
            parts[0] = (kept, swap(sent, bit))
        after, _ = lax.optimization_barrier((me, sent))
    for step in range(len(bits)):
        for chunk in range(len(parts)):
            if step or chunk:
                if step == 0 and chunk == 2:
                    parts[2], _ = lax.optimization_barrier((parts[2], sent))
                kept, sent, bit = halve(parts[chunk], chunk, step)
                parts[chunk] = (kept, swap(sent, bit))
    parts = [x for part in parts for x in part]

    own, msg, first = pl.pallas_call(
        functools.partial(residual_kernel, total_rows=total_rows),
        in_specs=[smem] + [vmem] * (1 + len(parts)),
        out_specs=[vmem, vmem, vmem],
        out_shape=[f32(block, cols), packed(1, 1 + block // 16 * tiles), packed(1 + tiles + -(-(obs_count - 16) * tiles // 16))],
        scratch_shapes=[pltpu.VMEM((tiles, block, LANES), jnp.float32)],
        compiler_params=params,
        name="residual",
    )(me, prior, *parts)

    msg = msg[0]
    mate = swap(msg, 0)
    border = [(i, i + 1) for i in range(1, count - 1, 2)]
    across = lax.ppermute(msg, "rows", border + [(target, source) for source, target in border])
    far = lax.ppermute(first, "rows", [(i + 2, i) for i in range(count - 2)])
    zero, one, two, gram = pl.pallas_call(
        functools.partial(krylov_kernel, total_rows=total_rows, rows_here=rows_here),
        in_specs=[smem, vmem, vmem, vmem],
        out_specs=[vmem] * 4,
        out_shape=[f32(obs_count, rows_here, cols)] * 3 + [f32(8, LANES)],
        scratch_shapes=[pltpu.VMEM((tiles, ENTRIES * 8, LANES), jnp.float32)],
        compiler_params=params,
        name="krylov",
    )(me, own, mate, across)

    grams = [
        pl.pallas_call(
            far_kernel, in_specs=[vmem] * 3, out_specs=vmem, out_shape=f32(8, LANES), compiler_params=params, name="far"
        )(gram, two, far)
    ]
    for bit in range(0, count.bit_length() - 1, 2):
        masks = [mask << bit for mask in (1, 2, 3) if mask << bit < count]
        gram = sum(grams[1:], grams[0])
        grams = [gram] + [flip(gram, mask) for mask in masks]
    out = pl.pallas_call(
        combine_kernel,
        in_specs=[vmem] * (len(grams) + 4),
        out_specs=vmem,
        out_shape=f32(obs_count, rows_here, cols),
        compiler_params=params,
        name="combine",
    )(*grams, prior, zero, one, two)
    return jnp.transpose(out, (1, 0, 2))


def solution(mesh):
    return jax.shard_map(
        on_device,
        mesh=mesh,
        in_specs=(
            P("rows", None, None, "tiles"),
            P("rows", None, "tiles"),
            P("rows", None, None, "tiles"),
            P(),
            P(),
            P(),
            P("rows", None, "tiles"),
        ),
        out_specs=P("rows", None, "tiles"),
        check_vma=False,
    )
```

```python
import functools
import math

import jax
import jax.numpy as jnp
from jax import lax
from jax.experimental import pallas as pl
from jax.experimental.pallas import tpu as pltpu
from jax.sharding import PartitionSpec as P

TO_RADIAN = math.pi / 18000.0
PRIOR_PULL = 0.1
SMOOTH_PULL = 0.5
SHIFT = 3.0
GAIN = 0.4
ENTRIES = 24
LANES = 128
QUANT = 32000.0
GROUP = LANES // 4
CHUNKS = 2


R_POLY = (0.9428089773, 0.04714460664, 0.007527079489, 0.001965302741, 9.052799897e-05, 0.0004621408027)
S_POLY = (0.6002109608, -0.09003726006, -0.007977343822, -0.001801806492, 3.702625389e-06, -0.0003981650976)
SIN_25 = (0.9999999567, -0.1666626093, 0.008276695349)
COS_25 = (0.9999999997, -0.4999999562, 0.04166553086, -0.001379415437)
SIN_15 = (0.999999998, -0.1666661418, 0.008312938059)
COS_15 = (0.9999999858, -0.4999963087, 0.04152366947)
SIN_90 = (0.9999999947, -0.1666665666, 0.008333024663, -0.00019807389, 2.601844464e-06)


def horner(coefs, x):
    acc = coefs[-1] * x + coefs[-2]
    for coef in coefs[-3::-1]:
        acc = acc * x + coef
    return acc


def of_degrees(coefs, x, x2, factor, odd):
    scaled = [factor * coef * TO_RADIAN ** (2 * k + odd) for k, coef in enumerate(coefs)]
    value = horner(scaled, x2)
    return value * x if odd else value


def ross_li(sun, view, azim):
    x = (sun - 4500).astype(jnp.float32)
    x2 = x * x
    half = math.sqrt(0.5)
    sin_x, cos_x = of_degrees(SIN_25, x, x2, half, 1), of_degrees(COS_25, x, x2, half, 0)
    cos_sun, sin_sun = cos_x - sin_x, cos_x + sin_x
    v = view.astype(jnp.float32)
    v2 = v * v
    sin_view, cos_view = of_degrees(SIN_15, v, v2, 1.0, 1), of_degrees(COS_15, v, v2, 1.0, 0)
    a = (9000 - azim).astype(jnp.float32)
    cos_azim = of_degrees(SIN_90, a, a * a, 1.0, 1)
    prod = cos_sun * cos_view
    cos_phase = prod + sin_sun * sin_view * cos_azim
    total = cos_sun + cos_view
    recip = pl.reciprocal(total * prod, approx=False)
    inv_total = recip * prod
    sec_prod = recip * total
    u = 1.0 - cos_phase
    u_up = 1.0 + cos_phase
    bent = u * (u * lax.rsqrt(u)) * horner(R_POLY, u)
    volume = (bent + (0.5 * math.pi) * cos_phase) * inv_total - 0.25 * math.pi
    sin2 = u * u_up
    sin_phase = sin2 * lax.rsqrt(sin2)
    w = jnp.maximum(1.0 - (2.0 * inv_total) * sin_phase, 1e-30)
    overlap = w * (w * lax.rsqrt(w)) * horner(S_POLY, w)
    geometric = sec_prod * (total * (overlap - 1.0) + 0.5 * u_up)
    return volume, geometric


def lane_group(shape):
    return lax.broadcasted_iota(jnp.int32, shape, len(shape) - 1) // GROUP


def pack(tiles, msg_ref, block):
    rows = tiles[0].shape[0]
    top = jnp.abs(tiles[0])
    for tile in tiles[1:]:
        top = jnp.maximum(top, jnp.abs(tile))
    for shift in (LANES // 2, LANES // 4):
        top = jnp.maximum(top, pltpu.roll(top, shift, axis=1))
    level = jnp.ceil(8.0 * jnp.log2(jnp.maximum(top, 1e-30)))
    factor = QUANT * jnp.exp2(-0.125 * level)
    group = lane_group((16, LANES))
    scales = level[0:16]
    for t in range(1, rows // 16):
        scales = jnp.where(group == t, level[16 * t : 16 * t + 16], scales)
    scales = scales.astype(jnp.int32).astype(jnp.int16)
    msg_ref[block, 0] = scales
    numbers = [jnp.round(tile * factor).astype(jnp.int32) for tile in tiles]
    for c, number in enumerate(numbers):
        coded = number.astype(jnp.int16)
        for t in range(rows // 16):
            msg_ref[block, 1 + t * len(tiles) + c] = coded[16 * t : 16 * t + 16]
    return scales, numbers


def as_float(x):
    return x.astype(jnp.int32).astype(jnp.float32)


def factors_of(scales, row_tiles):
    scales = as_float(scales)
    group = lane_group((16, LANES))
    factors = []
    for t in range(row_tiles):
        level = jnp.where(group == t, scales, 0.0)
        for shift in (LANES // 2, LANES // 4):
            level = level + pltpu.roll(level, shift, axis=1)
        factors.append(jnp.exp2(0.125 * level) * (1.0 / QUANT))
    return factors


def unpack(read, row_tiles, col_tiles):
    factors = factors_of(read(0), row_tiles)
    return [
        jnp.concatenate([as_float(read(1 + t * col_tiles + c)) * factors[t] for t in range(row_tiles)], axis=0) for c in range(col_tiles)
    ]


def sums_kernel(
    me_ref,
    ids_ref,
    gain_ref,
    weight_ref,
    reflect_hbm,
    conf_hbm,
    sun_hbm,
    prior_ref,
    keep_ref,
    msg_ref,
    sums_ref,
    kernels_ref,
    reflect_ref,
    conf_ref,
    sun_ref,
    sems,
    *,
    scale,
    rows_here,
    first_col,
):
    steps, dates, bands, tile_rows, _ = reflect_ref.shape
    lane_tiles = sums_ref.shape[0]
    me = me_ref[0]
    block = rows_here * ENTRIES
    obs_count = 3 * bands

    def copies(step):
        rows = pl.ds(pl.multiple_of(step // lane_tiles * tile_rows, tile_rows), tile_rows)
        cols = pl.ds(pl.multiple_of(first_col + step % lane_tiles * LANES, LANES), LANES)
        return (
            pltpu.make_async_copy(sun_hbm.at[:, :, rows, cols], sun_ref.at[step], sems.at[step, 0]),
            pltpu.make_async_copy(conf_hbm.at[:, rows, cols], conf_ref.at[step], sems.at[step, 1]),
            pltpu.make_async_copy(reflect_hbm.at[:, :, rows, cols], reflect_ref.at[step], sems.at[step, 2]),
        )

    def start(step, carry):
        for copy in copies(step):
            copy.start()
        return carry

    lax.fori_loop(0, steps, start, 0)

    def lane_tile(index, row_tile):
        step = row_tile * lane_tiles + index
        for copy in copies(step):
            copy.wait()
        sensors = [ids_ref[me * dates + d] for d in range(dates)]

        def store(top, entry, total):
            sums_ref[index, pl.ds(top * ENTRIES + entry, 8, stride=ENTRIES), :] = total

        def plus(total, term):
            return term if total is None else total + term

        for top in range(0, tile_rows, 8):
            here = slice(top, top + 8)
            normal = [None] * 6
            for d in range(dates):
                volume, geometric = ross_li(*[sun_ref[step, d, angle, here, :] for angle in range(3)])
                weight = conf_ref[step, d, here, :].astype(jnp.float32) * (weight_ref[sensors[d]] * scale)
                weighted_vol = weight * volume
                weighted_geo = weight * geometric
                for i, value in enumerate((weight, weighted_vol, weighted_geo)):
                    kernels_ref[d, i, here, :] = value
                terms = (weight, weighted_vol, weighted_geo, weighted_vol * volume, weighted_vol * geometric, weighted_geo * geometric)
                normal = [plus(total, term) for total, term in zip(normal, terms)]
            for k in range(6):
                store(top, obs_count + k, normal[k])
        for b in range(bands):
            observed = [None] * 3
            for d in range(dates):
                signal = reflect_ref[step, d, b].astype(jnp.float32) * gain_ref[sensors[d], b]
                observed = [plus(total, kernels_ref[d, i] * signal) for i, total in enumerate(observed)]
            for i in range(3):
                for top in range(0, tile_rows, 8):
                    store(top, 3 * b + i, observed[i][top : top + 8])
        return row_tile

    def row_tile_sums(row_tile, carry):
        lax.fori_loop(0, lane_tiles, lane_tile, row_tile)
        tiles = range(lane_tiles)
        first_row = row_tile * tile_rows
        for row, source in ((me * rows_here - 1 - first_row, 0), ((me + 1) * rows_here - first_row, rows_here - 1)):

            @pl.when((row >= 0) & (row < tile_rows))
            def _():
                for c in tiles:
                    lanes = slice(c * LANES, (c + 1) * LANES)
                    at = pl.ds(pl.multiple_of(row * ENTRIES, 8), obs_count)
                    part = jnp.concatenate([prior_ref[e, source : source + 1, lanes] for e in range(obs_count)], axis=0)
                    sums_ref[c, at, :] = sums_ref[c, at, :] + SMOOTH_PULL * part

        bit = me % 2
        per_tile = tile_rows // rows_here // 2
        for j in range(per_tile):
            own = pl.ds(pl.multiple_of((2 * j + bit) * block, 8), block)
            other = pl.ds(pl.multiple_of((2 * j + 1 - bit) * block, 8), block)
            for c in tiles:
                keep_ref[row_tile * per_tile + j, :, c * LANES : (c + 1) * LANES] = sums_ref[c, own, :]
            pack([sums_ref[c, other, :] for c in tiles], msg_ref, row_tile * per_tile + j)
        return carry

    lax.fori_loop(0, steps // lane_tiles, row_tile_sums, 0)


def partial_sums(me, reflect, clear_conf, sun_view, sensor_id, band_gain, sensor_weight, prior, scale, chunk):
    dates, bands, rows, cols = reflect.shape
    cols = cols // CHUNKS
    rows_here = prior.shape[1]
    count = rows // rows_here
    tile_rows = 16
    block = rows_here * ENTRIES
    lane_tiles = cols // LANES
    steps = rows // tile_rows * lane_tiles
    smem = pl.BlockSpec(memory_space=pltpu.SMEM)
    vmem = pl.BlockSpec(memory_space=pltpu.VMEM)
    hbm = pl.BlockSpec(memory_space=pl.ANY)
    return pl.pallas_call(
        functools.partial(sums_kernel, scale=scale, rows_here=rows_here, first_col=chunk * cols),
        grid=(1,),
        in_specs=[smem] * 4 + [hbm] * 3 + [pl.BlockSpec((3 * bands, rows_here, cols), lambda i: (0, 0, chunk))],
        out_specs=[vmem, vmem],
        out_shape=[
            jax.ShapeDtypeStruct((count // 2, block, cols), jnp.float32),
            jax.ShapeDtypeStruct((count // 2, 1 + block // 16 * lane_tiles, 16, LANES), jnp.int16),
        ],
        scratch_shapes=[
            pltpu.VMEM((lane_tiles, tile_rows * ENTRIES, LANES), jnp.float32),
            pltpu.VMEM((dates, 3, tile_rows, LANES), jnp.float32),
            pltpu.VMEM((steps, dates, bands, tile_rows, LANES), reflect.dtype),
            pltpu.VMEM((steps, dates, tile_rows, LANES), jnp.int32),
            pltpu.VMEM((steps, dates, 3, tile_rows, LANES), jnp.int32),
            pltpu.SemaphoreType.DMA((steps, 3)),
        ],
        compiler_params=pltpu.CompilerParams(vmem_limit_bytes=(62 if chunk == 0 else 52) * 2**20),
        name="partial_sums",
    )(me, sensor_id, band_gain, sensor_weight, reflect, clear_conf, sun_view, prior)


def add_split_kernel(bit_ref, *refs, place):
    *parts, keep_ref, msg_ref = refs
    count, block, _ = keep_ref.shape
    bit = bit_ref[0]

    def total(j):
        tiles = []
        for kept_ref, got_ref in zip(parts[0::2], parts[1::2]):
            here = kept_ref.shape[2] // LANES
            came = unpack(lambda at: got_ref[j, at], block // 16, here)
            tiles += [kept_ref[j, :, c * LANES : (c + 1) * LANES] + came[c] for c in range(here)]
        return tiles

    for q in range(count):
        low = q % 2**place
        first = (q - low) * 2 + low
        pack(total(first + (1 - bit) * 2**place), msg_ref, q)
        for c, tile in enumerate(total(first + bit * 2**place)):
            keep_ref[q, :, c * LANES : (c + 1) * LANES] = tile


def add_split(bit, place, *parts):
    count, block, _ = parts[0].shape
    cols = sum(kept.shape[2] for kept in parts[0::2])
    vmem = pl.BlockSpec(memory_space=pltpu.VMEM)
    return pl.pallas_call(
        functools.partial(add_split_kernel, place=place),
        in_specs=[pl.BlockSpec(memory_space=pltpu.SMEM)] + [vmem] * len(parts),
        out_specs=[vmem, vmem],
        out_shape=[
            jax.ShapeDtypeStruct((count // 2, block, cols), jnp.float32),
            jax.ShapeDtypeStruct((count // 2, 1 + block // 16 * (cols // LANES), 16, LANES), jnp.int16),
        ],
        compiler_params=pltpu.CompilerParams(vmem_limit_bytes=24 * 2**20),
        name="add_split",
    )(bit, *parts)


def take(ref, start, size, stride):
    at = pl.ds(start, size, stride=stride)
    return jnp.concatenate([ref[c, at, :] for c in range(ref.shape[0])], axis=1)


def put(ref, start, size, stride, value):
    at = pl.ds(start, size, stride=stride)
    for c in range(ref.shape[0]):
        ref[c, at, :] = value[:, c * LANES : (c + 1) * LANES]


def beside_columns(x):
    cols = x.shape[1]
    col = lax.broadcasted_iota(jnp.int32, x.shape, 1)
    left = jnp.where(col == 0, 0.0, pltpu.roll(x, 1, axis=1))
    right = jnp.where(col == cols - 1, 0.0, pltpu.roll(x, cols - 1, axis=1))
    return left + right


def degree_of(row, shape, total_rows):
    col = lax.broadcasted_iota(jnp.int32, shape, 1)
    edge = (
        (row == 0).astype(jnp.float32)
        + (row == total_rows - 1).astype(jnp.float32)
        + (col == 0).astype(jnp.float32)
        + (col == shape[1] - 1).astype(jnp.float32)
    )
    return 4.0 - edge


def couple(n, v):
    return (
        n[0] * v[0] + n[1] * v[1] + n[2] * v[2],
        n[1] * v[0] + n[3] * v[1] + n[4] * v[2],
        n[2] * v[0] + n[4] * v[1] + n[5] * v[2],
    )


def residual_kernel(me_ref, prior_ref, *refs, total_rows):
    obs_count, rows_here, cols = prior_ref.shape
    *parts, out_ref, msg_ref, first_ref, sums_ref = refs
    block = rows_here * ENTRIES
    tiles = cols // LANES
    at = 0
    for kept_ref, got_ref in zip(parts[0::2], parts[1::2]):
        here = kept_ref.shape[2] // LANES
        came = unpack(lambda place: got_ref[0, place], block // 16, here)
        for c in range(here):
            sums_ref[at] = kept_ref[0, :, c * LANES : (c + 1) * LANES] + came[c]
            at += 1
    shape = (rows_here, cols)
    row = me_ref[0] * rows_here + lax.broadcasted_iota(jnp.int32, shape, 0)
    degree = degree_of(row, shape, total_rows)
    normal = [take(sums_ref, obs_count + k, rows_here, ENTRIES) for k in range(6)]
    for b in range(obs_count // 3):
        fields = [prior_ref[3 * b + i] for i in range(3)]
        coupled = couple(normal, fields)
        for i in range(3):
            field = fields[i]
            beside = beside_columns(field)
            if rows_here > 1:
                zero = jnp.zeros((1, cols), jnp.float32)
                beside = beside + jnp.concatenate([zero, field[:-1]], axis=0) + jnp.concatenate([field[1:], zero], axis=0)
            entry = 3 * b + i
            observed = take(sums_ref, entry, rows_here, ENTRIES)
            put(sums_ref, entry, rows_here, ENTRIES, observed - coupled[i] - SMOOTH_PULL * (degree * field - beside))
    for c in range(tiles):
        out_ref[:, c * LANES : (c + 1) * LANES] = sums_ref[c]
    scales, numbers = pack([sums_ref[c] for c in range(tiles)], msg_ref, 0)
    first_ref[0] = scales
    for c in range(tiles):
        first_ref[1 + c] = numbers[c][0:16].astype(jnp.int16)
    left = jnp.concatenate([number[16:obs_count] for number in numbers], axis=0)
    spare = (first_ref.shape[0] - 1 - tiles) * 16 - left.shape[0]
    if spare:
        left = jnp.concatenate([left, jnp.zeros((spare, LANES), jnp.int32)], axis=0)
    for t in range(left.shape[0] // 16):
        first_ref[1 + tiles + t] = left[16 * t : 16 * t + 16].astype(jnp.int16)


def krylov_kernel(me_ref, own_ref, mate_ref, across_ref, zero_ref, one_ref, two_ref, gram_ref, window_ref, *, total_rows, rows_here):
    cols = own_ref.shape[1]
    obs_count = ENTRIES - 6
    tiles = cols // LANES
    row_tiles = own_ref.shape[0] // 16

    def lay(place, part, r):
        at = pl.ds(place, ENTRIES, stride=8)
        for c in range(tiles):
            window_ref[c, at, :] = part[c][r * ENTRIES : (r + 1) * ENTRIES]

    own = [own_ref[:, c * LANES : (c + 1) * LANES] for c in range(tiles)]
    mate = unpack(lambda place: mate_ref[place], row_tiles, tiles)
    across = unpack(lambda place: across_ref[place], row_tiles, tiles)
    odd = me_ref[0] % 2
    for r in range(2):
        lay(2 + r, own, r)
        lay(4 * (1 - odd) + r, mate, r)
        lay(4 * odd + r, across, r)
    for empty in (6, 7):
        put(window_ref, empty, ENTRIES, 8, jnp.zeros((ENTRIES, cols), jnp.float32))
    window = lambda entry: jnp.concatenate([window_ref[c, entry * 8 : entry * 8 + 8, :] for c in range(cols // LANES)], axis=1)
    shape = (8, cols)
    place = lax.broadcasted_iota(jnp.int32, shape, 0)
    row = me_ref[0] * rows_here + place - 2
    inside = ((row >= 0) & (row < total_rows)).astype(jnp.float32) * GAIN
    own_rows = (place == 2) | (place == 3)
    diag = inside * (PRIOR_PULL - SHIFT + SMOOTH_PULL * degree_of(row, shape, total_rows))
    pull = inside * SMOOTH_PULL
    normal = [window(obs_count + k) * inside for k in range(6)]
    acc = [jnp.zeros((8, LANES), jnp.float32) for _ in range(6)]

    def apply(v, last=False):
        coupled = couple(normal, v)
        out = []
        for i in range(3):
            x = v[i]
            above = pltpu.roll(x, 7, axis=0)
            beside = beside_columns(x) + (2.0 * above if last else above + pltpu.roll(x, 1, axis=0))
            out.append(coupled[i] + diag * x - pull * beside)
        return out

    def fold(x):
        total = x[:, 0:LANES]
        for c in range(LANES, cols, LANES):
            total = total + x[:, c : c + LANES]
        return total

    for b in range(obs_count // 3):
        zero = [window(3 * b + i) for i in range(3)]
        one = apply(zero)
        two = apply(one)
        three = apply(two, last=True)
        for i in range(3):
            zero_ref[3 * b + i] = zero[i][2:4]
            one_ref[3 * b + i] = one[i][2:4]
            two_ref[3 * b + i] = two[i][2:4]
            v = [zero[i], one[i], two[i], three[i]]
            for k in range(6):
                acc[k] = acc[k] + fold(v[k // 2] * v[(k + 1) // 2])
    own_tile = own_rows[:, 0:LANES]
    tile_row = lax.broadcasted_iota(jnp.int32, (8, LANES), 0)
    gram = jnp.zeros((8, LANES), jnp.float32)
    for k in range(6):
        moment = jnp.sum(jnp.where(own_tile, acc[k], 0.0))
        gram = jnp.where(tile_row == k, moment, gram)
    gram_ref[...] = gram


def far_kernel(gram_ref, two_ref, far_ref, out_ref):
    obs_count, _, cols = two_ref.shape
    tiles = cols // LANES
    rest = obs_count - 16
    factors = factors_of(far_ref[0], 2)
    left = jnp.concatenate([as_float(far_ref[t]) for t in range(1 + tiles, far_ref.shape[0])], axis=0)
    total = jnp.zeros((obs_count, LANES), jnp.float32)
    for c in range(tiles):
        far = jnp.concatenate([as_float(far_ref[1 + c]) * factors[0], left[rest * c : rest * (c + 1)] * factors[1][0:rest]], axis=0)
        mine = jnp.concatenate([two_ref[e, 1:2, c * LANES : (c + 1) * LANES] for e in range(obs_count)], axis=0)
        total = total + far * mine
    part = (-2.0 * (GAIN * SMOOTH_PULL) ** 3) * jnp.sum(total)
    row = lax.broadcasted_iota(jnp.int32, (8, LANES), 0)
    out_ref[...] = gram_ref[...] + jnp.where(row == 5, part, 0.0)


def combine_kernel(*refs):
    *gram_refs, prior_ref, zero_ref, one_ref, two_ref, out_ref = refs
    gram = gram_refs[0][...]
    for ref in gram_refs[1:]:
        gram = gram + ref[...]
    m = [gram[k : k + 1, :] for k in range(6)]
    h = {(i, j): m[i + j + 1] * (1.0 / GAIN) + SHIFT * m[i + j] for i in range(3) for j in range(i, 3)}
    l10 = h[0, 1] / h[0, 0]
    l20 = h[0, 2] / h[0, 0]
    d1 = h[1, 1] - l10 * h[0, 1]
    t = h[1, 2] - l20 * h[0, 1]
    ok1 = d1 > 1e-6 * h[1, 1]
    inv1 = jnp.where(ok1, 1.0 / jnp.where(ok1, d1, 1.0), 0.0)
    l21 = t * inv1
    d2 = h[2, 2] - l20 * h[0, 2] - l21 * t
    ok2 = ok1 & (d2 > 1e-6 * h[2, 2])
    inv2 = jnp.where(ok2, 1.0 / jnp.where(ok2, d2, 1.0), 0.0)
    z1 = m[1] - l10 * m[0]
    z2 = m[2] - l20 * m[0] - l21 * z1
    y2 = z2 * inv2
    y1 = z1 * inv1 - l21 * y2
    y0 = m[0] / h[0, 0] - l10 * y1 - l20 * y2
    cols = prior_ref.shape[2]
    for c in range(0, cols, LANES):
        lanes = slice(c, c + LANES)
        out_ref[:, :, lanes] = (
            prior_ref[:, :, lanes] + y0[None] * zero_ref[:, :, lanes] + y1[None] * one_ref[:, :, lanes] + y2[None] * two_ref[:, :, lanes]
        )


def on_device(reflect, clear_conf, sun_view, sensor_id, band_gain, sensor_weight, prior):
    rows_here, obs_count, cols = prior.shape
    prior = jnp.transpose(prior, (1, 0, 2))
    count = lax.axis_size("rows")
    total_rows = rows_here * count
    block = rows_here * ENTRIES
    tiles = cols // LANES
    me = lax.axis_index("rows").astype(jnp.int32).reshape(1)
    vmem = pl.BlockSpec(memory_space=pltpu.VMEM)
    smem = pl.BlockSpec(memory_space=pltpu.SMEM)
    params = pltpu.CompilerParams(vmem_limit_bytes=24 * 2**20)
    f32 = lambda *shape: jax.ShapeDtypeStruct(shape, jnp.float32)
    packed = lambda *shape: jax.ShapeDtypeStruct(shape + (16, LANES), jnp.int16)

    scale = 0.01 / (reflect.shape[0] * count)
    index = me
    parts = []
    for chunk in range(CHUNKS):
        kept, sent = partial_sums(
            index, reflect, clear_conf, sun_view, sensor_id, band_gain, sensor_weight, prior, scale, chunk
        )
        index, _ = lax.optimization_barrier((me, sent))
        parts.append((kept, sent))
    flip = lambda x, mask: lax.ppermute(x, "rows", [(i, i ^ mask) for i in range(count)])
    swap = lambda x, bit: flip(x, 1 << bit)
    parts = [(kept, swap(sent, 0)) for kept, sent in parts]
    bits = list(range(1, count.bit_length() - 1))
    for step in range(len(bits)):
        for chunk in range(CHUNKS):
            turned = chunk % 2 == 1 and len(bits) >= 2 and step < 2
            bit, place = (bits[1 - step], 1 - step) if turned else (bits[step], 0)
            kept, sent = add_split(me // 2**bit % 2, place, *parts[chunk])
            parts[chunk] = (kept, swap(sent, bit))
    parts = [x for part in parts for x in part]

    own, msg, first = pl.pallas_call(
        functools.partial(residual_kernel, total_rows=total_rows),
        in_specs=[smem] + [vmem] * (1 + len(parts)),
        out_specs=[vmem, vmem, vmem],
        out_shape=[f32(block, cols), packed(1, 1 + block // 16 * tiles), packed(1 + tiles + -(-(obs_count - 16) * tiles // 16))],
        scratch_shapes=[pltpu.VMEM((tiles, block, LANES), jnp.float32)],
        compiler_params=params,
        name="residual",
    )(me, prior, *parts)

    msg = msg[0]
    mate = swap(msg, 0)
    border = [(i, i + 1) for i in range(1, count - 1, 2)]
    across = lax.ppermute(msg, "rows", border + [(target, source) for source, target in border])
    far = lax.ppermute(first, "rows", [(i + 2, i) for i in range(count - 2)])
    zero, one, two, gram = pl.pallas_call(
        functools.partial(krylov_kernel, total_rows=total_rows, rows_here=rows_here),
        in_specs=[smem, vmem, vmem, vmem],
        out_specs=[vmem] * 4,
        out_shape=[f32(obs_count, rows_here, cols)] * 3 + [f32(8, LANES)],
        scratch_shapes=[pltpu.VMEM((tiles, ENTRIES * 8, LANES), jnp.float32)],
        compiler_params=params,
        name="krylov",
    )(me, own, mate, across)

    grams = [
        pl.pallas_call(
            far_kernel, in_specs=[vmem] * 3, out_specs=vmem, out_shape=f32(8, LANES), compiler_params=params, name="far"
        )(gram, two, far)
    ]
    top = count.bit_length() - 1
    rounds = [[mask << bit for mask in (1, 2, 3) if mask << bit < count] for bit in range(1, top, 2)] + [[1]]
    for masks in rounds:
        gram = sum(grams[1:], grams[0])
        grams = [gram] + [flip(gram, mask) for mask in masks]
    out = pl.pallas_call(
        combine_kernel,
        in_specs=[vmem] * (len(grams) + 4),
        out_specs=vmem,
        out_shape=f32(obs_count, rows_here, cols),
        compiler_params=params,
        name="combine",
    )(*grams, prior, zero, one, two)
    return jnp.transpose(out, (1, 0, 2))


def solution(mesh):
    return jax.shard_map(
        on_device,
        mesh=mesh,
        in_specs=(
            P("rows", None, None, "tiles"),
            P("rows", None, "tiles"),
            P("rows", None, None, "tiles"),
            P(),
            P(),
            P(),
            P("rows", None, "tiles"),
        ),
        out_specs=P("rows", None, "tiles"),
        check_vma=False,
    )
```

```python
import functools
import math

import jax
import jax.numpy as jnp
from jax import lax
from jax.experimental import pallas as pl
from jax.experimental.pallas import tpu as pltpu
from jax.sharding import PartitionSpec as P

TO_RADIAN = math.pi / 18000.0
PRIOR_PULL = 0.1
SMOOTH_PULL = 0.5
SHIFT = 3.0
GAIN = 0.4
ENTRIES = 24
LANES = 128
QUANT = 32000.0
GROUP = LANES // 4
CHUNKS = 2


R_POLY = (0.9428089773, 0.04714460664, 0.007527079489, 0.001965302741, 9.052799897e-05, 0.0004621408027)
S_POLY = (0.6002109608, -0.09003726006, -0.007977343822, -0.001801806492, 3.702625389e-06, -0.0003981650976)
SIN_25 = (0.9999999567, -0.1666626093, 0.008276695349)
COS_25 = (0.9999999997, -0.4999999562, 0.04166553086, -0.001379415437)
SIN_15 = (0.999999998, -0.1666661418, 0.008312938059)
COS_15 = (0.9999999858, -0.4999963087, 0.04152366947)
SIN_90 = (0.9999999947, -0.1666665666, 0.008333024663, -0.00019807389, 2.601844464e-06)


def horner(coefs, x):
    acc = coefs[-1] * x + coefs[-2]
    for coef in coefs[-3::-1]:
        acc = acc * x + coef
    return acc


def of_degrees(coefs, x, x2, factor, odd):
    scaled = [factor * coef * TO_RADIAN ** (2 * k + odd) for k, coef in enumerate(coefs)]
    value = horner(scaled, x2)
    return value * x if odd else value


def ross_li(sun, view, azim):
    x = (sun - 4500).astype(jnp.float32)
    x2 = x * x
    half = math.sqrt(0.5)
    sin_x, cos_x = of_degrees(SIN_25, x, x2, half, 1), of_degrees(COS_25, x, x2, half, 0)
    cos_sun, sin_sun = cos_x - sin_x, cos_x + sin_x
    v = view.astype(jnp.float32)
    v2 = v * v
    sin_view, cos_view = of_degrees(SIN_15, v, v2, 1.0, 1), of_degrees(COS_15, v, v2, 1.0, 0)
    a = (9000 - azim).astype(jnp.float32)
    cos_azim = of_degrees(SIN_90, a, a * a, 1.0, 1)
    prod = cos_sun * cos_view
    cos_phase = prod + sin_sun * sin_view * cos_azim
    total = cos_sun + cos_view
    recip = pl.reciprocal(total * prod, approx=False)
    inv_total = recip * prod
    sec_prod = recip * total
    u = 1.0 - cos_phase
    u_up = 1.0 + cos_phase
    bent = u * (u * lax.rsqrt(u)) * horner(R_POLY, u)
    volume = (bent + (0.5 * math.pi) * cos_phase) * inv_total - 0.25 * math.pi
    sin2 = u * u_up
    sin_phase = sin2 * lax.rsqrt(sin2)
    w = jnp.maximum(1.0 - (2.0 * inv_total) * sin_phase, 1e-30)
    overlap = w * (w * lax.rsqrt(w)) * horner(S_POLY, w)
    geometric = sec_prod * (total * (overlap - 1.0) + 0.5 * u_up)
    return volume, geometric


def lane_group(shape):
    return lax.broadcasted_iota(jnp.int32, shape, len(shape) - 1) // GROUP


def pack(tiles, msg_ref, block):
    rows = tiles[0].shape[0]
    top = jnp.abs(tiles[0])
    for tile in tiles[1:]:
        top = jnp.maximum(top, jnp.abs(tile))
    for shift in (LANES // 2, LANES // 4):
        top = jnp.maximum(top, pltpu.roll(top, shift, axis=1))
    level = jnp.ceil(8.0 * jnp.log2(jnp.maximum(top, 1e-30)))
    factor = QUANT * jnp.exp2(-0.125 * level)
    group = lane_group((16, LANES))
    scales = level[0:16]
    for t in range(1, rows // 16):
        scales = jnp.where(group == t, level[16 * t : 16 * t + 16], scales)
    scales = scales.astype(jnp.int32).astype(jnp.int16)
    msg_ref[block, 0] = scales
    numbers = [jnp.round(tile * factor).astype(jnp.int32) for tile in tiles]
    for c, number in enumerate(numbers):
        coded = number.astype(jnp.int16)
        for t in range(rows // 16):
            msg_ref[block, 1 + t * len(tiles) + c] = coded[16 * t : 16 * t + 16]
    return scales, numbers


def as_float(x):
    return x.astype(jnp.int32).astype(jnp.float32)


def factors_of(scales, row_tiles):
    scales = as_float(scales)
    group = lane_group((16, LANES))
    factors = []
    for t in range(row_tiles):
        level = jnp.where(group == t, scales, 0.0)
        for shift in (LANES // 2, LANES // 4):
            level = level + pltpu.roll(level, shift, axis=1)
        factors.append(jnp.exp2(0.125 * level) * (1.0 / QUANT))
    return factors


def unpack(read, row_tiles, col_tiles):
    factors = factors_of(read(0), row_tiles)
    return [
        jnp.concatenate([as_float(read(1 + t * col_tiles + c)) * factors[t] for t in range(row_tiles)], axis=0) for c in range(col_tiles)
    ]


def sums_kernel(
    me_ref,
    ids_ref,
    gain_ref,
    weight_ref,
    reflect_hbm,
    conf_hbm,
    sun_hbm,
    prior_ref,
    keep_ref,
    msg_ref,
    sums_ref,
    kernels_ref,
    reflect_ref,
    conf_ref,
    sun_ref,
    sems,
    *,
    scale,
    rows_here,
    first_col,
):
    steps, dates, bands, tile_rows, _ = reflect_ref.shape
    lane_tiles = sums_ref.shape[0]
    me = me_ref[0]
    block = rows_here * ENTRIES
    obs_count = 3 * bands

    def copies(step):
        rows = pl.ds(pl.multiple_of(step // lane_tiles * tile_rows, tile_rows), tile_rows)
        cols = pl.ds(pl.multiple_of(first_col + step % lane_tiles * LANES, LANES), LANES)
        return (
            pltpu.make_async_copy(sun_hbm.at[:, :, rows, cols], sun_ref.at[step], sems.at[step, 0]),
            pltpu.make_async_copy(conf_hbm.at[:, rows, cols], conf_ref.at[step], sems.at[step, 1]),
            pltpu.make_async_copy(reflect_hbm.at[:, :, rows, cols], reflect_ref.at[step], sems.at[step, 2]),
        )

    def start(step, carry):
        for copy in copies(step):
            copy.start()
        return carry

    lax.fori_loop(0, steps, start, 0)

    def lane_tile(index, row_tile):
        step = row_tile * lane_tiles + index
        for copy in copies(step):
            copy.wait()
        sensors = [ids_ref[me * dates + d] for d in range(dates)]

        def store(top, entry, total):
            sums_ref[index, pl.ds(top * ENTRIES + entry, 8, stride=ENTRIES), :] = total

        def plus(total, term):
            return term if total is None else total + term

        for top in range(0, tile_rows, 8):
            here = slice(top, top + 8)
            normal = [None] * 6
            for d in range(dates):
                volume, geometric = ross_li(*[sun_ref[step, d, angle, here, :] for angle in range(3)])
                weight = conf_ref[step, d, here, :].astype(jnp.float32) * (weight_ref[sensors[d]] * scale)
                weighted_vol = weight * volume
                weighted_geo = weight * geometric
                for i, value in enumerate((weight, weighted_vol, weighted_geo)):
                    kernels_ref[d, i, here, :] = value
                terms = (weight, weighted_vol, weighted_geo, weighted_vol * volume, weighted_vol * geometric, weighted_geo * geometric)
                normal = [plus(total, term) for total, term in zip(normal, terms)]
            for k in range(6):
                store(top, obs_count + k, normal[k])
        for b in range(bands):
            observed = [None] * 3
            for d in range(dates):
                signal = reflect_ref[step, d, b].astype(jnp.float32) * gain_ref[sensors[d], b]
                observed = [plus(total, kernels_ref[d, i] * signal) for i, total in enumerate(observed)]
            for i in range(3):
                for top in range(0, tile_rows, 8):
                    store(top, 3 * b + i, observed[i][top : top + 8])
        return row_tile

    def row_tile_sums(row_tile, carry):
        lax.fori_loop(0, lane_tiles, lane_tile, row_tile)
        tiles = range(lane_tiles)
        first_row = row_tile * tile_rows
        for row, source in ((me * rows_here - 1 - first_row, 0), ((me + 1) * rows_here - first_row, rows_here - 1)):

            @pl.when((row >= 0) & (row < tile_rows))
            def _():
                for c in tiles:
                    lanes = slice(c * LANES, (c + 1) * LANES)
                    at = pl.ds(pl.multiple_of(row * ENTRIES, 8), obs_count)
                    part = jnp.concatenate([prior_ref[e, source : source + 1, lanes] for e in range(obs_count)], axis=0)
                    sums_ref[c, at, :] = sums_ref[c, at, :] + SMOOTH_PULL * part

        bit = me % 2
        per_tile = tile_rows // rows_here // 2
        for j in range(per_tile):
            own = pl.ds(pl.multiple_of((2 * j + bit) * block, 8), block)
            other = pl.ds(pl.multiple_of((2 * j + 1 - bit) * block, 8), block)
            for c in tiles:
                keep_ref[row_tile * per_tile + j, :, c * LANES : (c + 1) * LANES] = sums_ref[c, own, :]
            pack([sums_ref[c, other, :] for c in tiles], msg_ref, row_tile * per_tile + j)
        return carry

    lax.fori_loop(0, steps // lane_tiles, row_tile_sums, 0)


def partial_sums(me, reflect, clear_conf, sun_view, sensor_id, band_gain, sensor_weight, prior, scale, chunk):
    dates, bands, rows, cols = reflect.shape
    cols = cols // CHUNKS
    rows_here = prior.shape[1]
    count = rows // rows_here
    tile_rows = 16
    block = rows_here * ENTRIES
    lane_tiles = cols // LANES
    steps = rows // tile_rows * lane_tiles
    smem = pl.BlockSpec(memory_space=pltpu.SMEM)
    vmem = pl.BlockSpec(memory_space=pltpu.VMEM)
    hbm = pl.BlockSpec(memory_space=pl.ANY)
    return pl.pallas_call(
        functools.partial(sums_kernel, scale=scale, rows_here=rows_here, first_col=chunk * cols),
        grid=(1,),
        in_specs=[smem] * 4 + [hbm] * 3 + [pl.BlockSpec((3 * bands, rows_here, cols), lambda i: (0, 0, chunk))],
        out_specs=[vmem, vmem],
        out_shape=[
            jax.ShapeDtypeStruct((count // 2, block, cols), jnp.float32),
            jax.ShapeDtypeStruct((count // 2, 1 + block // 16 * lane_tiles, 16, LANES), jnp.int16),
        ],
        scratch_shapes=[
            pltpu.VMEM((lane_tiles, tile_rows * ENTRIES, LANES), jnp.float32),
            pltpu.VMEM((dates, 3, tile_rows, LANES), jnp.float32),
            pltpu.VMEM((steps, dates, bands, tile_rows, LANES), reflect.dtype),
            pltpu.VMEM((steps, dates, tile_rows, LANES), jnp.int32),
            pltpu.VMEM((steps, dates, 3, tile_rows, LANES), jnp.int32),
            pltpu.SemaphoreType.DMA((steps, 3)),
        ],
        compiler_params=pltpu.CompilerParams(vmem_limit_bytes=(62 if chunk == 0 else 52) * 2**20),
        name="partial_sums",
    )(me, sensor_id, band_gain, sensor_weight, reflect, clear_conf, sun_view, prior)


def add_split_kernel(bit_ref, *refs, place):
    *parts, keep_ref, msg_ref = refs
    count, block, _ = keep_ref.shape
    bit = bit_ref[0]

    def total(j):
        tiles = []
        for kept_ref, got_ref in zip(parts[0::2], parts[1::2]):
            here = kept_ref.shape[2] // LANES
            came = unpack(lambda at: got_ref[j, at], block // 16, here)
            tiles += [kept_ref[j, :, c * LANES : (c + 1) * LANES] + came[c] for c in range(here)]
        return tiles

    for q in range(count):
        low = q % 2**place
        first = (q - low) * 2 + low
        pack(total(first + (1 - bit) * 2**place), msg_ref, q)
        for c, tile in enumerate(total(first + bit * 2**place)):
            keep_ref[q, :, c * LANES : (c + 1) * LANES] = tile


def add_split(bit, place, *parts):
    count, block, _ = parts[0].shape
    cols = sum(kept.shape[2] for kept in parts[0::2])
    vmem = pl.BlockSpec(memory_space=pltpu.VMEM)
    return pl.pallas_call(
        functools.partial(add_split_kernel, place=place),
        in_specs=[pl.BlockSpec(memory_space=pltpu.SMEM)] + [vmem] * len(parts),
        out_specs=[vmem, vmem],
        out_shape=[
            jax.ShapeDtypeStruct((count // 2, block, cols), jnp.float32),
            jax.ShapeDtypeStruct((count // 2, 1 + block // 16 * (cols // LANES), 16, LANES), jnp.int16),
        ],
        compiler_params=pltpu.CompilerParams(vmem_limit_bytes=24 * 2**20),
        name="add_split",
    )(bit, *parts)


def take(ref, start, size, stride):
    at = pl.ds(start, size, stride=stride)
    return jnp.concatenate([ref[c, at, :] for c in range(ref.shape[0])], axis=1)


def put(ref, start, size, stride, value):
    at = pl.ds(start, size, stride=stride)
    for c in range(ref.shape[0]):
        ref[c, at, :] = value[:, c * LANES : (c + 1) * LANES]


def beside_columns(x):
    cols = x.shape[1]
    col = lax.broadcasted_iota(jnp.int32, x.shape, 1)
    left = jnp.where(col == 0, 0.0, pltpu.roll(x, 1, axis=1))
    right = jnp.where(col == cols - 1, 0.0, pltpu.roll(x, cols - 1, axis=1))
    return left + right


def degree_of(row, shape, total_rows):
    col = lax.broadcasted_iota(jnp.int32, shape, 1)
    edge = (
        (row == 0).astype(jnp.float32)
        + (row == total_rows - 1).astype(jnp.float32)
        + (col == 0).astype(jnp.float32)
        + (col == shape[1] - 1).astype(jnp.float32)
    )
    return 4.0 - edge


def couple(n, v):
    return (
        n[0] * v[0] + n[1] * v[1] + n[2] * v[2],
        n[1] * v[0] + n[3] * v[1] + n[4] * v[2],
        n[2] * v[0] + n[4] * v[1] + n[5] * v[2],
    )


def residual_kernel(me_ref, prior_ref, *refs, total_rows):
    obs_count, rows_here, cols = prior_ref.shape
    *parts, out_ref, msg_ref, first_ref, sums_ref = refs
    block = rows_here * ENTRIES
    tiles = cols // LANES
    at = 0
    for kept_ref, got_ref in zip(parts[0::2], parts[1::2]):
        here = kept_ref.shape[2] // LANES
        came = unpack(lambda place: got_ref[0, place], block // 16, here)
        for c in range(here):
            sums_ref[at] = kept_ref[0, :, c * LANES : (c + 1) * LANES] + came[c]
            at += 1
    shape = (rows_here, cols)
    row = me_ref[0] * rows_here + lax.broadcasted_iota(jnp.int32, shape, 0)
    degree = degree_of(row, shape, total_rows)
    normal = [take(sums_ref, obs_count + k, rows_here, ENTRIES) for k in range(6)]
    for b in range(obs_count // 3):
        fields = [prior_ref[3 * b + i] for i in range(3)]
        coupled = couple(normal, fields)
        for i in range(3):
            field = fields[i]
            beside = beside_columns(field)
            if rows_here > 1:
                zero = jnp.zeros((1, cols), jnp.float32)
                beside = beside + jnp.concatenate([zero, field[:-1]], axis=0) + jnp.concatenate([field[1:], zero], axis=0)
            entry = 3 * b + i
            observed = take(sums_ref, entry, rows_here, ENTRIES)
            put(sums_ref, entry, rows_here, ENTRIES, observed - coupled[i] - SMOOTH_PULL * (degree * field - beside))
    for c in range(tiles):
        out_ref[:, c * LANES : (c + 1) * LANES] = sums_ref[c]
    scales, numbers = pack([sums_ref[c] for c in range(tiles)], msg_ref, 0)
    first_ref[0] = scales
    for c in range(tiles):
        first_ref[1 + c] = numbers[c][0:16].astype(jnp.int16)
    left = jnp.concatenate([number[16:obs_count] for number in numbers], axis=0)
    spare = (first_ref.shape[0] - 1 - tiles) * 16 - left.shape[0]
    if spare:
        left = jnp.concatenate([left, jnp.zeros((spare, LANES), jnp.int32)], axis=0)
    for t in range(left.shape[0] // 16):
        first_ref[1 + tiles + t] = left[16 * t : 16 * t + 16].astype(jnp.int16)


def krylov_kernel(me_ref, own_ref, mate_ref, across_ref, zero_ref, one_ref, two_ref, gram_ref, window_ref, *, total_rows, rows_here):
    cols = own_ref.shape[1]
    obs_count = ENTRIES - 6
    tiles = cols // LANES
    row_tiles = own_ref.shape[0] // 16

    def lay(place, part, r):
        at = pl.ds(place, ENTRIES, stride=8)
        for c in range(tiles):
            window_ref[c, at, :] = part[c][r * ENTRIES : (r + 1) * ENTRIES]

    own = [own_ref[:, c * LANES : (c + 1) * LANES] for c in range(tiles)]
    mate = unpack(lambda place: mate_ref[place], row_tiles, tiles)
    across = unpack(lambda place: across_ref[place], row_tiles, tiles)
    odd = me_ref[0] % 2
    for r in range(2):
        lay(2 + r, own, r)
        lay(4 * (1 - odd) + r, mate, r)
        lay(4 * odd + r, across, r)
    for empty in (6, 7):
        put(window_ref, empty, ENTRIES, 8, jnp.zeros((ENTRIES, cols), jnp.float32))
    window = lambda entry: jnp.concatenate([window_ref[c, entry * 8 : entry * 8 + 8, :] for c in range(cols // LANES)], axis=1)
    shape = (8, cols)
    place = lax.broadcasted_iota(jnp.int32, shape, 0)
    row = me_ref[0] * rows_here + place - 2
    inside = ((row >= 0) & (row < total_rows)).astype(jnp.float32) * GAIN
    own_rows = (place == 2) | (place == 3)
    diag = inside * (PRIOR_PULL - SHIFT + SMOOTH_PULL * degree_of(row, shape, total_rows))
    pull = inside * SMOOTH_PULL
    normal = [window(obs_count + k) * inside for k in range(6)]
    acc = [jnp.zeros((8, LANES), jnp.float32) for _ in range(6)]

    def apply(v, last=False):
        coupled = couple(normal, v)
        out = []
        for i in range(3):
            x = v[i]
            above = pltpu.roll(x, 7, axis=0)
            beside = beside_columns(x) + (2.0 * above if last else above + pltpu.roll(x, 1, axis=0))
            out.append(coupled[i] + diag * x - pull * beside)
        return out

    def fold(x):
        total = x[:, 0:LANES]
        for c in range(LANES, cols, LANES):
            total = total + x[:, c : c + LANES]
        return total

    for b in range(obs_count // 3):
        zero = [window(3 * b + i) for i in range(3)]
        one = apply(zero)
        two = apply(one)
        three = apply(two, last=True)
        for i in range(3):
            zero_ref[3 * b + i] = zero[i][2:4]
            one_ref[3 * b + i] = one[i][2:4]
            two_ref[3 * b + i] = two[i][2:4]
            v = [zero[i], one[i], two[i], three[i]]
            for k in range(6):
                acc[k] = acc[k] + fold(v[k // 2] * v[(k + 1) // 2])
    own_tile = own_rows[:, 0:LANES]
    tile_row = lax.broadcasted_iota(jnp.int32, (8, LANES), 0)
    gram = jnp.zeros((8, LANES), jnp.float32)
    for k in range(6):
        moment = jnp.sum(jnp.where(own_tile, acc[k], 0.0))
        gram = jnp.where(tile_row == k, moment, gram)
    gram_ref[...] = gram


def far_kernel(me_ref, gram_ref, two_ref, mate_ref, far_ref, out_ref):
    obs_count, _, cols = two_ref.shape
    tiles = cols // LANES
    rest = obs_count - 16
    core0 = me_ref[0] % 2 == 0
    from_mate = unpack(lambda place: mate_ref[place], 2, tiles)
    factors = factors_of(far_ref[0], 2)
    left = jnp.concatenate([as_float(far_ref[t]) for t in range(1 + tiles, far_ref.shape[0])], axis=0)
    total = jnp.zeros((obs_count, LANES), jnp.float32)
    for c in range(tiles):
        rows = as_float(far_ref[1 + c]) * factors[0], left[rest * c : rest * (c + 1)] * factors[1][0:rest]
        far = jnp.where(core0, from_mate[c][0:obs_count], jnp.concatenate(rows, axis=0))
        mine = jnp.concatenate([two_ref[e, 1:2, c * LANES : (c + 1) * LANES] for e in range(obs_count)], axis=0)
        total = total + far * mine
    part = (-2.0 * (GAIN * SMOOTH_PULL) ** 3) * jnp.sum(total)
    row = lax.broadcasted_iota(jnp.int32, (8, LANES), 0)
    out_ref[...] = gram_ref[...] + jnp.where(row == 5, part, 0.0)


def combine_kernel(*refs):
    *gram_refs, prior_ref, zero_ref, one_ref, two_ref, out_ref = refs
    gram = gram_refs[0][...]
    for ref in gram_refs[1:]:
        gram = gram + ref[...]
    m = [gram[k : k + 1, :] for k in range(6)]
    h = {(i, j): m[i + j + 1] * (1.0 / GAIN) + SHIFT * m[i + j] for i in range(3) for j in range(i, 3)}
    l10 = h[0, 1] / h[0, 0]
    l20 = h[0, 2] / h[0, 0]
    d1 = h[1, 1] - l10 * h[0, 1]
    t = h[1, 2] - l20 * h[0, 1]
    ok1 = d1 > 1e-6 * h[1, 1]
    inv1 = jnp.where(ok1, 1.0 / jnp.where(ok1, d1, 1.0), 0.0)
    l21 = t * inv1
    d2 = h[2, 2] - l20 * h[0, 2] - l21 * t
    ok2 = ok1 & (d2 > 1e-6 * h[2, 2])
    inv2 = jnp.where(ok2, 1.0 / jnp.where(ok2, d2, 1.0), 0.0)
    z1 = m[1] - l10 * m[0]
    z2 = m[2] - l20 * m[0] - l21 * z1
    y2 = z2 * inv2
    y1 = z1 * inv1 - l21 * y2
    y0 = m[0] / h[0, 0] - l10 * y1 - l20 * y2
    cols = prior_ref.shape[2]
    for c in range(0, cols, LANES):
        lanes = slice(c, c + LANES)
        out_ref[:, :, lanes] = (
            prior_ref[:, :, lanes] + y0[None] * zero_ref[:, :, lanes] + y1[None] * one_ref[:, :, lanes] + y2[None] * two_ref[:, :, lanes]
        )


def on_device(reflect, clear_conf, sun_view, sensor_id, band_gain, sensor_weight, prior):
    rows_here, obs_count, cols = prior.shape
    prior = jnp.transpose(prior, (1, 0, 2))
    count = lax.axis_size("rows")
    total_rows = rows_here * count
    block = rows_here * ENTRIES
    tiles = cols // LANES
    me = lax.axis_index("rows").astype(jnp.int32).reshape(1)
    vmem = pl.BlockSpec(memory_space=pltpu.VMEM)
    smem = pl.BlockSpec(memory_space=pltpu.SMEM)
    params = pltpu.CompilerParams(vmem_limit_bytes=24 * 2**20)
    f32 = lambda *shape: jax.ShapeDtypeStruct(shape, jnp.float32)
    packed = lambda *shape: jax.ShapeDtypeStruct(shape + (16, LANES), jnp.int16)

    scale = 0.01 / (reflect.shape[0] * count)
    index = me
    parts = []
    for chunk in range(CHUNKS):
        kept, sent = partial_sums(
            index, reflect, clear_conf, sun_view, sensor_id, band_gain, sensor_weight, prior, scale, chunk
        )
        index, _ = lax.optimization_barrier((me, sent))
        parts.append((kept, sent))
    flip = lambda x, mask: lax.ppermute(x, "rows", [(i, i ^ mask) for i in range(count)])
    swap = lambda x, bit: flip(x, 1 << bit)
    parts = [(kept, swap(sent, 0)) for kept, sent in parts]
    bits = list(range(1, count.bit_length() - 1))
    for step in range(len(bits)):
        for chunk in range(CHUNKS):
            turned = chunk % 2 == 1 and len(bits) >= 2 and step < 2
            bit, place = (bits[1 - step], 1 - step) if turned else (bits[step], 0)
            kept, sent = add_split(me // 2**bit % 2, place, *parts[chunk])
            parts[chunk] = (kept, swap(sent, bit))
    parts = [x for part in parts for x in part]

    own, msg, first = pl.pallas_call(
        functools.partial(residual_kernel, total_rows=total_rows),
        in_specs=[smem] + [vmem] * (1 + len(parts)),
        out_specs=[vmem, vmem, vmem],
        out_shape=[f32(block, cols), packed(1, 1 + block // 16 * tiles), packed(1 + tiles + -(-(obs_count - 16) * tiles // 16))],
        scratch_shapes=[pltpu.VMEM((tiles, block, LANES), jnp.float32)],
        compiler_params=params,
        name="residual",
    )(me, prior, *parts)

    msg = msg[0]
    mate = swap(msg, 0)
    border = [(i, i + 1) for i in range(1, count - 1, 2)]
    across = lax.ppermute(msg, "rows", border + [(target, source) for source, target in border])
    far = lax.ppermute(first, "rows", [(i + 2, i) for i in range(1, count - 2, 2)])
    beside = lax.ppermute(across[: 1 + 2 * tiles], "rows", [(i + 1, i) for i in range(0, count, 2)])
    zero, one, two, gram = pl.pallas_call(
        functools.partial(krylov_kernel, total_rows=total_rows, rows_here=rows_here),
        in_specs=[smem, vmem, vmem, vmem],
        out_specs=[vmem] * 4,
        out_shape=[f32(obs_count, rows_here, cols)] * 3 + [f32(8, LANES)],
        scratch_shapes=[pltpu.VMEM((tiles, ENTRIES * 8, LANES), jnp.float32)],
        compiler_params=params,
        name="krylov",
    )(me, own, mate, across)

    grams = [
        pl.pallas_call(
            far_kernel, in_specs=[smem] + [vmem] * 4, out_specs=vmem, out_shape=f32(8, LANES), compiler_params=params, name="far"
        )(me, gram, two, beside, far)
    ]
    for bit in range(0, count.bit_length() - 1, 2):
        masks = [mask << bit for mask in (1, 2, 3) if mask << bit < count]
        gram = sum(grams[1:], grams[0])
        grams = [gram] + [flip(gram, mask) for mask in masks]
    out = pl.pallas_call(
        combine_kernel,
        in_specs=[vmem] * (len(grams) + 4),
        out_specs=vmem,
        out_shape=f32(obs_count, rows_here, cols),
        compiler_params=params,
        name="combine",
    )(*grams, prior, zero, one, two)
    return jnp.transpose(out, (1, 0, 2))


def solution(mesh):
    return jax.shard_map(
        on_device,
        mesh=mesh,
        in_specs=(
            P("rows", None, None, "tiles"),
            P("rows", None, "tiles"),
            P("rows", None, None, "tiles"),
            P(),
            P(),
            P(),
            P("rows", None, "tiles"),
        ),
        out_specs=P("rows", None, "tiles"),
        check_vma=False,
    )
```

```python
import functools
import math

import jax
import jax.numpy as jnp
from jax import lax
from jax.experimental import pallas as pl
from jax.experimental.pallas import tpu as pltpu
from jax.sharding import PartitionSpec as P

TO_RADIAN = math.pi / 18000.0
PRIOR_PULL = 0.1
SMOOTH_PULL = 0.5
SHIFT = 3.0
GAIN = 0.4
ENTRIES = 24
LANES = 128
QUANT = 32000.0
GROUP = LANES // 4
CHUNKS = 2


R_POLY = (0.9428089773, 0.04714460664, 0.007527079489, 0.001965302741, 9.052799897e-05, 0.0004621408027)
S_POLY = (0.6002109608, -0.09003726006, -0.007977343822, -0.001801806492, 3.702625389e-06, -0.0003981650976)
SIN_25 = (0.9999999567, -0.1666626093, 0.008276695349)
COS_25 = (0.9999999997, -0.4999999562, 0.04166553086, -0.001379415437)
SIN_15 = (0.999999998, -0.1666661418, 0.008312938059)
COS_15 = (0.9999999858, -0.4999963087, 0.04152366947)
SIN_90 = (0.9999999947, -0.1666665666, 0.008333024663, -0.00019807389, 2.601844464e-06)


def horner(coefs, x):
    acc = coefs[-1] * x + coefs[-2]
    for coef in coefs[-3::-1]:
        acc = acc * x + coef
    return acc


def of_degrees(coefs, x, x2, factor, odd):
    scaled = [factor * coef * TO_RADIAN ** (2 * k + odd) for k, coef in enumerate(coefs)]
    value = horner(scaled, x2)
    return value * x if odd else value


def ross_li(sun, view, azim):
    x = (sun - 4500).astype(jnp.float32)
    x2 = x * x
    half = math.sqrt(0.5)
    sin_x, cos_x = of_degrees(SIN_25, x, x2, half, 1), of_degrees(COS_25, x, x2, half, 0)
    cos_sun, sin_sun = cos_x - sin_x, cos_x + sin_x
    v = view.astype(jnp.float32)
    v2 = v * v
    sin_view, cos_view = of_degrees(SIN_15, v, v2, 1.0, 1), of_degrees(COS_15, v, v2, 1.0, 0)
    a = (9000 - azim).astype(jnp.float32)
    cos_azim = of_degrees(SIN_90, a, a * a, 1.0, 1)
    prod = cos_sun * cos_view
    cos_phase = prod + sin_sun * sin_view * cos_azim
    total = cos_sun + cos_view
    recip = pl.reciprocal(total * prod, approx=False)
    inv_total = recip * prod
    sec_prod = recip * total
    u = 1.0 - cos_phase
    u_up = 1.0 + cos_phase
    bent = u * (u * lax.rsqrt(u)) * horner(R_POLY, u)
    volume = (bent + (0.5 * math.pi) * cos_phase) * inv_total - 0.25 * math.pi
    sin2 = u * u_up
    sin_phase = sin2 * lax.rsqrt(sin2)
    w = jnp.maximum(1.0 - (2.0 * inv_total) * sin_phase, 1e-30)
    overlap = w * (w * lax.rsqrt(w)) * horner(S_POLY, w)
    geometric = sec_prod * (total * (overlap - 1.0) + 0.5 * u_up)
    return volume, geometric


def lane_group(shape):
    return lax.broadcasted_iota(jnp.int32, shape, len(shape) - 1) // GROUP


def pack(tiles, msg_ref, block):
    rows = tiles[0].shape[0]
    top = jnp.abs(tiles[0])
    for tile in tiles[1:]:
        top = jnp.maximum(top, jnp.abs(tile))
    for shift in (LANES // 2, LANES // 4):
        top = jnp.maximum(top, pltpu.roll(top, shift, axis=1))
    level = jnp.ceil(8.0 * jnp.log2(jnp.maximum(top, 1e-30)))
    factor = QUANT * jnp.exp2(-0.125 * level)
    group = lane_group((16, LANES))
    scales = level[0:16]
    for t in range(1, rows // 16):
        scales = jnp.where(group == t, level[16 * t : 16 * t + 16], scales)
    scales = scales.astype(jnp.int32).astype(jnp.int16)
    msg_ref[block, 0] = scales
    numbers = [jnp.round(tile * factor).astype(jnp.int32) for tile in tiles]
    for c, number in enumerate(numbers):
        coded = number.astype(jnp.int16)
        for t in range(rows // 16):
            msg_ref[block, 1 + t * len(tiles) + c] = coded[16 * t : 16 * t + 16]
    return scales, numbers


def as_float(x):
    return x.astype(jnp.int32).astype(jnp.float32)


def factors_of(scales, row_tiles):
    scales = as_float(scales)
    group = lane_group((16, LANES))
    factors = []
    for t in range(row_tiles):
        level = jnp.where(group == t, scales, 0.0)
        for shift in (LANES // 2, LANES // 4):
            level = level + pltpu.roll(level, shift, axis=1)
        factors.append(jnp.exp2(0.125 * level) * (1.0 / QUANT))
    return factors


def unpack(read, row_tiles, col_tiles):
    factors = factors_of(read(0), row_tiles)
    return [
        jnp.concatenate([as_float(read(1 + t * col_tiles + c)) * factors[t] for t in range(row_tiles)], axis=0) for c in range(col_tiles)
    ]


def sums_kernel(
    me_ref,
    ids_ref,
    gain_ref,
    weight_ref,
    reflect_hbm,
    conf_hbm,
    sun_hbm,
    prior_ref,
    keep_ref,
    msg_ref,
    sums_ref,
    kernels_ref,
    reflect_ref,
    conf_ref,
    sun_ref,
    sems,
    *,
    scale,
    rows_here,
    first_col,
):
    steps, dates, bands, tile_rows, _ = reflect_ref.shape
    lane_tiles = sums_ref.shape[0]
    me = me_ref[0]
    block = rows_here * ENTRIES
    obs_count = 3 * bands

    def copies(step):
        rows = pl.ds(pl.multiple_of(step // lane_tiles * tile_rows, tile_rows), tile_rows)
        cols = pl.ds(pl.multiple_of(first_col + step % lane_tiles * LANES, LANES), LANES)
        return (
            pltpu.make_async_copy(sun_hbm.at[:, :, rows, cols], sun_ref.at[step], sems.at[step, 0]),
            pltpu.make_async_copy(conf_hbm.at[:, rows, cols], conf_ref.at[step], sems.at[step, 1]),
            pltpu.make_async_copy(reflect_hbm.at[:, :, rows, cols], reflect_ref.at[step], sems.at[step, 2]),
        )

    def start(step, carry):
        for copy in copies(step):
            copy.start()
        return carry

    lax.fori_loop(0, steps, start, 0)

    def lane_tile(index, row_tile):
        step = row_tile * lane_tiles + index
        for copy in copies(step):
            copy.wait()
        sensors = [ids_ref[me * dates + d] for d in range(dates)]

        def store(top, entry, total):
            sums_ref[index, pl.ds(top * ENTRIES + entry, 8, stride=ENTRIES), :] = total

        def plus(total, term):
            return term if total is None else total + term

        for top in range(0, tile_rows, 8):
            here = slice(top, top + 8)
            normal = [None] * 6
            for d in range(dates):
                volume, geometric = ross_li(*[sun_ref[step, d, angle, here, :] for angle in range(3)])
                weight = conf_ref[step, d, here, :].astype(jnp.float32) * (weight_ref[sensors[d]] * scale)
                weighted_vol = weight * volume
                weighted_geo = weight * geometric
                for i, value in enumerate((weight, weighted_vol, weighted_geo)):
                    kernels_ref[d, i, here, :] = value
                terms = (weight, weighted_vol, weighted_geo, weighted_vol * volume, weighted_vol * geometric, weighted_geo * geometric)
                normal = [plus(total, term) for total, term in zip(normal, terms)]
            for k in range(6):
                store(top, obs_count + k, normal[k])
        for b in range(bands):
            observed = [None] * 3
            for d in range(dates):
                signal = reflect_ref[step, d, b].astype(jnp.float32) * gain_ref[sensors[d], b]
                observed = [plus(total, kernels_ref[d, i] * signal) for i, total in enumerate(observed)]
            for i in range(3):
                for top in range(0, tile_rows, 8):
                    store(top, 3 * b + i, observed[i][top : top + 8])
        return row_tile

    def row_tile_sums(row_tile, carry):
        lax.fori_loop(0, lane_tiles, lane_tile, row_tile)
        tiles = range(lane_tiles)
        first_row = row_tile * tile_rows
        for row, source in ((me * rows_here - 1 - first_row, 0), ((me + 1) * rows_here - first_row, rows_here - 1)):

            @pl.when((row >= 0) & (row < tile_rows))
            def _():
                for c in tiles:
                    lanes = slice(c * LANES, (c + 1) * LANES)
                    at = pl.ds(pl.multiple_of(row * ENTRIES, 8), obs_count)
                    part = jnp.concatenate([prior_ref[e, source : source + 1, lanes] for e in range(obs_count)], axis=0)
                    sums_ref[c, at, :] = sums_ref[c, at, :] + SMOOTH_PULL * part

        bit = me % 2
        per_tile = tile_rows // rows_here // 2
        for j in range(per_tile):
            own = pl.ds(pl.multiple_of((2 * j + bit) * block, 8), block)
            other = pl.ds(pl.multiple_of((2 * j + 1 - bit) * block, 8), block)
            for c in tiles:
                keep_ref[row_tile * per_tile + j, :, c * LANES : (c + 1) * LANES] = sums_ref[c, own, :]
            pack([sums_ref[c, other, :] for c in tiles], msg_ref, row_tile * per_tile + j)
        return carry

    lax.fori_loop(0, steps // lane_tiles, row_tile_sums, 0)


def partial_sums(me, reflect, clear_conf, sun_view, sensor_id, band_gain, sensor_weight, prior, scale, chunk):
    dates, bands, rows, cols = reflect.shape
    cols = cols // CHUNKS
    rows_here = prior.shape[1]
    count = rows // rows_here
    tile_rows = 16
    block = rows_here * ENTRIES
    lane_tiles = cols // LANES
    steps = rows // tile_rows * lane_tiles
    smem = pl.BlockSpec(memory_space=pltpu.SMEM)
    vmem = pl.BlockSpec(memory_space=pltpu.VMEM)
    hbm = pl.BlockSpec(memory_space=pl.ANY)
    return pl.pallas_call(
        functools.partial(sums_kernel, scale=scale, rows_here=rows_here, first_col=chunk * cols),
        grid=(1,),
        in_specs=[smem] * 4 + [hbm] * 3 + [pl.BlockSpec((3 * bands, rows_here, cols), lambda i: (0, 0, chunk))],
        out_specs=[vmem, vmem],
        out_shape=[
            jax.ShapeDtypeStruct((count // 2, block, cols), jnp.float32),
            jax.ShapeDtypeStruct((count // 2, 1 + block // 16 * lane_tiles, 16, LANES), jnp.int16),
        ],
        scratch_shapes=[
            pltpu.VMEM((lane_tiles, tile_rows * ENTRIES, LANES), jnp.float32),
            pltpu.VMEM((dates, 3, tile_rows, LANES), jnp.float32),
            pltpu.VMEM((steps, dates, bands, tile_rows, LANES), reflect.dtype),
            pltpu.VMEM((steps, dates, tile_rows, LANES), jnp.int32),
            pltpu.VMEM((steps, dates, 3, tile_rows, LANES), jnp.int32),
            pltpu.SemaphoreType.DMA((steps, 3)),
        ],
        compiler_params=pltpu.CompilerParams(vmem_limit_bytes=(62 if chunk == 0 else 52) * 2**20),
        name="partial_sums",
    )(me, sensor_id, band_gain, sensor_weight, reflect, clear_conf, sun_view, prior)


def add_split_kernel(bit_ref, *refs, place):
    *parts, keep_ref, msg_ref = refs
    count, block, _ = keep_ref.shape
    bit = bit_ref[0]

    def total(j):
        tiles = []
        for kept_ref, got_ref in zip(parts[0::2], parts[1::2]):
            here = kept_ref.shape[2] // LANES
            came = unpack(lambda at: got_ref[j, at], block // 16, here)
            tiles += [kept_ref[j, :, c * LANES : (c + 1) * LANES] + came[c] for c in range(here)]
        return tiles

    for q in range(count):
        low = q % 2**place
        first = (q - low) * 2 + low
        pack(total(first + (1 - bit) * 2**place), msg_ref, q)
        for c, tile in enumerate(total(first + bit * 2**place)):
            keep_ref[q, :, c * LANES : (c + 1) * LANES] = tile


def add_split(bit, place, *parts):
    count, block, _ = parts[0].shape
    cols = sum(kept.shape[2] for kept in parts[0::2])
    vmem = pl.BlockSpec(memory_space=pltpu.VMEM)
    return pl.pallas_call(
        functools.partial(add_split_kernel, place=place),
        in_specs=[pl.BlockSpec(memory_space=pltpu.SMEM)] + [vmem] * len(parts),
        out_specs=[vmem, vmem],
        out_shape=[
            jax.ShapeDtypeStruct((count // 2, block, cols), jnp.float32),
            jax.ShapeDtypeStruct((count // 2, 1 + block // 16 * (cols // LANES), 16, LANES), jnp.int16),
        ],
        compiler_params=pltpu.CompilerParams(vmem_limit_bytes=24 * 2**20),
        name="add_split",
    )(bit, *parts)


def take(ref, start, size, stride):
    at = pl.ds(start, size, stride=stride)
    return jnp.concatenate([ref[c, at, :] for c in range(ref.shape[0])], axis=1)


def put(ref, start, size, stride, value):
    at = pl.ds(start, size, stride=stride)
    for c in range(ref.shape[0]):
        ref[c, at, :] = value[:, c * LANES : (c + 1) * LANES]


def beside_columns(x):
    cols = x.shape[1]
    col = lax.broadcasted_iota(jnp.int32, x.shape, 1)
    left = jnp.where(col == 0, 0.0, pltpu.roll(x, 1, axis=1))
    right = jnp.where(col == cols - 1, 0.0, pltpu.roll(x, cols - 1, axis=1))
    return left + right


def degree_of(row, shape, total_rows):
    col = lax.broadcasted_iota(jnp.int32, shape, 1)
    edge = (
        (row == 0).astype(jnp.float32)
        + (row == total_rows - 1).astype(jnp.float32)
        + (col == 0).astype(jnp.float32)
        + (col == shape[1] - 1).astype(jnp.float32)
    )
    return 4.0 - edge


def couple(n, v):
    return (
        n[0] * v[0] + n[1] * v[1] + n[2] * v[2],
        n[1] * v[0] + n[3] * v[1] + n[4] * v[2],
        n[2] * v[0] + n[4] * v[1] + n[5] * v[2],
    )


def residual_kernel(me_ref, prior_ref, *refs, total_rows):
    obs_count, rows_here, cols = prior_ref.shape
    *parts, out_ref, msg_ref, first_ref, sums_ref = refs
    block = rows_here * ENTRIES
    tiles = cols // LANES
    at = 0
    for kept_ref, got_ref in zip(parts[0::2], parts[1::2]):
        here = kept_ref.shape[2] // LANES
        came = unpack(lambda place: got_ref[0, place], block // 16, here)
        for c in range(here):
            sums_ref[at] = kept_ref[0, :, c * LANES : (c + 1) * LANES] + came[c]
            at += 1
    shape = (rows_here, cols)
    row = me_ref[0] * rows_here + lax.broadcasted_iota(jnp.int32, shape, 0)
    degree = degree_of(row, shape, total_rows)
    normal = [take(sums_ref, obs_count + k, rows_here, ENTRIES) for k in range(6)]
    for b in range(obs_count // 3):
        fields = [prior_ref[3 * b + i] for i in range(3)]
        coupled = couple(normal, fields)
        for i in range(3):
            field = fields[i]
            beside = beside_columns(field)
            if rows_here > 1:
                zero = jnp.zeros((1, cols), jnp.float32)
                beside = beside + jnp.concatenate([zero, field[:-1]], axis=0) + jnp.concatenate([field[1:], zero], axis=0)
            entry = 3 * b + i
            observed = take(sums_ref, entry, rows_here, ENTRIES)
            put(sums_ref, entry, rows_here, ENTRIES, observed - coupled[i] - SMOOTH_PULL * (degree * field - beside))
    for c in range(tiles):
        out_ref[:, c * LANES : (c + 1) * LANES] = sums_ref[c]
    scales, numbers = pack([sums_ref[c] for c in range(tiles)], msg_ref, 0)
    first_ref[0] = scales
    for c in range(tiles):
        first_ref[1 + c] = numbers[c][0:16].astype(jnp.int16)
    left = jnp.concatenate([number[16:obs_count] for number in numbers], axis=0)
    spare = (first_ref.shape[0] - 1 - tiles) * 16 - left.shape[0]
    if spare:
        left = jnp.concatenate([left, jnp.zeros((spare, LANES), jnp.int32)], axis=0)
    for t in range(left.shape[0] // 16):
        first_ref[1 + tiles + t] = left[16 * t : 16 * t + 16].astype(jnp.int16)


def krylov_kernel(me_ref, own_ref, mate_ref, across_ref, zero_ref, one_ref, two_ref, gram_ref, window_ref, *, total_rows, rows_here):
    cols = own_ref.shape[1]
    obs_count = ENTRIES - 6
    tiles = cols // LANES
    row_tiles = own_ref.shape[0] // 16

    def lay(place, part, r):
        at = pl.ds(place, ENTRIES, stride=8)
        for c in range(tiles):
            window_ref[c, at, :] = part[c][r * ENTRIES : (r + 1) * ENTRIES]

    own = [own_ref[:, c * LANES : (c + 1) * LANES] for c in range(tiles)]
    mate = unpack(lambda place: mate_ref[place], row_tiles, tiles)
    across = unpack(lambda place: across_ref[place], row_tiles, tiles)
    odd = me_ref[0] % 2
    for r in range(2):
        lay(2 + r, own, r)
        lay(4 * (1 - odd) + r, mate, r)
        lay(4 * odd + r, across, r)
    for empty in (6, 7):
        put(window_ref, empty, ENTRIES, 8, jnp.zeros((ENTRIES, cols), jnp.float32))
    window = lambda entry: jnp.concatenate([window_ref[c, entry * 8 : entry * 8 + 8, :] for c in range(cols // LANES)], axis=1)
    shape = (8, cols)
    place = lax.broadcasted_iota(jnp.int32, shape, 0)
    row = me_ref[0] * rows_here + place - 2
    inside = ((row >= 0) & (row < total_rows)).astype(jnp.float32) * GAIN
    own_rows = (place == 2) | (place == 3)
    diag = inside * (PRIOR_PULL - SHIFT + SMOOTH_PULL * degree_of(row, shape, total_rows))
    pull = inside * SMOOTH_PULL
    normal = [window(obs_count + k) * inside for k in range(6)]
    acc = [jnp.zeros((8, LANES), jnp.float32) for _ in range(6)]

    def apply(v, last=False):
        coupled = couple(normal, v)
        out = []
        for i in range(3):
            x = v[i]
            above = pltpu.roll(x, 7, axis=0)
            beside = beside_columns(x) + (2.0 * above if last else above + pltpu.roll(x, 1, axis=0))
            out.append(coupled[i] + diag * x - pull * beside)
        return out

    def fold(x):
        total = x[:, 0:LANES]
        for c in range(LANES, cols, LANES):
            total = total + x[:, c : c + LANES]
        return total

    for b in range(obs_count // 3):
        zero = [window(3 * b + i) for i in range(3)]
        one = apply(zero)
        two = apply(one)
        three = apply(two, last=True)
        for i in range(3):
            zero_ref[3 * b + i] = zero[i][2:4]
            one_ref[3 * b + i] = one[i][2:4]
            two_ref[3 * b + i] = two[i][2:4]
            v = [zero[i], one[i], two[i], three[i]]
            for k in range(6):
                acc[k] = acc[k] + fold(v[k // 2] * v[(k + 1) // 2])
    own_tile = own_rows[:, 0:LANES]
    tile_row = lax.broadcasted_iota(jnp.int32, (8, LANES), 0)
    gram = jnp.zeros((8, LANES), jnp.float32)
    for k in range(6):
        moment = jnp.sum(jnp.where(own_tile, acc[k], 0.0))
        gram = jnp.where(tile_row == k, moment, gram)
    gram_ref[...] = gram


def far_kernel(gram_ref, two_ref, far_ref, out_ref):
    obs_count, _, cols = two_ref.shape
    tiles = cols // LANES
    rest = obs_count - 16
    factors = factors_of(far_ref[0], 2)
    left = jnp.concatenate([as_float(far_ref[t]) for t in range(1 + tiles, far_ref.shape[0])], axis=0)
    total = jnp.zeros((obs_count, LANES), jnp.float32)
    for c in range(tiles):
        far = jnp.concatenate([as_float(far_ref[1 + c]) * factors[0], left[rest * c : rest * (c + 1)] * factors[1][0:rest]], axis=0)
        mine = jnp.concatenate([two_ref[e, 1:2, c * LANES : (c + 1) * LANES] for e in range(obs_count)], axis=0)
        total = total + far * mine
    part = (-2.0 * (GAIN * SMOOTH_PULL) ** 3) * jnp.sum(total)
    row = lax.broadcasted_iota(jnp.int32, (8, LANES), 0)
    out_ref[...] = gram_ref[...] + jnp.where(row == 5, part, 0.0)


def combine_kernel(gram_ref, prior_ref, zero_ref, one_ref, two_ref, out_ref):
    gram = gram_ref[0]
    for k in range(1, gram_ref.shape[0]):
        gram = gram + gram_ref[k]
    m = [gram[k : k + 1, :] for k in range(6)]
    h = {(i, j): m[i + j + 1] * (1.0 / GAIN) + SHIFT * m[i + j] for i in range(3) for j in range(i, 3)}
    l10 = h[0, 1] / h[0, 0]
    l20 = h[0, 2] / h[0, 0]
    d1 = h[1, 1] - l10 * h[0, 1]
    t = h[1, 2] - l20 * h[0, 1]
    ok1 = d1 > 1e-6 * h[1, 1]
    inv1 = jnp.where(ok1, 1.0 / jnp.where(ok1, d1, 1.0), 0.0)
    l21 = t * inv1
    d2 = h[2, 2] - l20 * h[0, 2] - l21 * t
    ok2 = ok1 & (d2 > 1e-6 * h[2, 2])
    inv2 = jnp.where(ok2, 1.0 / jnp.where(ok2, d2, 1.0), 0.0)
    z1 = m[1] - l10 * m[0]
    z2 = m[2] - l20 * m[0] - l21 * z1
    y2 = z2 * inv2
    y1 = z1 * inv1 - l21 * y2
    y0 = m[0] / h[0, 0] - l10 * y1 - l20 * y2
    cols = prior_ref.shape[2]
    for c in range(0, cols, LANES):
        lanes = slice(c, c + LANES)
        out_ref[:, :, lanes] = (
            prior_ref[:, :, lanes] + y0[None] * zero_ref[:, :, lanes] + y1[None] * one_ref[:, :, lanes] + y2[None] * two_ref[:, :, lanes]
        )


def on_device(reflect, clear_conf, sun_view, sensor_id, band_gain, sensor_weight, prior):
    rows_here, obs_count, cols = prior.shape
    prior = jnp.transpose(prior, (1, 0, 2))
    count = lax.axis_size("rows")
    total_rows = rows_here * count
    block = rows_here * ENTRIES
    tiles = cols // LANES
    me = lax.axis_index("rows").astype(jnp.int32).reshape(1)
    vmem = pl.BlockSpec(memory_space=pltpu.VMEM)
    smem = pl.BlockSpec(memory_space=pltpu.SMEM)
    params = pltpu.CompilerParams(vmem_limit_bytes=24 * 2**20)
    f32 = lambda *shape: jax.ShapeDtypeStruct(shape, jnp.float32)
    packed = lambda *shape: jax.ShapeDtypeStruct(shape + (16, LANES), jnp.int16)

    scale = 0.01 / (reflect.shape[0] * count)
    index = me
    parts = []
    for chunk in range(CHUNKS):
        kept, sent = partial_sums(
            index, reflect, clear_conf, sun_view, sensor_id, band_gain, sensor_weight, prior, scale, chunk
        )
        index, _ = lax.optimization_barrier((me, sent))
        parts.append((kept, sent))
    flip = lambda x, mask: lax.ppermute(x, "rows", [(i, i ^ mask) for i in range(count)])
    swap = lambda x, bit: flip(x, 1 << bit)
    parts = [(kept, swap(sent, 0)) for kept, sent in parts]
    bits = list(range(1, count.bit_length() - 1))
    for step in range(len(bits)):
        for chunk in range(CHUNKS):
            turned = chunk % 2 == 1 and len(bits) >= 2 and step < 2
            bit, place = (bits[1 - step], 1 - step) if turned else (bits[step], 0)
            kept, sent = add_split(me // 2**bit % 2, place, *parts[chunk])
            parts[chunk] = (kept, swap(sent, bit))
    parts = [x for part in parts for x in part]

    own, msg, first = pl.pallas_call(
        functools.partial(residual_kernel, total_rows=total_rows),
        in_specs=[smem] + [vmem] * (1 + len(parts)),
        out_specs=[vmem, vmem, vmem],
        out_shape=[f32(block, cols), packed(1, 1 + block // 16 * tiles), packed(1 + tiles + -(-(obs_count - 16) * tiles // 16))],
        scratch_shapes=[pltpu.VMEM((tiles, block, LANES), jnp.float32)],
        compiler_params=params,
        name="residual",
    )(me, prior, *parts)

    msg = msg[0]
    mate = swap(msg, 0)
    border = [(i, i + 1) for i in range(1, count - 1, 2)]
    across = lax.ppermute(msg, "rows", border + [(target, source) for source, target in border])
    far = lax.ppermute(first, "rows", [(i + 2, i) for i in range(count - 2)])
    zero, one, two, gram = pl.pallas_call(
        functools.partial(krylov_kernel, total_rows=total_rows, rows_here=rows_here),
        in_specs=[smem, vmem, vmem, vmem],
        out_specs=[vmem] * 4,
        out_shape=[f32(obs_count, rows_here, cols)] * 3 + [f32(8, LANES)],
        scratch_shapes=[pltpu.VMEM((tiles, ENTRIES * 8, LANES), jnp.float32)],
        compiler_params=params,
        name="krylov",
    )(me, own, mate, across)

    gram = pl.pallas_call(
        far_kernel, in_specs=[vmem] * 3, out_specs=vmem, out_shape=f32(8, LANES), compiler_params=params, name="far"
    )(gram, two, far)
    grams = lax.all_to_all(jnp.broadcast_to(gram[None], (count, 8, LANES)), "rows", 0, 0)
    out = pl.pallas_call(
        combine_kernel,
        in_specs=[vmem] * 5,
        out_specs=vmem,
        out_shape=f32(obs_count, rows_here, cols),
        compiler_params=params,
        name="combine",
    )(grams, prior, zero, one, two)
    return jnp.transpose(out, (1, 0, 2))


def solution(mesh):
    return jax.shard_map(
        on_device,
        mesh=mesh,
        in_specs=(
            P("rows", None, None, "tiles"),
            P("rows", None, "tiles"),
            P("rows", None, None, "tiles"),
            P(),
            P(),
            P(),
            P("rows", None, "tiles"),
        ),
        out_specs=P("rows", None, "tiles"),
        check_vma=False,
    )
```

```python
import functools
import math

import jax
import jax.numpy as jnp
from jax import lax
from jax.experimental import pallas as pl
from jax.experimental.pallas import tpu as pltpu
from jax.sharding import PartitionSpec as P

TO_RADIAN = math.pi / 18000.0
PRIOR_PULL = 0.1
SMOOTH_PULL = 0.5
SHIFT = 3.0
GAIN = 0.4
ENTRIES = 24
LANES = 128
QUANT = 32000.0
GROUP = LANES // 4
CHUNKS = 2


R_POLY = (0.9428089773, 0.04714460664, 0.007527079489, 0.001965302741, 9.052799897e-05, 0.0004621408027)
S_POLY = (0.6002109608, -0.09003726006, -0.007977343822, -0.001801806492, 3.702625389e-06, -0.0003981650976)
SIN_25 = (0.9999999567, -0.1666626093, 0.008276695349)
COS_25 = (0.9999999997, -0.4999999562, 0.04166553086, -0.001379415437)
SIN_15 = (0.999999998, -0.1666661418, 0.008312938059)
COS_15 = (0.9999999858, -0.4999963087, 0.04152366947)
SIN_90 = (0.9999999947, -0.1666665666, 0.008333024663, -0.00019807389, 2.601844464e-06)


def horner(coefs, x):
    acc = coefs[-1] * x + coefs[-2]
    for coef in coefs[-3::-1]:
        acc = acc * x + coef
    return acc


def of_degrees(coefs, x, x2, factor, odd):
    scaled = [factor * coef * TO_RADIAN ** (2 * k + odd) for k, coef in enumerate(coefs)]
    value = horner(scaled, x2)
    return value * x if odd else value


def ross_li(sun, view, azim):
    x = (sun - 4500).astype(jnp.float32)
    x2 = x * x
    half = math.sqrt(0.5)
    sin_x, cos_x = of_degrees(SIN_25, x, x2, half, 1), of_degrees(COS_25, x, x2, half, 0)
    cos_sun, sin_sun = cos_x - sin_x, cos_x + sin_x
    v = view.astype(jnp.float32)
    v2 = v * v
    sin_view, cos_view = of_degrees(SIN_15, v, v2, 1.0, 1), of_degrees(COS_15, v, v2, 1.0, 0)
    a = (9000 - azim).astype(jnp.float32)
    cos_azim = of_degrees(SIN_90, a, a * a, 1.0, 1)
    prod = cos_sun * cos_view
    cos_phase = prod + sin_sun * sin_view * cos_azim
    total = cos_sun + cos_view
    recip = pl.reciprocal(total * prod, approx=False)
    inv_total = recip * prod
    sec_prod = recip * total
    u = 1.0 - cos_phase
    u_up = 1.0 + cos_phase
    bent = u * (u * lax.rsqrt(u)) * horner(R_POLY, u)
    volume = (bent + (0.5 * math.pi) * cos_phase) * inv_total - 0.25 * math.pi
    sin2 = u * u_up
    sin_phase = sin2 * lax.rsqrt(sin2)
    w = jnp.maximum(1.0 - (2.0 * inv_total) * sin_phase, 1e-30)
    overlap = w * (w * lax.rsqrt(w)) * horner(S_POLY, w)
    geometric = sec_prod * (total * (overlap - 1.0) + 0.5 * u_up)
    return volume, geometric


def lane_group(shape):
    return lax.broadcasted_iota(jnp.int32, shape, len(shape) - 1) // GROUP


def pack(tiles, msg_ref, block):
    rows = tiles[0].shape[0]
    top = jnp.abs(tiles[0])
    for tile in tiles[1:]:
        top = jnp.maximum(top, jnp.abs(tile))
    for shift in (LANES // 2, LANES // 4):
        top = jnp.maximum(top, pltpu.roll(top, shift, axis=1))
    level = jnp.ceil(8.0 * jnp.log2(jnp.maximum(top, 1e-30)))
    factor = QUANT * jnp.exp2(-0.125 * level)
    group = lane_group((16, LANES))
    scales = level[0:16]
    for t in range(1, rows // 16):
        scales = jnp.where(group == t, level[16 * t : 16 * t + 16], scales)
    scales = scales.astype(jnp.int32).astype(jnp.int16)
    msg_ref[block, 0] = scales
    numbers = [jnp.round(tile * factor).astype(jnp.int32) for tile in tiles]
    for c, number in enumerate(numbers):
        coded = number.astype(jnp.int16)
        for t in range(rows // 16):
            msg_ref[block, 1 + t * len(tiles) + c] = coded[16 * t : 16 * t + 16]
    return scales, numbers


def as_float(x):
    return x.astype(jnp.int32).astype(jnp.float32)


def factors_of(scales, row_tiles):
    scales = as_float(scales)
    group = lane_group((16, LANES))
    factors = []
    for t in range(row_tiles):
        level = jnp.where(group == t, scales, 0.0)
        for shift in (LANES // 2, LANES // 4):
            level = level + pltpu.roll(level, shift, axis=1)
        factors.append(jnp.exp2(0.125 * level) * (1.0 / QUANT))
    return factors


def unpack(read, row_tiles, col_tiles):
    factors = factors_of(read(0), row_tiles)
    return [
        jnp.concatenate([as_float(read(1 + t * col_tiles + c)) * factors[t] for t in range(row_tiles)], axis=0) for c in range(col_tiles)
    ]


def sums_kernel(
    me_ref,
    ids_ref,
    gain_ref,
    weight_ref,
    reflect_hbm,
    conf_hbm,
    sun_hbm,
    prior_ref,
    keep_ref,
    msg_ref,
    sums_ref,
    kernels_ref,
    reflect_ref,
    conf_ref,
    sun_ref,
    sems,
    *,
    scale,
    rows_here,
    first_col,
):
    steps, dates, bands, tile_rows, _ = reflect_ref.shape
    lane_tiles = sums_ref.shape[0]
    me = me_ref[0]
    block = rows_here * ENTRIES
    obs_count = 3 * bands

    def copies(step):
        rows = pl.ds(pl.multiple_of(step // lane_tiles * tile_rows, tile_rows), tile_rows)
        cols = pl.ds(pl.multiple_of(first_col + step % lane_tiles * LANES, LANES), LANES)
        return (
            pltpu.make_async_copy(sun_hbm.at[:, :, rows, cols], sun_ref.at[step], sems.at[step, 0]),
            pltpu.make_async_copy(conf_hbm.at[:, rows, cols], conf_ref.at[step], sems.at[step, 1]),
            pltpu.make_async_copy(reflect_hbm.at[:, :, rows, cols], reflect_ref.at[step], sems.at[step, 2]),
        )

    def start(step, carry):
        for copy in copies(step):
            copy.start()
        return carry

    lax.fori_loop(0, steps, start, 0)

    def lane_tile(index, row_tile):
        step = row_tile * lane_tiles + index
        for copy in copies(step):
            copy.wait()
        sensors = [ids_ref[me * dates + d] for d in range(dates)]

        def store(top, entry, total):
            sums_ref[index, pl.ds(top * ENTRIES + entry, 8, stride=ENTRIES), :] = total

        def plus(total, term):
            return term if total is None else total + term

        for top in range(0, tile_rows, 8):
            here = slice(top, top + 8)
            normal = [None] * 6
            for d in range(dates):
                volume, geometric = ross_li(*[sun_ref[step, d, angle, here, :] for angle in range(3)])
                weight = conf_ref[step, d, here, :].astype(jnp.float32) * (weight_ref[sensors[d]] * scale)
                weighted_vol = weight * volume
                weighted_geo = weight * geometric
                for i, value in enumerate((weight, weighted_vol, weighted_geo)):
                    kernels_ref[d, i, here, :] = value
                terms = (weight, weighted_vol, weighted_geo, weighted_vol * volume, weighted_vol * geometric, weighted_geo * geometric)
                normal = [plus(total, term) for total, term in zip(normal, terms)]
            for k in range(6):
                store(top, obs_count + k, normal[k])
        for b in range(bands):
            observed = [None] * 3
            for d in range(dates):
                signal = reflect_ref[step, d, b].astype(jnp.float32) * gain_ref[sensors[d], b]
                observed = [plus(total, kernels_ref[d, i] * signal) for i, total in enumerate(observed)]
            for i in range(3):
                for top in range(0, tile_rows, 8):
                    store(top, 3 * b + i, observed[i][top : top + 8])
        return row_tile

    def row_tile_sums(row_tile, carry):
        lax.fori_loop(0, lane_tiles, lane_tile, row_tile)
        tiles = range(lane_tiles)
        first_row = row_tile * tile_rows
        for row, source in ((me * rows_here - 1 - first_row, 0), ((me + 1) * rows_here - first_row, rows_here - 1)):

            @pl.when((row >= 0) & (row < tile_rows))
            def _():
                for c in tiles:
                    lanes = slice(c * LANES, (c + 1) * LANES)
                    at = pl.ds(pl.multiple_of(row * ENTRIES, 8), obs_count)
                    part = jnp.concatenate([prior_ref[e, source : source + 1, lanes] for e in range(obs_count)], axis=0)
                    sums_ref[c, at, :] = sums_ref[c, at, :] + SMOOTH_PULL * part

        bit = me % 2
        per_tile = tile_rows // rows_here // 2
        for j in range(per_tile):
            own = pl.ds(pl.multiple_of((2 * j + bit) * block, 8), block)
            other = pl.ds(pl.multiple_of((2 * j + 1 - bit) * block, 8), block)
            for c in tiles:
                keep_ref[row_tile * per_tile + j, :, c * LANES : (c + 1) * LANES] = sums_ref[c, own, :]
            pack([sums_ref[c, other, :] for c in tiles], msg_ref, row_tile * per_tile + j)
        return carry

    lax.fori_loop(0, steps // lane_tiles, row_tile_sums, 0)


def partial_sums(me, reflect, clear_conf, sun_view, sensor_id, band_gain, sensor_weight, prior, scale, chunk):
    dates, bands, rows, cols = reflect.shape
    cols = cols // CHUNKS
    rows_here = prior.shape[1]
    count = rows // rows_here
    tile_rows = 16
    block = rows_here * ENTRIES
    lane_tiles = cols // LANES
    steps = rows // tile_rows * lane_tiles
    smem = pl.BlockSpec(memory_space=pltpu.SMEM)
    vmem = pl.BlockSpec(memory_space=pltpu.VMEM)
    hbm = pl.BlockSpec(memory_space=pl.ANY)
    return pl.pallas_call(
        functools.partial(sums_kernel, scale=scale, rows_here=rows_here, first_col=chunk * cols),
        grid=(1,),
        in_specs=[smem] * 4 + [hbm] * 3 + [pl.BlockSpec((3 * bands, rows_here, cols), lambda i: (0, 0, chunk))],
        out_specs=[vmem, vmem],
        out_shape=[
            jax.ShapeDtypeStruct((count // 2, block, cols), jnp.float32),
            jax.ShapeDtypeStruct((count // 2, 1 + block // 16 * lane_tiles, 16, LANES), jnp.int16),
        ],
        scratch_shapes=[
            pltpu.VMEM((lane_tiles, tile_rows * ENTRIES, LANES), jnp.float32),
            pltpu.VMEM((dates, 3, tile_rows, LANES), jnp.float32),
            pltpu.VMEM((steps, dates, bands, tile_rows, LANES), reflect.dtype),
            pltpu.VMEM((steps, dates, tile_rows, LANES), jnp.int32),
            pltpu.VMEM((steps, dates, 3, tile_rows, LANES), jnp.int32),
            pltpu.SemaphoreType.DMA((steps, 3)),
        ],
        compiler_params=pltpu.CompilerParams(vmem_limit_bytes=(62 if chunk == 0 else 52) * 2**20),
        name="partial_sums",
    )(me, sensor_id, band_gain, sensor_weight, reflect, clear_conf, sun_view, prior)


def add_split_kernel(bit_ref, *refs, place):
    *parts, keep_ref, msg_ref = refs
    count, block, _ = keep_ref.shape
    bit = bit_ref[0]

    def total(j):
        tiles = []
        for kept_ref, got_ref in zip(parts[0::2], parts[1::2]):
            here = kept_ref.shape[2] // LANES
            came = unpack(lambda at: got_ref[j, at], block // 16, here)
            tiles += [kept_ref[j, :, c * LANES : (c + 1) * LANES] + came[c] for c in range(here)]
        return tiles

    for q in range(count):
        low = q % 2**place
        first = (q - low) * 2 + low
        pack(total(first + (1 - bit) * 2**place), msg_ref, q)
        for c, tile in enumerate(total(first + bit * 2**place)):
            keep_ref[q, :, c * LANES : (c + 1) * LANES] = tile


def add_split(bit, place, *parts):
    count, block, _ = parts[0].shape
    cols = sum(kept.shape[2] for kept in parts[0::2])
    vmem = pl.BlockSpec(memory_space=pltpu.VMEM)
    return pl.pallas_call(
        functools.partial(add_split_kernel, place=place),
        in_specs=[pl.BlockSpec(memory_space=pltpu.SMEM)] + [vmem] * len(parts),
        out_specs=[vmem, vmem],
        out_shape=[
            jax.ShapeDtypeStruct((count // 2, block, cols), jnp.float32),
            jax.ShapeDtypeStruct((count // 2, 1 + block // 16 * (cols // LANES), 16, LANES), jnp.int16),
        ],
        compiler_params=pltpu.CompilerParams(vmem_limit_bytes=24 * 2**20),
        name="add_split",
    )(bit, *parts)


def take(ref, start, size, stride):
    at = pl.ds(start, size, stride=stride)
    return jnp.concatenate([ref[c, at, :] for c in range(ref.shape[0])], axis=1)


def put(ref, start, size, stride, value):
    at = pl.ds(start, size, stride=stride)
    for c in range(ref.shape[0]):
        ref[c, at, :] = value[:, c * LANES : (c + 1) * LANES]


def beside_columns(x):
    cols = x.shape[1]
    col = lax.broadcasted_iota(jnp.int32, x.shape, 1)
    left = jnp.where(col == 0, 0.0, pltpu.roll(x, 1, axis=1))
    right = jnp.where(col == cols - 1, 0.0, pltpu.roll(x, cols - 1, axis=1))
    return left + right


def degree_of(row, shape, total_rows):
    col = lax.broadcasted_iota(jnp.int32, shape, 1)
    edge = (
        (row == 0).astype(jnp.float32)
        + (row == total_rows - 1).astype(jnp.float32)
        + (col == 0).astype(jnp.float32)
        + (col == shape[1] - 1).astype(jnp.float32)
    )
    return 4.0 - edge


def couple(n, v):
    return (
        n[0] * v[0] + n[1] * v[1] + n[2] * v[2],
        n[1] * v[0] + n[3] * v[1] + n[4] * v[2],
        n[2] * v[0] + n[4] * v[1] + n[5] * v[2],
    )


def residual_kernel(me_ref, prior_ref, *refs, total_rows):
    obs_count, rows_here, cols = prior_ref.shape
    *parts, out_ref, msg_ref, first_ref, sums_ref = refs
    block = rows_here * ENTRIES
    tiles = cols // LANES
    at = 0
    for kept_ref, got_ref in zip(parts[0::2], parts[1::2]):
        here = kept_ref.shape[2] // LANES
        came = unpack(lambda place: got_ref[0, place], block // 16, here)
        for c in range(here):
            sums_ref[at] = kept_ref[0, :, c * LANES : (c + 1) * LANES] + came[c]
            at += 1
    shape = (rows_here, cols)
    row = me_ref[0] * rows_here + lax.broadcasted_iota(jnp.int32, shape, 0)
    degree = degree_of(row, shape, total_rows)
    normal = [take(sums_ref, obs_count + k, rows_here, ENTRIES) for k in range(6)]
    for b in range(obs_count // 3):
        fields = [prior_ref[3 * b + i] for i in range(3)]
        coupled = couple(normal, fields)
        for i in range(3):
            field = fields[i]
            beside = beside_columns(field)
            if rows_here > 1:
                zero = jnp.zeros((1, cols), jnp.float32)
                beside = beside + jnp.concatenate([zero, field[:-1]], axis=0) + jnp.concatenate([field[1:], zero], axis=0)
            entry = 3 * b + i
            observed = take(sums_ref, entry, rows_here, ENTRIES)
            put(sums_ref, entry, rows_here, ENTRIES, observed - coupled[i] - SMOOTH_PULL * (degree * field - beside))
    for c in range(tiles):
        out_ref[:, c * LANES : (c + 1) * LANES] = sums_ref[c]
    scales, numbers = pack([sums_ref[c] for c in range(tiles)], msg_ref, 0)
    first_ref[0] = scales
    for c in range(tiles):
        first_ref[1 + c] = numbers[c][0:16].astype(jnp.int16)
    left = jnp.concatenate([number[16:obs_count] for number in numbers], axis=0)
    spare = (first_ref.shape[0] - 1 - tiles) * 16 - left.shape[0]
    if spare:
        left = jnp.concatenate([left, jnp.zeros((spare, LANES), jnp.int32)], axis=0)
    for t in range(left.shape[0] // 16):
        first_ref[1 + tiles + t] = left[16 * t : 16 * t + 16].astype(jnp.int16)


def krylov_kernel(me_ref, own_ref, mate_ref, across_ref, zero_ref, one_ref, two_ref, gram_ref, window_ref, *, total_rows, rows_here):
    cols = own_ref.shape[1]
    obs_count = ENTRIES - 6
    tiles = cols // LANES
    row_tiles = own_ref.shape[0] // 16

    def lay(place, part, r):
        at = pl.ds(place, ENTRIES, stride=8)
        for c in range(tiles):
            window_ref[c, at, :] = part[c][r * ENTRIES : (r + 1) * ENTRIES]

    own = [own_ref[:, c * LANES : (c + 1) * LANES] for c in range(tiles)]
    mate = unpack(lambda place: mate_ref[place], row_tiles, tiles)
    across = unpack(lambda place: across_ref[place], row_tiles, tiles)
    odd = me_ref[0] % 2
    for r in range(2):
        lay(2 + r, own, r)
        lay(4 * (1 - odd) + r, mate, r)
        lay(4 * odd + r, across, r)
    for empty in (6, 7):
        put(window_ref, empty, ENTRIES, 8, jnp.zeros((ENTRIES, cols), jnp.float32))
    window = lambda entry: jnp.concatenate([window_ref[c, entry * 8 : entry * 8 + 8, :] for c in range(cols // LANES)], axis=1)
    shape = (8, cols)
    place = lax.broadcasted_iota(jnp.int32, shape, 0)
    row = me_ref[0] * rows_here + place - 2
    inside = ((row >= 0) & (row < total_rows)).astype(jnp.float32) * GAIN
    own_rows = (place == 2) | (place == 3)
    diag = inside * (PRIOR_PULL - SHIFT + SMOOTH_PULL * degree_of(row, shape, total_rows))
    pull = inside * SMOOTH_PULL
    normal = [window(obs_count + k) * inside for k in range(6)]
    acc = [jnp.zeros((8, LANES), jnp.float32) for _ in range(6)]

    def apply(v, last=False):
        coupled = couple(normal, v)
        out = []
        for i in range(3):
            x = v[i]
            above = pltpu.roll(x, 7, axis=0)
            beside = beside_columns(x) + (2.0 * above if last else above + pltpu.roll(x, 1, axis=0))
            out.append(coupled[i] + diag * x - pull * beside)
        return out

    def fold(x):
        total = x[:, 0:LANES]
        for c in range(LANES, cols, LANES):
            total = total + x[:, c : c + LANES]
        return total

    for b in range(obs_count // 3):
        zero = [window(3 * b + i) for i in range(3)]
        one = apply(zero)
        two = apply(one)
        three = apply(two, last=True)
        for i in range(3):
            zero_ref[3 * b + i] = zero[i][2:4]
            one_ref[3 * b + i] = one[i][2:4]
            two_ref[3 * b + i] = two[i][2:4]
            v = [zero[i], one[i], two[i], three[i]]
            for k in range(6):
                acc[k] = acc[k] + fold(v[k // 2] * v[(k + 1) // 2])
    own_tile = own_rows[:, 0:LANES]
    tile_row = lax.broadcasted_iota(jnp.int32, (8, LANES), 0)
    gram = jnp.zeros((8, LANES), jnp.float32)
    for k in range(6):
        moment = jnp.sum(jnp.where(own_tile, acc[k], 0.0))
        gram = jnp.where(tile_row == k, moment, gram)
    gram_ref[...] = gram


def far_kernel(gram_ref, two_ref, far_ref, out_ref):
    obs_count, _, cols = two_ref.shape
    tiles = cols // LANES
    rest = obs_count - 16
    factors = factors_of(far_ref[0], 2)
    left = jnp.concatenate([as_float(far_ref[t]) for t in range(1 + tiles, far_ref.shape[0])], axis=0)
    total = jnp.zeros((obs_count, LANES), jnp.float32)
    for c in range(tiles):
        far = jnp.concatenate([as_float(far_ref[1 + c]) * factors[0], left[rest * c : rest * (c + 1)] * factors[1][0:rest]], axis=0)
        mine = jnp.concatenate([two_ref[e, 1:2, c * LANES : (c + 1) * LANES] for e in range(obs_count)], axis=0)
        total = total + far * mine
    part = (-2.0 * (GAIN * SMOOTH_PULL) ** 3) * jnp.sum(total)
    row = lax.broadcasted_iota(jnp.int32, (8, LANES), 0)
    out_ref[...] = gram_ref[...] + jnp.where(row == 5, part, 0.0)


def combine_kernel(*refs):
    *gram_refs, prior_ref, zero_ref, one_ref, two_ref, out_ref = refs
    gram = gram_refs[0][...]
    for ref in gram_refs[1:]:
        gram = gram + ref[...]
    m = [gram[k : k + 1, :] for k in range(6)]
    h = {(i, j): m[i + j + 1] * (1.0 / GAIN) + SHIFT * m[i + j] for i in range(3) for j in range(i, 3)}
    l10 = h[0, 1] / h[0, 0]
    l20 = h[0, 2] / h[0, 0]
    d1 = h[1, 1] - l10 * h[0, 1]
    t = h[1, 2] - l20 * h[0, 1]
    ok1 = d1 > 1e-6 * h[1, 1]
    inv1 = jnp.where(ok1, 1.0 / jnp.where(ok1, d1, 1.0), 0.0)
    l21 = t * inv1
    d2 = h[2, 2] - l20 * h[0, 2] - l21 * t
    ok2 = ok1 & (d2 > 1e-6 * h[2, 2])
    inv2 = jnp.where(ok2, 1.0 / jnp.where(ok2, d2, 1.0), 0.0)
    z1 = m[1] - l10 * m[0]
    z2 = m[2] - l20 * m[0] - l21 * z1
    y2 = z2 * inv2
    y1 = z1 * inv1 - l21 * y2
    y0 = m[0] / h[0, 0] - l10 * y1 - l20 * y2
    cols = prior_ref.shape[2]
    for c in range(0, cols, LANES):
        lanes = slice(c, c + LANES)
        out_ref[:, :, lanes] = (
            prior_ref[:, :, lanes] + y0[None] * zero_ref[:, :, lanes] + y1[None] * one_ref[:, :, lanes] + y2[None] * two_ref[:, :, lanes]
        )


def on_device(reflect, clear_conf, sun_view, sensor_id, band_gain, sensor_weight, prior):
    rows_here, obs_count, cols = prior.shape
    prior = jnp.transpose(prior, (1, 0, 2))
    count = lax.axis_size("rows")
    total_rows = rows_here * count
    block = rows_here * ENTRIES
    tiles = cols // LANES
    me = lax.axis_index("rows").astype(jnp.int32).reshape(1)
    vmem = pl.BlockSpec(memory_space=pltpu.VMEM)
    smem = pl.BlockSpec(memory_space=pltpu.SMEM)
    params = pltpu.CompilerParams(vmem_limit_bytes=24 * 2**20)
    f32 = lambda *shape: jax.ShapeDtypeStruct(shape, jnp.float32)
    packed = lambda *shape: jax.ShapeDtypeStruct(shape + (16, LANES), jnp.int16)

    scale = 0.01 / (reflect.shape[0] * count)
    index = me
    parts = []
    for chunk in range(CHUNKS):
        kept, sent = partial_sums(
            index, reflect, clear_conf, sun_view, sensor_id, band_gain, sensor_weight, prior, scale, chunk
        )
        index, _ = lax.optimization_barrier((me, sent))
        parts.append((kept, sent))
    flip = lambda x, mask: lax.ppermute(x, "rows", [(i, i ^ mask) for i in range(count)])
    swap = lambda x, bit: flip(x, 1 << bit)
    parts = [(kept, swap(sent, 0)) for kept, sent in parts]
    bits = list(range(1, count.bit_length() - 1))
    for step in range(len(bits)):
        for chunk in range(CHUNKS):
            turned = chunk % 2 == 1 and len(bits) >= 2 and step < 2
            bit, place = (bits[1 - step], 1 - step) if turned else (bits[step], 0)
            kept, sent = add_split(me // 2**bit % 2, place, *parts[chunk])
            parts[chunk] = (kept, swap(sent, bit))
    parts = [x for part in parts for x in part]

    own, msg, first = pl.pallas_call(
        functools.partial(residual_kernel, total_rows=total_rows),
        in_specs=[smem] + [vmem] * (1 + len(parts)),
        out_specs=[vmem, vmem, vmem],
        out_shape=[f32(block, cols), packed(1, 1 + block // 16 * tiles), packed(1 + tiles + -(-(obs_count - 16) * tiles // 16))],
        scratch_shapes=[pltpu.VMEM((tiles, block, LANES), jnp.float32)],
        compiler_params=params,
        name="residual",
    )(me, prior, *parts)

    msg = msg[0]
    mate = swap(msg, 0)
    border = [(i, i + 1) for i in range(1, count - 1, 2)]
    across = lax.ppermute(msg, "rows", border + [(target, source) for source, target in border])
    far = lax.ppermute(first, "rows", [(i + 2, i) for i in range(count - 2)])
    zero, one, two, gram = pl.pallas_call(
        functools.partial(krylov_kernel, total_rows=total_rows, rows_here=rows_here),
        in_specs=[smem, vmem, vmem, vmem],
        out_specs=[vmem] * 4,
        out_shape=[f32(obs_count, rows_here, cols)] * 3 + [f32(8, LANES)],
        scratch_shapes=[pltpu.VMEM((tiles, ENTRIES * 8, LANES), jnp.float32)],
        compiler_params=params,
        name="krylov",
    )(me, own, mate, across)

    grams = [
        pl.pallas_call(
            far_kernel, in_specs=[vmem] * 3, out_specs=vmem, out_shape=f32(8, LANES), compiler_params=params, name="far"
        )(gram, two, far)
    ]
    for bit in reversed(range(0, count.bit_length() - 1, 2)):
        masks = [mask << bit for mask in (1, 2, 3) if mask << bit < count]
        gram = sum(grams[1:], grams[0])
        grams = [gram] + [flip(gram, mask) for mask in masks]
    out = pl.pallas_call(
        combine_kernel,
        in_specs=[vmem] * (len(grams) + 4),
        out_specs=vmem,
        out_shape=f32(obs_count, rows_here, cols),
        compiler_params=params,
        name="combine",
    )(*grams, prior, zero, one, two)
    return jnp.transpose(out, (1, 0, 2))


def solution(mesh):
    return jax.shard_map(
        on_device,
        mesh=mesh,
        in_specs=(
            P("rows", None, None, "tiles"),
            P("rows", None, "tiles"),
            P("rows", None, None, "tiles"),
            P(),
            P(),
            P(),
            P("rows", None, "tiles"),
        ),
        out_specs=P("rows", None, "tiles"),
        check_vma=False,
    )
```

```python
import functools
import math

import jax
import jax.numpy as jnp
from jax import lax
from jax.experimental import pallas as pl
from jax.experimental.pallas import tpu as pltpu
from jax.sharding import PartitionSpec as P

TO_RADIAN = math.pi / 18000.0
PRIOR_PULL = 0.1
SMOOTH_PULL = 0.5
SHIFT = 3.0
GAIN = 0.4
ENTRIES = 24
LANES = 128
QUANT = 32000.0
GROUP = LANES // 4
SHARES = (5, 3)


R_POLY = (0.9428089773, 0.04714460664, 0.007527079489, 0.001965302741, 9.052799897e-05, 0.0004621408027)
S_POLY = (0.6002109608, -0.09003726006, -0.007977343822, -0.001801806492, 3.702625389e-06, -0.0003981650976)
SIN_25 = (0.9999999567, -0.1666626093, 0.008276695349)
COS_25 = (0.9999999997, -0.4999999562, 0.04166553086, -0.001379415437)
SIN_15 = (0.999999998, -0.1666661418, 0.008312938059)
COS_15 = (0.9999999858, -0.4999963087, 0.04152366947)
SIN_90 = (0.9999999947, -0.1666665666, 0.008333024663, -0.00019807389, 2.601844464e-06)


def horner(coefs, x):
    acc = coefs[-1] * x + coefs[-2]
    for coef in coefs[-3::-1]:
        acc = acc * x + coef
    return acc


def of_degrees(coefs, x, x2, factor, odd):
    scaled = [factor * coef * TO_RADIAN ** (2 * k + odd) for k, coef in enumerate(coefs)]
    value = horner(scaled, x2)
    return value * x if odd else value


def ross_li(sun, view, azim):
    x = (sun - 4500).astype(jnp.float32)
    x2 = x * x
    half = math.sqrt(0.5)
    sin_x, cos_x = of_degrees(SIN_25, x, x2, half, 1), of_degrees(COS_25, x, x2, half, 0)
    cos_sun, sin_sun = cos_x - sin_x, cos_x + sin_x
    v = view.astype(jnp.float32)
    v2 = v * v
    sin_view, cos_view = of_degrees(SIN_15, v, v2, 1.0, 1), of_degrees(COS_15, v, v2, 1.0, 0)
    a = (9000 - azim).astype(jnp.float32)
    cos_azim = of_degrees(SIN_90, a, a * a, 1.0, 1)
    prod = cos_sun * cos_view
    cos_phase = prod + sin_sun * sin_view * cos_azim
    total = cos_sun + cos_view
    recip = pl.reciprocal(total * prod, approx=False)
    inv_total = recip * prod
    sec_prod = recip * total
    u = 1.0 - cos_phase
    u_up = 1.0 + cos_phase
    bent = u * (u * lax.rsqrt(u)) * horner(R_POLY, u)
    volume = (bent + (0.5 * math.pi) * cos_phase) * inv_total - 0.25 * math.pi
    sin2 = u * u_up
    sin_phase = sin2 * lax.rsqrt(sin2)
    w = jnp.maximum(1.0 - (2.0 * inv_total) * sin_phase, 1e-30)
    overlap = w * (w * lax.rsqrt(w)) * horner(S_POLY, w)
    geometric = sec_prod * (total * (overlap - 1.0) + 0.5 * u_up)
    return volume, geometric


def lane_group(shape):
    return lax.broadcasted_iota(jnp.int32, shape, len(shape) - 1) // GROUP


def pack(tiles, msg_ref, block):
    rows = tiles[0].shape[0]
    top = jnp.abs(tiles[0])
    for tile in tiles[1:]:
        top = jnp.maximum(top, jnp.abs(tile))
    for shift in (LANES // 2, LANES // 4):
        top = jnp.maximum(top, pltpu.roll(top, shift, axis=1))
    level = jnp.ceil(8.0 * jnp.log2(jnp.maximum(top, 1e-30)))
    factor = QUANT * jnp.exp2(-0.125 * level)
    group = lane_group((16, LANES))
    scales = level[0:16]
    for t in range(1, rows // 16):
        scales = jnp.where(group == t, level[16 * t : 16 * t + 16], scales)
    scales = scales.astype(jnp.int32).astype(jnp.int16)
    msg_ref[block, 0] = scales
    numbers = [jnp.round(tile * factor).astype(jnp.int32) for tile in tiles]
    for c, number in enumerate(numbers):
        coded = number.astype(jnp.int16)
        for t in range(rows // 16):
            msg_ref[block, 1 + t * len(tiles) + c] = coded[16 * t : 16 * t + 16]
    return scales, numbers


def as_float(x):
    return x.astype(jnp.int32).astype(jnp.float32)


def factors_of(scales, row_tiles):
    scales = as_float(scales)
    group = lane_group((16, LANES))
    factors = []
    for t in range(row_tiles):
        level = jnp.where(group == t, scales, 0.0)
        for shift in (LANES // 2, LANES // 4):
            level = level + pltpu.roll(level, shift, axis=1)
        factors.append(jnp.exp2(0.125 * level) * (1.0 / QUANT))
    return factors


def unpack(read, row_tiles, col_tiles):
    factors = factors_of(read(0), row_tiles)
    return [
        jnp.concatenate([as_float(read(1 + t * col_tiles + c)) * factors[t] for t in range(row_tiles)], axis=0) for c in range(col_tiles)
    ]


def sums_kernel(
    me_ref,
    ids_ref,
    gain_ref,
    weight_ref,
    reflect_hbm,
    conf_hbm,
    sun_hbm,
    prior_ref,
    keep_ref,
    msg_ref,
    sums_ref,
    kernels_ref,
    reflect_ref,
    conf_ref,
    sun_ref,
    sems,
    *,
    scale,
    rows_here,
    first_col,
):
    steps, dates, bands, tile_rows, _ = reflect_ref.shape
    lane_tiles = sums_ref.shape[0]
    me = me_ref[0]
    block = rows_here * ENTRIES
    obs_count = 3 * bands

    def copies(step):
        rows = pl.ds(pl.multiple_of(step // lane_tiles * tile_rows, tile_rows), tile_rows)
        cols = pl.ds(pl.multiple_of(first_col + step % lane_tiles * LANES, LANES), LANES)
        return (
            pltpu.make_async_copy(sun_hbm.at[:, :, rows, cols], sun_ref.at[step], sems.at[step, 0]),
            pltpu.make_async_copy(conf_hbm.at[:, rows, cols], conf_ref.at[step], sems.at[step, 1]),
            pltpu.make_async_copy(reflect_hbm.at[:, :, rows, cols], reflect_ref.at[step], sems.at[step, 2]),
        )

    def start(step, carry):
        for copy in copies(step):
            copy.start()
        return carry

    lax.fori_loop(0, steps, start, 0)

    def lane_tile(index, row_tile):
        step = row_tile * lane_tiles + index
        for copy in copies(step):
            copy.wait()
        sensors = [ids_ref[me * dates + d] for d in range(dates)]

        def store(top, entry, total):
            sums_ref[index, pl.ds(top * ENTRIES + entry, 8, stride=ENTRIES), :] = total

        def plus(total, term):
            return term if total is None else total + term

        for top in range(0, tile_rows, 8):
            here = slice(top, top + 8)
            normal = [None] * 6
            for d in range(dates):
                volume, geometric = ross_li(*[sun_ref[step, d, angle, here, :] for angle in range(3)])
                weight = conf_ref[step, d, here, :].astype(jnp.float32) * (weight_ref[sensors[d]] * scale)
                weighted_vol = weight * volume
                weighted_geo = weight * geometric
                for i, value in enumerate((weight, weighted_vol, weighted_geo)):
                    kernels_ref[d, i, here, :] = value
                terms = (weight, weighted_vol, weighted_geo, weighted_vol * volume, weighted_vol * geometric, weighted_geo * geometric)
                normal = [plus(total, term) for total, term in zip(normal, terms)]
            for k in range(6):
                store(top, obs_count + k, normal[k])
        for b in range(bands):
            observed = [None] * 3
            for d in range(dates):
                signal = reflect_ref[step, d, b].astype(jnp.float32) * gain_ref[sensors[d], b]
                observed = [plus(total, kernels_ref[d, i] * signal) for i, total in enumerate(observed)]
            for i in range(3):
                for top in range(0, tile_rows, 8):
                    store(top, 3 * b + i, observed[i][top : top + 8])
        return row_tile

    def row_tile_sums(row_tile, carry):
        lax.fori_loop(0, lane_tiles, lane_tile, row_tile)
        tiles = range(lane_tiles)
        first_row = row_tile * tile_rows
        for row, source in ((me * rows_here - 1 - first_row, 0), ((me + 1) * rows_here - first_row, rows_here - 1)):

            @pl.when((row >= 0) & (row < tile_rows))
            def _():
                for c in tiles:
                    lanes = slice(first_col + c * LANES, first_col + (c + 1) * LANES)
                    at = pl.ds(pl.multiple_of(row * ENTRIES, 8), obs_count)
                    part = jnp.concatenate([prior_ref[e, source : source + 1, lanes] for e in range(obs_count)], axis=0)
                    sums_ref[c, at, :] = sums_ref[c, at, :] + SMOOTH_PULL * part

        bit = me % 2
        per_tile = tile_rows // rows_here // 2
        for j in range(per_tile):
            own = pl.ds(pl.multiple_of((2 * j + bit) * block, 8), block)
            other = pl.ds(pl.multiple_of((2 * j + 1 - bit) * block, 8), block)
            for c in tiles:
                keep_ref[row_tile * per_tile + j, :, c * LANES : (c + 1) * LANES] = sums_ref[c, own, :]
            pack([sums_ref[c, other, :] for c in tiles], msg_ref, row_tile * per_tile + j)
        return carry

    lax.fori_loop(0, steps // lane_tiles, row_tile_sums, 0)


def partial_sums(me, reflect, clear_conf, sun_view, sensor_id, band_gain, sensor_weight, prior, scale, first_col, cols):
    dates, bands, rows, _ = reflect.shape
    rows_here = prior.shape[1]
    count = rows // rows_here
    tile_rows = 16
    block = rows_here * ENTRIES
    lane_tiles = cols // LANES
    steps = rows // tile_rows * lane_tiles
    smem = pl.BlockSpec(memory_space=pltpu.SMEM)
    vmem = pl.BlockSpec(memory_space=pltpu.VMEM)
    hbm = pl.BlockSpec(memory_space=pl.ANY)
    return pl.pallas_call(
        functools.partial(sums_kernel, scale=scale, rows_here=rows_here, first_col=first_col),
        in_specs=[smem] * 4 + [hbm] * 3 + [vmem],
        out_specs=[vmem, vmem],
        out_shape=[
            jax.ShapeDtypeStruct((count // 2, block, cols), jnp.float32),
            jax.ShapeDtypeStruct((count // 2, 1 + block // 16 * lane_tiles, 16, LANES), jnp.int16),
        ],
        scratch_shapes=[
            pltpu.VMEM((lane_tiles, tile_rows * ENTRIES, LANES), jnp.float32),
            pltpu.VMEM((dates, 3, tile_rows, LANES), jnp.float32),
            pltpu.VMEM((steps, dates, bands, tile_rows, LANES), reflect.dtype),
            pltpu.VMEM((steps, dates, tile_rows, LANES), jnp.int32),
            pltpu.VMEM((steps, dates, 3, tile_rows, LANES), jnp.int32),
            pltpu.SemaphoreType.DMA((steps, 3)),
        ],
        compiler_params=pltpu.CompilerParams(vmem_limit_bytes=(62 if first_col == 0 else 52) * 2**20),
        name="partial_sums",
    )(me, sensor_id, band_gain, sensor_weight, reflect, clear_conf, sun_view, prior)


def add_split_kernel(bit_ref, *refs, place):
    *parts, keep_ref, msg_ref = refs
    count, block, _ = keep_ref.shape
    bit = bit_ref[0]

    def total(j):
        tiles = []
        for kept_ref, got_ref in zip(parts[0::2], parts[1::2]):
            here = kept_ref.shape[2] // LANES
            came = unpack(lambda at: got_ref[j, at], block // 16, here)
            tiles += [kept_ref[j, :, c * LANES : (c + 1) * LANES] + came[c] for c in range(here)]
        return tiles

    for q in range(count):
        low = q % 2**place
        first = (q - low) * 2 + low
        pack(total(first + (1 - bit) * 2**place), msg_ref, q)
        for c, tile in enumerate(total(first + bit * 2**place)):
            keep_ref[q, :, c * LANES : (c + 1) * LANES] = tile


def add_split(bit, place, *parts):
    count, block, _ = parts[0].shape
    cols = sum(kept.shape[2] for kept in parts[0::2])
    vmem = pl.BlockSpec(memory_space=pltpu.VMEM)
    return pl.pallas_call(
        functools.partial(add_split_kernel, place=place),
        in_specs=[pl.BlockSpec(memory_space=pltpu.SMEM)] + [vmem] * len(parts),
        out_specs=[vmem, vmem],
        out_shape=[
            jax.ShapeDtypeStruct((count // 2, block, cols), jnp.float32),
            jax.ShapeDtypeStruct((count // 2, 1 + block // 16 * (cols // LANES), 16, LANES), jnp.int16),
        ],
        compiler_params=pltpu.CompilerParams(vmem_limit_bytes=24 * 2**20),
        name="add_split",
    )(bit, *parts)


def take(ref, start, size, stride):
    at = pl.ds(start, size, stride=stride)
    return jnp.concatenate([ref[c, at, :] for c in range(ref.shape[0])], axis=1)


def put(ref, start, size, stride, value):
    at = pl.ds(start, size, stride=stride)
    for c in range(ref.shape[0]):
        ref[c, at, :] = value[:, c * LANES : (c + 1) * LANES]


def beside_columns(x):
    cols = x.shape[1]
    col = lax.broadcasted_iota(jnp.int32, x.shape, 1)
    left = jnp.where(col == 0, 0.0, pltpu.roll(x, 1, axis=1))
    right = jnp.where(col == cols - 1, 0.0, pltpu.roll(x, cols - 1, axis=1))
    return left + right


def degree_of(row, shape, total_rows):
    col = lax.broadcasted_iota(jnp.int32, shape, 1)
    edge = (
        (row == 0).astype(jnp.float32)
        + (row == total_rows - 1).astype(jnp.float32)
        + (col == 0).astype(jnp.float32)
        + (col == shape[1] - 1).astype(jnp.float32)
    )
    return 4.0 - edge


def couple(n, v):
    return (
        n[0] * v[0] + n[1] * v[1] + n[2] * v[2],
        n[1] * v[0] + n[3] * v[1] + n[4] * v[2],
        n[2] * v[0] + n[4] * v[1] + n[5] * v[2],
    )


def residual_kernel(me_ref, prior_ref, *refs, total_rows):
    obs_count, rows_here, cols = prior_ref.shape
    *parts, out_ref, msg_ref, first_ref, sums_ref = refs
    block = rows_here * ENTRIES
    tiles = cols // LANES
    at = 0
    for kept_ref, got_ref in zip(parts[0::2], parts[1::2]):
        here = kept_ref.shape[2] // LANES
        came = unpack(lambda place: got_ref[0, place], block // 16, here)
        for c in range(here):
            sums_ref[at] = kept_ref[0, :, c * LANES : (c + 1) * LANES] + came[c]
            at += 1
    shape = (rows_here, cols)
    row = me_ref[0] * rows_here + lax.broadcasted_iota(jnp.int32, shape, 0)
    degree = degree_of(row, shape, total_rows)
    normal = [take(sums_ref, obs_count + k, rows_here, ENTRIES) for k in range(6)]
    for b in range(obs_count // 3):
        fields = [prior_ref[3 * b + i] for i in range(3)]
        coupled = couple(normal, fields)
        for i in range(3):
            field = fields[i]
            beside = beside_columns(field)
            if rows_here > 1:
                zero = jnp.zeros((1, cols), jnp.float32)
                beside = beside + jnp.concatenate([zero, field[:-1]], axis=0) + jnp.concatenate([field[1:], zero], axis=0)
            entry = 3 * b + i
            observed = take(sums_ref, entry, rows_here, ENTRIES)
            put(sums_ref, entry, rows_here, ENTRIES, observed - coupled[i] - SMOOTH_PULL * (degree * field - beside))
    for c in range(tiles):
        out_ref[:, c * LANES : (c + 1) * LANES] = sums_ref[c]
    scales, numbers = pack([sums_ref[c] for c in range(tiles)], msg_ref, 0)
    first_ref[0] = scales
    for c in range(tiles):
        first_ref[1 + c] = numbers[c][0:16].astype(jnp.int16)
    left = jnp.concatenate([number[16:obs_count] for number in numbers], axis=0)
    spare = (first_ref.shape[0] - 1 - tiles) * 16 - left.shape[0]
    if spare:
        left = jnp.concatenate([left, jnp.zeros((spare, LANES), jnp.int32)], axis=0)
    for t in range(left.shape[0] // 16):
        first_ref[1 + tiles + t] = left[16 * t : 16 * t + 16].astype(jnp.int16)


def krylov_kernel(me_ref, own_ref, mate_ref, across_ref, zero_ref, one_ref, two_ref, gram_ref, window_ref, *, total_rows, rows_here):
    cols = own_ref.shape[1]
    obs_count = ENTRIES - 6
    tiles = cols // LANES
    row_tiles = own_ref.shape[0] // 16

    def lay(place, part, r):
        at = pl.ds(place, ENTRIES, stride=8)
        for c in range(tiles):
            window_ref[c, at, :] = part[c][r * ENTRIES : (r + 1) * ENTRIES]

    own = [own_ref[:, c * LANES : (c + 1) * LANES] for c in range(tiles)]
    mate = unpack(lambda place: mate_ref[place], row_tiles, tiles)
    across = unpack(lambda place: across_ref[place], row_tiles, tiles)
    odd = me_ref[0] % 2
    for r in range(2):
        lay(2 + r, own, r)
        lay(4 * (1 - odd) + r, mate, r)
        lay(4 * odd + r, across, r)
    for empty in (6, 7):
        put(window_ref, empty, ENTRIES, 8, jnp.zeros((ENTRIES, cols), jnp.float32))
    window = lambda entry: jnp.concatenate([window_ref[c, entry * 8 : entry * 8 + 8, :] for c in range(cols // LANES)], axis=1)
    shape = (8, cols)
    place = lax.broadcasted_iota(jnp.int32, shape, 0)
    row = me_ref[0] * rows_here + place - 2
    inside = ((row >= 0) & (row < total_rows)).astype(jnp.float32) * GAIN
    own_rows = (place == 2) | (place == 3)
    diag = inside * (PRIOR_PULL - SHIFT + SMOOTH_PULL * degree_of(row, shape, total_rows))
    pull = inside * SMOOTH_PULL
    normal = [window(obs_count + k) * inside for k in range(6)]
    acc = [jnp.zeros((8, LANES), jnp.float32) for _ in range(6)]

    def apply(v, last=False):
        coupled = couple(normal, v)
        out = []
        for i in range(3):
            x = v[i]
            above = pltpu.roll(x, 7, axis=0)
            beside = beside_columns(x) + (2.0 * above if last else above + pltpu.roll(x, 1, axis=0))
            out.append(coupled[i] + diag * x - pull * beside)
        return out

    def fold(x):
        total = x[:, 0:LANES]
        for c in range(LANES, cols, LANES):
            total = total + x[:, c : c + LANES]
        return total

    for b in range(obs_count // 3):
        zero = [window(3 * b + i) for i in range(3)]
        one = apply(zero)
        two = apply(one)
        three = apply(two, last=True)
        for i in range(3):
            zero_ref[3 * b + i] = zero[i][2:4]
            one_ref[3 * b + i] = one[i][2:4]
            two_ref[3 * b + i] = two[i][2:4]
            v = [zero[i], one[i], two[i], three[i]]
            for k in range(6):
                acc[k] = acc[k] + fold(v[k // 2] * v[(k + 1) // 2])
    own_tile = own_rows[:, 0:LANES]
    tile_row = lax.broadcasted_iota(jnp.int32, (8, LANES), 0)
    gram = jnp.zeros((8, LANES), jnp.float32)
    for k in range(6):
        moment = jnp.sum(jnp.where(own_tile, acc[k], 0.0))
        gram = jnp.where(tile_row == k, moment, gram)
    gram_ref[...] = gram


def far_kernel(gram_ref, two_ref, far_ref, out_ref):
    obs_count, _, cols = two_ref.shape
    tiles = cols // LANES
    rest = obs_count - 16
    factors = factors_of(far_ref[0], 2)
    left = jnp.concatenate([as_float(far_ref[t]) for t in range(1 + tiles, far_ref.shape[0])], axis=0)
    total = jnp.zeros((obs_count, LANES), jnp.float32)
    for c in range(tiles):
        far = jnp.concatenate([as_float(far_ref[1 + c]) * factors[0], left[rest * c : rest * (c + 1)] * factors[1][0:rest]], axis=0)
        mine = jnp.concatenate([two_ref[e, 1:2, c * LANES : (c + 1) * LANES] for e in range(obs_count)], axis=0)
        total = total + far * mine
    part = (-2.0 * (GAIN * SMOOTH_PULL) ** 3) * jnp.sum(total)
    row = lax.broadcasted_iota(jnp.int32, (8, LANES), 0)
    out_ref[...] = gram_ref[...] + jnp.where(row == 5, part, 0.0)


def combine_kernel(*refs):
    *gram_refs, prior_ref, zero_ref, one_ref, two_ref, out_ref = refs
    gram = gram_refs[0][...]
    for ref in gram_refs[1:]:
        gram = gram + ref[...]
    m = [gram[k : k + 1, :] for k in range(6)]
    h = {(i, j): m[i + j + 1] * (1.0 / GAIN) + SHIFT * m[i + j] for i in range(3) for j in range(i, 3)}
    l10 = h[0, 1] / h[0, 0]
    l20 = h[0, 2] / h[0, 0]
    d1 = h[1, 1] - l10 * h[0, 1]
    t = h[1, 2] - l20 * h[0, 1]
    ok1 = d1 > 1e-6 * h[1, 1]
    inv1 = jnp.where(ok1, 1.0 / jnp.where(ok1, d1, 1.0), 0.0)
    l21 = t * inv1
    d2 = h[2, 2] - l20 * h[0, 2] - l21 * t
    ok2 = ok1 & (d2 > 1e-6 * h[2, 2])
    inv2 = jnp.where(ok2, 1.0 / jnp.where(ok2, d2, 1.0), 0.0)
    z1 = m[1] - l10 * m[0]
    z2 = m[2] - l20 * m[0] - l21 * z1
    y2 = z2 * inv2
    y1 = z1 * inv1 - l21 * y2
    y0 = m[0] / h[0, 0] - l10 * y1 - l20 * y2
    cols = prior_ref.shape[2]
    for c in range(0, cols, LANES):
        lanes = slice(c, c + LANES)
        out_ref[:, :, lanes] = (
            prior_ref[:, :, lanes] + y0[None] * zero_ref[:, :, lanes] + y1[None] * one_ref[:, :, lanes] + y2[None] * two_ref[:, :, lanes]
        )


def on_device(reflect, clear_conf, sun_view, sensor_id, band_gain, sensor_weight, prior):
    rows_here, obs_count, cols = prior.shape
    prior = jnp.transpose(prior, (1, 0, 2))
    count = lax.axis_size("rows")
    total_rows = rows_here * count
    block = rows_here * ENTRIES
    tiles = cols // LANES
    me = lax.axis_index("rows").astype(jnp.int32).reshape(1)
    vmem = pl.BlockSpec(memory_space=pltpu.VMEM)
    smem = pl.BlockSpec(memory_space=pltpu.SMEM)
    params = pltpu.CompilerParams(vmem_limit_bytes=24 * 2**20)
    f32 = lambda *shape: jax.ShapeDtypeStruct(shape, jnp.float32)
    packed = lambda *shape: jax.ShapeDtypeStruct(shape + (16, LANES), jnp.int16)

    scale = 0.01 / (reflect.shape[0] * count)
    index = me
    parts = []
    for chunk, share in enumerate(SHARES):
        part = cols // sum(SHARES)
        first_col = part * sum(SHARES[:chunk])
        kept, sent = partial_sums(
            index, reflect, clear_conf, sun_view, sensor_id, band_gain, sensor_weight, prior, scale, first_col, part * share
        )
        index, _ = lax.optimization_barrier((me, sent))
        parts.append((kept, sent))
    flip = lambda x, mask: lax.ppermute(x, "rows", [(i, i ^ mask) for i in range(count)])
    swap = lambda x, bit: flip(x, 1 << bit)
    parts = [(kept, swap(sent, 0)) for kept, sent in parts]
    bits = list(range(1, count.bit_length() - 1))
    for step in range(len(bits)):
        for chunk in range(len(SHARES)):
            turned = chunk % 2 == 1 and len(bits) >= 2 and step < 2
            bit, place = (bits[1 - step], 1 - step) if turned else (bits[step], 0)
            kept, sent = add_split(me // 2**bit % 2, place, *parts[chunk])
            parts[chunk] = (kept, swap(sent, bit))
    parts = [x for part in parts for x in part]

    own, msg, first = pl.pallas_call(
        functools.partial(residual_kernel, total_rows=total_rows),
        in_specs=[smem] + [vmem] * (1 + len(parts)),
        out_specs=[vmem, vmem, vmem],
        out_shape=[f32(block, cols), packed(1, 1 + block // 16 * tiles), packed(1 + tiles + -(-(obs_count - 16) * tiles // 16))],
        scratch_shapes=[pltpu.VMEM((tiles, block, LANES), jnp.float32)],
        compiler_params=params,
        name="residual",
    )(me, prior, *parts)

    msg = msg[0]
    mate = swap(msg, 0)
    border = [(i, i + 1) for i in range(1, count - 1, 2)]
    across = lax.ppermute(msg, "rows", border + [(target, source) for source, target in border])
    far = lax.ppermute(first, "rows", [(i + 2, i) for i in range(count - 2)])
    zero, one, two, gram = pl.pallas_call(
        functools.partial(krylov_kernel, total_rows=total_rows, rows_here=rows_here),
        in_specs=[smem, vmem, vmem, vmem],
        out_specs=[vmem] * 4,
        out_shape=[f32(obs_count, rows_here, cols)] * 3 + [f32(8, LANES)],
        scratch_shapes=[pltpu.VMEM((tiles, ENTRIES * 8, LANES), jnp.float32)],
        compiler_params=params,
        name="krylov",
    )(me, own, mate, across)

    grams = [
        pl.pallas_call(
            far_kernel, in_specs=[vmem] * 3, out_specs=vmem, out_shape=f32(8, LANES), compiler_params=params, name="far"
        )(gram, two, far)
    ]
    for bit in range(0, count.bit_length() - 1, 2):
        masks = [mask << bit for mask in (1, 2, 3) if mask << bit < count]
        gram = sum(grams[1:], grams[0])
        grams = [gram] + [flip(gram, mask) for mask in masks]
    out = pl.pallas_call(
        combine_kernel,
        in_specs=[vmem] * (len(grams) + 4),
        out_specs=vmem,
        out_shape=f32(obs_count, rows_here, cols),
        compiler_params=params,
        name="combine",
    )(*grams, prior, zero, one, two)
    return jnp.transpose(out, (1, 0, 2))


def solution(mesh):
    return jax.shard_map(
        on_device,
        mesh=mesh,
        in_specs=(
            P("rows", None, None, "tiles"),
            P("rows", None, "tiles"),
            P("rows", None, None, "tiles"),
            P(),
            P(),
            P(),
            P("rows", None, "tiles"),
        ),
        out_specs=P("rows", None, "tiles"),
        check_vma=False,
    )
```
